32 devices in a mesh: dp: 4 (over z), fsdp: 8 (over y, x, core).
Axes of the slice: x: 2, y: 2, z: 4, core: 2. Of those that a mesh axis runs over, the one named last changes fastest.
Arguments:
- tokens: bfloat16 [128, 64, 768], P(('dp', 'fsdp')), may hold values from -6 to 6
- memory: bfloat16 [128, 228, 768], P(('dp', 'fsdp')), may hold values from -6 to 6
- lengths: int32 [128], P(('dp', 'fsdp')), may hold values from 1 to 64, 5120 in all
- cotangent: bfloat16 [128, 64, 768], P(('dp', 'fsdp')), may hold values from -6 to 6
- self_qkv: bfloat16 [768, 2304], P(('dp', 'fsdp')), may hold values from -0.21875 to 0.21875
- self_out: bfloat16 [768, 768], P(('dp', 'fsdp')), may hold values from -0.5 to 0.5
- cross_q: bfloat16 [768, 768], P(('dp', 'fsdp')), may hold values from -0.21875 to 0.21875
- cross_kv: bfloat16 [768, 1536], P(('dp', 'fsdp')), may hold values from -0.21875 to 0.21875
- cross_out: bfloat16 [768, 768], P(('dp', 'fsdp')), may hold values from -0.875 to 0.875
- mlp_in: bfloat16 [768, 3072], P(('dp', 'fsdp')), may hold values from -0.21875 to 0.21875
- mlp_out: bfloat16 [3072, 768], P(('dp', 'fsdp')), may hold values from -0.15625 to 0.15625
- norm_gains: bfloat16 [3, 768], P(None, ('dp', 'fsdp')), may hold values from 0.099609375 to 1.8984375
- norm_biases: bfloat16 [3, 768], P(None, ('dp', 'fsdp')), may hold values from -1.5 to 1.5
Outputs:
- output: bfloat16 [128, 64, 768], P(('dp', 'fsdp'))
- grad_tokens: bfloat16 [128, 64, 768], P(('dp', 'fsdp'))
- grad_memory: bfloat16 [128, 228, 768], P(('dp', 'fsdp'))
- grad_self_qkv: float32 [768, 2304], P(('dp', 'fsdp'))
- grad_self_out: float32 [768, 768], P(('dp', 'fsdp'))
- grad_cross_q: float32 [768, 768], P(('dp', 'fsdp'))
- grad_cross_kv: float32 [768, 1536], P(('dp', 'fsdp'))
- grad_cross_out: float32 [768, 768], P(('dp', 'fsdp'))
- grad_mlp_in: float32 [768, 3072], P(('dp', 'fsdp'))
- grad_mlp_out: float32 [3072, 768], P(('dp', 'fsdp'))
- grad_gains: float32 [3, 768], P(None, ('dp', 'fsdp'))
- grad_biases: float32 [3, 768], P(None, ('dp', 'fsdp'))
The draws below stay inside these ranges and needn't reach their ends.
Inputs may be any that keep to these rules, and one draw needn't show every extreme that they name: `lengths`: slots of a suffix at or beyond its length are padding; some suffix has length 64.
All inputs are finite; a program needn't handle non-finite values. No bound on the sum of `lengths` on one device may be relied on, other than what follows from the above.
Results may differ from the reference program's by a relative error of at most 0.02.
Values may be sent and summed in bfloat16 or wider, within the bound.
No kernel may reach another device: no remote copies, remote signals or barrier semaphores. Data moves between devices by JAX's collectives and lax.ppermute only.
A program may use at most 192 MiB of HBM per device.

```python
import math
import jax
import jax.numpy as jnp
import numpy as np
from jax import lax

D = 768
HEADS = 12
HEAD = 64
FF = 3072
LEN = 64
MEM = 228
SEQS = 128


def shard_levels(own_key, extent, cuts, low, top_value):
    def one(axis_at, shards_of):
        heights = jax.random.uniform(jax.random.fold_in(jax.random.fold_in(own_key, 6), axis_at), (shards_of,), jnp.float32, low / len(cuts), top_value / len(cuts))
        return jnp.repeat(jnp.exp(heights), extent[axis_at] // shards_of).reshape((-1,) + (1,) * (len(extent) - axis_at - 1))

    level = one(*cuts[0])
    for cut in cuts[1:]:
        level = level * one(*cut)
    return level


def length_profile(count, total, limit, slope):
    loads = [(1 << 20) // math.isqrt(rank ** slope) + 1 for rank in range(2, count + 1)]
    spare, holding = total - limit - (count - 1), [1] * (count - 1)
    while spare > 0:
        free = [i for i in range(count - 1) if holding[i] < limit]
        mass, left = sum([loads[i] for i in free]), spare
        for i in free:
            more = min(limit - holding[i], max(1, left * loads[i] // mass), spare)
            holding[i] = holding[i] + more
            spare = spare - more
    return np.array([limit] + holding)


def ragged_sizes(rng, count, total, most, lean):
    if count == 2:
        one = jax.random.randint(rng, (), max(1, total - most), min(most, total - 1) + 1)
        return jnp.stack([one, total - one])
    tallies = jnp.asarray(length_profile(count, total, most, lean), jnp.int32)
    pairs = (count - 1) // 2
    source_of, sink = tallies[1:1 + 2 * pairs:2], tallies[2:2 + 2 * pairs:2]
    room = jnp.minimum(source_of - 1, most - sink)
    moved = jax.random.randint(jax.random.fold_in(rng, 1), (pairs,), 0, 1 << 20) % (room + 1)
    tallies = tallies.at[1:1 + 2 * pairs:2].set(source_of - moved).at[2:2 + 2 * pairs:2].set(sink + moved)
    return tallies[jax.random.permutation(jax.random.fold_in(rng, 2), count)]


def centred(rng, extent, width, bound, split=(), kind=jnp.bfloat16):
    values = width * jax.random.normal(rng, extent, jnp.float32)
    if split:
        values = values * shard_levels(rng, extent, split, -0.22, 0.18)
    return jnp.clip(values, -bound, bound).astype(kind)


def setup_inputs(seed: int = 0) -> dict:
    splits = jax.random.split(jax.random.key(seed), 14)
    tokens = centred(splits[0], (SEQS, LEN, D), 1.0, 6.0, ((0, 32),))
    memory = centred(splits[1], (SEQS, MEM, D), 1.0, 6.0, ((0, 32),))
    lengths = ragged_sizes(splits[2], SEQS, SEQS * 5 * LEN // 8, LEN, 2).astype(jnp.int32)
    cotangent = centred(splits[3], (SEQS, LEN, D), 1.0, 6.0, ((0, 32),))
    self_qkv = centred(splits[4], (D, 3 * D), D ** -0.5, 0.21875, ((0, 32),))
    self_out = centred(splits[5], (D, D), (D // 6) ** -0.5, 0.5, ((0, 32),))
    cross_q = centred(splits[6], (D, D), D ** -0.5, 0.21875, ((0, 32),))
    cross_kv = centred(splits[7], (D, 2 * D), D ** -0.5, 0.21875, ((0, 32),))
    cross_out = centred(splits[8], (D, D), (D // 16) ** -0.5, 0.875, ((0, 32),))
    mlp_in = centred(splits[9], (D, FF), D ** -0.5, 0.21875, ((0, 32),))
    mlp_out = centred(splits[10], (FF, D), (FF // 2) ** -0.5, 0.15625, ((0, 32),))
    norm_gains = jnp.clip(1.0 + 0.18 * jax.random.normal(splits[11], (3, D), jnp.float32), 0.099609375, 1.8984375).astype(jnp.bfloat16)
    norm_biases = centred(splits[12], (3, D), 0.3, 1.5, ((1, 32),))
    return {"tokens": tokens, "memory": memory, "lengths": lengths, "cotangent": cotangent, "self_qkv": self_qkv, "self_out": self_out, "cross_q": cross_q, "cross_kv": cross_kv, "cross_out": cross_out, "mlp_in": mlp_in, "mlp_out": mlp_out, "norm_gains": norm_gains, "norm_biases": norm_biases}


@jax.custom_vjp
def low(v):
    return lax.optimization_barrier(v.astype(jnp.bfloat16)).astype(jnp.float32)

@jax.custom_vjp
def low_back(v):
    return v

def low_keep(v):
    return (low(v), None)

def low_pass(kept, grad):
    return (grad,)

def back_keep(v):
    return (v, None)

def back_low(kept, grad):
    return (low(grad),)
low.defvjp(low_keep, low_pass)
low_back.defvjp(back_keep, back_low)
highest = lax.Precision.HIGHEST
epsilon = 1e-06
big_negative = -1e+30

def both_ways(v):
    return low(low_back(v))

def norm_rows(values, gain, bias):
    mean = lax.optimization_barrier(jnp.mean(values, -1, keepdims=True))
    centered = values - mean
    spread = lax.optimization_barrier(jnp.mean(centered * centered, -1, keepdims=True))
    return centered * lax.rsqrt(spread + epsilon) * gain + bias

def project(values, weight):
    return jnp.einsum('bld,de->ble', values, weight, precision=highest)

def heads_of(values):
    return values.reshape(values.shape[0], values.shape[1], HEADS, HEAD)

def attend(query, keys, values, valid):
    scores = jnp.einsum('bqhe,bkhe->bhqk', query, keys, precision=highest) * HEAD ** (-0.5)
    scores = low_back(scores)
    scores = jnp.where(valid[:, None], scores, big_negative)
    peak = lax.optimization_barrier(jnp.max(scores, -1, keepdims=True))
    expo = jnp.exp(scores - peak)
    probs = low(expo / lax.optimization_barrier(jnp.sum(expo, -1, keepdims=True)))
    mixed = jnp.einsum('bhqk,bkhe->bqhe', probs, values, precision=highest)
    return both_ways(mixed.reshape(mixed.shape[0], mixed.shape[1], D))

def layer(tokens, memory, self_qkv, self_out, cross_q, cross_kv, cross_out, mlp_in, mlp_out, norm_gains, norm_biases, valid):
    first = low(norm_rows(tokens, norm_gains[0], norm_biases[0]))
    packed = both_ways(project(first, self_qkv))
    query = heads_of(packed[..., :D])
    keys = heads_of(packed[..., D:2 * D])
    values = heads_of(packed[..., 2 * D:])
    resid_one = tokens + low_back(project(attend(query, keys, values, valid), self_out))
    second = low(norm_rows(resid_one, norm_gains[1], norm_biases[1]))
    cross_query = heads_of(both_ways(project(second, cross_q)))
    cross_packed = both_ways(project(memory, cross_kv))
    full = jnp.ones((tokens.shape[0], tokens.shape[1], memory.shape[1]), bool)
    cross_mixed = attend(cross_query, heads_of(cross_packed[..., :D]), heads_of(cross_packed[..., D:]), full)
    resid_two = resid_one + low_back(project(cross_mixed, cross_out))
    third = low(norm_rows(resid_two, norm_gains[2], norm_biases[2]))
    inner = low_back(project(third, mlp_in))
    hidden = low(jax.nn.gelu(inner, approximate=False))
    return resid_two + low_back(project(hidden, mlp_out))

def reference(tokens, memory, lengths, cotangent, self_qkv, self_out, cross_q, cross_kv, cross_out, mlp_in, mlp_out, norm_gains, norm_biases):
    weights = tuple((w.astype(jnp.float32) for w in (self_qkv, self_out, cross_q, cross_kv, cross_out, mlp_in, mlp_out, norm_gains, norm_biases)))
    group = math.gcd(SEQS, 64)
    count = SEQS // group
    tok_all = tokens.astype(jnp.float32).reshape(count, group, LEN, D)
    mem_all = memory.astype(jnp.float32).reshape(count, group, MEM, D)
    cot_all = cotangent.astype(jnp.float32).reshape(count, group, LEN, D)
    len_all = lengths.astype(jnp.int32).reshape(count, group)
    positions = jnp.arange(LEN, dtype=jnp.int32)
    causal = positions[:, None] >= positions[None, :]

    def step(totals, pieces):
        tok_group, mem_group, len_group, cot_group = pieces
        live = positions[None, :] < len_group[:, None]
        valid = causal[None] & live[:, None, :]

        def forward(tok_value, mem_value, *weight_values):
            return layer(tok_value, mem_value, *weight_values, valid)
        result, pull = jax.vjp(forward, tok_group, mem_group, *weights)
        grads = pull(cot_group * live[..., None].astype(cot_group.dtype))
        totals = tuple((t + g for t, g in zip(totals, grads[2:])))
        return (totals, (result, grads[0], grads[1]))
    zeros = tuple((jnp.zeros_like(w) for w in weights))
    totals, (results, grad_tok, grad_mem) = lax.scan(step, zeros, (tok_all, mem_all, len_all, cot_all))
    output = results.reshape(SEQS, LEN, D).astype(jnp.bfloat16)
    grad_tokens = grad_tok.reshape(SEQS, LEN, D).astype(jnp.bfloat16)
    grad_memory = grad_mem.reshape(SEQS, MEM, D).astype(jnp.bfloat16)
    return (output, grad_tokens, grad_memory, totals[0], totals[1], totals[2], totals[3], totals[4], totals[5], totals[6], totals[7], totals[8])
```

```python
import jax
import jax.numpy as jnp
import numpy as np
from jax import lax
from jax.experimental import pallas as pl
from jax.experimental.pallas import tpu as pltpu
from jax.sharding import PartitionSpec as P

AXES = ("dp", "fsdp")
HEADS = 12
HALF = HEADS // 2
HEAD = 64
D = 768
DH = D // 2
LEN = 64
EPS = 1e-06
NEG = -1e30
SCALE = HEAD ** (-0.5)
F32 = jnp.float32
BF = jnp.bfloat16
VMEM_LIMIT = 48 << 20

VM = pl.BlockSpec(memory_space=pltpu.VMEM)
SM = pl.BlockSpec(memory_space=pltpu.SMEM)
ANY = pl.BlockSpec(memory_space=pl.ANY)


def sds(shape, dtype):
    return jax.ShapeDtypeStruct(shape, dtype)


def kernel_call(body, ins, in_specs, outs, out_specs=None, scratch=(), flops=0):
    nbytes = sum(int(np.prod(a.shape)) * a.dtype.itemsize for a in list(ins) + list(outs))
    return pl.pallas_call(
        body,
        out_shape=list(outs),
        in_specs=list(in_specs),
        out_specs=[VM] * len(outs) if out_specs is None else list(out_specs),
        scratch_shapes=list(scratch),
        compiler_params=pltpu.CompilerParams(vmem_limit_bytes=VMEM_LIMIT),
        cost_estimate=pl.CostEstimate(flops=flops, bytes_accessed=nbytes, transcendentals=0),
    )(*ins)


def nn(a, b):
    return lax.dot_general(a, b, (((1,), (0,)), ((), ())), preferred_element_type=F32)


def nt(a, b):
    return lax.dot_general(a, b, (((1,), (1,)), ((), ())), preferred_element_type=F32)


def tn(a, b):
    return lax.dot_general(a, b, (((0,), (0,)), ((), ())), preferred_element_type=F32)


def normalise(v):
    mean = jnp.mean(v, -1, keepdims=True)
    cen = v - mean
    inv = lax.rsqrt(jnp.mean(cen * cen, -1, keepdims=True) + EPS)
    return cen * inv, inv


def norm_back(v, gain, dy):
    xhat, inv = normalise(v)
    dxh = dy * gain
    m1 = jnp.mean(dxh, -1, keepdims=True)
    m2 = jnp.mean(dxh * xhat, -1, keepdims=True)
    dx = inv * (dxh - m1 - xhat * m2)
    return dx, jnp.sum(dy * xhat, 0, keepdims=True), jnp.sum(dy, 0, keepdims=True)


def head_of_lane(rows):
    return lax.shift_right_logical(lax.broadcasted_iota(jnp.int32, (rows, DH), 1), 6)


def spread(q):
    head = head_of_lane(1)
    parts = [q * (head == h).astype(F32).astype(q.dtype) for h in range(HALF)]
    return jnp.concatenate(parts, 0)


def fold(o):
    head = head_of_lane(LEN)
    total = jnp.where(head == 0, o[:LEN], 0.0)
    for h in range(1, HALF):
        total = jnp.where(head == h, o[h * LEN : (h + 1) * LEN], total)
    return total


def attend(q, k, v, allowed):
    st = nt(k, spread(q)) * SCALE
    st = jnp.where(allowed, st, NEG)
    e = jnp.exp(st - jnp.max(st, 0, keepdims=True))
    p = (e * (1.0 / jnp.sum(e, 0, keepdims=True))).astype(BF)
    return p, fold(tn(p, v)).astype(BF)


def attend_back(g, q, k, v, p):
    gs, qs = spread(g), spread(q)
    dp = nt(v, gs)
    pf = p.astype(F32)
    t = pf * dp
    ds = (t - pf * jnp.sum(t, 0, keepdims=True)).astype(BF)
    dq = (fold(tn(ds, k)) * SCALE).astype(BF)
    dk = (nn(ds, qs) * SCALE).astype(BF)
    dv = nn(p, gs).astype(BF)
    return dq, dk, dv


def seq_rows(s):
    return pl.ds(pl.multiple_of(s * LEN, LEN), LEN)


def half_lanes(c):
    return pl.ds(pl.multiple_of(c * DH, DH), DH)


def loop(n, body, unroll=1):
    def step(i, carry):
        body(i)
        return carry

    lax.fori_loop(0, n, step, 0, unroll=unroll)


def assemble_kernel(cols, blk, offs_ref, *refs):
    n = len(cols)
    pieces, outs, sems = refs[:4], refs[4 : 4 + n], refs[4 + n]
    copies = []
    for q in range(4):
        for r in range(4):
            for o, (lo, hi, which) in enumerate(cols):
                row = pl.multiple_of(offs_ref[which, q * 4 + r] * blk, 16)
                copies.append(
                    pltpu.make_async_copy(
                        pieces[q].at[pl.ds(r * blk, blk), pl.ds(lo, hi - lo)],
                        outs[o].at[pl.ds(row, blk), :],
                        sems.at[(q * 4 + r) * n + o],
                    )
                )
    for cp in copies:
        cp.start()
    for cp in copies:
        cp.wait()


def assemble(pieces, offs, cols):
    blk = pieces[0].shape[0] // 4
    body = lambda *refs: assemble_kernel(cols, blk, *refs)
    outs = [sds((16 * blk, hi - lo), BF) for lo, hi, _ in cols]
    return kernel_call(
        body,
        [offs, *pieces],
        [SM] + [ANY] * 4,
        outs,
        [ANY] * len(outs),
        [pltpu.SemaphoreType.DMA((16 * len(cols),))],
    )


def send_out(dw, offs_ref, outs, sems, blk):
    copies = []
    for q in range(4):
        for r in range(4):
            row = pl.multiple_of(offs_ref[0, q * 4 + r] * blk, 16)
            copies.append(
                pltpu.make_async_copy(
                    dw.at[pl.ds(row, blk), :],
                    outs[q].at[pl.ds(r * blk, blk), :],
                    sems.at[q * 4 + r],
                )
            )
    for cp in copies:
        cp.start()
    for cp in copies:
        cp.wait()


def self_kernel(lens, core, tok, gcol, wqkv, wkeep, wrecv, first, packed, probs, mixed, partial, vec):
    c = core[0]
    vec[...] = jnp.transpose(gcol[...].astype(F32))[:8]
    gain, bias = vec[0:1], vec[3:4]

    def norm(s):
        xhat, _ = normalise(tok[seq_rows(s), :].astype(F32))
        first[seq_rows(s), :] = (xhat * gain + bias).astype(BF)

    loop(8, norm)

    def proj(b):
        rows = pl.ds(pl.multiple_of(b * 256, 256), 256)
        packed[rows, :] = nn(first[rows, :], wqkv[...]).astype(BF)

    loop(2, proj)
    key = lax.broadcasted_iota(jnp.int32, (LEN, DH), 0)
    query = lax.broadcasted_iota(jnp.int32, (LEN, DH), 1) & (LEN - 1)

    def att(s):
        allowed = (key <= query) & (key < lens[s])
        rows = seq_rows(s)
        p, m = attend(packed[rows, 0:DH], packed[rows, DH : 2 * DH], packed[rows, 2 * DH :], allowed)
        probs[s] = p
        mixed[rows, :] = m

    loop(8, att, 2)
    partial[:, half_lanes(c)] = nn(mixed[...], wkeep[...]).astype(BF)
    partial[:, half_lanes(1 - c)] = nn(mixed[...], wrecv[...]).astype(BF)


def kv_kernel(mem, wckv, kv):
    def step(b):
        rows = pl.ds(pl.multiple_of(b * 480, 480), 480)
        kv[rows, :] = nn(mem[rows, :], wckv[...]).astype(BF)

    loop(mem.shape[0] // 480, step)


def swapped(s):
    return pl.ds(pl.multiple_of(((s + 4) & 7) * LEN, LEN), LEN)


def cross_kernel(mem_len, core, tok, part, recv, vec, wcq, wkeep, wrecv, kv, resid, second, cq, probs, mixed, partial):
    c = core[0]
    gain, bias = vec[1:2], vec[4:5]

    def norm(s):
        rows = seq_rows(s)
        both = part[rows, :].astype(F32) + recv[swapped(s), :].astype(F32)
        v = tok[rows, :].astype(F32) + both
        resid[rows, :] = v
        xhat, _ = normalise(v)
        second[rows, :] = (xhat * gain + bias).astype(BF)

    loop(8, norm)
    cq[...] = nn(second[...], wcq[...]).astype(BF)
    pad = probs.shape[1]
    allowed = lax.broadcasted_iota(jnp.int32, (pad, DH), 0) < mem_len

    def att(s):
        rows = seq_rows(s)
        keys = pl.ds(pl.multiple_of(s * pad, 16), pad)
        p, m = attend(cq[rows, :], kv[keys, 0:DH], kv[keys, DH:], allowed)
        probs[s] = p
        mixed[rows, :] = m

    loop(8, att, 2)
    partial[:, half_lanes(c)] = nn(mixed[...], wkeep[...]).astype(BF)
    partial[:, half_lanes(1 - c)] = nn(mixed[...], wrecv[...]).astype(BF)


def inner_kernel(resid, part, recv, vec, win, resid_two, third, hidden, slope):
    gain, bias = vec[2:3], vec[5:6]

    def norm(s):
        rows = seq_rows(s)
        both = part[rows, :].astype(F32) + recv[swapped(s), :].astype(F32)
        v = resid[rows, :] + both
        resid_two[rows, :] = v
        xhat, _ = normalise(v)
        third[rows, :] = (xhat * gain + bias).astype(BF)

    loop(8, norm)
    width = win.shape[1]

    def step(b):
        rows = pl.ds(pl.multiple_of(b * 128, 128), 128)
        x = nn(third[rows, :], win[...])
        cdf = 0.5 + 0.5 * lax.erf(x * (0.5**0.5))
        hidden[rows, :] = (x * cdf).astype(BF)
        density = jnp.exp(x * x * -0.5) * ((2.0 * np.pi) ** -0.5)
        slope[rows, :] = (cdf + x * density).astype(BF)

    loop(4, step)


def mlp_kernel(hidden, slope, g, wout, win, partial, ginner, gthird):
    def step(b):
        rows = pl.ds(pl.multiple_of(b * 256, 256), 256)
        partial[rows, :] = nn(hidden[rows, :], wout[...]).astype(BF)
        gh = nt(g[rows, :], wout[...])
        ginner[rows, :] = (gh * slope[rows, :].astype(F32)).astype(BF)
        gthird[rows, :] = nt(ginner[rows, :], win[...]).astype(BF)

    loop(2, step)


def dmlpout_kernel(offs, hidden, g, *refs):
    outs, dw, sems = refs[:4], refs[4], refs[5]
    for b in range(0, dw.shape[0], 512):
        dw[b : b + 512, :] = tn(hidden[:, b : b + 512], g[...]).astype(BF)
    send_out(dw, offs, outs, sems, dw.shape[0] // 16)


def dmlpin_kernel(offs, third, ginner, *refs):
    outs, dw, sems = refs[:4], refs[4], refs[5]
    for b in range(0, dw.shape[0], 256):
        dw[b : b + 256, :] = tn(third[:, b : b + 256], ginner[...]).astype(BF)
    send_out(dw, offs, outs, sems, dw.shape[0] // 16)


def cross_back_kernel(
    core, resid, part, recv, g, vec, wcq, wkeep, wrecv, kv, cq, probs, gresid, gtwo, dcq, dkv, gsecond, dvec, gm
):
    c = core[0]
    gain = vec[2:3]
    dvec[...] = jnp.zeros_like(dvec)

    def norm(s):
        rows = seq_rows(s)
        dy = part[rows, :].astype(F32) + recv[swapped(s), :].astype(F32)
        dx, dg, db = norm_back(resid[rows, :], gain, dy)
        total = g[rows, :].astype(F32) + dx
        gresid[rows, :] = total
        gtwo[rows, :] = total.astype(BF)

        @pl.when(s < 4)
        def _():
            dvec[0:1, :] += dg
            dvec[1:2, :] += db

    loop(8, norm)
    gm[...] = (nt(gtwo[:, half_lanes(c)], wkeep[...]) + nt(gtwo[:, half_lanes(1 - c)], wrecv[...])).astype(BF)
    pad = probs.shape[1]

    def att(s):
        rows = seq_rows(s)
        keys = pl.ds(pl.multiple_of(s * pad, 16), pad)
        dq, dk, dv = attend_back(gm[rows, :], cq[rows, :], kv[keys, 0:DH], kv[keys, DH:], probs[s])
        dcq[rows, :] = dq
        dkv[keys, 0:DH] = dk
        dkv[keys, DH:] = dv

    loop(8, att, 2)
    gsecond[...] = nt(dcq[...], wcq[...]).astype(BF)


def out_grad(dw, lo, c, mine, other, g):
    cols = half_lanes(c)
    dw[half_lanes(c), lo : lo + DH] = tn(mine[...], g[:, cols]).astype(BF)
    rest = tn(other[256:, :], g[:256, cols]) + tn(other[:256, :], g[256:, cols])
    dw[half_lanes(1 - c), lo : lo + DH] = rest.astype(BF)


def dcross_kernel(offs, core, mixed, mixed_other, gtwo, second, dcq, mem, dkv, wckv, *refs):
    outs, gmem, dw, sems = refs[:4], refs[4], refs[5], refs[6]
    out_grad(dw, 0, core[0], mixed, mixed_other, gtwo)
    dw[:, DH : 2 * DH] = tn(second[...], dcq[...]).astype(BF)
    for b in range(0, D, 256):
        dw[b : b + 256, 2 * DH :] = tn(mem[:, b : b + 256], dkv[...]).astype(BF)

    def step(b):
        rows = pl.ds(pl.multiple_of(b * 480, 480), 480)
        gmem[rows, :] = nt(dkv[rows, :], wckv[...]).astype(BF)

    loop(mem.shape[0] // 480, step)
    send_out(dw, offs, outs, sems, D // 16)


def self_back_kernel(
    core, resid, part, recv, gresid_two, vec, wqkv, wkeep, wrecv, packed, probs, gresid, gone, dpacked, gfirst, dvec, gm
):
    c = core[0]
    gain = vec[1:2]
    dvec[...] = jnp.zeros_like(dvec)

    def norm(s):
        rows = seq_rows(s)
        dy = part[rows, :].astype(F32) + recv[swapped(s), :].astype(F32)
        dx, dg, db = norm_back(resid[rows, :], gain, dy)
        total = gresid_two[rows, :] + dx
        gresid[rows, :] = total
        gone[rows, :] = total.astype(BF)

        @pl.when(s < 4)
        def _():
            dvec[0:1, :] += dg
            dvec[1:2, :] += db

    loop(8, norm)
    gm[...] = (nt(gone[:, half_lanes(c)], wkeep[...]) + nt(gone[:, half_lanes(1 - c)], wrecv[...])).astype(BF)

    def att(s):
        rows = seq_rows(s)
        dq, dk, dv = attend_back(
            gm[rows, :], packed[rows, 0:DH], packed[rows, DH : 2 * DH], packed[rows, 2 * DH :], probs[s]
        )
        dpacked[rows, 0:DH] = dq
        dpacked[rows, DH : 2 * DH] = dk
        dpacked[rows, 2 * DH :] = dv

    loop(8, att, 2)
    gfirst[...] = nt(dpacked[...], wqkv[...]).astype(BF)


def dself_kernel(offs, core, mixed, mixed_other, gone, first, dpacked, *refs):
    outs, dw, sems = refs[:4], refs[4], refs[5]
    out_grad(dw, 0, core[0], mixed, mixed_other, gone)
    for b in range(0, D, 256):
        dw[b : b + 256, DH:] = tn(first[:, b : b + 256], dpacked[...]).astype(BF)
    send_out(dw, offs, outs, sems, D // 16)


def tokens_back_kernel(tok, part, recv, gresid, vec, gtok, dvec):
    gain = vec[0:1]
    dvec[...] = jnp.zeros_like(dvec)

    def norm(s):
        rows = seq_rows(s)
        dy = part[rows, :].astype(F32) + recv[rows, :].astype(F32)
        dx, dg, db = norm_back(tok[rows, :].astype(F32), gain, dy)
        gtok[rows, :] = (gresid[rows, :] + dx).astype(BF)
        dvec[0:1, :] += dg
        dvec[1:2, :] += db

    loop(4, norm)


class Moves:
    def __init__(self, mesh):
        self.nz, self.nf = mesh.shape["dp"], mesh.shape["fsdp"]
        self.n = self.nz * self.nf
        self.doubling = self.nz == 4 and self.nf == 8

    def permute(self, x, target):
        pairs = [(d, target(d // self.nf, (d % self.nf) // 2, d % 2)) for d in range(self.n)]
        return lax.ppermute(x, AXES, [(a, (z * self.nf) + 2 * yx + c) for a, (z, yx, c) in pairs])

    def sibling(self, x):
        return self.permute(x, lambda z, yx, c: (z, yx, 1 - c))

    def near_z(self, x):
        return self.permute(x, lambda z, yx, c: (z ^ 1, yx, c))

    def far_z(self, x):
        return self.permute(x, lambda z, yx, c: (z ^ 2, yx, c))

    def side_a(self, x):
        return self.permute(x, lambda z, yx, c: (z, yx ^ (1 + c), c))

    def side_b(self, x):
        return self.permute(x, lambda z, yx, c: (z, yx ^ (2 - c), c))

    def gather(self, piece):
        two = jnp.concatenate([piece, self.near_z(piece)], 0)
        four = jnp.concatenate([two, self.far_z(two)], 0)
        a = self.side_a(four)
        b = self.side_b(four)
        return [four, a, b, self.side_b(a)]

    def scatter(self, parts):
        own, a, b, ab = parts
        blk = own.shape[0] // 4
        got_ab = self.side_a(ab)
        got_a = self.side_a(a)
        got_b = self.side_b(b + got_ab)
        total = own.astype(F32) + got_a.astype(F32) + got_b.astype(F32)
        got = self.far_z(total[2 * blk :].astype(BF))
        total = total[: 2 * blk] + got.astype(F32)
        got = self.near_z(total[blk:].astype(BF))
        return total[:blk] + got.astype(F32)


def per_device(moves, tokens, memory, lengths, cotangent, self_qkv, self_out, cross_q, cross_kv, cross_out, mlp_in, mlp_out, norm_gains, norm_biases):
    seqs, mem_len = memory.shape[0], memory.shape[1]
    rows = seqs * LEN
    place = lax.axis_index(AXES)
    c = place % 2
    chip = place // 2
    core = jnp.reshape(c, (1,)).astype(jnp.int32)
    wr, hr = self_qkv.shape[0], mlp_out.shape[0]
    ff = mlp_in.shape[1]
    fh = ff // 2

    pad = -(-mem_len // 16) * 16
    live = jnp.arange(LEN, dtype=jnp.int32)[None, :] < lengths[:, None]
    g_own = jnp.where(live[..., None], cotangent, jnp.zeros_like(cotangent)).reshape(rows, D)
    tok_own = tokens.reshape(rows, D)
    mem_own = jnp.pad(memory, ((0, 0), (0, pad - mem_len), (0, 0))).reshape(seqs * pad, D)

    def pair_up(x):
        return jnp.concatenate([x, moves.sibling(x)], 0)

    def col_half(w, groups, which):
        w = w.reshape(w.shape[0], groups, 2, w.shape[1] // (2 * groups))
        return lax.dynamic_index_in_dim(w, which, 2, keepdims=False).reshape(w.shape[0], -1)

    vectors = jnp.concatenate([norm_gains, norm_biases], 0).T
    vectors = jnp.pad(vectors, ((0, 0), (0, 128 - vectors.shape[1])))

    def halves(which):
        one = jnp.concatenate([col_half(self_qkv, 3, which), col_half(self_out, 1, which), vectors], 1)
        two = jnp.concatenate(
            [col_half(cross_out, 1, which), col_half(cross_q, 1, which), col_half(cross_kv, 2, which)], 1
        )
        three = col_half(mlp_in, ff // (2 * hr), which)
        return one, two, three

    if moves.doubling:
        keep, send = halves(c), halves(1 - c)

        def chip_rows(mine, other):
            got = moves.sibling(other)
            return jnp.where(c == 0, jnp.concatenate([mine, got], 0), jnp.concatenate([got, mine], 0))

        bits = jnp.arange(4, dtype=jnp.int32)
        plane = jnp.stack([jnp.int32(0), 1 + c, 2 - c, jnp.int32(3)]).astype(jnp.int32)
        z, yx = chip // 4, chip % 4
        chips = ((z ^ bits)[None, :] * 4 + (yx ^ plane)[:, None]).reshape(16).astype(jnp.int32)
        gathered = [moves.gather(chip_rows(m, o)) for m, o in zip(keep, send)]
        gathered.append(moves.gather(mlp_out))
    else:
        chips = jnp.arange(16, dtype=jnp.int32)
        whole = lambda w: lax.all_gather(w, AXES, axis=0, tiled=True)
        split = lambda w: [w[i * w.shape[0] // 4 : (i + 1) * w.shape[0] // 4] for i in range(4)]
        rowed = whole(mlp_out).reshape(moves.n // 2, 2, hr, D)
        gathered = [split(whole(w)) for w in halves(c)]
        gathered.append(split(lax.dynamic_index_in_dim(rowed, c, 1, keepdims=False).reshape(fh, D)))
    turned = ((chips // 8) ^ c) * 8 + chips % 8
    offs = jnp.stack([chips, turned]).astype(jnp.int32)

    tok = pair_up(tok_own)
    lens = pair_up(lengths)
    g = pair_up(g_own)
    mem = pair_up(mem_own)

    w_qkv, w_out, g_col = assemble(gathered[0], offs, [(0, 3 * DH, 0), (3 * DH, 4 * DH, 1), (4 * DH, 4 * DH + 128, 0)])
    out_keep, out_recv = w_out[:DH], moves.sibling(w_out[DH:])
    w_cout, w_cq, w_ckv = assemble(gathered[1], offs, [(0, DH, 1), (DH, 2 * DH, 0), (2 * DH, 4 * DH, 0)])
    cout_keep, cout_recv = w_cout[:DH], moves.sibling(w_cout[DH:])
    (w_in,) = assemble(gathered[2], offs, [(0, fh, 0)])
    (w_mlpout,) = assemble(gathered[3], offs, [(0, D, 0)])

    r2 = 2 * rows
    s2 = 2 * seqs
    flops = lambda m, k, n: 2 * m * k * n
    first, packed, probs, mixed, part, vec = kernel_call(
        self_kernel,
        [lens, core, tok, g_col, w_qkv, out_keep, out_recv],
        [SM, SM] + [VM] * 5,
        [
            sds((r2, D), BF),
            sds((r2, 3 * DH), BF),
            sds((s2, LEN, DH), BF),
            sds((r2, DH), BF),
            sds((r2, D), BF),
            sds((8, D), F32),
        ],
        flops=flops(r2, D, 4 * DH),
    )
    recv = moves.sibling(part)
    mixed_other = moves.sibling(mixed)
    (kv,) = kernel_call(kv_kernel, [mem, w_ckv], [VM, VM], [sds(mem.shape, BF)], flops=flops(mem.shape[0], D, D))
    resid_one, second, cq, cprobs, cmixed, part = kernel_call(
        lambda *refs: cross_kernel(mem_len, *refs),
        [core, tok, part, recv, vec, w_cq, cout_keep, cout_recv, kv],
        [SM] + [VM] * 8,
        [
            sds((r2, D), F32),
            sds((r2, D), BF),
            sds((r2, DH), BF),
            sds((s2, pad, DH), BF),
            sds((r2, DH), BF),
            sds((r2, D), BF),
        ],
        flops=flops(r2, D, 3 * DH),
    )
    recv = moves.sibling(part)
    cmixed_other = moves.sibling(cmixed)
    resid_two, third, hidden, slope = kernel_call(
        inner_kernel,
        [resid_one, part, recv, vec, w_in],
        [VM] * 5,
        [sds((r2, D), F32), sds((r2, D), BF), sds((r2, fh), BF), sds((r2, fh), BF)],
        flops=flops(r2, D, fh),
    )

    def grads(body, ins, specs, nrows, ncols, extra=(), cost=0):
        blk = nrows // 16
        return kernel_call(
            body,
            [offs, *ins],
            [SM, *specs],
            [sds((4 * blk, ncols), BF)] * 4 + list(extra),
            [ANY] * 4 + [VM] * len(extra),
            [pltpu.VMEM((nrows, ncols), BF), pltpu.SemaphoreType.DMA((16,))],
            flops=cost,
        )

    d_mlpout = grads(dmlpout_kernel, [hidden, g], [VM] * 2, fh, D, cost=flops(r2, D, fh))
    part, ginner, gthird = kernel_call(
        mlp_kernel,
        [hidden, slope, g, w_mlpout, w_in],
        [VM] * 5,
        [sds((r2, D), BF), sds((r2, fh), BF), sds((r2, D), BF)],
        flops=3 * flops(r2, D, fh),
    )
    recv = moves.sibling(gthird)
    got = moves.sibling(part[rows:])
    output = (resid_two[:rows] + (part[:rows].astype(F32) + got.astype(F32))).astype(BF)
    d_mlpin = grads(dmlpin_kernel, [third, ginner], [VM] * 2, D, fh, cost=flops(r2, D, fh))
    gresid_two, gtwo, dcq, dkv, gsecond, dvec_two = kernel_call(
        cross_back_kernel,
        [core, resid_two, gthird, recv, g, vec, w_cq, cout_keep, cout_recv, kv, cq, cprobs],
        [SM] + [VM] * 11,
        [
            sds((r2, D), F32),
            sds((r2, D), BF),
            sds((r2, DH), BF),
            sds(kv.shape, BF),
            sds((r2, D), BF),
            sds((8, D), F32),
        ],
        scratch=[pltpu.VMEM((r2, DH), BF)],
        flops=flops(r2, D, 3 * DH),
    )
    recv = moves.sibling(gsecond)
    *d_cross, gmem = grads(
        dcross_kernel,
        [core, cmixed, cmixed_other, gtwo, second, dcq, mem, dkv, w_ckv],
        [SM] + [VM] * 8,
        D,
        4 * DH,
        [sds(mem.shape, BF)],
        cost=2 * flops(mem.shape[0], D, D),
    )
    half = seqs * pad
    got = moves.sibling(gmem[half:])
    grad_memory = (gmem[:half].astype(F32) + got.astype(F32)).astype(BF)
    grad_memory = grad_memory.reshape(seqs, pad, D)[:, :mem_len]
    gresid_one, gone, dpacked, gfirst, dvec_one = kernel_call(
        self_back_kernel,
        [core, resid_one, gsecond, recv, gresid_two, vec, w_qkv, out_keep, out_recv, packed, probs],
        [SM] + [VM] * 10,
        [
            sds((r2, D), F32),
            sds((r2, D), BF),
            sds((r2, 3 * DH), BF),
            sds((r2, D), BF),
            sds((8, D), F32),
        ],
        scratch=[pltpu.VMEM((r2, DH), BF)],
        flops=flops(r2, D, 4 * DH),
    )
    recv = moves.sibling(gfirst[rows:])
    d_self = grads(
        dself_kernel,
        [core, mixed, mixed_other, gone, first, dpacked],
        [SM] + [VM] * 5,
        D,
        4 * DH,
        cost=flops(r2, D, 4 * DH),
    )
    grad_tokens, dvec_zero = kernel_call(
        tokens_back_kernel,
        [tok_own, gfirst[:rows], recv, gresid_one[:rows], vec],
        [VM] * 5,
        [sds((rows, D), BF), sds((8, D), F32)],
    )
    dvec = jnp.concatenate(
        [dvec_zero[0:1], dvec_one[0:1], dvec_two[0:1], dvec_zero[1:2], dvec_one[1:2], dvec_two[1:2]], 0
    )

    if moves.doubling:
        sum_mlpout = moves.scatter(d_mlpout)

        def own_rows(parts):
            total = moves.scatter(parts)
            mine = lax.dynamic_slice_in_dim(total, c * wr, wr, 0)
            got = moves.sibling(lax.dynamic_slice_in_dim(total, (1 - c) * wr, wr, 0))
            return jnp.where(c == 0, mine, got), jnp.where(c == 0, got, mine)

        in_halves, cross_halves, self_halves = own_rows(d_mlpin), own_rows(d_cross), own_rows(d_self)
        for step in (moves.sibling, moves.near_z, moves.far_z, moves.side_a, moves.side_b):
            dvec = dvec + step(dvec)
    else:

        def placed(parts):
            term = jnp.concatenate(parts, 0).astype(F32)
            both = jnp.stack([jnp.where(c == 0, term, 0.0), jnp.where(c == 1, term, 0.0)], 1)
            total = lax.psum_scatter(both, AXES, scatter_dimension=0, tiled=True)
            return total[:, 0], total[:, 1]

        in_halves, cross_halves, self_halves = placed(d_mlpin), placed(d_cross), placed(d_self)
        term = jnp.concatenate(d_mlpout, 0).astype(F32).reshape(moves.n // 2, 1, hr, D)
        both = jnp.concatenate([jnp.where(c == 0, term, 0.0), jnp.where(c == 1, term, 0.0)], 1)
        sum_mlpout = lax.psum_scatter(both.reshape(ff, D), AXES, scatter_dimension=0, tiled=True)
        dvec = lax.psum(dvec, AXES)

    def join(pair, lo, hi, groups):
        parts = [p[:, lo:hi].reshape(wr, groups, 1, (hi - lo) // groups) for p in pair]
        return jnp.concatenate(parts, 2).reshape(wr, 2 * (hi - lo))

    own_vec = lax.dynamic_slice_in_dim(dvec, place * wr, wr, 1)
    return (
        output.reshape(tokens.shape),
        grad_tokens.reshape(tokens.shape),
        grad_memory,
        join(self_halves, DH, 4 * DH, 3),
        join(self_halves, 0, DH, 1),
        join(cross_halves, DH, 2 * DH, 1),
        join(cross_halves, 2 * DH, 4 * DH, 2),
        join(cross_halves, 0, DH, 1),
        join(in_halves, 0, fh, ff // (2 * hr)),
        sum_mlpout,
        own_vec[:3],
        own_vec[3:],
    )


def solution(mesh):
    batch = P(AXES, None, None)
    rows = P(AXES, None)
    cols = P(None, AXES)
    moves = Moves(mesh)
    in_specs = (batch, batch, P(AXES), batch) + (rows,) * 7 + (cols,) * 2
    out_specs = (batch,) * 3 + (rows,) * 7 + (cols,) * 2
    return jax.shard_map(
        lambda *args: per_device(moves, *args),
        mesh=mesh,
        in_specs=in_specs,
        out_specs=out_specs,
        check_vma=False,
    )
```

```python
import jax
import jax.numpy as jnp
import numpy as np
from jax import lax
from jax.experimental import pallas as pl
from jax.experimental.pallas import tpu as pltpu
from jax.sharding import PartitionSpec as P

AXES = ("dp", "fsdp")
HEADS = 12
HALF = HEADS // 2
HEAD = 64
D = 768
DH = D // 2
LEN = 64
EPS = 1e-06
NEG = -1e30
SCALE = HEAD ** (-0.5)
F32 = jnp.float32
BF = jnp.bfloat16
VMEM_LIMIT = 48 << 20

VM = pl.BlockSpec(memory_space=pltpu.VMEM)
SM = pl.BlockSpec(memory_space=pltpu.SMEM)
ANY = pl.BlockSpec(memory_space=pl.ANY)


def sds(shape, dtype):
    return jax.ShapeDtypeStruct(shape, dtype)


def kernel_call(body, ins, in_specs, outs, out_specs=None, scratch=(), flops=0, after=()):
    n, skip = len(ins), len(after)
    run = body if not after else (lambda *refs: body(*refs[:n], *refs[n + skip :]))
    nbytes = sum(int(np.prod(a.shape)) * a.dtype.itemsize for a in list(ins) + list(outs))
    return pl.pallas_call(
        run,
        out_shape=list(outs),
        in_specs=list(in_specs) + [ANY] * skip,
        out_specs=[VM] * len(outs) if out_specs is None else list(out_specs),
        scratch_shapes=list(scratch),
        compiler_params=pltpu.CompilerParams(vmem_limit_bytes=VMEM_LIMIT),
        cost_estimate=pl.CostEstimate(flops=16 * flops + 16 * 10**9, bytes_accessed=nbytes, transcendentals=0),
    )(*ins, *after)


def tie(x, *earlier):
    return pl.pallas_call(
        lambda *refs: None,
        out_shape=sds(x.shape, x.dtype),
        in_specs=[ANY] * (1 + len(earlier)),
        out_specs=ANY,
        input_output_aliases={0: 0},
        cost_estimate=pl.CostEstimate(flops=0, bytes_accessed=0, transcendentals=0),
    )(x, *earlier)


def nn(a, b):
    return lax.dot_general(a, b, (((1,), (0,)), ((), ())), preferred_element_type=F32)


def nt(a, b):
    return lax.dot_general(a, b, (((1,), (1,)), ((), ())), preferred_element_type=F32)


def tn(a, b):
    return lax.dot_general(a, b, (((0,), (0,)), ((), ())), preferred_element_type=F32)


def normalise(v):
    mean = jnp.mean(v, -1, keepdims=True)
    cen = v - mean
    inv = lax.rsqrt(jnp.mean(cen * cen, -1, keepdims=True) + EPS)
    return cen * inv, inv


def norm_back(v, gain, dy):
    xhat, inv = normalise(v)
    dxh = dy * gain
    m1 = jnp.mean(dxh, -1, keepdims=True)
    m2 = jnp.mean(dxh * xhat, -1, keepdims=True)
    dx = inv * (dxh - m1 - xhat * m2)
    return dx, jnp.sum(dy * xhat, 0, keepdims=True), jnp.sum(dy, 0, keepdims=True)


def head_of_lane(rows):
    return lax.shift_right_logical(lax.broadcasted_iota(jnp.int32, (rows, DH), 1), 6)


def spread(q):
    head = head_of_lane(1)
    parts = [q * (head == h).astype(F32).astype(q.dtype) for h in range(HALF)]
    return jnp.concatenate(parts, 0)


def fold(o):
    head = head_of_lane(LEN)
    total = jnp.where(head == 0, o[:LEN], 0.0)
    for h in range(1, HALF):
        total = jnp.where(head == h, o[h * LEN : (h + 1) * LEN], total)
    return total


def attend(q, k, v, allowed):
    st = nt(k, spread(q)) * SCALE
    st = jnp.where(allowed, st, NEG)
    e = jnp.exp(st - jnp.max(st, 0, keepdims=True))
    p = (e * (1.0 / jnp.sum(e, 0, keepdims=True))).astype(BF)
    return p, fold(tn(p, v)).astype(BF)


def attend_back(g, q, k, v, p):
    gs, qs = spread(g), spread(q)
    dp = nt(v, gs)
    pf = p.astype(F32)
    t = pf * dp
    ds = (t - pf * jnp.sum(t, 0, keepdims=True)).astype(BF)
    dq = (fold(tn(ds, k)) * SCALE).astype(BF)
    dk = (nn(ds, qs) * SCALE).astype(BF)
    dv = nn(p, gs).astype(BF)
    return dq, dk, dv


def seq_rows(s):
    return pl.ds(pl.multiple_of(s * LEN, LEN), LEN)


def half_lanes(c):
    return pl.ds(pl.multiple_of(c * DH, DH), DH)


def loop(n, body, unroll=1):
    def step(i, carry):
        body(i)
        return carry

    lax.fori_loop(0, n, step, 0, unroll=unroll)


def assemble_kernel(cols, blk, offs_ref, *refs):
    n = len(cols)
    n_out = 1 + max(c[2] for c in cols)
    pieces, outs, sems = refs[:4], refs[4 : 4 + n_out], refs[4 + n_out]
    copies = []
    for q in range(4):
        for r in range(4):
            for i, (lo, hi, o, which, step, shift) in enumerate(cols):
                row = pl.multiple_of(offs_ref[which, q * 4 + r] * step + shift, 16)
                copies.append(
                    pltpu.make_async_copy(
                        pieces[q].at[pl.ds(r * blk, blk), pl.ds(lo, hi - lo)],
                        outs[o].at[pl.ds(row, blk), :],
                        sems.at[(q * 4 + r) * n + i],
                    )
                )
    for cp in copies:
        cp.start()
    for cp in copies:
        cp.wait()


def assemble(pieces, offs, cols, shapes):
    blk = pieces[0].shape[0] // 4
    body = lambda *refs: assemble_kernel(cols, blk, *refs)
    return kernel_call(
        body,
        [offs, *pieces],
        [SM] + [ANY] * 4,
        [sds(shape, BF) for shape in shapes],
        [ANY] * len(shapes),
        [pltpu.SemaphoreType.DMA((16 * len(cols),))],
    )


def send_out(dw, offs_ref, outs, sems):
    own, to_b, to_a = outs
    blk = dw.shape[0] // 16
    copies = []
    for q, (dst, base) in enumerate(((own, 0), (to_a, 0), (to_b, 0), (to_a, 4))):
        for r in range(4):
            row = pl.multiple_of(offs_ref[0, q * 4 + r] * blk, 16)
            copies.append(
                pltpu.make_async_copy(
                    dw.at[pl.ds(row, blk), :],
                    dst.at[pl.ds((base + r) * blk, blk), :],
                    sems.at[q * 4 + r],
                )
            )
    for cp in copies:
        cp.start()
    for cp in copies:
        cp.wait()


def pack_kernel(core, qkv, out, cq, ckv, cout, win, gains, biases, keep, send, vecs):
    c = core[0]
    vecs[...] = jnp.zeros_like(vecs)
    vecs[0:3, 0:24] = gains[...].astype(F32)
    vecs[3:6, 0:24] = biases[...].astype(F32)
    rows = keep.shape[0]
    wide = jnp.transpose(vecs[...])[:rows].astype(BF)
    for dst, which in ((keep, c), (send, 1 - c)):
        at = 0
        for w, groups in ((qkv, 3), (None, 0), (out, 1), (cout, 1), (cq, 1), (ckv, 2)):
            if w is None:
                dst[:, at : at + 128] = wide
                at += 128
            for k in range(groups):
                lanes = pl.ds(pl.multiple_of(k * D + which * DH, 128), DH)
                dst[:, at : at + DH] = w[:, lanes]
                at += DH
    hr = 96
    for k in range(win.shape[1] // (2 * hr)):
        first = win[:, 2 * k * hr : (2 * k + 1) * hr]
        second = win[:, (2 * k + 1) * hr : (2 * k + 2) * hr]
        keep[:, at + k * hr : at + (k + 1) * hr] = jnp.where(c == 0, first, second)
        send[:, at + k * hr : at + (k + 1) * hr] = jnp.where(c == 0, second, first)


def prepare_kernel(own, other, tok, g, mem, lens, xhat):
    rows = tok.shape[0] // 2
    nmem = mem.shape[0] // 2
    for b, src in ((0, own), (1, other)):
        tok[b * rows : (b + 1) * rows, :] = src[0:rows, :]
        g[b * rows : (b + 1) * rows, :] = src[rows : 2 * rows, :]
        mem[b * nmem : (b + 1) * nmem, :] = src[2 * rows : 2 * rows + nmem, :]
        lens[4 * b : 4 * b + 4, :] = src[2 * rows + nmem :, :].astype(F32)[:4]

    def norm(s):
        xhat[seq_rows(s), :] = normalise(tok[seq_rows(s), :].astype(F32))[0]

    loop(8, norm)


def self_kernel(lens, xhat, gcol, wqkv, first, packed, probs, mixed, vec):
    vec[...] = jnp.transpose(gcol[...].astype(F32))[:8]
    gain, bias = vec[0:1], vec[3:4]

    def norm(s):
        first[seq_rows(s), :] = (xhat[seq_rows(s), :] * gain + bias).astype(BF)

    loop(8, norm)

    def proj(b):
        rows = pl.ds(pl.multiple_of(b * 256, 256), 256)
        packed[rows, :] = nn(first[rows, :], wqkv[...]).astype(BF)

    loop(2, proj)
    key = lax.broadcasted_iota(jnp.int32, (LEN, DH), 0)
    query = lax.broadcasted_iota(jnp.int32, (LEN, DH), 1) & (LEN - 1)

    def att(s):
        allowed = (key <= query) & (key.astype(F32) < lens[pl.ds(s, 1), 0:DH])
        rows = seq_rows(s)
        p, m = attend(packed[rows, 0:DH], packed[rows, DH : 2 * DH], packed[rows, 2 * DH :], allowed)
        probs[s] = p
        mixed[rows, :] = m

    loop(8, att, 2)


def out_kernel(core, mixed, wkeep, wrecv, comb):
    c = core[0]
    comb[:, half_lanes(c)] = nn(mixed[...], wkeep[...]).astype(BF)
    comb[:, half_lanes(1 - c)] = nn(mixed[...], wrecv[...]).astype(BF)
    comb[:, D:] = mixed[...]


def kv_kernel(mem, wckv, kv):
    def step(b):
        rows = pl.ds(pl.multiple_of(b * 480, 480), 480)
        kv[rows, :] = nn(mem[rows, :], wckv[...]).astype(BF)

    loop(mem.shape[0] // 480, step)


def swapped(s):
    return pl.ds(pl.multiple_of(((s + 4) & 7) * LEN, LEN), LEN)


def cross_kernel(mem_len, core, tok, part, recv, vec, wcq, wkeep, wrecv, kv, resid, second, cq, probs, comb):
    c = core[0]
    gain, bias = vec[1:2], vec[4:5]

    def norm(s):
        rows = seq_rows(s)
        both = part[rows, 0:D].astype(F32) + recv[swapped(s), 0:D].astype(F32)
        v = tok[rows, :].astype(F32) + both
        resid[rows, :] = v
        xhat, _ = normalise(v)
        second[rows, :] = (xhat * gain + bias).astype(BF)

    loop(8, norm)
    cq[...] = nn(second[...], wcq[...]).astype(BF)
    pad = probs.shape[1]
    allowed = lax.broadcasted_iota(jnp.int32, (pad, DH), 0) < mem_len

    def att(s):
        rows = seq_rows(s)
        keys = pl.ds(pl.multiple_of(s * pad, 16), pad)
        p, m = attend(cq[rows, :], kv[keys, 0:DH], kv[keys, DH:], allowed)
        probs[s] = p
        comb[rows, D:] = m

    loop(8, att, 2)
    comb[:, half_lanes(c)] = nn(comb[:, D:], wkeep[...]).astype(BF)
    comb[:, half_lanes(1 - c)] = nn(comb[:, D:], wrecv[...]).astype(BF)


def inner_kernel(resid, part, recv, vec, win, resid_two, third, hidden, slope):
    gain, bias = vec[2:3], vec[5:6]

    def norm(s):
        rows = seq_rows(s)
        both = part[rows, 0:D].astype(F32) + recv[swapped(s), 0:D].astype(F32)
        v = resid[rows, :] + both
        resid_two[rows, :] = v
        xhat, _ = normalise(v)
        third[rows, :] = (xhat * gain + bias).astype(BF)

    loop(8, norm)
    width = win.shape[1]

    def step(b):
        rows = pl.ds(pl.multiple_of(b * 128, 128), 128)
        x = nn(third[rows, :], win[...])
        cdf = 0.5 + 0.5 * lax.erf(x * (0.5**0.5))
        hidden[rows, :] = (x * cdf).astype(BF)
        density = jnp.exp(x * x * -0.5) * ((2.0 * np.pi) ** -0.5)
        slope[rows, :] = (cdf + x * density).astype(BF)

    loop(4, step)


def mlp_kernel(hidden, slope, g, wout, win, own, comb, ginner):
    half = own.shape[0]

    def back(b):
        rows = pl.ds(pl.multiple_of(b * 256, 256), 256)
        gh = nt(g[rows, :], wout[...])
        ginner[rows, :] = (gh * slope[rows, :].astype(F32)).astype(BF)
        comb[rows, :] = nt(ginner[rows, :], win[...]).astype(BF)

    loop(2, back)
    own[...] = nn(hidden[0:half, :], wout[...]).astype(BF)
    comb[2 * half :, :] = nn(hidden[half:, :], wout[...]).astype(BF)


def dmlpout_kernel(offs, hidden, g, *refs):
    outs, dw, sems = refs[:3], refs[3], refs[4]
    blk = dw.shape[0] // 16
    for b in range(4):
        part = tn(hidden[:, b * 8 * blk : (b + 1) * 8 * blk], g[...]).astype(BF)
        for k in range(8):
            row = (4 * b + k // 2) * blk
            dw[row : row + blk, (k % 2) * D : (k % 2 + 1) * D] = part[k * blk : (k + 1) * blk]
    send_out(dw, offs, outs, sems)


def dmlpin_kernel(offs, third, ginner, *refs):
    outs, dw, sems = refs[:3], refs[3], refs[4]
    for b in range(0, dw.shape[0], 256):
        dw[b : b + 256, :] = tn(third[:, b : b + 256], ginner[...]).astype(BF)
    send_out(dw, offs, outs, sems)


def cross_back_kernel(
    core, resid, part, recv, own, g, vec, wcq, wkeep, wrecv, kv, cq, probs, output, gresid, gtwo, dcq, dkv, gsecond, dvec, gm
):
    c = core[0]
    gain = vec[2:3]
    dvec[...] = jnp.zeros_like(dvec)

    def norm(s):
        rows = seq_rows(s)
        dy = part[rows, :].astype(F32) + recv[swapped(s), :].astype(F32)
        dx, dg, db = norm_back(resid[rows, :], gain, dy)
        total = g[rows, :].astype(F32) + dx
        gresid[rows, :] = total
        gtwo[rows, :] = total.astype(BF)

        @pl.when(s < 4)
        def _():
            dvec[0:1, :] += dg
            dvec[1:2, :] += db
            extra = own[rows, :].astype(F32) + recv[pl.ds(pl.multiple_of(512 + s * LEN, LEN), LEN), :].astype(F32)
            output[rows, :] = (resid[rows, :] + extra).astype(BF)

    loop(8, norm)
    gm[...] = (nt(gtwo[:, half_lanes(c)], wkeep[...]) + nt(gtwo[:, half_lanes(1 - c)], wrecv[...])).astype(BF)
    pad = probs.shape[1]

    def att(s):
        rows = seq_rows(s)
        keys = pl.ds(pl.multiple_of(s * pad, 16), pad)
        dq, dk, dv = attend_back(gm[rows, :], cq[rows, :], kv[keys, 0:DH], kv[keys, DH:], probs[s])
        dcq[rows, :] = dq
        dkv[keys, 0:DH] = dk
        dkv[keys, DH:] = dv

    loop(8, att, 2)
    gsecond[...] = nt(dcq[...], wcq[...]).astype(BF)


def out_grad(dw, lo, c, mine, other, g):
    cols = half_lanes(c)
    dw[half_lanes(c), lo : lo + DH] = tn(mine[:, D:], g[:, cols]).astype(BF)
    rest = tn(other[256:, D:], g[:256, cols]) + tn(other[:256, D:], g[256:, cols])
    dw[half_lanes(1 - c), lo : lo + DH] = rest.astype(BF)


def dcross_kernel(offs, core, mixed, mixed_other, gtwo, second, dcq, mem, dkv, wckv, *refs):
    outs, gmem, dw, sems = refs[:3], refs[3:5], refs[5], refs[6]
    out_grad(dw, 0, core[0], mixed, mixed_other, gtwo)
    dw[:, DH : 2 * DH] = tn(second[...], dcq[...]).astype(BF)
    for b in range(0, D, 256):
        dw[b : b + 256, 2 * DH :] = tn(mem[:, b : b + 256], dkv[...]).astype(BF)

    half = mem.shape[0] // 2
    for b in range(0, half, 480):
        gmem[0][b : b + 480, :] = nt(dkv[b : b + 480, :], wckv[...]).astype(BF)
        gmem[1][b : b + 480, :] = nt(dkv[half + b : half + b + 480, :], wckv[...]).astype(BF)
    send_out(dw, offs, outs, sems)


def self_back_kernel(
    core, xhat, resid, part, recv, gresid_two, vec, wqkv, wkeep, wrecv, packed, probs, gresid, gone, dpacked, gfirst_own, gfirst_other, dvec, gm
):
    c = core[0]
    gain = vec[1:2]
    dvec[...] = jnp.zeros_like(dvec)

    def norm(s):
        rows = seq_rows(s)
        dy = part[rows, :].astype(F32) + recv[swapped(s), :].astype(F32)
        dx, dg, db = norm_back(resid[rows, :], gain, dy)
        total = gresid_two[rows, :] + dx
        gresid[rows, :] = total
        gone[rows, :] = total.astype(BF)

        @pl.when(s < 4)
        def _():
            dvec[0:1, :] += dg
            dvec[1:2, :] += db

    loop(8, norm)
    gm[...] = (nt(gone[:, half_lanes(c)], wkeep[...]) + nt(gone[:, half_lanes(1 - c)], wrecv[...])).astype(BF)

    def att(s):
        rows = seq_rows(s)
        dq, dk, dv = attend_back(
            gm[rows, :], packed[rows, 0:DH], packed[rows, DH : 2 * DH], packed[rows, 2 * DH :], probs[s]
        )
        dpacked[rows, 0:DH] = dq
        dpacked[rows, DH : 2 * DH] = dk
        dpacked[rows, 2 * DH :] = dv

    loop(8, att, 2)
    half = gfirst_own.shape[0]
    for b, dst in ((0, gfirst_own), (half, gfirst_other)):
        term = nt(dpacked[b : b + half, :], wqkv[...])
        dst[...] = term.astype(BF)
        dvec[2:3, :] += jnp.sum(term * xhat[b : b + half, :], 0, keepdims=True)
        dvec[3:4, :] += jnp.sum(term, 0, keepdims=True)


def dself_kernel(offs, core, mixed, mixed_other, gone, first, dpacked, dvec_two, dvec_one, *refs):
    outs, dw, vecs, sems = refs[:3], refs[3], refs[4], refs[5]
    out_grad(dw, 0, core[0], mixed, mixed_other, gone)
    for b in range(0, D, 256):
        dw[b : b + 256, DH : 4 * DH] = tn(first[:, b : b + 256], dpacked[...]).astype(BF)
    vecs[...] = jnp.zeros_like(vecs)
    for i, (v, row) in enumerate(((dvec_one, 2), (dvec_one, 0), (dvec_two, 0), (dvec_one, 3), (dvec_one, 1), (dvec_two, 1))):
        vecs[i : i + 1, :] = v[row : row + 1, :]
    dw[:, 4 * DH :] = jnp.transpose(vecs[...]).astype(BF)
    send_out(dw, offs, outs, sems)


def tokens_back_kernel(tok, part, recv, gresid, vec, gmem, gmem_recv, gtok, gmemory):
    gmemory[...] = (gmem[...].astype(F32) + gmem_recv[...].astype(F32)).astype(BF)
    gain = vec[0:1]

    def norm(s):
        rows = seq_rows(s)
        dy = part[rows, :].astype(F32) + recv[rows, :].astype(F32)
        dx, _, _ = norm_back(tok[rows, :].astype(F32), gain, dy)
        gtok[rows, :] = (gresid[rows, :] + dx).astype(BF)

    loop(4, norm)


def join_kernel(core, mine, got, *outs):
    c = core[0]
    at = 0
    for out in outs[: 2 if mine.shape[1] > 4 * DH else 3]:
        for k in range(out.shape[1] // D):
            out[:, pl.ds(pl.multiple_of(k * D + c * DH, 128), DH)] = mine[:, at : at + DH]
            out[:, pl.ds(pl.multiple_of(k * D + (1 - c) * DH, 128), DH)] = got[:, at : at + DH]
            at += DH
    if mine.shape[1] > at:
        gains, biases, wide = outs[2:]
        rows = mine.shape[0]
        wide[...] = jnp.zeros_like(wide)
        wide[0:rows, :] = mine[:, at:] + got[:, at:]
        turned = jnp.transpose(wide[...])
        gains[...] = turned[0:3, 0:rows]
        biases[...] = turned[3:6, 0:rows]


class Moves:
    def __init__(self, mesh):
        self.nz, self.nf = mesh.shape["dp"], mesh.shape["fsdp"]
        self.n = self.nz * self.nf
        self.doubling = self.nz == 4 and self.nf == 8

    def permute(self, x, target):
        pairs = [(d, target(d // self.nf, (d % self.nf) // 2, d % 2)) for d in range(self.n)]
        return lax.ppermute(x, AXES, [(a, (z * self.nf) + 2 * yx + c) for a, (z, yx, c) in pairs])

    def sibling(self, x):
        return self.permute(x, lambda z, yx, c: (z, yx, 1 - c))

    def near_z(self, x):
        return self.permute(x, lambda z, yx, c: (z ^ 1, yx, c))

    def far_z(self, x):
        return self.permute(x, lambda z, yx, c: (z ^ 2, yx, c))

    def side_a(self, x):
        return self.permute(x, lambda z, yx, c: (z, yx ^ (1 + c), c))

    def side_b(self, x):
        return self.permute(x, lambda z, yx, c: (z, yx ^ (2 - c), c))

    def opposite_z(self, x):
        return self.permute(x, lambda z, yx, c: (z ^ 3, yx, c))


def per_device(moves, tokens, memory, lengths, cotangent, self_qkv, self_out, cross_q, cross_kv, cross_out, mlp_in, mlp_out, norm_gains, norm_biases):
    seqs, mem_len = memory.shape[0], memory.shape[1]
    rows = seqs * LEN
    place = lax.axis_index(AXES)
    c = place % 2
    chip = place // 2
    core = jnp.reshape(c, (1,)).astype(jnp.int32)
    wr, hr = self_qkv.shape[0], mlp_out.shape[0]
    ff = mlp_in.shape[1]
    fh = ff // 2
    r2, s2 = 2 * rows, 2 * seqs
    wb = D // 16
    flops = lambda m, k, n: 2 * m * k * n

    pad = -(-mem_len // 16) * 16
    live = jnp.arange(LEN, dtype=jnp.int32)[None, :] < lengths[:, None]
    g_own = jnp.where(live[..., None], cotangent, jnp.zeros_like(cotangent)).reshape(rows, D)
    tok_own = tokens.reshape(rows, D)
    mem_own = jnp.pad(memory, ((0, 0), (0, pad - mem_len), (0, 0))).reshape(seqs * pad, D)
    len_own = jnp.broadcast_to(jnp.pad(lengths, (0, 16 - seqs)).astype(BF)[:, None], (16, D))

    def prepare(own, other):
        return kernel_call(
            prepare_kernel,
            [own, other],
            [VM] * 2,
            [sds((r2, D), BF)] * 2 + [sds((s2 * pad, D), BF), sds((8, D), F32), sds((r2, D), F32)],
        )

    def self_attention(pieces, chips, prepared):
        w_qkv, g_col = assemble(
            pieces,
            chips[None],
            [(0, 3 * DH, 0, 0, wb, 0), (3 * DH, 3 * DH + 128, 1, 0, wb, 0)],
            [(D, 3 * DH), (D, 128)],
        )
        return w_qkv, *kernel_call(
            self_kernel,
            [prepared[3], prepared[4], g_col, w_qkv],
            [VM] * 4,
            [sds((r2, D), BF), sds((r2, 3 * DH), BF), sds((s2, LEN, DH), BF), sds((r2, DH), BF), sds((8, D), F32)],
            flops=flops(r2, D, 3 * DH),
        )

    if moves.doubling:
        keep, send = kernel_call(
            pack_kernel,
            [core, self_qkv, self_out, cross_q, cross_kv, cross_out, mlp_in, norm_gains, norm_biases],
            [SM] + [VM] * 8,
            [sds((wr, 12 * DH + 128), BF)] * 2,
            scratch=[pltpu.VMEM((128, 128), F32)],
        )
        got = moves.sibling(send)
        own = jnp.concatenate([tok_own, g_own, mem_own, len_own], 0)
        other = moves.sibling(own)

        def chip_rows(lo, hi):
            a, b = keep[:, lo:hi], got[:, lo:hi]
            return jnp.where(c == 0, jnp.concatenate([a, b], 0), jnp.concatenate([b, a], 0))

        bits = jnp.arange(4, dtype=jnp.int32)
        plane = jnp.stack([jnp.int32(0), 1 + c, 2 - c, jnp.int32(3)]).astype(jnp.int32)
        z, yx = chip // 4, chip % 4
        chips = ((z ^ bits)[None, :] * 4 + (yx ^ plane)[:, None]).reshape(16).astype(jnp.int32)
        one = chip_rows(0, 3 * DH + 128)
        one = jnp.concatenate([one, moves.near_z(one), moves.far_z(one), moves.opposite_z(one)], 0)
        prepared = prepare(own, other)
        one = tie(one, prepared[0])
        rest = jnp.concatenate([chip_rows(3 * DH + 128, 12 * DH + 128), mlp_out[: 2 * wr], mlp_out[2 * wr :]], 1)
        rest = tie(rest, one)
        rest = jnp.concatenate([rest, moves.near_z(rest)], 0)
        a, b = moves.side_a(one), moves.side_b(one)
        gathered = [[one, a, b, moves.side_b(a)]]
        kernels_done = self_attention(gathered[0], chips, prepared)

        def far_part(lo, hi, earlier):
            two = tie(rest[:, lo:hi], earlier)
            far = moves.far_z(two)
            return far, jnp.concatenate([two, far], 0)

        far, four = far_part(0, 5 * DH, a)
        four = tie(four, gathered[0][3])
        a, b = moves.side_a(four), moves.side_b(four)
        gathered.append([four, a, b, moves.side_b(a)])
        far, four = far_part(5 * DH, 9 * DH, far)
        four = tie(four, b, kernels_done[1])
        a, b = moves.side_a(four), moves.side_b(four)
        gathered.append([four, a, b, moves.side_b(a)])
        far, four_last = far_part(9 * DH, 13 * DH, far)
        b_before = b
    else:
        own = jnp.concatenate([tok_own, g_own, mem_own, len_own], 0)
        other = moves.sibling(own)
        chips = jnp.arange(16, dtype=jnp.int32)
        whole = lambda w: lax.all_gather(w, AXES, axis=0, tiled=True)
        split = lambda w: [w[i * w.shape[0] // 4 : (i + 1) * w.shape[0] // 4] for i in range(4)]

        def col_half(w, groups):
            w = w.reshape(w.shape[0], groups, 2, w.shape[1] // (2 * groups))
            return lax.dynamic_index_in_dim(w, c, 2, keepdims=False).reshape(w.shape[0], -1)

        vectors = jnp.pad(jnp.concatenate([norm_gains, norm_biases], 0).T, ((0, 0), (0, 122)))
        one = jnp.concatenate([col_half(self_qkv, 3), vectors], 1)
        two = jnp.concatenate([col_half(w, w.shape[1] // D) for w in (self_out, cross_out, cross_q, cross_kv)], 1)
        rowed = whole(mlp_out).reshape(moves.n // 2, 2, hr, D)
        gathered = [split(whole(w)) for w in (one, two, col_half(mlp_in, ff // (2 * hr)))]
        rowed = lax.dynamic_index_in_dim(rowed, c, 1, keepdims=False).reshape(16, 2, fh // 32, D)
        gathered.append(split(rowed.transpose(0, 2, 1, 3).reshape(D, 2 * D)))
        prepared = prepare(own, other)
        kernels_done = self_attention(gathered[0], chips, prepared)
    turned = ((chips // 8) ^ c) * 16 + chips % 8
    offs = jnp.stack([chips, turned, turned + 8]).astype(jnp.int32)

    tok, g, mem, lens, xhat = prepared
    w_qkv, first, packed, probs, mixed, vec = kernels_done
    w_outs, w_cq, w_ckv = assemble(
        gathered[1],
        offs,
        [
            (0, DH, 0, 1, wb, 0),
            (DH, 2 * DH, 0, 2, wb, 0),
            (2 * DH, 3 * DH, 1, 0, wb, 0),
            (3 * DH, 5 * DH, 2, 0, wb, 0),
        ],
        [(2 * D, DH), (D, DH), (D, 2 * DH)],
    )
    outs_recv = moves.sibling(w_outs[D:])
    out_keep, out_recv, cout_keep, cout_recv = w_outs[:DH], outs_recv[:DH], w_outs[DH:D], outs_recv[DH:]

    (comb,) = kernel_call(
        out_kernel,
        [core, mixed, out_keep, out_recv],
        [SM] + [VM] * 3,
        [sds((r2, 3 * DH), BF)],
        flops=flops(r2, DH, D),
    )
    recv = moves.sibling(comb)
    self_mixed = (comb, recv)
    (kv,) = kernel_call(kv_kernel, [mem, w_ckv], [VM, VM], [sds(mem.shape, BF)], flops=flops(mem.shape[0], D, D))
    if moves.doubling:
        four = tie(four_last, b_before, kv, recv)
        a, b = moves.side_a(four), moves.side_b(four)
        gathered.append([four, a, b, moves.side_b(a)])
    resid_one, second, cq, cprobs, comb = kernel_call(
        lambda *refs: cross_kernel(mem_len, *refs),
        [core, tok, comb, recv, vec, w_cq, cout_keep, cout_recv, kv],
        [SM] + [VM] * 8,
        [
            sds((r2, D), F32),
            sds((r2, D), BF),
            sds((r2, DH), BF),
            sds((s2, pad, DH), BF),
            sds((r2, 3 * DH), BF),
        ],
        flops=flops(r2, D, 3 * DH),
    )
    recv = moves.sibling(comb)
    cross_mixed = (comb, recv)
    (w_in,) = assemble(gathered[2], offs, [(0, fh, 0, 0, wb, 0)], [(D, fh)])
    resid_two, third, hidden, slope = kernel_call(
        inner_kernel,
        [resid_one, comb, recv, vec, w_in],
        [VM] * 5,
        [sds((r2, D), F32), sds((r2, D), BF), sds((r2, fh), BF), sds((r2, fh), BF)],
        flops=flops(r2, D, fh),
        after=gathered[3][1:3],
    )

    def grads(body, ins, specs, ncols, extra=(), scratch=(), cost=0, after=()):
        return kernel_call(
            body,
            [offs, *ins],
            [SM, *specs],
            [sds((4 * wb, ncols), BF)] * 2 + [sds((8 * wb, ncols), BF)] + list(extra),
            [ANY] * 3 + [VM] * len(extra),
            [pltpu.VMEM((D, ncols), BF), *scratch, pltpu.SemaphoreType.DMA((16,))],
            flops=cost,
            after=after,
        )

    def step_a(parts):
        return moves.side_a(parts[2]) if moves.doubling else None

    def step_b(parts, got):
        half = 4 * wb
        return moves.side_b(parts[1] + got[half:]) if moves.doubling else None

    def plane_sum(parts, got_a, got_b):
        return parts[0].astype(F32) + got_a[: 4 * wb].astype(F32) + got_b.astype(F32) if moves.doubling else None

    def step_far(total):
        return moves.far_z(total[2 * wb :].astype(BF)) if moves.doubling else None

    def step_near(total, got):
        if not moves.doubling:
            return None
        total = total[: 2 * wb] + got.astype(F32)
        return total[:wb] + moves.near_z(total[wb:].astype(BF)).astype(F32)

    def there(*arrays):
        return [x for x in arrays if x is not None]

    d_mlpout = grads(dmlpout_kernel, [hidden, g], [VM] * 2, 2 * D, cost=flops(r2, D, fh), after=gathered[3][3:])
    a_one = step_a(d_mlpout)
    (w_mlpout,) = assemble(gathered[3], offs, [(0, D, 0, 0, 2 * wb, 0), (D, 2 * D, 0, 0, 2 * wb, wb)], [(fh, D)])
    part, comb, ginner = kernel_call(
        mlp_kernel,
        [hidden, slope, g, w_mlpout, w_in],
        [VM] * 5,
        [sds((rows, D), BF), sds((3 * rows, D), BF), sds((r2, fh), BF)],
        flops=3 * flops(r2, D, fh),
    )
    recv = moves.sibling(comb)
    d_mlpin = grads(dmlpin_kernel, [third, ginner], [VM] * 2, fh, cost=flops(r2, D, fh))
    a_two = step_a(d_mlpin)
    b_one = step_b(d_mlpout, a_one)
    output, gresid_two, gtwo, dcq, dkv, gsecond, dvec_two = kernel_call(
        cross_back_kernel,
        [core, resid_two, comb, recv, part, g, vec, w_cq, cout_keep, cout_recv, kv, cq, cprobs],
        [SM] + [VM] * 12,
        [
            sds((rows, D), BF),
            sds((r2, D), F32),
            sds((r2, D), BF),
            sds((r2, DH), BF),
            sds(kv.shape, BF),
            sds((r2, D), BF),
            sds((8, D), F32),
        ],
        scratch=[pltpu.VMEM((r2, DH), BF)],
        flops=flops(r2, D, 3 * DH),
        after=there(a_one),
    )
    recv = moves.sibling(gsecond)
    sum_one = plane_sum(d_mlpout, a_one, b_one)
    far_one = step_far(sum_one)
    b_two = step_b(d_mlpin, a_two)
    *d_cross, gmem, gmem_other = grads(
        dcross_kernel,
        [core, *cross_mixed, gtwo, second, dcq, mem, dkv, w_ckv],
        [SM] + [VM] * 8,
        4 * DH,
        [sds((seqs * pad, D), BF)] * 2,
        cost=2 * flops(mem.shape[0], D, D),
        after=there(a_two, b_one),
    )
    a_three = step_a(d_cross)
    sum_two = plane_sum(d_mlpin, a_two, b_two)
    far_two = step_far(sum_two)
    own_one = step_near(sum_one, far_one)
    gmem_recv = moves.sibling(gmem_other)
    gresid_one, gone, dpacked, gfirst, gfirst_other, dvec_one = kernel_call(
        self_back_kernel,
        [core, xhat, resid_one, gsecond, recv, gresid_two, vec, w_qkv, out_keep, out_recv, packed, probs],
        [SM] + [VM] * 11,
        [
            sds((r2, D), F32),
            sds((r2, D), BF),
            sds((r2, 3 * DH), BF),
            sds((rows, D), BF),
            sds((rows, D), BF),
            sds((8, D), F32),
        ],
        scratch=[pltpu.VMEM((r2, DH), BF)],
        flops=flops(r2, D, 4 * DH),
        after=there(far_one, b_two),
    )
    recv = moves.sibling(gfirst_other)
    b_three = step_b(d_cross, a_three)
    own_two = step_near(sum_two, far_two)
    d_self = grads(
        dself_kernel,
        [core, *self_mixed, gone, first, dpacked, dvec_two, dvec_one],
        [SM] + [VM] * 7,
        4 * DH + 128,
        scratch=[pltpu.VMEM((128, D), F32)],
        cost=flops(r2, D, 4 * DH),
        after=there(a_three, own_one, far_two),
    )
    a_four = step_a(d_self)
    sum_three = plane_sum(d_cross, a_three, b_three)
    far_three = step_far(sum_three)
    grad_tokens, grad_memory = kernel_call(
        tokens_back_kernel,
        [tok_own, gfirst, recv, gresid_one[:rows], vec, gmem, gmem_recv],
        [VM] * 7,
        [sds((rows, D), BF), sds(gmem.shape, BF)],
        after=there(b_three, own_two),
    )
    grad_memory = grad_memory.reshape(seqs, pad, D)[:, :mem_len]
    if moves.doubling:

        def own_rows(total):
            mine = lax.dynamic_slice_in_dim(total, c * wr, wr, 0)
            return mine, moves.sibling(lax.dynamic_slice_in_dim(total, (1 - c) * wr, wr, 0))

        def join(pair, *shapes, scratch=()):
            return kernel_call(
                join_kernel, [core, *pair], [SM, VM, VM], [sds(shape, F32) for shape in shapes], scratch=scratch
            )

        three = step_near(sum_three, far_three)
        sum_four = plane_sum(d_self, a_four, step_b(d_self, a_four))
        low = sum_four.astype(BF)
        four = sum_four[:wb] + moves.near_z(low[wb : 2 * wb]).astype(F32)
        four = four + moves.far_z(low[2 * wb : 3 * wb]).astype(F32) + moves.opposite_z(low[3 * wb :]).astype(F32)
        sum_mlpout = jnp.concatenate([own_one[:, :D], own_one[:, D:]], 0)
        mine, got = own_rows(own_two)
        pair = (jnp.where(c == 0, mine, got), jnp.where(c == 0, got, mine))
        parts = [p.reshape(wr, ff // (2 * hr), 1, hr) for p in pair]
        grad_in = jnp.concatenate(parts, 2).reshape(wr, ff)
        grad_cout, grad_cq, grad_ckv = join(own_rows(three), (wr, D), (wr, D), (wr, 2 * D))
        grad_out, grad_qkv, own_gains, own_biases = join(
            own_rows(four), (wr, D), (wr, 3 * D), (3, wr), (3, wr), scratch=[pltpu.VMEM((128, 128), F32)]
        )
    else:

        def placed(parts):
            own, to_b, to_a = parts
            term = jnp.concatenate([own, to_a[: 4 * wb], to_b, to_a[4 * wb :]], 0).astype(F32)
            both = jnp.stack([jnp.where(c == 0, term, 0.0), jnp.where(c == 1, term, 0.0)], 1)
            return lax.psum_scatter(both, AXES, scatter_dimension=0, tiled=True)

        def joined(total, lo, hi, groups):
            return total[:, :, lo:hi].reshape(wr, 2, groups, -1).transpose(0, 2, 1, 3).reshape(wr, -1)

        total = placed(d_cross)
        grad_cout, grad_cq, grad_ckv = (
            joined(total, 0, DH, 1),
            joined(total, DH, 2 * DH, 1),
            joined(total, 2 * DH, 4 * DH, 2),
        )
        total = placed(d_self)
        grad_out, grad_qkv = joined(total, 0, DH, 1), joined(total, DH, 4 * DH, 3)
        vectors = jnp.sum(total[:, :, 4 * DH : 4 * DH + 6], 1).T
        own_gains, own_biases = vectors[:3], vectors[3:]
        grad_in = joined(placed(d_mlpin), 0, fh, ff // (2 * hr))
        own, to_b, to_a = d_mlpout
        term = jnp.concatenate([own, to_a[: 4 * wb], to_b, to_a[4 * wb :]], 0).astype(F32)
        term = term.reshape(16, wb, 2, D).transpose(0, 2, 1, 3).reshape(moves.n // 2, 1, hr, D)
        both = jnp.concatenate([jnp.where(c == 0, term, 0.0), jnp.where(c == 1, term, 0.0)], 1)
        sum_mlpout = lax.psum_scatter(both.reshape(ff, D), AXES, scatter_dimension=0, tiled=True)

    return (
        output.reshape(tokens.shape),
        grad_tokens.reshape(tokens.shape),
        grad_memory,
        grad_qkv,
        grad_out,
        grad_cq,
        grad_ckv,
        grad_cout,
        grad_in,
        sum_mlpout,
        own_gains,
        own_biases,
    )


def solution(mesh):
    batch = P(AXES, None, None)
    rows = P(AXES, None)
    cols = P(None, AXES)
    moves = Moves(mesh)
    in_specs = (batch, batch, P(AXES), batch) + (rows,) * 7 + (cols,) * 2
    out_specs = (batch,) * 3 + (rows,) * 7 + (cols,) * 2
    return jax.shard_map(
        lambda *args: per_device(moves, *args),
        mesh=mesh,
        in_specs=in_specs,
        out_specs=out_specs,
        check_vma=False,
    )
```

```python
import jax
import jax.numpy as jnp
import numpy as np
from jax import lax
from jax.experimental import pallas as pl
from jax.experimental.pallas import tpu as pltpu
from jax.sharding import PartitionSpec as P

AXES = ("dp", "fsdp")
HEADS = 12
HALF = HEADS // 2
HEAD = 64
D = 768
DH = D // 2
LEN = 64
EPS = 1e-06
NEG = -1e30
SCALE = HEAD ** (-0.5)
F32 = jnp.float32
BF = jnp.bfloat16
VMEM_LIMIT = 20 << 20

VM = pl.BlockSpec(memory_space=pltpu.VMEM)
SM = pl.BlockSpec(memory_space=pltpu.SMEM)
ANY = pl.BlockSpec(memory_space=pl.ANY)


def sds(shape, dtype):
    return jax.ShapeDtypeStruct(shape, dtype)


STAGE = VM


class Staged:
    def __init__(self, ref, copy):
        self.ref, self.copy, self.waited = ref, copy, False
        self.shape = ref.shape

    def ready(self):
        if not self.waited:
            self.copy.wait()
            self.waited = True
        return self.ref


PENDING = {}


def flush(*refs):
    for r in refs:
        if id(r) in PENDING:
            PENDING[id(r)].start()
            PENDING[id(r)] = None


def ready(*refs):
    out = [r.ready() if isinstance(r, Staged) else r for r in refs]
    return out[0] if len(out) == 1 else out


def kernel_call(body, ins, in_specs, outs, out_specs=None, scratch=(), cost=5, after=(), limit=None):
    n, skip, m, k = len(ins), len(after), len(outs), len(scratch)
    out_specs = [VM] * m if out_specs is None else list(out_specs)
    staged_in = [i for i, spec in enumerate(in_specs) if spec == 'stage']
    staged_out = [i for i, spec in enumerate(out_specs) if spec == 'stage']
    buffers = [pltpu.VMEM(ins[i].shape, ins[i].dtype) for i in staged_in]
    buffers += [pltpu.VMEM(outs[i].shape, outs[i].dtype) for i in staged_out]
    extra = [*buffers, pltpu.SemaphoreType.DMA((len(buffers),))] if buffers else []

    def run(*refs):
        ins, outs = list(refs[:n]), list(refs[n + skip : n + skip + m])
        own = refs[n + skip + m : n + skip + m + k]
        PENDING.clear()
        if not buffers:
            body(*ins, *outs, *own)
            return
        held, sems = refs[n + skip + m + k : -1], refs[-1]
        for j, i in enumerate(staged_in):
            copy = pltpu.make_async_copy(ins[i], held[j], sems.at[j])
            copy.start()
            ins[i] = Staged(held[j], copy)
        copies = []
        for j, i in enumerate(staged_out, len(staged_in)):
            copies.append(pltpu.make_async_copy(held[j], outs[i], sems.at[j]))
            outs[i] = held[j]
            PENDING[id(held[j])] = copies[-1]
        body(*ins, *outs, *own)
        ready(*ins)
        for cp in PENDING.values():
            if cp is not None:
                cp.start()
        for cp in copies:
            cp.wait()

    place = lambda spec: ANY if spec == 'stage' else spec
    return pl.pallas_call(
        run,
        out_shape=list(outs),
        in_specs=[place(spec) for spec in in_specs] + [ANY] * skip,
        out_specs=[place(spec) for spec in out_specs],
        scratch_shapes=[*scratch, *extra],
        compiler_params=pltpu.CompilerParams(vmem_limit_bytes=limit or VMEM_LIMIT),
        cost_estimate=pl.CostEstimate(flops=cost * 16 * 10**9, bytes_accessed=0, transcendentals=0),
    )(*ins, *after)


def tie(x, *earlier):
    return pl.pallas_call(
        lambda *refs: None,
        out_shape=sds(x.shape, x.dtype),
        in_specs=[ANY] * (1 + len(earlier)),
        out_specs=ANY,
        input_output_aliases={0: 0},
        compiler_params=pltpu.CompilerParams(vmem_limit_bytes=1 << 20),
        cost_estimate=pl.CostEstimate(flops=0, bytes_accessed=0, transcendentals=0),
    )(x, *earlier)


def nn(a, b):
    return lax.dot_general(a, b, (((1,), (0,)), ((), ())), preferred_element_type=F32)


def nt(a, b):
    return lax.dot_general(a, b, (((1,), (1,)), ((), ())), preferred_element_type=F32)


def tn(a, b):
    return lax.dot_general(a, b, (((0,), (0,)), ((), ())), preferred_element_type=F32)


def normalise(v):
    mean = jnp.mean(v, -1, keepdims=True)
    cen = v - mean
    inv = lax.rsqrt(jnp.mean(cen * cen, -1, keepdims=True) + EPS)
    return cen * inv, inv


def norm_back(v, gain, dy):
    xhat, inv = normalise(v)
    dxh = dy * gain
    m1 = jnp.mean(dxh, -1, keepdims=True)
    m2 = jnp.mean(dxh * xhat, -1, keepdims=True)
    dx = inv * (dxh - m1 - xhat * m2)
    return dx, jnp.sum(dy * xhat, 0, keepdims=True), jnp.sum(dy, 0, keepdims=True)


def head_of_lane(rows):
    return lax.shift_right_logical(lax.broadcasted_iota(jnp.int32, (rows, DH), 1), 6)


def spread(q):
    head = head_of_lane(1)
    parts = [q * (head == h).astype(F32).astype(q.dtype) for h in range(HALF)]
    return jnp.concatenate(parts, 0)


def fold(o):
    head = head_of_lane(LEN)
    total = jnp.where(head == 0, o[:LEN], 0.0)
    for h in range(1, HALF):
        total = jnp.where(head == h, o[h * LEN : (h + 1) * LEN], total)
    return total


def attend(q, k, v, allowed):
    st = nt(k, spread(q)) * SCALE
    st = jnp.where(allowed, st, NEG)
    e = jnp.exp(st - jnp.max(st, 0, keepdims=True))
    p = (e * (1.0 / jnp.sum(e, 0, keepdims=True))).astype(BF)
    return p, fold(tn(p, v)).astype(BF)


def attend_back(g, q, k, v, p):
    gs, qs = spread(g), spread(q)
    dp = nt(v, gs)
    pf = p.astype(F32)
    t = pf * dp
    ds = (t - pf * jnp.sum(t, 0, keepdims=True)).astype(BF)
    dq = (fold(tn(ds, k)) * SCALE).astype(BF)
    dk = (nn(ds, qs) * SCALE).astype(BF)
    dv = nn(p, gs).astype(BF)
    return dq, dk, dv


def seq_rows(s):
    return pl.ds(pl.multiple_of(s * LEN, LEN), LEN)


def half_lanes(c):
    return pl.ds(pl.multiple_of(c * DH, DH), DH)


def loop(n, body, unroll=1):
    def step(i, carry):
        body(i)
        return carry

    lax.fori_loop(0, n, step, 0, unroll=unroll)


class Rows:
    def __init__(self, pieces, offs_ref, which, cols, targets, sems):
        blk = pieces[0].shape[0] // 4
        self.copies = []
        for i, (lo, hi, o, step, shift) in enumerate(cols):
            for q in range(4):
                for r in range(4):
                    row = pl.multiple_of(offs_ref[which, q * 4 + r] * step + shift, 16)
                    self.copies.append(
                        pltpu.make_async_copy(
                            pieces[q].at[pl.ds(r * blk, blk), pl.ds(lo, hi - lo)],
                            targets[o].at[pl.ds(row, blk), :],
                            sems.at[i * 16 + q * 4 + r],
                        )
                    )
        for cp in self.copies:
            cp.start()

    def wait(self):
        for cp in self.copies:
            cp.wait()


def place_rows(pieces, offs, which, cols, shape):
    def body(offs_ref, *refs):
        Rows(refs[:4], offs_ref, which, cols, refs[4:5], refs[5]).wait()

    return kernel_call(
        body,
        [offs, *pieces],
        [SM] + [ANY] * 4,
        [sds(shape, BF)],
        [VM],
        [pltpu.SemaphoreType.DMA((16 * len(cols),))],
        cost=1,
    )[0]


def out_rows(pieces, offs, lo):
    blk = pieces[0].shape[0] // 4
    return place_rows(pieces, offs, 1, [(lo, lo + DH, 0, blk, 0)], (16 * blk, DH))


def send_out(dw, offs_ref, outs, sems):
    own, to_b, to_a = outs
    blk = dw.shape[0] // 16
    copies = []
    for q, (dst, base) in enumerate(((own, 0), (to_a, 0), (to_b, 0), (to_a, 4))):
        for r in range(4):
            row = pl.multiple_of(offs_ref[0, q * 4 + r] * blk, 16)
            copies.append(
                pltpu.make_async_copy(
                    dw.at[pl.ds(row, blk), :],
                    dst.at[pl.ds((base + r) * blk, blk), :],
                    sems.at[q * 4 + r],
                )
            )
    for cp in copies:
        cp.start()
    for cp in copies:
        cp.wait()


def pack_kernel(core, qkv, out, cq, ckv, cout, win, gains, biases, keep, send, vecs):
    c = core[0]
    qkv, out, cq, ckv, cout, win, gains, biases = ready(qkv, out, cq, ckv, cout, win, gains, biases)
    vecs[...] = jnp.zeros_like(vecs)
    vecs[0:3, 0:24] = gains[...].astype(F32)
    vecs[3:6, 0:24] = biases[...].astype(F32)
    rows = keep.shape[0]
    wide = jnp.transpose(vecs[...])[:rows].astype(BF)
    for dst, which in ((keep, c), (send, 1 - c)):
        at = 0
        for w, groups in ((qkv, 3), (out, 1), (None, 0), (cout, 1), (cq, 1), (ckv, 2)):
            if w is None:
                dst[:, at : at + 128] = wide
                at += 128
            for k in range(groups):
                lanes = pl.ds(pl.multiple_of(k * D + which * DH, 128), DH)
                dst[:, at : at + DH] = w[:, lanes]
                at += DH
    hr = 96
    for k in range(win.shape[1] // (2 * hr)):
        first = win[:, 2 * k * hr : (2 * k + 1) * hr]
        second = win[:, (2 * k + 1) * hr : (2 * k + 2) * hr]
        keep[:, at + k * hr : at + (k + 1) * hr] = jnp.where(c == 0, first, second)
        send[:, at + k * hr : at + (k + 1) * hr] = jnp.where(c == 0, second, first)


def order_kernel(core, keep, got, wout, one, two, rest):
    c = core[0]
    keep, got, wout = ready(keep, got, wout)
    rows = keep.shape[0]
    at = 0
    for dst in (one, two, rest):
        width = min(dst.shape[1], keep.shape[1] - at)
        a, b = keep[:, at : at + width], got[:, at : at + width]
        dst[0:rows, 0:width] = jnp.where(c == 0, a, b)
        dst[rows:, 0:width] = jnp.where(c == 0, b, a)
        at += width
    rest[:, width : width + D] = wout[0 : 2 * rows, :]
    rest[:, width + D :] = wout[2 * rows :, :]


def cat(parts, after=()):
    shape = (sum(p.shape[0] for p in parts), parts[0].shape[1])
    n = len(parts)

    def body(*refs):
        held, sems = refs[n + 1 :]
        copies, at = [], 0
        for i, r in enumerate(refs[:n]):
            copies.append(pltpu.make_async_copy(r, held.at[pl.ds(at, r.shape[0]), :], sems.at[i]))
            at += r.shape[0]
        for cp in copies:
            cp.start()
        for cp in copies:
            cp.wait()
        out = pltpu.make_async_copy(held, refs[n], sems.at[n])
        out.start()
        out.wait()

    scratch = [pltpu.VMEM(shape, BF), pltpu.SemaphoreType.DMA((n + 1,))]
    return kernel_call(body, parts, [ANY] * n, [sds(shape, BF)], [ANY], scratch, cost=1, after=after)[0]


def split_cat(first, second, after=()):
    rows, width = first.shape[0], first.shape[1] // 2

    def body(*refs):
        held, sems = refs[4:]
        copies = []
        for i in range(2):
            copies.append(pltpu.make_async_copy(refs[i], held.at[pl.ds(i * rows, rows), :], sems.at[i]))
        for cp in copies:
            cp.start()
        for cp in copies:
            cp.wait()
        copies = []
        for j in range(2):
            copies.append(pltpu.make_async_copy(held.at[:, pl.ds(j * width, width)], refs[2 + j], sems.at[2 + j]))
        for cp in copies:
            cp.start()
        for cp in copies:
            cp.wait()

    outs = [sds((2 * rows, width), BF)] * 2
    scratch = [pltpu.VMEM((2 * rows, 2 * width), BF), pltpu.SemaphoreType.DMA((4,))]
    return kernel_call(body, [first, second], [ANY] * 2, outs, [ANY] * 2, scratch, cost=1, after=after)


def prepare_kernel(lens, tok_own, tok_other, cot_own, cot_other, mem_own, mem_other, tok, g, mem, xhat):
    tok_own, tok_other = ready(tok_own, tok_other)
    rows = tok.shape[0] // 2
    seqs, length = mem_own.shape[0], mem_own.shape[1]
    pad = mem.shape[0] // (2 * seqs)
    for b, src in ((0, tok_own), (1, tok_other)):
        tok[b * rows : (b + 1) * rows, :] = src[...]
    flush(tok)

    def norm(s):
        xhat[seq_rows(s), :] = normalise(tok[seq_rows(s), :].astype(F32))[0]

    loop(2 * seqs, norm)
    flush(xhat)
    mem_own, mem_other = ready(mem_own, mem_other)
    for b, src in ((0, mem_own), (1, mem_other)):
        for s in range(seqs):
            at = (b * seqs + s) * pad
            mem[at + length - length % 16 : at + pad, :] = jnp.zeros((pad - length + length % 16, D), BF)
            mem[at : at + length, :] = src[s]
    flush(mem)
    cot_own, cot_other = ready(cot_own, cot_other)
    place = lax.broadcasted_iota(jnp.int32, (LEN, D), 0)
    for b, src in ((0, cot_own), (1, cot_other)):
        for s in range(seqs):
            at = (b * seqs + s) * LEN
            live = (place < lens[b * seqs + s]).astype(F32)
            g[at : at + LEN, :] = (src[s * LEN : (s + 1) * LEN, :].astype(F32) * live).astype(BF)


def self_kernel(lens, core, offs, a, b, ab, own, xhat, keep, back, first, packed, probs, comb, vec, wqkv, gcol, sems):
    c = core[0]
    blk = D // 16
    rows = Rows((own, a, b, ab), offs, 0, [(4 * DH, 4 * DH + 128, 1, blk, 0), (0, 3 * DH, 0, blk, 0)], (wqkv, gcol), sems)
    rows.wait()
    flush(wqkv)
    xhat = ready(xhat)
    vec[...] = jnp.transpose(gcol[...].astype(F32))[:8]
    gain, bias = vec[0:1], vec[3:4]

    def norm(s):
        first[seq_rows(s), :] = (xhat[seq_rows(s), :] * gain + bias).astype(BF)

    loop(8, norm)
    flush(first)

    def proj(b):
        rows = pl.ds(pl.multiple_of(b * 256, 256), 256)
        packed[rows, :] = nn(first[rows, :], wqkv[...]).astype(BF)

    loop(2, proj)
    flush(packed)
    key = lax.broadcasted_iota(jnp.int32, (LEN, DH), 0)
    query = lax.broadcasted_iota(jnp.int32, (LEN, DH), 1) & (LEN - 1)

    def att(s):
        allowed = (key <= query) & (key < lens[s])
        rows = seq_rows(s)
        p, m = attend(packed[rows, 0:DH], packed[rows, DH : 2 * DH], packed[rows, 2 * DH :], allowed)
        probs[s] = p
        comb[rows, D:] = m

    loop(8, att, 2)
    flush(probs)
    keep, back = ready(keep, back)
    comb[:, half_lanes(c)] = nn(comb[:, D:], keep[:DH, :]).astype(BF)
    comb[:, half_lanes(1 - c)] = nn(comb[:, D:], back[DH:, :]).astype(BF)


def kv_kernel(offs, a, b, ab, own, mem, kv, wckv, wcq, sems):
    blk = D // 16
    rows = Rows((own, a, b, ab), offs, 0, [(2 * DH, 4 * DH, 0, blk, 0), (DH, 2 * DH, 1, blk, 0)], (wckv, wcq), sems)
    mem = ready(mem)
    rows.wait()
    flush(wckv, wcq)

    def step(b):
        rows = pl.ds(pl.multiple_of(b * 480, 480), 480)
        kv[rows, :] = nn(mem[rows, :], wckv[...]).astype(BF)

    loop(mem.shape[0] // 480, step)


def swapped(s):
    return pl.ds(pl.multiple_of(((s + 4) & 7) * LEN, LEN), LEN)


def cross_kernel(mem_len, core, vec, tok, part, recv, wcq, kv, keep, back, resid, second, cq, probs, comb):
    c = core[0]
    vec, tok, part, recv = ready(vec, tok, part, recv)
    gain, bias = vec[1:2], vec[4:5]

    def norm(s):
        rows = seq_rows(s)
        both = part[rows, 0:D].astype(F32) + recv[swapped(s), 0:D].astype(F32)
        v = tok[rows, :].astype(F32) + both
        resid[rows, :] = v
        xhat, _ = normalise(v)
        second[rows, :] = (xhat * gain + bias).astype(BF)

    loop(8, norm)
    flush(resid, second)
    wcq = ready(wcq)
    cq[...] = nn(second[...], wcq[...]).astype(BF)
    flush(cq)
    kv = ready(kv)
    pad = probs.shape[1]
    allowed = lax.broadcasted_iota(jnp.int32, (pad, DH), 0) < mem_len

    def att(s):
        rows = seq_rows(s)
        keys = pl.ds(pl.multiple_of(s * pad, 16), pad)
        p, m = attend(cq[rows, :], kv[keys, 0:DH], kv[keys, DH:], allowed)
        probs[s] = p
        comb[rows, D:] = m

    loop(8, att, 2)
    flush(probs)
    keep, back = ready(keep, back)
    comb[:, half_lanes(c)] = nn(comb[:, D:], keep[:DH, :]).astype(BF)
    comb[:, half_lanes(1 - c)] = nn(comb[:, D:], back[DH:, :]).astype(BF)


def keys_and_cross_kernel(
    mem_len, offs, a, b, ab, own, mem, core, vec, tok, part, recv, keep, back, kv, wckv, wcq, resid, second, cq, probs, comb, sems
):
    kv_kernel(offs, a, b, ab, own, mem, kv, wckv, wcq, sems)
    cross_kernel(mem_len, core, vec, tok, part, recv, wcq, kv, keep, back, resid, second, cq, probs, comb)


def inner_kernel(resid, part, recv, vec, win, resid_two, third, hidden, slope):
    resid, part, recv, vec = ready(resid, part, recv, vec)
    gain, bias = vec[2:3], vec[5:6]

    def norm(s):
        rows = seq_rows(s)
        both = part[rows, 0:D].astype(F32) + recv[swapped(s), 0:D].astype(F32)
        v = resid[rows, :] + both
        resid_two[rows, :] = v
        xhat, _ = normalise(v)
        third[rows, :] = (xhat * gain + bias).astype(BF)

    loop(8, norm)
    flush(resid_two, third)
    win = ready(win)

    def step(b):
        rows = pl.ds(pl.multiple_of(b * 128, 128), 128)
        x = nn(third[rows, :], win[...])
        cdf = 0.5 + 0.5 * lax.erf(x * (0.5**0.5))
        hidden[rows, :] = (x * cdf).astype(BF)
        density = jnp.exp(x * x * -0.5) * ((2.0 * np.pi) ** -0.5)
        slope[rows, :] = (cdf + x * density).astype(BF)

    loop(4, step)


def mlp_kernel(offs, pa, pb, pab, pown, g, slope, win, hidden, own, comb, ginner, wout, sems):
    half = own.shape[0]
    blk = D // 16
    cols = [(0, D, 0, 2 * blk, 0), (D, 2 * D, 0, 2 * blk, blk)]
    columns = Rows((pown, pa, pb, pab), offs, 0, cols, (wout,), sems)
    g, slope = ready(g, slope)
    columns.wait()
    win = ready(win)

    def back(b):
        rows = pl.ds(pl.multiple_of(b * 256, 256), 256)
        gh = nt(g[rows, :], wout[...])
        ginner[rows, :] = (gh * slope[rows, :].astype(F32)).astype(BF)
        comb[rows, :] = nt(ginner[rows, :], win[...]).astype(BF)

    loop(2, back)
    flush(ginner)
    hidden = ready(hidden)
    own[...] = nn(hidden[0:half, :], wout[...]).astype(BF)
    comb[2 * half :, :] = nn(hidden[half:, :], wout[...]).astype(BF)


def dmlpout_kernel(offs, hidden, g, *refs):
    outs, dw, sems = refs[:3], refs[3], refs[4]
    hidden, g = ready(hidden, g)
    blk = dw.shape[0] // 16
    for b in range(4):
        part = tn(hidden[:, b * 8 * blk : (b + 1) * 8 * blk], g[...]).astype(BF)
        for k in range(8):
            row = (4 * b + k // 2) * blk
            dw[row : row + blk, (k % 2) * D : (k % 2 + 1) * D] = part[k * blk : (k + 1) * blk]
    send_out(dw, offs, outs, sems)


def mlp_and_grad_kernel(
    offs, pa, pb, pab, pown, g, slope, win, hidden, third, own, comb, to_own, to_b, to_a, ginner, wout, dw, sems, more_sems
):
    mlp_kernel(offs, pa, pb, pab, pown, g, slope, win, hidden, own, comb, ginner, wout, sems)
    dmlpin_kernel(offs, third, ginner, to_own, to_b, to_a, dw, more_sems)


def dmlpin_kernel(offs, third, ginner, *refs):
    third, ginner = ready(third, ginner)
    outs, dw, sems = refs[:3], refs[3], refs[4]
    for b in range(0, dw.shape[0], 256):
        dw[b : b + 256, :] = tn(third[:, b : b + 256], ginner[...]).astype(BF)
    send_out(dw, offs, outs, sems)


def cross_back_kernel(
    core, vec, resid, part, recv, own, g, keep, back, kv, cq, probs, wcq, output, gresid, gtwo, dcq, dkv, gsecond, dvec, gm
):
    c = core[0]
    vec, resid, part, recv, own, g = ready(vec, resid, part, recv, own, g)
    gain = vec[2:3]
    dvec[...] = jnp.zeros_like(dvec)

    def norm(s):
        rows = seq_rows(s)
        dy = part[rows, :].astype(F32) + recv[swapped(s), :].astype(F32)
        dx, dg, db = norm_back(resid[rows, :], gain, dy)
        total = g[rows, :].astype(F32) + dx
        gresid[rows, :] = total
        gtwo[rows, :] = total.astype(BF)

        @pl.when(s < 4)
        def _():
            dvec[0:1, :] += dg
            dvec[1:2, :] += db
            extra = own[rows, :].astype(F32) + recv[pl.ds(pl.multiple_of(512 + s * LEN, LEN), LEN), :].astype(F32)
            output[rows, :] = (resid[rows, :] + extra).astype(BF)

    loop(8, norm)
    flush(output, gresid, gtwo, dvec)
    keep, back = ready(keep, back)
    gm[...] = (nt(gtwo[:, half_lanes(c)], keep[:DH, :]) + nt(gtwo[:, half_lanes(1 - c)], back[DH:, :])).astype(BF)
    pad = probs.shape[1]
    kv, cq, probs = ready(kv, cq, probs)

    def att(s):
        rows = seq_rows(s)
        keys = pl.ds(pl.multiple_of(s * pad, 16), pad)
        dq, dk, dv = attend_back(gm[rows, :], cq[rows, :], kv[keys, 0:DH], kv[keys, DH:], probs[s])
        dcq[rows, :] = dq
        dkv[keys, 0:DH] = dk
        dkv[keys, DH:] = dv

    loop(8, att, 2)
    flush(dcq, dkv)
    wcq = ready(wcq)
    gsecond[...] = nt(dcq[...], wcq[...]).astype(BF)


def out_grad(dw, lo, c, mine, other, g):
    cols = half_lanes(c)
    dw[half_lanes(c), lo : lo + DH] = tn(mine[:, D:], g[:, cols]).astype(BF)
    rest = tn(other[256:, D:], g[:256, cols]) + tn(other[:256, D:], g[256:, cols])
    dw[half_lanes(1 - c), lo : lo + DH] = rest.astype(BF)


def dcross_kernel(offs, core, mixed, mixed_other, gtwo, second, dcq, dkv, wckv, mem, *refs):
    outs, gmem, dw, sems = refs[:3], refs[3:5], refs[5], refs[6]
    mixed, mixed_other, gtwo = ready(mixed, mixed_other, gtwo)
    out_grad(dw, 0, core[0], mixed, mixed_other, gtwo)
    second, dcq = ready(second, dcq)
    dw[:, DH : 2 * DH] = tn(second[...], dcq[...]).astype(BF)
    dkv, wckv = ready(dkv, wckv)
    half = dkv.shape[0] // 2
    for i, dst in ((1, gmem[1]), (0, gmem[0])):
        for b in range(0, half, 480):
            dst[b : b + 480, :] = nt(dkv[i * half + b : i * half + b + 480, :], wckv[...]).astype(BF)
    flush(*gmem)
    mem = ready(mem)
    for b in range(0, D, 256):
        dw[b : b + 256, 2 * DH :] = tn(mem[:, b : b + 256], dkv[...]).astype(BF)
    send_out(dw, offs, outs, sems)


def self_back_kernel(
    core, vec, resid, part, recv, gresid_two, keep, back, packed, probs, wqkv, xhat, gresid, gone, dpacked, gfirst_own, gfirst_other, dvec, gm
):
    c = core[0]
    vec, resid, part, recv, gresid_two = ready(vec, resid, part, recv, gresid_two)
    gain = vec[1:2]
    dvec[...] = jnp.zeros_like(dvec)

    def norm(s):
        rows = seq_rows(s)
        dy = part[rows, :].astype(F32) + recv[swapped(s), :].astype(F32)
        dx, dg, db = norm_back(resid[rows, :], gain, dy)
        total = gresid_two[rows, :] + dx
        gone[rows, :] = total.astype(BF)

        @pl.when(s < 4)
        def _():
            gresid[rows, :] = total
            dvec[0:1, :] += dg
            dvec[1:2, :] += db

    loop(8, norm)
    flush(gresid, gone)
    keep, back = ready(keep, back)
    gm[...] = (nt(gone[:, half_lanes(c)], keep[:DH, :]) + nt(gone[:, half_lanes(1 - c)], back[DH:, :])).astype(BF)
    packed, probs = ready(packed, probs)

    def att(s):
        rows = seq_rows(s)
        dq, dk, dv = attend_back(
            gm[rows, :], packed[rows, 0:DH], packed[rows, DH : 2 * DH], packed[rows, 2 * DH :], probs[s]
        )
        dpacked[rows, 0:DH] = dq
        dpacked[rows, DH : 2 * DH] = dk
        dpacked[rows, 2 * DH :] = dv

    loop(8, att, 2)
    flush(dpacked)
    wqkv, xhat = ready(wqkv, xhat)
    half = gfirst_own.shape[0]
    for b, dst in ((half, gfirst_other), (0, gfirst_own)):
        term = nt(dpacked[b : b + half, :], wqkv[...])
        dst[...] = term.astype(BF)
        flush(dst)
        dvec[2:3, :] += jnp.sum(term * xhat[b : b + half, :], 0, keepdims=True)
        dvec[3:4, :] += jnp.sum(term, 0, keepdims=True)


def dself_kernel(offs, core, mixed, mixed_other, gone, first, dpacked, dvec_two, dvec_one, *refs):
    outs, dw, vecs, sems = refs[:3], refs[3], refs[4], refs[5]
    mixed, mixed_other, gone = ready(mixed, mixed_other, gone)
    out_grad(dw, 0, core[0], mixed, mixed_other, gone)
    first, dpacked, dvec_two, dvec_one = ready(first, dpacked, dvec_two, dvec_one)
    for b in range(0, D, 256):
        dw[b : b + 256, DH : 4 * DH] = tn(first[:, b : b + 256], dpacked[...]).astype(BF)
    vecs[...] = jnp.zeros_like(vecs)
    for i, (v, row) in enumerate(((dvec_one, 2), (dvec_one, 0), (dvec_two, 0), (dvec_one, 3), (dvec_one, 1), (dvec_two, 1))):
        vecs[i : i + 1, :] = v[row : row + 1, :]
    dw[:, 4 * DH :] = jnp.transpose(vecs[...]).astype(BF)
    send_out(dw, offs, outs, sems)


def tokens_back_kernel(vec, tok, part, recv, gresid, gmem, gmem_recv, gtok, gmemory):
    vec, tok, part, recv, gresid = ready(vec, tok, part, recv, gresid)
    gain = vec[0:1]

    def norm(s):
        rows = seq_rows(s)
        dy = part[rows, :].astype(F32) + recv[rows, :].astype(F32)
        dx, _, _ = norm_back(tok[rows, :].astype(F32), gain, dy)
        gtok[rows, :] = (gresid[rows, :] + dx).astype(BF)

    loop(4, norm)
    flush(gtok)
    gmem, gmem_recv = ready(gmem, gmem_recv)
    gmemory[...] = (gmem[...].astype(F32) + gmem_recv[...].astype(F32)).astype(BF)


def merge_kernel(kinds, *refs):
    counts = {"pass": (2, 1), "sum": (3, 4), "end": (4, 1)}
    at, out = 0, sum(counts[kind][0] for kind in kinds)
    refs = ready(*refs)
    for kind in kinds:
        ins, outs = refs[at : at + counts[kind][0]], refs[out : out + counts[kind][1]]
        at, out = at + len(ins), out + len(outs)
        if kind == "pass":
            half = ins[0].shape[0]
            outs[0][...] = (ins[0][...].astype(F32) + ins[1][half:, :].astype(F32)).astype(BF)
        elif kind == "end":
            outs[0][...] = ins[0][...] + ins[1][...].astype(F32) + ins[2][...].astype(F32) + ins[3][...].astype(F32)
        else:
            blk = ins[0].shape[0] // 4
            for i in range(4):
                rows = slice(i * blk, (i + 1) * blk)
                total = ins[0][rows, :].astype(F32) + ins[1][rows, :].astype(F32) + ins[2][rows, :].astype(F32)
                outs[i][...] = total.astype(outs[i].dtype)


def merge(jobs, after=()):
    ins, outs = [], []
    for kind, *arrays in jobs:
        ins += arrays
        rows, width = arrays[0].shape
        if kind == "sum":
            outs += [sds((rows // 4, width), F32)] + [sds((rows // 4, width), BF)] * 3
        else:
            outs.append(sds((rows, width), BF if kind == "pass" else F32))
    kinds = [job[0] for job in jobs]
    return kernel_call(
        lambda *refs: merge_kernel(kinds, *refs),
        ins,
        [STAGE] * len(ins),
        outs,
        [STAGE] * len(outs),
        cost=1,
        after=after,
    )


def join_kernel(core, mine, got, *outs):
    c = core[0]
    mine, got = ready(mine, got)
    at = 0
    for out in outs[: 2 if mine.shape[1] > 4 * DH else 3]:
        for k in range(out.shape[1] // D):
            out[:, pl.ds(pl.multiple_of(k * D + c * DH, 128), DH)] = mine[:, at : at + DH]
            out[:, pl.ds(pl.multiple_of(k * D + (1 - c) * DH, 128), DH)] = got[:, at : at + DH]
            at += DH
    if mine.shape[1] > at:
        gains, biases, wide = outs[2:]
        rows = mine.shape[0]
        wide[...] = jnp.zeros_like(wide)
        wide[0:rows, :] = mine[:, at:] + got[:, at:]
        turned = jnp.transpose(wide[...])
        gains[...] = turned[0:3, 0:rows]
        biases[...] = turned[3:6, 0:rows]


class Moves:
    def __init__(self, mesh):
        self.nz, self.nf = mesh.shape["dp"], mesh.shape["fsdp"]
        self.n = self.nz * self.nf
        self.doubling = self.nz == 4 and self.nf == 8

    def permute(self, x, target):
        pairs = [(d, target(d // self.nf, (d % self.nf) // 2, d % 2)) for d in range(self.n)]
        return lax.ppermute(x, AXES, [(a, (z * self.nf) + 2 * yx + c) for a, (z, yx, c) in pairs])

    def sibling(self, x):
        return self.permute(x, lambda z, yx, c: (z, yx, 1 - c))

    def near_z(self, x):
        return self.permute(x, lambda z, yx, c: (z ^ 1, yx, c))

    def far_z(self, x):
        return self.permute(x, lambda z, yx, c: (z ^ 2, yx, c))

    def side_a(self, x):
        return self.permute(x, lambda z, yx, c: (z, yx ^ (1 + c), c))

    def side_b(self, x):
        return self.permute(x, lambda z, yx, c: (z, yx ^ (2 - c), c))

    def opposite_z(self, x):
        return self.permute(x, lambda z, yx, c: (z ^ 3, yx, c))


def per_device(moves, tokens, memory, lengths, cotangent, self_qkv, self_out, cross_q, cross_kv, cross_out, mlp_in, mlp_out, norm_gains, norm_biases):
    seqs, mem_len = memory.shape[0], memory.shape[1]
    rows = seqs * LEN
    place = lax.axis_index(AXES)
    c = place % 2
    chip = place // 2
    core = jnp.reshape(c, (1,)).astype(jnp.int32)
    wr, hr = self_qkv.shape[0], mlp_out.shape[0]
    ff = mlp_in.shape[1]
    fh = ff // 2
    r2, s2 = 2 * rows, 2 * seqs
    wb = D // 16
    pad = -(-mem_len // 16) * 16
    fast = moves.doubling


    def prepare(lens, pairs, after=()):
        return kernel_call(
            prepare_kernel,
            [lens, *pairs],
            [SM] + [STAGE] * 6,
            [sds((r2, D), BF)] * 2 + [sds((s2 * pad, D), BF), sds((r2, D), F32)],
            [STAGE] * 4,
            after=after,
        )

    def self_attention(pieces, lens, xhat, keep, back, after=()):
        own, a, b, ab = pieces
        return kernel_call(
            self_kernel,
            [lens, core, offs, a, b, ab, own, xhat, keep, back],
            [SM] * 3 + [ANY] * 4 + [STAGE] * 3,
            [
                sds((r2, D), BF),
                sds((r2, 3 * DH), BF),
                sds((s2, LEN, DH), BF),
                sds((r2, 3 * DH), BF),
                sds((8, D), F32),
                sds((D, 3 * DH), BF),
            ],
            [STAGE] * 6,
            [pltpu.VMEM((D, 128), BF), pltpu.SemaphoreType.DMA((32,))],
            cost=6,
            after=after,
        )

    def cross_attention(pieces, mem, vec, tok, comb, recv, keep, back, after=()):
        own, a, b, ab = pieces
        kv_rows = s2 * pad
        return kernel_call(
            lambda *refs: keys_and_cross_kernel(mem_len, *refs),
            [offs, a, b, ab, own, mem, core, vec, tok, comb, recv, keep, back],
            [SM] + [ANY] * 4 + [STAGE, SM] + [STAGE] * 6,
            [
                sds((kv_rows, D), BF),
                sds((D, 2 * DH), BF),
                sds((D, DH), BF),
                sds((r2, D), F32),
                sds((r2, D), BF),
                sds((r2, DH), BF),
                sds((s2, pad, DH), BF),
                sds((r2, 3 * DH), BF),
            ],
            [STAGE] * 8,
            [pltpu.SemaphoreType.DMA((32,))],
            cost=12,
            after=after,
        )

    def inner_part(resid_one, comb, recv, vec, w_in, after=()):
        return kernel_call(
            inner_kernel,
            [resid_one, comb, recv, vec, w_in],
            [STAGE] * 5,
            [sds((r2, D), F32), sds((r2, D), BF), sds((r2, fh), BF), sds((r2, fh), BF)],
            [STAGE] * 4,
            cost=5,
            after=after,
        )

    def inner_weight(pieces):
        return place_rows(pieces, offs, 0, [(0, fh, 0, wb, 0)], (D, fh))

    def grads(body, ins, specs, ncols, extra=(), scratch=(), cost=5, after=()):
        return kernel_call(
            body,
            [offs, *ins],
            [SM, *specs],
            [sds((4 * wb, ncols), BF)] * 2 + [sds((8 * wb, ncols), BF)] + list(extra),
            [ANY] * 3 + [STAGE] * len(extra),
            [pltpu.VMEM((D, ncols), BF), *scratch, pltpu.SemaphoreType.DMA((16,))],
            cost=cost,
            after=after,
        )

    def mlp_part(pieces, g, slope, w_in, hidden, third, after=()):
        own, a, b, ab = pieces
        return kernel_call(
            mlp_and_grad_kernel,
            [offs, a, b, ab, own, g, slope, w_in, hidden, third],
            [SM] + [ANY] * 4 + [STAGE] * 5,
            [sds((rows, D), BF), sds((3 * rows, D), BF)]
            + [sds((4 * wb, fh), BF)] * 2
            + [sds((8 * wb, fh), BF)],
            [STAGE] * 2 + [ANY] * 3,
            [
                pltpu.VMEM((r2, fh), BF),
                pltpu.VMEM((fh, D), BF),
                pltpu.VMEM((D, fh), BF),
                pltpu.SemaphoreType.DMA((32,)),
                pltpu.SemaphoreType.DMA((16,)),
            ],
            cost=11,
            after=after,
        )

    def cross_back(resid_two, comb, recv, part, after=()):
        return kernel_call(
            cross_back_kernel,
            [core, vec, resid_two, comb, recv, part, g, *cout, kv, cq, cprobs, w_cq],
            [SM] + [STAGE] * 12,
            [
                sds((rows, D), BF),
                sds((r2, D), F32),
                sds((r2, D), BF),
                sds((r2, DH), BF),
                sds(kv.shape, BF),
                sds((r2, D), BF),
                sds((8, D), F32),
            ],
            [STAGE] * 7,
            scratch=[pltpu.VMEM((r2, DH), BF)],
            cost=11,
            after=after,
        )

    def self_back(gsecond, recv, gresid_two, after=()):
        return kernel_call(
            self_back_kernel,
            [core, vec, resid_one, gsecond, recv, gresid_two, *out, packed, probs, w_qkv, xhat],
            [SM] + [STAGE] * 11,
            [
                sds((rows, D), F32),
                sds((r2, D), BF),
                sds((r2, 3 * DH), BF),
                sds((rows, D), BF),
                sds((rows, D), BF),
                sds((8, D), F32),
            ],
            [STAGE] * 6,
            scratch=[pltpu.VMEM((r2, DH), BF)],
            cost=9,
            after=after,
        )

    def cross_grads(after=()):
        return grads(
            dcross_kernel,
            [core, *cross_mixed, gtwo, second, dcq, dkv, w_ckv, mem],
            [SM] + [STAGE] * 8,
            4 * DH,
            [sds((seqs * pad, D), BF)] * 2,
            cost=10,
            after=after,
        )

    def self_grads(after=()):
        return grads(
            dself_kernel,
            [core, *self_mixed, gone, first, dpacked, dvec_two, dvec_one],
            [SM] + [STAGE] * 7,
            4 * DH + 128,
            scratch=[pltpu.VMEM((128, D), F32)],
            cost=6,
            after=after,
        )

    def tokens_back(recv, gmem_recv, after=()):
        return kernel_call(
            tokens_back_kernel,
            [vec, tokens.reshape(rows, D), gfirst, recv, gresid_one, gmem, gmem_recv],
            [STAGE] * 7,
            [sds((rows, D), BF), sds(gmem.shape, BF)],
            [STAGE] * 2,
            cost=4,
            after=after,
        )

    sib = moves.sibling
    pairs = []
    for x in (tokens.reshape(rows, D), cotangent.reshape(rows, D), memory):
        pairs += [x, sib(x)]
    lens = jnp.concatenate([lengths, sib(lengths)], 0)


    bits = jnp.arange(4, dtype=jnp.int32)
    if fast:
        plane = jnp.stack([jnp.int32(0), 1 + c, 2 - c, jnp.int32(3)]).astype(jnp.int32)
        z, yx = chip // 4, chip % 4
        chips = ((z ^ bits)[None, :] * 4 + (yx ^ plane)[:, None]).reshape(16).astype(jnp.int32)
    else:
        chips = jnp.arange(16, dtype=jnp.int32)
    turned = ((chips // 8) ^ c) * 8 + chips % 8
    offs = jnp.stack([chips, turned]).astype(jnp.int32)
    widths = (4 * DH + 128, 4 * DH, 4 * DH)

    if fast:
        keep, send = kernel_call(
            pack_kernel,
            [core, self_qkv, self_out, cross_q, cross_kv, cross_out, mlp_in, norm_gains, norm_biases],
            [SM] + ["stage"] * 8,
            [sds((wr, sum(widths)), BF)] * 2,
            [STAGE] * 2,
            scratch=[pltpu.VMEM((128, 128), F32)],
            cost=1,
            limit=60 << 20,
        )
        one, two, rest = kernel_call(
            order_kernel,
            [core, keep, sib(send), mlp_out],
            [SM] + [STAGE] * 3,
            [sds((2 * wr, w), BF) for w in (widths[0], widths[1], 8 * DH)],
            [STAGE] * 3,
            cost=1,
            after=[lens, pairs[1], pairs[3]],
        )
        along = [moves.near_z(one), moves.far_z(one), moves.opposite_z(one)]
        near_two = moves.near_z(two)
        tok, g, mem, xhat = prepare(lens, pairs, after=(one,))
        one = cat([one, *along], after=(tok, near_two))
        two = cat([two, near_two], after=(one,))
        rest = tie(rest, two)
        a1, b1, far_two, near_rest = moves.side_a(one), moves.side_b(one), moves.far_z(two), moves.near_z(rest)
        a1 = tie(a1, b1)
        two = cat([two, far_two], after=(a1, near_rest))
        three, four = split_cat(rest, near_rest, after=(two,))
        ab1, a2, b2, far_three = moves.side_b(a1), moves.side_a(two), moves.side_b(two), moves.far_z(three)
        a2 = tie(a2, b2, ab1)
        three = cat([three, far_three], after=(a2,))
        out = out_rows([one, a1, b1, ab1], offs, 3 * DH)
        out = (out, sib(out))
        four, three, a2 = tie(four, out[1], three), tie(three, out[1]), tie(a2, out[1])
        ab2, a3, b3, far_four = moves.side_b(a2), moves.side_a(three), moves.side_b(three), moves.far_z(four)
        first, packed, probs, comb, vec, w_qkv = self_attention([one, a1, b1, ab1], lens, xhat, *out, after=(four,))
        a3 = tie(a3, b3, ab2, comb)
        four = cat([four, far_four], after=(a3,))
        cout = out_rows([two, a2, b2, ab2], offs, 0)
        cout = (cout, sib(cout))
        comb = tie(comb, four)
        self_mixed = (comb, sib(comb))
        ab3, a4, b4 = moves.side_b(a3), moves.side_a(four), moves.side_b(four)
        kv, w_ckv, w_cq, resid_one, second, cq, cprobs, comb = cross_attention(
            [two, a2, b2, ab2], mem, vec, tok, *self_mixed, *cout, after=(four,)
        )
        a4 = tie(a4, b4, ab3, comb)
        ab4 = moves.side_b(a4)
        comb = tie(comb, a4)
        cross_mixed = (comb, sib(comb))
        w_in = inner_weight([three, a3, b3, ab3])
        resid_two, third, hidden, slope = inner_part(resid_one, *cross_mixed, vec, w_in)
        last = [four, a4, b4, ab4]
        after = (ab4,)
    else:
        tok, g, mem, xhat = prepare(lens, pairs)
        whole = lambda w: lax.all_gather(w, AXES, axis=0, tiled=True)
        split = lambda w: [w[i * w.shape[0] // 4 : (i + 1) * w.shape[0] // 4] for i in range(4)]

        def col_half(w, groups):
            w = w.reshape(w.shape[0], groups, 2, w.shape[1] // (2 * groups))
            return lax.dynamic_index_in_dim(w, c, 2, keepdims=False).reshape(w.shape[0], -1)

        vectors = jnp.pad(jnp.concatenate([norm_gains, norm_biases], 0).T, ((0, 0), (0, 122)))
        one = jnp.concatenate([col_half(self_qkv, 3), col_half(self_out, 1), vectors], 1)
        two = jnp.concatenate([col_half(w, w.shape[1] // D) for w in (cross_out, cross_q, cross_kv)], 1)
        one, two = split(whole(one)), split(whole(two))
        three = split(whole(col_half(mlp_in, ff // (2 * hr))))
        out, cout = out_rows(one, offs, 3 * DH), out_rows(two, offs, 0)
        out, cout = (out, sib(out)), (cout, sib(cout))
        rowed = whole(mlp_out).reshape(moves.n // 2, 2, hr, D)
        rowed = lax.dynamic_index_in_dim(rowed, c, 1, keepdims=False).reshape(16, 2, fh // 32, D)
        last = split(rowed.transpose(0, 2, 1, 3).reshape(D, 2 * D))
        first, packed, probs, comb, vec, w_qkv = self_attention(one, lens, xhat, *out)
        self_mixed = (comb, sib(comb))
        kv, w_ckv, w_cq, resid_one, second, cq, cprobs, comb = cross_attention(
            two, mem, vec, tok, *self_mixed, *cout
        )
        cross_mixed = (comb, sib(comb))
        w_in = inner_weight(three)
        resid_two, third, hidden, slope = inner_part(resid_one, *cross_mixed, vec, w_in)
        after = ()


    side_a, side_b = moves.side_a, moves.side_b

    def along_z(blocks):
        return [moves.near_z(blocks[0]), moves.far_z(blocks[1]), moves.opposite_z(blocks[2])]

    d_mlpout = grads(dmlpout_kernel, [hidden, g], [STAGE] * 2, 2 * D, after=after)
    if fast:
        got_a1 = side_a(d_mlpout[2])
    part, comb, *d_mlpin = mlp_part(last, g, slope, w_in, hidden, third, after=d_mlpout[:1])
    if fast:
        (on,) = merge([("pass", d_mlpout[1], got_a1)], after=(part,))
        comb = tie(comb, on)
        got_b1, got_a2 = side_b(on), side_a(tie(d_mlpin[2], on))
        after = (on,)
    recv = sib(comb)
    output, gresid_two, gtwo, dcq, dkv, gsecond, dvec_two = cross_back(resid_two, comb, recv, part, after=after)
    if fast:
        on, kept1, *sums1 = merge([("pass", d_mlpin[1], got_a2), ("sum", d_mlpout[0], got_a1, got_b1)], after=(dcq,))
        got_b2, got_z1 = side_b(on), along_z(sums1)
        gsecond = tie(gsecond, on)
        after = (on,)
    recv = sib(gsecond)
    *d_cross, gmem, gmem_other = cross_grads(after=after)
    if fast:
        kept2, *sums2, total1 = merge([("sum", d_mlpin[0], got_a2, got_b2), ("end", kept1, *got_z1)], after=(gmem,))
        got_z2, got_a3 = along_z(sums2), side_a(tie(d_cross[2], kept2))
        after = (kept2,)
    gresid_one, gone, dpacked, gfirst, gfirst_other, dvec_one = self_back(gsecond, recv, gresid_two, after=after)
    if fast:
        on, total2 = merge([("pass", d_cross[1], got_a3), ("end", kept2, *got_z2)], after=(gone,))
        got_b3 = side_b(on)
        gfirst_other, gmem_other = tie(gfirst_other, on), tie(gmem_other, on)
        after = (on,)
    recv, gmem_recv = sib(gfirst_other), sib(gmem_other)
    d_self = self_grads(after=after)
    if fast:
        kept3, *sums3 = merge([("sum", d_cross[0], got_a3, got_b3)], after=[d_self[0], recv, gmem_recv])
        got_z3, got_a4 = along_z(sums3), side_a(tie(d_self[2], kept3))
        after = (kept3,)
    grad_tokens, grad_memory = tokens_back(recv, gmem_recv, after=after)
    grad_memory = grad_memory.reshape(seqs, pad, D)[:, :mem_len]

    if fast:
        on, total3 = merge([("pass", d_self[1], got_a4), ("end", kept3, *got_z3)], after=(grad_tokens,))
        got_b4 = side_b(on)
        kept4, *sums4 = merge([("sum", d_self[0], got_a4, got_b4)])
        got_z4 = along_z(sums4)
        (total4,) = merge([("end", kept4, *got_z4)])
        total = [total1, total2, total3, total4]

        def own_rows(total):
            mine = lax.dynamic_slice_in_dim(total, c * wr, wr, 0)
            return mine, sib(lax.dynamic_slice_in_dim(total, (1 - c) * wr, wr, 0))

        def join(pair, *shapes, scratch=()):
            return kernel_call(
                join_kernel,
                [core, *pair],
                [SM, STAGE, STAGE],
                [sds(shape, F32) for shape in shapes],
                [STAGE] * len(shapes),
                scratch=scratch,
                cost=1,
            )

        sum_mlpout = jnp.concatenate([total[0][:, :D], total[0][:, D:]], 0)
        mine, got = own_rows(total[1])
        pair = (jnp.where(c == 0, mine, got), jnp.where(c == 0, got, mine))
        parts = [p.reshape(wr, ff // (2 * hr), 1, hr) for p in pair]
        grad_in = jnp.concatenate(parts, 2).reshape(wr, ff)
        grad_cout, grad_cq, grad_ckv = join(own_rows(total[2]), (wr, D), (wr, D), (wr, 2 * D))
        grad_out, grad_qkv, own_gains, own_biases = join(
            own_rows(total[3]), (wr, D), (wr, 3 * D), (3, wr), (3, wr), scratch=[pltpu.VMEM((128, 128), F32)]
        )
    else:

        def placed(parts):
            own, to_b, to_a = parts
            term = jnp.concatenate([own, to_a[: 4 * wb], to_b, to_a[4 * wb :]], 0).astype(F32)
            both = jnp.stack([jnp.where(c == 0, term, 0.0), jnp.where(c == 1, term, 0.0)], 1)
            return lax.psum_scatter(both, AXES, scatter_dimension=0, tiled=True)

        def joined(total, lo, hi, groups):
            return total[:, :, lo:hi].reshape(wr, 2, groups, -1).transpose(0, 2, 1, 3).reshape(wr, -1)

        total = placed(d_cross)
        grad_cout, grad_cq, grad_ckv = (
            joined(total, 0, DH, 1),
            joined(total, DH, 2 * DH, 1),
            joined(total, 2 * DH, 4 * DH, 2),
        )
        total = placed(d_self)
        grad_out, grad_qkv = joined(total, 0, DH, 1), joined(total, DH, 4 * DH, 3)
        vectors = jnp.sum(total[:, :, 4 * DH : 4 * DH + 6], 1).T
        own_gains, own_biases = vectors[:3], vectors[3:]
        grad_in = joined(placed(d_mlpin), 0, fh, ff // (2 * hr))
        own, to_b, to_a = d_mlpout
        term = jnp.concatenate([own, to_a[: 4 * wb], to_b, to_a[4 * wb :]], 0).astype(F32)
        term = term.reshape(16, wb, 2, D).transpose(0, 2, 1, 3).reshape(moves.n // 2, 1, hr, D)
        both = jnp.concatenate([jnp.where(c == 0, term, 0.0), jnp.where(c == 1, term, 0.0)], 1)
        sum_mlpout = lax.psum_scatter(both.reshape(ff, D), AXES, scatter_dimension=0, tiled=True)

    return (
        output.reshape(tokens.shape),
        grad_tokens.reshape(tokens.shape),
        grad_memory,
        grad_qkv,
        grad_out,
        grad_cq,
        grad_ckv,
        grad_cout,
        grad_in,
        sum_mlpout,
        own_gains,
        own_biases,
    )


def solution(mesh):
    batch = P(AXES, None, None)
    rows = P(AXES, None)
    cols = P(None, AXES)
    moves = Moves(mesh)
    in_specs = (batch, batch, P(AXES), batch) + (rows,) * 7 + (cols,) * 2
    out_specs = (batch,) * 3 + (rows,) * 7 + (cols,) * 2
    return jax.shard_map(
        lambda *args: per_device(moves, *args),
        mesh=mesh,
        in_specs=in_specs,
        out_specs=out_specs,
        check_vma=False,
    )
```

```python
import jax
import jax.numpy as jnp
import numpy as np
from jax import lax
from jax.experimental import pallas as pl
from jax.experimental.pallas import tpu as pltpu
from jax.sharding import PartitionSpec as P

AXES = ("dp", "fsdp")
HEADS = 12
HALF = HEADS // 2
HEAD = 64
D = 768
DH = D // 2
LEN = 64
EPS = 1e-06
NEG = -1e30
SCALE = HEAD ** (-0.5)
F32 = jnp.float32
BF = jnp.bfloat16
VMEM_LIMIT = 14 << 20

VM = pl.BlockSpec(memory_space=pltpu.VMEM)
SM = pl.BlockSpec(memory_space=pltpu.SMEM)
ANY = pl.BlockSpec(memory_space=pl.ANY)


def sds(shape, dtype):
    return jax.ShapeDtypeStruct(shape, dtype)


STAGE = VM


class Staged:
    def __init__(self, ref, copy):
        self.ref, self.copy, self.waited = ref, copy, False
        self.shape = ref.shape

    def ready(self):
        if not self.waited:
            self.copy.wait()
            self.waited = True
        return self.ref


PENDING = {}


def flush(*refs):
    for r in refs:
        if id(r) in PENDING:
            PENDING[id(r)].start()
            PENDING[id(r)] = None


def ready(*refs):
    out = [r.ready() if isinstance(r, Staged) else r for r in refs]
    return out[0] if len(out) == 1 else out


def kernel_call(body, ins, in_specs, outs, out_specs=None, scratch=(), cost=5, after=(), limit=None, hold=()):
    n, skip, m, k = len(ins), len(after) + len(hold), len(outs), len(scratch)
    out_specs = [VM] * m if out_specs is None else list(out_specs)
    staged_in = [i for i, spec in enumerate(in_specs) if spec == 'stage']
    staged_out = [i for i, spec in enumerate(out_specs) if spec == 'stage']
    buffers = [pltpu.VMEM(ins[i].shape, ins[i].dtype) for i in staged_in]
    buffers += [pltpu.VMEM(outs[i].shape, outs[i].dtype) for i in staged_out]
    extra = [*buffers, pltpu.SemaphoreType.DMA((len(buffers),))] if buffers else []

    def run(*refs):
        ins, outs = list(refs[:n]), list(refs[n + skip : n + skip + m])
        own = refs[n + skip + m : n + skip + m + k]
        PENDING.clear()
        if not buffers:
            body(*ins, *outs, *own)
            return
        held, sems = refs[n + skip + m + k : -1], refs[-1]
        for j, i in enumerate(staged_in):
            copy = pltpu.make_async_copy(ins[i], held[j], sems.at[j])
            copy.start()
            ins[i] = Staged(held[j], copy)
        copies = []
        for j, i in enumerate(staged_out, len(staged_in)):
            copies.append(pltpu.make_async_copy(held[j], outs[i], sems.at[j]))
            outs[i] = held[j]
            PENDING[id(held[j])] = copies[-1]
        body(*ins, *outs, *own)
        ready(*ins)
        for cp in PENDING.values():
            if cp is not None:
                cp.start()
        for cp in copies:
            cp.wait()

    space = lambda spec: ANY if spec == 'stage' else spec
    return pl.pallas_call(
        run,
        out_shape=list(outs),
        in_specs=[space(spec) for spec in in_specs] + [ANY] * len(after) + [VM] * len(hold),
        out_specs=[space(spec) for spec in out_specs],
        scratch_shapes=[*scratch, *extra],
        compiler_params=pltpu.CompilerParams(vmem_limit_bytes=limit or VMEM_LIMIT),
        cost_estimate=pl.CostEstimate(flops=cost * 7 * 10**9, bytes_accessed=0, transcendentals=0),
    )(*ins, *after, *hold)


def tie(x, *earlier):
    return pl.pallas_call(
        lambda *refs: None,
        out_shape=sds(x.shape, x.dtype),
        in_specs=[ANY] * (1 + len(earlier)),
        out_specs=ANY,
        input_output_aliases={0: 0},
        compiler_params=pltpu.CompilerParams(vmem_limit_bytes=1 << 20),
        cost_estimate=pl.CostEstimate(flops=0, bytes_accessed=0, transcendentals=0),
    )(x, *earlier)


def nn(a, b):
    return lax.dot_general(a, b, (((1,), (0,)), ((), ())), preferred_element_type=F32)


def nt(a, b):
    return lax.dot_general(a, b, (((1,), (1,)), ((), ())), preferred_element_type=F32)


def tn(a, b):
    return lax.dot_general(a, b, (((0,), (0,)), ((), ())), preferred_element_type=F32)


def normalise(v):
    mean = jnp.mean(v, -1, keepdims=True)
    cen = v - mean
    inv = lax.rsqrt(jnp.mean(cen * cen, -1, keepdims=True) + EPS)
    return cen * inv, inv


def norm_back(v, gain, dy):
    xhat, inv = normalise(v)
    dxh = dy * gain
    m1 = jnp.mean(dxh, -1, keepdims=True)
    m2 = jnp.mean(dxh * xhat, -1, keepdims=True)
    dx = inv * (dxh - m1 - xhat * m2)
    return dx, jnp.sum(dy * xhat, 0, keepdims=True), jnp.sum(dy, 0, keepdims=True)


def head_of_lane(rows):
    return lax.shift_right_logical(lax.broadcasted_iota(jnp.int32, (rows, DH), 1), 6)


def spread(q):
    head = head_of_lane(1)
    parts = [q * (head == h).astype(F32).astype(q.dtype) for h in range(HALF)]
    return jnp.concatenate(parts, 0)


def fold(o):
    head = head_of_lane(LEN)
    total = jnp.where(head == 0, o[:LEN], 0.0)
    for h in range(1, HALF):
        total = jnp.where(head == h, o[h * LEN : (h + 1) * LEN], total)
    return total


def attend(q, k, v, allowed):
    st = nt(k, spread(q)) * SCALE
    st = jnp.where(allowed, st, NEG)
    e = jnp.exp(st - jnp.max(st, 0, keepdims=True))
    p = (e * (1.0 / jnp.sum(e, 0, keepdims=True))).astype(BF)
    return p, fold(tn(p, v)).astype(BF)


def attend_back(g, q, k, v, p):
    gs, qs = spread(g), spread(q)
    dp = nt(v, gs)
    pf = p.astype(F32)
    t = pf * dp
    ds = (t - pf * jnp.sum(t, 0, keepdims=True)).astype(BF)
    dq = (fold(tn(ds, k)) * SCALE).astype(BF)
    dk = (nn(ds, qs) * SCALE).astype(BF)
    dv = nn(p, gs).astype(BF)
    return dq, dk, dv


def seq_rows(s):
    return pl.ds(pl.multiple_of(s * LEN, LEN), LEN)


def half_lanes(c):
    return pl.ds(pl.multiple_of(c * DH, DH), DH)


def loop(n, body, unroll=1):
    def step(i, carry):
        body(i)
        return carry

    lax.fori_loop(0, n, step, 0, unroll=unroll)


def columns_first(pieces, q, r):
    blk = pieces[0].shape[0] // 4
    return pieces[q], r * blk


def place(pieces, offs_ref, which, cols, targets):
    blk = pieces[0].shape[0] // 4
    for lo, hi, o, step, shift in cols:
        for q in range(4):
            for r in range(4):
                row = pl.multiple_of(offs_ref[which, q * 4 + r] * step + shift, 16)
                targets[o][pl.ds(row, blk), :] = pieces[q][r * blk : (r + 1) * blk, lo:hi]


def place_levels(near, far, offs_ref, step, shift, target):
    blk = near.shape[0] // 8
    lo = 0
    for level, src in ((0, near), *((2, part) for part in far)):
        at = 0 if level == 0 else lo
        for q in range(4):
            for r in range(2):
                row = pl.multiple_of(offs_ref[0, q * 4 + level + r] * step + shift, 16)
                rows = slice((r * 4 + q) * blk, (r * 4 + q + 1) * blk)
                target[pl.ds(row, blk), at : at + src.shape[1]] = src[rows, :]
        lo += src.shape[1] if level else 0


def place_rows(pieces, offs, which, cols, shape, hold=()):
    def body(offs_ref, *refs):
        place(refs[:4], offs_ref, which, cols, refs[4:5])

    return kernel_call(body, [offs, *pieces], [SM] + [VM] * 4, [sds(shape, BF)], cost=1, hold=hold)[0]


def out_rows(pieces, offs, lo):
    blk = pieces[0].shape[0] // 4
    return place_rows(pieces, offs, 1, [(lo, lo + DH, 0, blk, 0)], (16 * blk, DH))


def send_out(dw, offs_ref, outs):
    own, to_b, to_a = outs
    blk = dw.shape[0] // 16
    for q, (dst, base) in enumerate(((own, 0), (to_a, 0), (to_b, 0), (to_a, 4))):
        for r in range(4):
            row = pl.multiple_of(offs_ref[0, q * 4 + r] * blk, 16)
            dst[(base + r) * blk : (base + r + 1) * blk, :] = dw[pl.ds(row, blk), :]


def pack_kernel(core, qkv, out, cq, ckv, cout, win, gains, biases, keep, send, vecs):
    c = core[0]
    qkv, out, cq, ckv, cout, win, gains, biases = ready(qkv, out, cq, ckv, cout, win, gains, biases)
    vecs[...] = jnp.zeros_like(vecs)
    vecs[0:3, 0:24] = gains[...].astype(F32)
    vecs[3:6, 0:24] = biases[...].astype(F32)
    rows = keep.shape[0]
    wide = jnp.transpose(vecs[...])[:rows].astype(BF)
    for dst, which in ((keep, c), (send, 1 - c)):
        at = 0
        for w, groups in ((qkv, 3), (out, 1), (None, 0), (cout, 1), (cq, 1), (ckv, 2)):
            if w is None:
                dst[:, at : at + 128] = wide
                at += 128
            for k in range(groups):
                lanes = pl.ds(pl.multiple_of(k * D + which * DH, 128), DH)
                dst[:, at : at + DH] = w[:, lanes]
                at += DH
    hr = 96
    for k in range(win.shape[1] // (2 * hr)):
        first = win[:, 2 * k * hr : (2 * k + 1) * hr]
        second = win[:, (2 * k + 1) * hr : (2 * k + 2) * hr]
        keep[:, at + k * hr : at + (k + 1) * hr] = jnp.where(c == 0, first, second)
        send[:, at + k * hr : at + (k + 1) * hr] = jnp.where(c == 0, second, first)


def order_kernel(core, keep, got, wout, both, one, three, last):
    c = core[0]
    keep, got, wout = ready(keep, got, wout)
    rows = keep.shape[0]
    for b, (top, under) in enumerate(((keep, got), (got, keep))):
        for dst, at, width in ((both, 0, both.shape[1]), (one, 0, one.shape[1]), (three, both.shape[1], 4 * DH)):
            dst[b * rows : (b + 1) * rows, :width] = jnp.where(c == 0, top[:, at : at + width], under[:, at : at + width])
    three[:, 4 * DH :] = wout[0 : 2 * rows, :]
    last[...] = wout[2 * rows :, :]


def cats(jobs, after=()):
    arrays, places, outs = [], [], []
    for job in jobs:
        at, outs = 0, [*outs, sds((sum(x.shape[0] for x, _, _ in job), job[0][2]), BF)]
        for x, lo, width in job:
            arrays.append(x)
            places.append((len(outs) - 1, at, lo, width))
            at += x.shape[0]
    n = len(arrays)

    def body(*refs):
        for src, (o, at, lo, width) in zip(refs[:n], places):
            refs[n + o][at : at + src.shape[0], :] = src[:, lo : lo + width]

    return kernel_call(body, arrays, [VM] * n, outs, cost=1, after=after)


def whole(*arrays):
    return [(x, 0, x.shape[1]) for x in arrays]


def prepare_kernel(lens, tok_own, tok_other, cot_own, cot_other, mem_own, mem_other, tok, g, mem, xhat):
    tok_own, tok_other = ready(tok_own, tok_other)
    rows = tok.shape[0] // 2
    seqs, length = mem_own.shape[0], mem_own.shape[1]
    pad = mem.shape[0] // (2 * seqs)
    for b, src in ((0, tok_own), (1, tok_other)):
        tok[b * rows : (b + 1) * rows, :] = src[...]
    flush(tok)

    def norm(s):
        xhat[seq_rows(s), :] = normalise(tok[seq_rows(s), :].astype(F32))[0]

    loop(2 * seqs, norm)
    flush(xhat)
    mem_own, mem_other = ready(mem_own, mem_other)
    for b, src in ((0, mem_own), (1, mem_other)):
        for s in range(seqs):
            at = (b * seqs + s) * pad
            mem[at + length - length % 16 : at + pad, :] = jnp.zeros((pad - length + length % 16, D), BF)
            mem[at : at + length, :] = src[s]
    flush(mem)
    cot_own, cot_other = ready(cot_own, cot_other)
    place = lax.broadcasted_iota(jnp.int32, (LEN, D), 0)
    for b, src in ((0, cot_own), (1, cot_other)):
        for s in range(seqs):
            at = (b * seqs + s) * LEN
            live = (place < lens[b * seqs + s]).astype(F32)
            g[at : at + LEN, :] = (src[s * LEN : (s + 1) * LEN, :].astype(F32) * live).astype(BF)


def self_kernel(lens, core, offs, own, a, b, ab, xhat, keep, back, first, packed, probs, comb, vec, wqkv, gcol):
    c = core[0]
    blk = D // 16
    place((own, a, b, ab), offs, 0, [(4 * DH, 4 * DH + 128, 1, blk, 0), (0, 3 * DH, 0, blk, 0)], (wqkv, gcol))
    xhat = ready(xhat)
    vec[...] = jnp.transpose(gcol[...].astype(F32))[:8]
    gain, bias = vec[0:1], vec[3:4]

    def norm(s):
        first[seq_rows(s), :] = (xhat[seq_rows(s), :] * gain + bias).astype(BF)

    loop(8, norm)
    flush(first)

    def proj(b):
        rows = pl.ds(pl.multiple_of(b * 256, 256), 256)
        packed[rows, :] = nn(first[rows, :], wqkv[...]).astype(BF)

    loop(2, proj)
    flush(packed)
    key = lax.broadcasted_iota(jnp.int32, (LEN, DH), 0)
    query = lax.broadcasted_iota(jnp.int32, (LEN, DH), 1) & (LEN - 1)

    def att(s):
        allowed = (key <= query) & (key < lens[s])
        rows = seq_rows(s)
        p, m = attend(packed[rows, 0:DH], packed[rows, DH : 2 * DH], packed[rows, 2 * DH :], allowed)
        probs[s] = p
        comb[rows, D:] = m

    loop(8, att, 2)
    flush(probs)
    keep, back = ready(keep, back)
    comb[:, half_lanes(c)] = nn(comb[:, D:], keep[:DH, :]).astype(BF)
    comb[:, half_lanes(1 - c)] = nn(comb[:, D:], back[DH:, :]).astype(BF)


def kv_kernel(offs, own, a, b, ab, mem, kv, wckv, wcq):
    blk = D // 16
    place((own, a, b, ab), offs, 0, [(2 * DH, 4 * DH, 0, blk, 0), (DH, 2 * DH, 1, blk, 0)], (wckv, wcq))
    mem = ready(mem)

    def step(b):
        rows = pl.ds(pl.multiple_of(b * 480, 480), 480)
        kv[rows, :] = nn(mem[rows, :], wckv[...]).astype(BF)

    loop(mem.shape[0] // 480, step)


def swapped(s):
    return pl.ds(pl.multiple_of(((s + 4) & 7) * LEN, LEN), LEN)


def cross_kernel(mem_len, core, vec, tok, part, recv, wcq, kv, keep, back, resid, second, cq, probs, comb):
    c = core[0]
    vec, tok, part, recv = ready(vec, tok, part, recv)
    gain, bias = vec[1:2], vec[4:5]

    def norm(s):
        rows = seq_rows(s)
        both = part[rows, 0:D].astype(F32) + recv[swapped(s), 0:D].astype(F32)
        v = tok[rows, :].astype(F32) + both
        resid[rows, :] = v
        xhat, _ = normalise(v)
        second[rows, :] = (xhat * gain + bias).astype(BF)

    loop(8, norm)
    flush(resid, second)
    wcq = ready(wcq)
    cq[...] = nn(second[...], wcq[...]).astype(BF)
    flush(cq)
    kv = ready(kv)
    pad = probs.shape[1]
    allowed = lax.broadcasted_iota(jnp.int32, (pad, DH), 0) < mem_len

    def att(s):
        rows = seq_rows(s)
        keys = pl.ds(pl.multiple_of(s * pad, 16), pad)
        p, m = attend(cq[rows, :], kv[keys, 0:DH], kv[keys, DH:], allowed)
        probs[s] = p
        comb[rows, D:] = m

    loop(8, att, 2)
    flush(probs)
    keep, back = ready(keep, back)
    comb[:, half_lanes(c)] = nn(comb[:, D:], keep[:DH, :]).astype(BF)
    comb[:, half_lanes(1 - c)] = nn(comb[:, D:], back[DH:, :]).astype(BF)


def keys_and_cross_kernel(
    mem_len, offs, own, a, b, ab, mem, core, vec, tok, part, recv, keep, back, kv, wckv, wcq, resid, second, cq, probs, comb
):
    kv_kernel(offs, own, a, b, ab, mem, kv, wckv, wcq)
    cross_kernel(mem_len, core, vec, tok, part, recv, wcq, kv, keep, back, resid, second, cq, probs, comb)


def inner_kernel(resid, part, recv, vec, win, resid_two, third, hidden, slope):
    resid, part, recv, vec = ready(resid, part, recv, vec)
    gain, bias = vec[2:3], vec[5:6]

    def norm(s):
        rows = seq_rows(s)
        both = part[rows, 0:D].astype(F32) + recv[swapped(s), 0:D].astype(F32)
        v = resid[rows, :] + both
        resid_two[rows, :] = v
        xhat, _ = normalise(v)
        third[rows, :] = (xhat * gain + bias).astype(BF)

    loop(8, norm)
    flush(resid_two, third)
    win = ready(win)

    def step(b):
        rows = pl.ds(pl.multiple_of(b * 128, 128), 128)
        x = nn(third[rows, :], win[...])
        cdf = 0.5 + 0.5 * lax.erf(x * (0.5**0.5))
        hidden[rows, :] = (x * cdf).astype(BF)
        density = jnp.exp(x * x * -0.5) * ((2.0 * np.pi) ** -0.5)
        slope[rows, :] = (cdf + x * density).astype(BF)

    loop(4, step)


def mlp_kernel(offs, pieces, near, far, g, slope, win, hidden, own, comb, ginner, wout):
    half = own.shape[0]
    blk = D // 16
    place(pieces, offs, 0, [(0, D, 0, 2 * blk, 0)], (wout,))
    place_levels(near, far, offs, 2 * blk, blk, wout)
    g, slope, win = ready(g, slope, win)

    def back(b):
        rows = pl.ds(pl.multiple_of(b * 256, 256), 256)
        gh = nt(g[rows, :], wout[...])
        ginner[rows, :] = (gh * slope[rows, :].astype(F32)).astype(BF)
        comb[rows, :] = nt(ginner[rows, :], win[...]).astype(BF)

    loop(2, back)
    flush(ginner)
    hidden = ready(hidden)
    own[...] = nn(hidden[0:half, :], wout[...]).astype(BF)
    comb[2 * half :, :] = nn(hidden[half:, :], wout[...]).astype(BF)


def dmlpout_kernel(offs, hidden, g, to_own, to_b, to_a, dw):
    hidden, g = ready(hidden, g)
    blk = dw.shape[0] // 16
    for b in range(4):
        part = tn(hidden[:, b * 8 * blk : (b + 1) * 8 * blk], g[...]).astype(BF)
        for k in range(8):
            row = (4 * b + k // 2) * blk
            dw[row : row + blk, (k % 2) * D : (k % 2 + 1) * D] = part[k * blk : (k + 1) * blk]
    send_out(dw, offs, (to_own, to_b, to_a))


def mlp_and_grad_kernel(
    offs, pown, pa, pb, pab, near, far_a, far_b, g, slope, win, hidden, third, own, comb, to_own, to_b, to_a, ginner, wout, dw
):
    mlp_kernel(offs, (pown, pa, pb, pab), near, (far_a, far_b), g, slope, win, hidden, own, comb, ginner, wout)
    dmlpin_kernel(offs, third, ginner, to_own, to_b, to_a, dw)


def dmlpin_kernel(offs, third, ginner, *refs):
    third, ginner = ready(third, ginner)
    outs, dw = refs[:3], refs[3]
    for b in range(0, dw.shape[0], 256):
        dw[b : b + 256, :] = tn(third[:, b : b + 256], ginner[...]).astype(BF)
    send_out(dw, offs, outs)


def cross_back_kernel(
    core, vec, resid, part, recv, own, g, keep, back, kv, cq, probs, wcq, output, gresid, gtwo, dcq, dkv, gsecond, dvec, gm
):
    c = core[0]
    vec, resid, part, recv, own, g = ready(vec, resid, part, recv, own, g)
    gain = vec[2:3]
    dvec[...] = jnp.zeros_like(dvec)

    def norm(s):
        rows = seq_rows(s)
        dy = part[rows, :].astype(F32) + recv[swapped(s), :].astype(F32)
        dx, dg, db = norm_back(resid[rows, :], gain, dy)
        total = g[rows, :].astype(F32) + dx
        gresid[rows, :] = total
        gtwo[rows, :] = total.astype(BF)

        @pl.when(s < 4)
        def _():
            dvec[0:1, :] += dg
            dvec[1:2, :] += db
            extra = own[rows, :].astype(F32) + recv[pl.ds(pl.multiple_of(512 + s * LEN, LEN), LEN), :].astype(F32)
            output[rows, :] = (resid[rows, :] + extra).astype(BF)

    loop(8, norm)
    flush(output, gresid, gtwo, dvec)
    keep, back = ready(keep, back)
    gm[...] = (nt(gtwo[:, half_lanes(c)], keep[:DH, :]) + nt(gtwo[:, half_lanes(1 - c)], back[DH:, :])).astype(BF)
    pad = probs.shape[1]
    kv, cq, probs = ready(kv, cq, probs)

    def att(s):
        rows = seq_rows(s)
        keys = pl.ds(pl.multiple_of(s * pad, 16), pad)
        dq, dk, dv = attend_back(gm[rows, :], cq[rows, :], kv[keys, 0:DH], kv[keys, DH:], probs[s])
        dcq[rows, :] = dq
        dkv[keys, 0:DH] = dk
        dkv[keys, DH:] = dv

    loop(8, att, 2)
    flush(dcq, dkv)
    wcq = ready(wcq)
    gsecond[...] = nt(dcq[...], wcq[...]).astype(BF)


def out_grad(dw, lo, c, mine, other, g):
    cols = half_lanes(c)
    dw[half_lanes(c), lo : lo + DH] = tn(mine[:, D:], g[:, cols]).astype(BF)
    rest = tn(other[256:, D:], g[:256, cols]) + tn(other[:256, D:], g[256:, cols])
    dw[half_lanes(1 - c), lo : lo + DH] = rest.astype(BF)


def dcross_kernel(offs, core, mixed, mixed_other, gtwo, second, dcq, dkv, wckv, mem, *refs):
    outs, gmem, dw = refs[:3], refs[3:5], refs[5]
    mixed, mixed_other, gtwo = ready(mixed, mixed_other, gtwo)
    out_grad(dw, 0, core[0], mixed, mixed_other, gtwo)
    second, dcq = ready(second, dcq)
    dw[:, DH : 2 * DH] = tn(second[...], dcq[...]).astype(BF)
    dkv, wckv = ready(dkv, wckv)
    half = dkv.shape[0] // 2
    for i, dst in ((1, gmem[1]), (0, gmem[0])):
        for b in range(0, half, 480):
            dst[b : b + 480, :] = nt(dkv[i * half + b : i * half + b + 480, :], wckv[...]).astype(BF)
    flush(*gmem)
    mem = ready(mem)
    for b in range(0, D, 256):
        dw[b : b + 256, 2 * DH :] = tn(mem[:, b : b + 256], dkv[...]).astype(BF)
    send_out(dw, offs, outs)


def self_back_kernel(
    core, vec, resid, part, recv, gresid_two, keep, back, packed, probs, wqkv, xhat, gresid, gone, dpacked, gfirst_own, gfirst_other, dvec, gm
):
    c = core[0]
    vec, resid, part, recv, gresid_two = ready(vec, resid, part, recv, gresid_two)
    gain = vec[1:2]
    dvec[...] = jnp.zeros_like(dvec)

    def norm(s):
        rows = seq_rows(s)
        dy = part[rows, :].astype(F32) + recv[swapped(s), :].astype(F32)
        dx, dg, db = norm_back(resid[rows, :], gain, dy)
        total = gresid_two[rows, :] + dx
        gone[rows, :] = total.astype(BF)

        @pl.when(s < 4)
        def _():
            gresid[rows, :] = total
            dvec[0:1, :] += dg
            dvec[1:2, :] += db

    loop(8, norm)
    flush(gresid, gone)
    keep, back = ready(keep, back)
    gm[...] = (nt(gone[:, half_lanes(c)], keep[:DH, :]) + nt(gone[:, half_lanes(1 - c)], back[DH:, :])).astype(BF)
    packed, probs = ready(packed, probs)

    def att(s):
        rows = seq_rows(s)
        dq, dk, dv = attend_back(
            gm[rows, :], packed[rows, 0:DH], packed[rows, DH : 2 * DH], packed[rows, 2 * DH :], probs[s]
        )
        dpacked[rows, 0:DH] = dq
        dpacked[rows, DH : 2 * DH] = dk
        dpacked[rows, 2 * DH :] = dv

    loop(8, att, 2)
    flush(dpacked)
    wqkv, xhat = ready(wqkv, xhat)
    half = gfirst_own.shape[0]
    for b, dst in ((half, gfirst_other), (0, gfirst_own)):
        term = nt(dpacked[b : b + half, :], wqkv[...])
        dst[...] = term.astype(BF)
        flush(dst)
        dvec[2:3, :] += jnp.sum(term * xhat[b : b + half, :], 0, keepdims=True)
        dvec[3:4, :] += jnp.sum(term, 0, keepdims=True)


def dself_kernel(offs, core, mixed, mixed_other, gone, first, dpacked, dvec_two, dvec_one, *refs):
    outs, dw, vecs = refs[:3], refs[3], refs[4]
    mixed, mixed_other, gone = ready(mixed, mixed_other, gone)
    out_grad(dw, 0, core[0], mixed, mixed_other, gone)
    first, dpacked, dvec_two, dvec_one = ready(first, dpacked, dvec_two, dvec_one)
    for b in range(0, D, 256):
        dw[b : b + 256, DH : 4 * DH] = tn(first[:, b : b + 256], dpacked[...]).astype(BF)
    vecs[...] = jnp.zeros_like(vecs)
    for i, (v, row) in enumerate(((dvec_one, 2), (dvec_one, 0), (dvec_two, 0), (dvec_one, 3), (dvec_one, 1), (dvec_two, 1))):
        vecs[i : i + 1, :] = v[row : row + 1, :]
    dw[:, 4 * DH :] = jnp.transpose(vecs[...]).astype(BF)
    send_out(dw, offs, outs)


def tokens_back_kernel(vec, tok, part, recv, gresid, gmem, gmem_recv, gtok, gmemory):
    vec, tok, part, recv, gresid = ready(vec, tok, part, recv, gresid)
    gain = vec[0:1]

    def norm(s):
        rows = seq_rows(s)
        dy = part[rows, :].astype(F32) + recv[rows, :].astype(F32)
        dx, _, _ = norm_back(tok[rows, :].astype(F32), gain, dy)
        gtok[rows, :] = (gresid[rows, :] + dx).astype(BF)

    loop(4, norm)
    flush(gtok)
    gmem, gmem_recv = ready(gmem, gmem_recv)
    gmemory[...] = (gmem[...].astype(F32) + gmem_recv[...].astype(F32)).astype(BF)


def merge_kernel(kinds, *refs):
    counts = {"pass": (2, 1), "sum": (3, 4), "end": (4, 1)}
    at, out = 0, sum(counts[kind][0] for kind in kinds)
    refs = ready(*refs)
    for kind in kinds:
        ins, outs = refs[at : at + counts[kind][0]], refs[out : out + counts[kind][1]]
        at, out = at + len(ins), out + len(outs)
        if kind == "pass":
            half = ins[0].shape[0]
            outs[0][...] = (ins[0][...].astype(F32) + ins[1][half:, :].astype(F32)).astype(BF)
        elif kind == "end":
            outs[0][...] = ins[0][...] + ins[1][...].astype(F32) + ins[2][...].astype(F32) + ins[3][...].astype(F32)
        else:
            blk = ins[0].shape[0] // 4
            for i in range(4):
                rows = slice(i * blk, (i + 1) * blk)
                total = ins[0][rows, :].astype(F32) + ins[1][rows, :].astype(F32) + ins[2][rows, :].astype(F32)
                outs[i][...] = total.astype(outs[i].dtype)


def merge(jobs, after=()):
    ins, outs = [], []
    for kind, *arrays in jobs:
        ins += arrays
        rows, width = arrays[0].shape
        if kind == "sum":
            outs += [sds((rows // 4, width), F32)] + [sds((rows // 4, width), BF)] * 3
        else:
            outs.append(sds((rows, width), BF if kind == "pass" else F32))
    kinds = [job[0] for job in jobs]
    return kernel_call(
        lambda *refs: merge_kernel(kinds, *refs),
        ins,
        [STAGE] * len(ins),
        outs,
        [STAGE] * len(outs),
        cost=1,
        after=after,
    )


def join_kernel(core, mine, got, *outs):
    c = core[0]
    mine, got = ready(mine, got)
    at = 0
    for out in outs[: 2 if mine.shape[1] > 4 * DH else 3]:
        for k in range(out.shape[1] // D):
            out[:, pl.ds(pl.multiple_of(k * D + c * DH, 128), DH)] = mine[:, at : at + DH]
            out[:, pl.ds(pl.multiple_of(k * D + (1 - c) * DH, 128), DH)] = got[:, at : at + DH]
            at += DH
    if mine.shape[1] > at:
        gains, biases, wide = outs[2:]
        rows = mine.shape[0]
        wide[...] = jnp.zeros_like(wide)
        wide[0:rows, :] = mine[:, at:] + got[:, at:]
        turned = jnp.transpose(wide[...])
        gains[...] = turned[0:3, 0:rows]
        biases[...] = turned[3:6, 0:rows]


class Moves:
    def __init__(self, mesh):
        self.nz, self.nf = mesh.shape["dp"], mesh.shape["fsdp"]
        self.n = self.nz * self.nf
        self.doubling = self.nz == 4 and self.nf == 8

    def permute(self, x, target):
        pairs = [(d, target(d // self.nf, (d % self.nf) // 2, d % 2)) for d in range(self.n)]
        return lax.ppermute(x, AXES, [(a, (z * self.nf) + 2 * yx + c) for a, (z, yx, c) in pairs])

    def sibling(self, x):
        return self.permute(x, lambda z, yx, c: (z, yx, 1 - c))

    def near_z(self, x):
        return self.permute(x, lambda z, yx, c: (z ^ 1, yx, c))

    def far_z(self, x):
        return self.permute(x, lambda z, yx, c: (z ^ 2, yx, c))

    def side_a(self, x):
        return self.permute(x, lambda z, yx, c: (z, yx ^ (1 + c), c))

    def side_b(self, x):
        return self.permute(x, lambda z, yx, c: (z, yx ^ (2 - c), c))

    def opposite_z(self, x):
        return self.permute(x, lambda z, yx, c: (z ^ 3, yx, c))


def per_device(moves, tokens, memory, lengths, cotangent, self_qkv, self_out, cross_q, cross_kv, cross_out, mlp_in, mlp_out, norm_gains, norm_biases):
    seqs, mem_len = memory.shape[0], memory.shape[1]
    rows = seqs * LEN
    place = lax.axis_index(AXES)
    c = place % 2
    chip = place // 2
    core = jnp.reshape(c, (1,)).astype(jnp.int32)
    wr, hr = self_qkv.shape[0], mlp_out.shape[0]
    ff = mlp_in.shape[1]
    fh = ff // 2
    r2, s2 = 2 * rows, 2 * seqs
    wb = D // 16
    pad = -(-mem_len // 16) * 16
    fast = moves.doubling


    def prepare(lens, pairs, after=()):
        return kernel_call(
            prepare_kernel,
            [lens, *pairs],
            [SM] + [STAGE] * 6,
            [sds((r2, D), BF)] * 2 + [sds((s2 * pad, D), BF), sds((r2, D), F32)],
            [STAGE] * 4,
            after=after,
        )

    def self_attention(pieces, lens, xhat, keep, back, after=()):
        return kernel_call(
            self_kernel,
            [lens, core, offs, *pieces, xhat, keep, back],
            [SM] * 3 + [VM] * 4 + [STAGE] * 3,
            [
                sds((r2, D), BF),
                sds((r2, 3 * DH), BF),
                sds((s2, LEN, DH), BF),
                sds((r2, 3 * DH), BF),
                sds((8, D), F32),
                sds((D, 3 * DH), BF),
            ],
            [STAGE] * 6,
            [pltpu.VMEM((D, 128), BF)],
            cost=6,
            after=after,
        )

    def cross_attention(pieces, mem, vec, tok, comb, recv, keep, back, after=()):
        kv_rows = s2 * pad
        return kernel_call(
            lambda *refs: keys_and_cross_kernel(mem_len, *refs),
            [offs, *pieces, mem, core, vec, tok, comb, recv, keep, back],
            [SM] + [VM] * 4 + [STAGE, SM] + [STAGE] * 6,
            [
                sds((kv_rows, D), BF),
                sds((D, 2 * DH), BF),
                sds((D, DH), BF),
                sds((r2, D), F32),
                sds((r2, D), BF),
                sds((r2, DH), BF),
                sds((s2, pad, DH), BF),
                sds((r2, 3 * DH), BF),
            ],
            [STAGE] * 8,
            cost=12,
            after=after,
        )

    def inner_part(resid_one, comb, recv, vec, w_in, hold=()):
        return kernel_call(
            inner_kernel,
            [resid_one, comb, recv, vec, w_in],
            [STAGE] * 5,
            [sds((r2, D), F32), sds((r2, D), BF), sds((r2, fh), BF), sds((r2, fh), BF)],
            [STAGE] * 4,
            cost=5,
            hold=hold,
        )

    def inner_weight(pieces, hold=()):
        return place_rows(pieces, offs, 0, [(0, fh, 0, wb, 0)], (D, fh), hold)

    def grads(body, ins, specs, ncols, extra=(), scratch=(), cost=5, after=(), hold=()):
        return kernel_call(
            body,
            [offs, *ins],
            [SM, *specs],
            [sds((n * wb, ncols), BF) for n in (4, 4, 8)] + list(extra),
            scratch=[pltpu.VMEM((D, ncols), BF), *scratch],
            cost=cost,
            after=after,
            hold=hold,
        )

    def mlp_part(pieces, g, slope, w_in, hidden, third, after=(), hold=()):
        return kernel_call(
            mlp_and_grad_kernel,
            [offs, *pieces, g, slope, w_in, hidden, third],
            [SM] + [VM] * 12,
            [sds((rows, D), BF), sds((3 * rows, D), BF)] + [sds((n * wb, fh), BF) for n in (4, 4, 8)],
            scratch=[pltpu.VMEM((r2, fh), BF), pltpu.VMEM((fh, D), BF), pltpu.VMEM((D, fh), BF)],
            cost=11,
            after=after,
            hold=hold,
        )

    def cross_back(resid_two, comb, recv, part, after=()):
        return kernel_call(
            cross_back_kernel,
            [core, vec, resid_two, comb, recv, part, g, *cout, kv, cq, cprobs, w_cq],
            [SM] + [STAGE] * 12,
            [
                sds((rows, D), BF),
                sds((r2, D), F32),
                sds((r2, D), BF),
                sds((r2, DH), BF),
                sds(kv.shape, BF),
                sds((r2, D), BF),
                sds((8, D), F32),
            ],
            [STAGE] * 7,
            scratch=[pltpu.VMEM((r2, DH), BF)],
            cost=11,
            after=after,
        )

    def self_back(gsecond, recv, gresid_two, after=()):
        return kernel_call(
            self_back_kernel,
            [core, vec, resid_one, gsecond, recv, gresid_two, *out, packed, probs, w_qkv, xhat],
            [SM] + [STAGE] * 11,
            [
                sds((rows, D), F32),
                sds((r2, D), BF),
                sds((r2, 3 * DH), BF),
                sds((rows, D), BF),
                sds((rows, D), BF),
                sds((8, D), F32),
            ],
            [STAGE] * 6,
            scratch=[pltpu.VMEM((r2, DH), BF)],
            cost=9,
            after=after,
        )

    def cross_grads(after=()):
        return grads(
            dcross_kernel,
            [core, *cross_mixed, gtwo, second, dcq, dkv, w_ckv, mem],
            [SM] + [STAGE] * 8,
            4 * DH,
            [sds((seqs * pad, D), BF)] * 2,
            cost=10,
            after=after,
        )

    def self_grads(after=()):
        return grads(
            dself_kernel,
            [core, *self_mixed, gone, first, dpacked, dvec_two, dvec_one],
            [SM] + [STAGE] * 7,
            4 * DH + 128,
            scratch=[pltpu.VMEM((128, D), F32)],
            cost=6,
            after=after,
        )

    def tokens_back(recv, gmem_recv, after=()):
        return kernel_call(
            tokens_back_kernel,
            [vec, tokens.reshape(rows, D), gfirst, recv, gresid_one, gmem, gmem_recv],
            [STAGE] * 7,
            [sds((rows, D), BF), sds(gmem.shape, BF)],
            [STAGE] * 2,
            cost=4,
            after=after,
        )

    sib = moves.sibling
    pairs = []
    for x in (tokens.reshape(rows, D), cotangent.reshape(rows, D), memory):
        pairs += [x, sib(x)]
    lens = jnp.concatenate([lengths, sib(lengths)], 0)


    bits = jnp.arange(4, dtype=jnp.int32)
    if fast:
        plane = jnp.stack([jnp.int32(0), 1 + c, 2 - c, jnp.int32(3)]).astype(jnp.int32)
        z, yx = chip // 4, chip % 4
        chips = ((z ^ bits)[None, :] * 4 + (yx ^ plane)[:, None]).reshape(16).astype(jnp.int32)
    else:
        chips = jnp.arange(16, dtype=jnp.int32)
    turned = ((chips // 8) ^ c) * 8 + chips % 8
    offs = jnp.stack([chips, turned]).astype(jnp.int32)
    widths = (4 * DH + 128, 4 * DH, 4 * DH)

    if fast:
        keep, send = kernel_call(
            pack_kernel,
            [core, self_qkv, self_out, cross_q, cross_kv, cross_out, mlp_in, norm_gains, norm_biases],
            [SM] + ["stage"] * 8,
            [sds((wr, sum(widths)), BF)] * 2,
            [STAGE] * 2,
            scratch=[pltpu.VMEM((128, 128), F32)],
            cost=1,
            limit=60 << 20,
        )
        both, one, three, last = kernel_call(
            order_kernel,
            [core, keep, sib(send), mlp_out],
            [SM] + [STAGE] * 3,
            [sds((2 * wr, w), BF) for w in (widths[0] + widths[1], widths[0], 6 * DH, 2 * DH)],
            [STAGE] * 4,
            cost=1,
            after=[lens, pairs[1], pairs[3]],
        )
        near, far, side_a, side_b = moves.near_z, moves.far_z, moves.side_a, moves.side_b
        near_both, along, a_last, b_last = near(both), [far(one), moves.opposite_z(one)], side_a(last), side_b(last)
        tok, g, mem, xhat = prepare(lens, pairs, after=(one,))
        one, two = cats(
            [
                [(one, 0, widths[0]), (near_both, 0, widths[0]), *whole(*along)],
                [(both, widths[0], widths[1]), (near_both, widths[0], widths[1])],
            ],
            after=(tok, a_last, b_last),
        )
        three, ab_last = tie(three, one), tie(a_last, one)
        a1, b1, far_two, near_three, ab_last = side_a(one), side_b(one), far(two), near(three), side_b(ab_last)
        a1 = tie(a1, b1)
        two, last, four, three = cats(
            [
                whole(two, far_two),
                whole(last, a_last, b_last, ab_last),
                [(three, 4 * DH, D), (near_three, 4 * DH, D)],
                [(three, 0, 4 * DH), (near_three, 0, 4 * DH)],
            ],
            after=(a1,),
        )
        ab1, a2, b2, far_three, near_last = side_b(a1), side_a(two), side_b(two), far(three), near(last)
        a2 = tie(a2, b2, ab1)
        three, last, *parts = cats(
            [
                whole(three, far_three),
                whole(last, near_last),
                [(last, 0, DH), (near_last, 0, DH)],
                [(last, DH, DH), (near_last, DH, DH)],
            ],
            after=(a2,),
        )
        out = out_rows([one, a1, b1, ab1], offs, 3 * DH)
        out = (out, sib(out))
        three, a2, four = tie(three, out[1]), tie(a2, out[1]), tie(four, out[1])
        ab2, a3, b3, far_four, far_a = side_b(a2), side_a(three), side_b(three), far(four), far(tie(parts[0], out[1]))
        first, packed, probs, comb, vec, w_qkv = self_attention([one, a1, b1, ab1], lens, xhat, *out, after=(three,))
        a3 = tie(a3, b3, ab2, comb, far_a)
        (four,) = cats([whole(four, far_four)], after=(a3,))
        comb = tie(comb, four)
        cout = out_rows([two, a2, b2, ab2], offs, 0)
        cout = (cout, sib(cout))
        self_mixed = (comb, sib(comb))
        ab3, a4, b4, far_b = side_b(a3), side_a(four), side_b(four), far(tie(parts[1], four))
        kv, w_ckv, w_cq, resid_one, second, cq, cprobs, comb = cross_attention(
            [two, a2, b2, ab2], mem, vec, tok, *self_mixed, *cout
        )
        comb = tie(comb, ab3, a4, b4, far_b)
        cross_mixed, ab4 = (comb, sib(comb)), side_b(tie(a4, comb))
        hold = [kv, cprobs, cq, w_cq, *cout, w_ckv, second]
        w_in = inner_weight([three, a3, b3, ab3], hold)
        resid_two, third, hidden, slope = inner_part(resid_one, *cross_mixed, vec, w_in, hold)
        last = [four, a4, b4, ab4, last, far_a, far_b]
    else:
        tok, g, mem, xhat = prepare(lens, pairs)
        everywhere = lambda w: lax.all_gather(w, AXES, axis=0, tiled=True)
        split = lambda w: [w[i * w.shape[0] // 4 : (i + 1) * w.shape[0] // 4] for i in range(4)]

        def col_half(w, groups):
            w = w.reshape(w.shape[0], groups, 2, w.shape[1] // (2 * groups))
            return lax.dynamic_index_in_dim(w, c, 2, keepdims=False).reshape(w.shape[0], -1)

        vectors = jnp.pad(jnp.concatenate([norm_gains, norm_biases], 0).T, ((0, 0), (0, 122)))
        one = jnp.concatenate([col_half(self_qkv, 3), col_half(self_out, 1), vectors], 1)
        two = jnp.concatenate([col_half(w, w.shape[1] // D) for w in (cross_out, cross_q, cross_kv)], 1)
        one, two = split(everywhere(one)), split(everywhere(two))
        three = split(everywhere(col_half(mlp_in, ff // (2 * hr))))
        out, cout = out_rows(one, offs, 3 * DH), out_rows(two, offs, 0)
        out, cout = (out, sib(out)), (cout, sib(cout))
        rowed = everywhere(mlp_out).reshape(moves.n // 2, 2, hr, D)
        rowed = lax.dynamic_index_in_dim(rowed, c, 1, keepdims=False).reshape(16, 2, fh // 32, D)
        rowed = rowed.transpose(1, 0, 2, 3)
        levels = rowed[1].reshape(4, 4, wb, D).transpose(1, 0, 2, 3).reshape(D, D)
        last = split(rowed[0].reshape(D, D)) + [levels[: D // 2], levels[D // 2 :, :DH], levels[D // 2 :, DH:]]
        hold = ()
        first, packed, probs, comb, vec, w_qkv = self_attention(one, lens, xhat, *out)
        self_mixed = (comb, sib(comb))
        kv, w_ckv, w_cq, resid_one, second, cq, cprobs, comb = cross_attention(
            two, mem, vec, tok, *self_mixed, *cout
        )
        cross_mixed = (comb, sib(comb))
        w_in = inner_weight(three)
        resid_two, third, hidden, slope = inner_part(resid_one, *cross_mixed, vec, w_in)


    near, far, side_a, side_b = moves.near_z, moves.far_z, moves.side_a, moves.side_b
    after = ()

    def along_z(blocks):
        return [near(blocks[0]), far(blocks[1]), moves.opposite_z(blocks[2])]

    held = [resid_two, vec]
    d_mlpout = grads(dmlpout_kernel, [hidden, g], [STAGE] * 2, 2 * D, hold=[*hold, *held, third])
    if fast:
        got_a1 = side_a(d_mlpout[2])
    part, comb, *d_mlpin = mlp_part(last, g, slope, w_in, hidden, third, after=d_mlpout[:1], hold=[*hold, *held])
    if fast:
        (on,) = merge([("pass", d_mlpout[1], got_a1)], after=(part,))
        comb = tie(comb, on)
        got_b1, got_a2 = side_b(on), side_a(tie(d_mlpin[2], on))
        after = (on,)
    recv = sib(comb)
    output, gresid_two, gtwo, dcq, dkv, gsecond, dvec_two = cross_back(resid_two, comb, recv, part, after=after)
    if fast:
        on, kept1, *sums1 = merge([("pass", d_mlpin[1], got_a2), ("sum", d_mlpout[0], got_a1, got_b1)], after=(dcq,))
        got_b2, got_z1 = side_b(on), along_z(sums1)
        gsecond = tie(gsecond, on)
        after = (on,)
    recv = sib(gsecond)
    *d_cross, gmem, gmem_other = cross_grads(after=after)
    if fast:
        kept2, *sums2, total1 = merge([("sum", d_mlpin[0], got_a2, got_b2), ("end", kept1, *got_z1)], after=(gmem,))
        got_z2, got_a3 = along_z(sums2), side_a(tie(d_cross[2], kept2))
        after = (kept2,)
    gresid_one, gone, dpacked, gfirst, gfirst_other, dvec_one = self_back(gsecond, recv, gresid_two, after=after)
    if fast:
        on, total2 = merge([("pass", d_cross[1], got_a3), ("end", kept2, *got_z2)], after=(gone,))
        got_b3 = side_b(on)
        gfirst_other, gmem_other = tie(gfirst_other, on), tie(gmem_other, on)
        after = (on,)
    recv, gmem_recv = sib(gfirst_other), sib(gmem_other)
    d_self = self_grads(after=after)
    if fast:
        kept3, *sums3 = merge([("sum", d_cross[0], got_a3, got_b3)], after=[d_self[0], recv, gmem_recv])
        got_z3, got_a4 = along_z(sums3), side_a(tie(d_self[2], kept3))
        after = (kept3,)
    grad_tokens, grad_memory = tokens_back(recv, gmem_recv, after=after)
    grad_memory = grad_memory.reshape(seqs, pad, D)[:, :mem_len]

    if fast:
        on, total3 = merge([("pass", d_self[1], got_a4), ("end", kept3, *got_z3)], after=(grad_tokens,))
        got_b4 = side_b(on)
        kept4, *sums4 = merge([("sum", d_self[0], got_a4, got_b4)])
        got_z4 = along_z(sums4)
        (total4,) = merge([("end", kept4, *got_z4)])
        total = [total1, total2, total3, total4]

        def own_rows(total):
            mine = lax.dynamic_slice_in_dim(total, c * wr, wr, 0)
            return mine, sib(lax.dynamic_slice_in_dim(total, (1 - c) * wr, wr, 0))

        def join(pair, *shapes, scratch=()):
            return kernel_call(
                join_kernel,
                [core, *pair],
                [SM, STAGE, STAGE],
                [sds(shape, F32) for shape in shapes],
                [STAGE] * len(shapes),
                scratch=scratch,
                cost=1,
            )

        sum_mlpout = jnp.concatenate([total[0][:, :D], total[0][:, D:]], 0)
        mine, got = own_rows(total[1])
        pair = (jnp.where(c == 0, mine, got), jnp.where(c == 0, got, mine))
        parts = [p.reshape(wr, ff // (2 * hr), 1, hr) for p in pair]
        grad_in = jnp.concatenate(parts, 2).reshape(wr, ff)
        grad_cout, grad_cq, grad_ckv = join(own_rows(total[2]), (wr, D), (wr, D), (wr, 2 * D))
        grad_out, grad_qkv, own_gains, own_biases = join(
            own_rows(total[3]), (wr, D), (wr, 3 * D), (3, wr), (3, wr), scratch=[pltpu.VMEM((128, 128), F32)]
        )
    else:

        def placed(parts):
            own, to_b, to_a = parts
            term = jnp.concatenate([own, to_a[: 4 * wb], to_b, to_a[4 * wb :]], 0).astype(F32)
            both = jnp.stack([jnp.where(c == 0, term, 0.0), jnp.where(c == 1, term, 0.0)], 1)
            return lax.psum_scatter(both, AXES, scatter_dimension=0, tiled=True)

        def joined(total, lo, hi, groups):
            return total[:, :, lo:hi].reshape(wr, 2, groups, -1).transpose(0, 2, 1, 3).reshape(wr, -1)

        total = placed(d_cross)
        grad_cout, grad_cq, grad_ckv = (
            joined(total, 0, DH, 1),
            joined(total, DH, 2 * DH, 1),
            joined(total, 2 * DH, 4 * DH, 2),
        )
        total = placed(d_self)
        grad_out, grad_qkv = joined(total, 0, DH, 1), joined(total, DH, 4 * DH, 3)
        vectors = jnp.sum(total[:, :, 4 * DH : 4 * DH + 6], 1).T
        own_gains, own_biases = vectors[:3], vectors[3:]
        grad_in = joined(placed(d_mlpin), 0, fh, ff // (2 * hr))
        own, to_b, to_a = d_mlpout
        term = jnp.concatenate([own, to_a[: 4 * wb], to_b, to_a[4 * wb :]], 0).astype(F32)
        term = term.reshape(16, wb, 2, D).transpose(0, 2, 1, 3).reshape(moves.n // 2, 1, hr, D)
        both = jnp.concatenate([jnp.where(c == 0, term, 0.0), jnp.where(c == 1, term, 0.0)], 1)
        sum_mlpout = lax.psum_scatter(both.reshape(ff, D), AXES, scatter_dimension=0, tiled=True)

    return (
        output.reshape(tokens.shape),
        grad_tokens.reshape(tokens.shape),
        grad_memory,
        grad_qkv,
        grad_out,
        grad_cq,
        grad_ckv,
        grad_cout,
        grad_in,
        sum_mlpout,
        own_gains,
        own_biases,
    )


def solution(mesh):
    batch = P(AXES, None, None)
    rows = P(AXES, None)
    cols = P(None, AXES)
    moves = Moves(mesh)
    in_specs = (batch, batch, P(AXES), batch) + (rows,) * 7 + (cols,) * 2
    out_specs = (batch,) * 3 + (rows,) * 7 + (cols,) * 2
    return jax.shard_map(
        lambda *args: per_device(moves, *args),
        mesh=mesh,
        in_specs=in_specs,
        out_specs=out_specs,
        check_vma=False,
    )
```

```python
import jax
import jax.numpy as jnp
import numpy as np
from jax import lax
from jax.experimental import pallas as pl
from jax.experimental.pallas import tpu as pltpu
from jax.sharding import PartitionSpec as P

AXES = ("dp", "fsdp")
HEADS = 12
HALF = HEADS // 2
HEAD = 64
D = 768
DH = D // 2
LEN = 64
EPS = 1e-06
NEG = -1e30
SCALE = HEAD ** (-0.5)
F32 = jnp.float32
BF = jnp.bfloat16
VMEM_LIMIT = 14 << 20

VM = pl.BlockSpec(memory_space=pltpu.VMEM)
SM = pl.BlockSpec(memory_space=pltpu.SMEM)
ANY = pl.BlockSpec(memory_space=pl.ANY)


def sds(shape, dtype):
    return jax.ShapeDtypeStruct(shape, dtype)


STAGE = VM


class Staged:
    def __init__(self, ref, copy):
        self.ref, self.copy, self.waited = ref, copy, False
        self.shape = ref.shape

    def ready(self):
        if not self.waited:
            self.copy.wait()
            self.waited = True
        return self.ref


PENDING = {}


def flush(*refs):
    for r in refs:
        if id(r) in PENDING:
            PENDING[id(r)].start()
            PENDING[id(r)] = None


def ready(*refs):
    out = [r.ready() if isinstance(r, Staged) else r for r in refs]
    return out[0] if len(out) == 1 else out


def kernel_call(body, ins, in_specs, outs, out_specs=None, scratch=(), cost=5, after=(), limit=None, hold=()):
    n, skip, m, k = len(ins), len(after) + len(hold), len(outs), len(scratch)
    out_specs = [VM] * m if out_specs is None else list(out_specs)
    staged_in = [i for i, spec in enumerate(in_specs) if spec == 'stage']
    staged_out = [i for i, spec in enumerate(out_specs) if spec == 'stage']
    buffers = [pltpu.VMEM(ins[i].shape, ins[i].dtype) for i in staged_in]
    buffers += [pltpu.VMEM(outs[i].shape, outs[i].dtype) for i in staged_out]
    extra = [*buffers, pltpu.SemaphoreType.DMA((len(buffers),))] if buffers else []

    def run(*refs):
        ins, outs = list(refs[:n]), list(refs[n + skip : n + skip + m])
        own = refs[n + skip + m : n + skip + m + k]
        PENDING.clear()
        if not buffers:
            body(*ins, *outs, *own)
            return
        held, sems = refs[n + skip + m + k : -1], refs[-1]
        for j, i in enumerate(staged_in):
            copy = pltpu.make_async_copy(ins[i], held[j], sems.at[j])
            copy.start()
            ins[i] = Staged(held[j], copy)
        copies = []
        for j, i in enumerate(staged_out, len(staged_in)):
            copies.append(pltpu.make_async_copy(held[j], outs[i], sems.at[j]))
            outs[i] = held[j]
            PENDING[id(held[j])] = copies[-1]
        body(*ins, *outs, *own)
        ready(*ins)
        for cp in PENDING.values():
            if cp is not None:
                cp.start()
        for cp in copies:
            cp.wait()

    space = lambda spec: ANY if spec == 'stage' else spec
    return pl.pallas_call(
        run,
        out_shape=list(outs),
        in_specs=[space(spec) for spec in in_specs] + [ANY] * len(after) + [VM] * len(hold),
        out_specs=[space(spec) for spec in out_specs],
        scratch_shapes=[*scratch, *extra],
        compiler_params=pltpu.CompilerParams(vmem_limit_bytes=limit or VMEM_LIMIT),
        cost_estimate=pl.CostEstimate(flops=cost * 7 * 10**9, bytes_accessed=0, transcendentals=0),
    )(*ins, *after, *hold)


def tie(x, *earlier):
    return pl.pallas_call(
        lambda *refs: None,
        out_shape=sds(x.shape, x.dtype),
        in_specs=[ANY] * (1 + len(earlier)),
        out_specs=ANY,
        input_output_aliases={0: 0},
        compiler_params=pltpu.CompilerParams(vmem_limit_bytes=1 << 20),
        cost_estimate=pl.CostEstimate(flops=0, bytes_accessed=0, transcendentals=0),
    )(x, *earlier)


def nn(a, b):
    return lax.dot_general(a, b, (((1,), (0,)), ((), ())), preferred_element_type=F32)


def nt(a, b):
    return lax.dot_general(a, b, (((1,), (1,)), ((), ())), preferred_element_type=F32)


def tn(a, b):
    return lax.dot_general(a, b, (((0,), (0,)), ((), ())), preferred_element_type=F32)


def normalise(v):
    mean = jnp.mean(v, -1, keepdims=True)
    cen = v - mean
    inv = lax.rsqrt(jnp.mean(cen * cen, -1, keepdims=True) + EPS)
    return cen * inv, inv


def norm_back(v, gain, dy):
    xhat, inv = normalise(v)
    dxh = dy * gain
    m1 = jnp.mean(dxh, -1, keepdims=True)
    m2 = jnp.mean(dxh * xhat, -1, keepdims=True)
    dx = inv * (dxh - m1 - xhat * m2)
    return dx, jnp.sum(dy * xhat, 0, keepdims=True), jnp.sum(dy, 0, keepdims=True)


GROUPS = ((0, 256), (256, DH))


def head_of_lane(rows, width):
    return lax.shift_right_logical(lax.broadcasted_iota(jnp.int32, (rows, width), 1), 6)


def spread(q):
    head = head_of_lane(1, q.shape[1])
    parts = [q * (head == h).astype(F32).astype(q.dtype) for h in range(q.shape[1] // HEAD)]
    return jnp.concatenate(parts, 0)


def fold(o):
    head = head_of_lane(LEN, o.shape[1])
    total = jnp.where(head == 0, o[:LEN], 0.0)
    for h in range(1, o.shape[1] // HEAD):
        total = jnp.where(head == h, o[h * LEN : (h + 1) * LEN], total)
    return total


def attend(q, k, v, allowed):
    probs, mixed = [], []
    for lo, hi in GROUPS:
        st = nt(k[:, lo:hi], spread(q[:, lo:hi])) * SCALE
        st = jnp.where(allowed[:, lo:hi], st, NEG)
        e = jnp.exp(st - jnp.max(st, 0, keepdims=True))
        p = (e * (1.0 / jnp.sum(e, 0, keepdims=True))).astype(BF)
        probs.append(p)
        mixed.append(fold(tn(p, v[:, lo:hi])).astype(BF))
    return jnp.concatenate(probs, 1), jnp.concatenate(mixed, 1)


def attend_back(g, q, k, v, p):
    dq, dk, dv = [], [], []
    for lo, hi in GROUPS:
        gs, qs, low = spread(g[:, lo:hi]), spread(q[:, lo:hi]), p[:, lo:hi]
        dp = nt(v[:, lo:hi], gs)
        pf = low.astype(F32)
        t = pf * dp
        ds = (t - pf * jnp.sum(t, 0, keepdims=True)).astype(BF)
        dq.append((fold(tn(ds, k[:, lo:hi])) * SCALE).astype(BF))
        dk.append((nn(ds, qs) * SCALE).astype(BF))
        dv.append(nn(low, gs).astype(BF))
    return [jnp.concatenate(x, 1) for x in (dq, dk, dv)]


def seq_rows(s):
    return pl.ds(pl.multiple_of(s * LEN, LEN), LEN)


def half_lanes(c):
    return pl.ds(pl.multiple_of(c * DH, DH), DH)


def loop(n, body, unroll=1):
    def step(i, carry):
        body(i)
        return carry

    lax.fori_loop(0, n, step, 0, unroll=unroll)


def columns_first(pieces, q, r):
    blk = pieces[0].shape[0] // 4
    return pieces[q], r * blk


def place(pieces, offs_ref, which, cols, targets):
    blk = pieces[0].shape[0] // 4
    for lo, hi, o, step, shift in cols:
        for q in range(4):
            for r in range(4):
                row = pl.multiple_of(offs_ref[which, q * 4 + r] * step + shift, 16)
                targets[o][pl.ds(row, blk), :] = pieces[q][r * blk : (r + 1) * blk, lo:hi]


def place_levels(near, far, offs_ref, step, shift, target):
    blk = near.shape[0] // 8
    lo = 0
    for level, src in ((0, near), *((2, part) for part in far)):
        at = 0 if level == 0 else lo
        for q in range(4):
            for r in range(2):
                row = pl.multiple_of(offs_ref[0, q * 4 + level + r] * step + shift, 16)
                rows = slice((r * 4 + q) * blk, (r * 4 + q + 1) * blk)
                target[pl.ds(row, blk), at : at + src.shape[1]] = src[rows, :]
        lo += src.shape[1] if level else 0


def place_rows(pieces, offs, which, cols, shape, hold=()):
    def body(offs_ref, *refs):
        place(refs[:4], offs_ref, which, cols, refs[4:5])

    return kernel_call(body, [offs, *pieces], [SM] + [VM] * 4, [sds(shape, BF)], cost=1, hold=hold)[0]


def out_rows(pieces, offs, lo):
    blk = pieces[0].shape[0] // 4
    return place_rows(pieces, offs, 1, [(lo, lo + DH, 0, blk, 0)], (16 * blk, DH))


def send_out(dw, offs_ref, outs):
    blk = dw.shape[0] // 16
    for q in range(4):
        for r in range(4):
            row = pl.multiple_of(offs_ref[0, q * 4 + r] * blk, 16)
            outs[q][r * blk : (r + 1) * blk, :] = dw[pl.ds(row, blk), :]


def pack_kernel(core, qkv, out, cq, ckv, cout, win, gains, biases, keep, send, vecs):
    c = core[0]
    qkv, out, cq, ckv, cout, win, gains, biases = ready(qkv, out, cq, ckv, cout, win, gains, biases)
    vecs[...] = jnp.zeros_like(vecs)
    vecs[0:3, 0:24] = gains[...].astype(F32)
    vecs[3:6, 0:24] = biases[...].astype(F32)
    rows = keep.shape[0]
    wide = jnp.transpose(vecs[...])[:rows].astype(BF)
    for dst, which in ((keep, c), (send, 1 - c)):
        at = 0
        for w, groups in ((qkv, 3), (out, 1), (None, 0), (cout, 1), (cq, 1), (ckv, 2)):
            if w is None:
                dst[:, at : at + 128] = wide
                at += 128
            for k in range(groups):
                lanes = pl.ds(pl.multiple_of(k * D + which * DH, 128), DH)
                dst[:, at : at + DH] = w[:, lanes]
                at += DH
    hr = 96
    for k in range(win.shape[1] // (2 * hr)):
        first = win[:, 2 * k * hr : (2 * k + 1) * hr]
        second = win[:, (2 * k + 1) * hr : (2 * k + 2) * hr]
        keep[:, at + k * hr : at + (k + 1) * hr] = jnp.where(c == 0, first, second)
        send[:, at + k * hr : at + (k + 1) * hr] = jnp.where(c == 0, second, first)


def order_kernel(core, keep, got, wout, both, one, three, last):
    c = core[0]
    keep, got, wout = ready(keep, got, wout)
    rows = keep.shape[0]
    for b, (top, under) in enumerate(((keep, got), (got, keep))):
        for dst, at, width in ((both, 0, both.shape[1]), (one, 0, one.shape[1]), (three, both.shape[1], 4 * DH)):
            dst[b * rows : (b + 1) * rows, :width] = jnp.where(c == 0, top[:, at : at + width], under[:, at : at + width])
    three[:, 4 * DH :] = wout[0 : 2 * rows, :]
    last[...] = wout[2 * rows :, :]


def cats(jobs, after=()):
    arrays, places, outs = [], [], []
    for job in jobs:
        at, outs = 0, [*outs, sds((sum(x.shape[0] for x, _, _ in job), job[0][2]), BF)]
        for x, lo, width in job:
            arrays.append(x)
            places.append((len(outs) - 1, at, lo, width))
            at += x.shape[0]
    n = len(arrays)

    def body(*refs):
        for src, (o, at, lo, width) in zip(refs[:n], places):
            refs[n + o][at : at + src.shape[0], :] = src[:, lo : lo + width]

    return kernel_call(body, arrays, [VM] * n, outs, cost=1, after=after)


def whole(*arrays):
    return [(x, 0, x.shape[1]) for x in arrays]


def prepare_kernel(lens, tok_own, tok_other, cot_own, cot_other, mem_own, mem_other, tok, g, mem, xhat):
    tok_own, tok_other = ready(tok_own, tok_other)
    rows = tok.shape[0] // 2
    seqs, length = mem_own.shape[0], mem_own.shape[1]
    pad = mem.shape[0] // (2 * seqs)
    for b, src in ((0, tok_own), (1, tok_other)):
        tok[b * rows : (b + 1) * rows, :] = src[...]
    flush(tok)

    def norm(s):
        xhat[seq_rows(s), :] = normalise(tok[seq_rows(s), :].astype(F32))[0]

    loop(2 * seqs, norm, 2)
    flush(xhat)
    mem_own, mem_other = ready(mem_own, mem_other)
    for b, src in ((0, mem_own), (1, mem_other)):
        for s in range(seqs):
            at = (b * seqs + s) * pad
            mem[at + length - length % 16 : at + pad, :] = jnp.zeros((pad - length + length % 16, D), BF)
            mem[at : at + length, :] = src[s]
    flush(mem)
    cot_own, cot_other = ready(cot_own, cot_other)
    place = lax.broadcasted_iota(jnp.int32, (LEN, D), 0)
    for b, src in ((0, cot_own), (1, cot_other)):
        for s in range(seqs):
            at = (b * seqs + s) * LEN
            live = (place < lens[b * seqs + s]).astype(F32)
            g[at : at + LEN, :] = (src[s * LEN : (s + 1) * LEN, :].astype(F32) * live).astype(BF)


def self_kernel(lens, core, offs, own, a, b, ab, xhat, keep, back, first, packed, probs, comb, vec, wqkv, gcol):
    c = core[0]
    blk = D // 16
    place((own, a, b, ab), offs, 0, [(4 * DH, 4 * DH + 128, 1, blk, 0), (0, 3 * DH, 0, blk, 0)], (wqkv, gcol))
    xhat = ready(xhat)
    vec[...] = jnp.transpose(gcol[...].astype(F32))[:8]
    gain, bias = vec[0:1], vec[3:4]

    def norm(s):
        first[seq_rows(s), :] = (xhat[seq_rows(s), :] * gain + bias).astype(BF)

    loop(8, norm, 2)
    flush(first)

    def proj(b):
        rows = pl.ds(pl.multiple_of(b * 256, 256), 256)
        packed[rows, :] = nn(first[rows, :], wqkv[...]).astype(BF)

    loop(2, proj)
    flush(packed)
    key = lax.broadcasted_iota(jnp.int32, (LEN, DH), 0)
    query = lax.broadcasted_iota(jnp.int32, (LEN, DH), 1) & (LEN - 1)

    def att(s):
        allowed = (key <= query) & (key < lens[s])
        rows = seq_rows(s)
        p, m = attend(packed[rows, 0:DH], packed[rows, DH : 2 * DH], packed[rows, 2 * DH :], allowed)
        probs[s] = p
        comb[rows, D:] = m

    loop(8, att, 2)
    flush(probs)
    keep, back = ready(keep, back)
    comb[:, half_lanes(c)] = nn(comb[:, D:], keep[:DH, :]).astype(BF)
    comb[:, half_lanes(1 - c)] = nn(comb[:, D:], back[DH:, :]).astype(BF)


def kv_kernel(offs, own, a, b, ab, mem, kv, wckv, wcq):
    blk = D // 16
    place((own, a, b, ab), offs, 0, [(2 * DH, 4 * DH, 0, blk, 0), (DH, 2 * DH, 1, blk, 0)], (wckv, wcq))
    mem = ready(mem)

    def step(b):
        rows = pl.ds(pl.multiple_of(b * 480, 480), 480)
        kv[rows, :] = nn(mem[rows, :], wckv[...]).astype(BF)

    loop(mem.shape[0] // 480, step)


def swapped(s):
    return pl.ds(pl.multiple_of(((s + 4) & 7) * LEN, LEN), LEN)


def cross_kernel(mem_len, core, vec, tok, part, recv, wcq, kv, keep, back, resid, second, cq, probs, comb):
    c = core[0]
    vec, tok, part, recv = ready(vec, tok, part, recv)
    gain, bias = vec[1:2], vec[4:5]

    def norm(s):
        rows = seq_rows(s)
        both = part[rows, 0:D].astype(F32) + recv[swapped(s), 0:D].astype(F32)
        v = tok[rows, :].astype(F32) + both
        resid[rows, :] = v
        xhat, _ = normalise(v)
        second[rows, :] = (xhat * gain + bias).astype(BF)

    loop(8, norm, 2)
    flush(resid, second)
    wcq = ready(wcq)
    cq[...] = nn(second[...], wcq[...]).astype(BF)
    flush(cq)
    kv = ready(kv)
    pad = probs.shape[1]
    allowed = lax.broadcasted_iota(jnp.int32, (pad, DH), 0) < mem_len

    def att(s):
        rows = seq_rows(s)
        keys = pl.ds(pl.multiple_of(s * pad, 16), pad)
        p, m = attend(cq[rows, :], kv[keys, 0:DH], kv[keys, DH:], allowed)
        probs[s] = p
        comb[rows, D:] = m

    loop(8, att, 2)
    flush(probs)
    keep, back = ready(keep, back)
    comb[:, half_lanes(c)] = nn(comb[:, D:], keep[:DH, :]).astype(BF)
    comb[:, half_lanes(1 - c)] = nn(comb[:, D:], back[DH:, :]).astype(BF)


def keys_and_cross_kernel(
    mem_len, offs, own, a, b, ab, mem, core, vec, tok, part, recv, keep, back, kv, wckv, wcq, resid, second, cq, probs, comb
):
    kv_kernel(offs, own, a, b, ab, mem, kv, wckv, wcq)
    cross_kernel(mem_len, core, vec, tok, part, recv, wcq, kv, keep, back, resid, second, cq, probs, comb)


def inner_kernel(resid, part, recv, vec, win, resid_two, third, hidden, slope):
    resid, part, recv, vec = ready(resid, part, recv, vec)
    gain, bias = vec[2:3], vec[5:6]

    def norm(s):
        rows = seq_rows(s)
        both = part[rows, 0:D].astype(F32) + recv[swapped(s), 0:D].astype(F32)
        v = resid[rows, :] + both
        resid_two[rows, :] = v
        xhat, _ = normalise(v)
        third[rows, :] = (xhat * gain + bias).astype(BF)

    loop(8, norm, 2)
    flush(resid_two, third)
    win = ready(win)

    def step(b):
        rows = pl.ds(pl.multiple_of(b * 128, 128), 128)
        x = nn(third[rows, :], win[...])
        cdf = 0.5 + 0.5 * lax.erf(x * (0.5**0.5))
        hidden[rows, :] = (x * cdf).astype(BF)
        density = jnp.exp(x * x * -0.5) * ((2.0 * np.pi) ** -0.5)
        slope[rows, :] = (cdf + x * density).astype(BF)

    loop(4, step)


def mlp_kernel(offs, pieces, near, far, g, slope, win, hidden, own, comb, ginner, wout):
    half = own.shape[0]
    blk = D // 16
    place(pieces, offs, 0, [(0, D, 0, 2 * blk, 0)], (wout,))
    place_levels(near, far, offs, 2 * blk, blk, wout)
    g, slope, win = ready(g, slope, win)

    def back(b):
        rows = pl.ds(pl.multiple_of(b * 256, 256), 256)
        gh = nt(g[rows, :], wout[...])
        ginner[rows, :] = (gh * slope[rows, :].astype(F32)).astype(BF)
        comb[rows, :] = nt(ginner[rows, :], win[...]).astype(BF)

    loop(2, back)
    flush(ginner)
    hidden = ready(hidden)
    own[...] = nn(hidden[0:half, :], wout[...]).astype(BF)
    comb[2 * half :, :] = nn(hidden[half:, :], wout[...]).astype(BF)


def dmlpout_kernel(offs, hidden, g, *refs):
    outs, dw = refs[:4], refs[4]
    hidden, g = ready(hidden, g)
    blk = dw.shape[0] // 16
    for b in range(4):
        part = tn(hidden[:, b * 8 * blk : (b + 1) * 8 * blk], g[...]).astype(BF)
        for k in range(8):
            row = (4 * b + k // 2) * blk
            dw[row : row + blk, (k % 2) * D : (k % 2 + 1) * D] = part[k * blk : (k + 1) * blk]
    send_out(dw, offs, outs)


def mlp_and_grad_kernel(
    offs, pown, pa, pb, pab, near, far_a, far_b, g, slope, win, hidden, third, own, comb, d_own, d_a, d_b, d_ab, ginner, wout, dw
):
    mlp_kernel(offs, (pown, pa, pb, pab), near, (far_a, far_b), g, slope, win, hidden, own, comb, ginner, wout)
    dmlpin_kernel(offs, third, ginner, d_own, d_a, d_b, d_ab, dw)


def dmlpin_kernel(offs, third, ginner, *refs):
    third, ginner = ready(third, ginner)
    outs, dw = refs[:4], refs[4]
    for b in range(0, dw.shape[0], 256):
        dw[b : b + 256, :] = tn(third[:, b : b + 256], ginner[...]).astype(BF)
    send_out(dw, offs, outs)


def cross_back_kernel(
    core, vec, resid, part, recv, own, g, keep, back, kv, cq, probs, wcq, output, gresid, gtwo, dcq, dkv, gsecond, dvec, gm
):
    c = core[0]
    vec, resid, part, recv, own, g = ready(vec, resid, part, recv, own, g)
    gain = vec[2:3]
    dvec[...] = jnp.zeros_like(dvec)

    def norm(s):
        rows = seq_rows(s)
        dy = part[rows, :].astype(F32) + recv[swapped(s), :].astype(F32)
        dx, dg, db = norm_back(resid[rows, :], gain, dy)
        total = g[rows, :].astype(F32) + dx
        gresid[rows, :] = total
        gtwo[rows, :] = total.astype(BF)

        @pl.when(s < 4)
        def _():
            dvec[0:1, :] += dg
            dvec[1:2, :] += db
            extra = own[rows, :].astype(F32) + recv[pl.ds(pl.multiple_of(512 + s * LEN, LEN), LEN), :].astype(F32)
            output[rows, :] = (resid[rows, :] + extra).astype(BF)

    loop(8, norm, 2)
    flush(output, gresid, gtwo, dvec)
    keep, back = ready(keep, back)
    gm[...] = (nt(gtwo[:, half_lanes(c)], keep[:DH, :]) + nt(gtwo[:, half_lanes(1 - c)], back[DH:, :])).astype(BF)
    pad = probs.shape[1]
    kv, cq, probs = ready(kv, cq, probs)

    def att(s):
        rows = seq_rows(s)
        keys = pl.ds(pl.multiple_of(s * pad, 16), pad)
        dq, dk, dv = attend_back(gm[rows, :], cq[rows, :], kv[keys, 0:DH], kv[keys, DH:], probs[s])
        dcq[rows, :] = dq
        dkv[keys, 0:DH] = dk
        dkv[keys, DH:] = dv

    loop(8, att, 2)
    flush(dcq, dkv)
    wcq = ready(wcq)
    gsecond[...] = nt(dcq[...], wcq[...]).astype(BF)


def out_grad(dw, lo, c, mine, other, g):
    cols = half_lanes(c)
    dw[half_lanes(c), lo : lo + DH] = tn(mine[:, D:], g[:, cols]).astype(BF)
    rest = tn(other[256:, D:], g[:256, cols]) + tn(other[:256, D:], g[256:, cols])
    dw[half_lanes(1 - c), lo : lo + DH] = rest.astype(BF)


def dcross_kernel(offs, core, mixed, mixed_other, gtwo, second, dcq, dkv, wckv, mem, *refs):
    outs, gmem, dw = refs[:4], refs[4:6], refs[6]
    mixed, mixed_other, gtwo = ready(mixed, mixed_other, gtwo)
    out_grad(dw, 0, core[0], mixed, mixed_other, gtwo)
    second, dcq = ready(second, dcq)
    dw[:, DH : 2 * DH] = tn(second[...], dcq[...]).astype(BF)
    dkv, wckv = ready(dkv, wckv)
    half = dkv.shape[0] // 2
    for i, dst in ((1, gmem[1]), (0, gmem[0])):
        for b in range(0, half, 480):
            dst[b : b + 480, :] = nt(dkv[i * half + b : i * half + b + 480, :], wckv[...]).astype(BF)
    flush(*gmem)
    mem = ready(mem)
    for b in range(0, D, 256):
        dw[b : b + 256, 2 * DH :] = tn(mem[:, b : b + 256], dkv[...]).astype(BF)
    send_out(dw, offs, outs)


def cross_back_and_grads_kernel(
    offs, core, vec, resid, part, recv, own, g, keep, back, kv, cq, probs, wcq, mixed, mixed_other, second, wckv, mem,
    output, gresid, gsecond, dvec, gmem_own, gmem_other, d_own, d_a, d_b, d_ab, gtwo, dcq, dkv, gm, dw
):
    cross_back_kernel(
        core, vec, resid, part, recv, own, g, keep, back, kv, cq, probs, wcq, output, gresid, gtwo, dcq, dkv, gsecond, dvec, gm
    )
    dcross_kernel(
        offs, core, mixed, mixed_other, gtwo, second, dcq, dkv, wckv, mem, d_own, d_a, d_b, d_ab, gmem_own, gmem_other, dw
    )


def self_back_kernel(
    core, vec, resid, part, recv, gresid_two, keep, back, packed, probs, wqkv, xhat, gresid, gone, dpacked, gfirst_own, gfirst_other, dvec, gm
):
    c = core[0]
    vec, resid, part, recv, gresid_two = ready(vec, resid, part, recv, gresid_two)
    gain = vec[1:2]
    dvec[...] = jnp.zeros_like(dvec)

    def norm(s):
        rows = seq_rows(s)
        dy = part[rows, :].astype(F32) + recv[swapped(s), :].astype(F32)
        dx, dg, db = norm_back(resid[rows, :], gain, dy)
        total = gresid_two[rows, :] + dx
        gone[rows, :] = total.astype(BF)

        @pl.when(s < 4)
        def _():
            gresid[rows, :] = total
            dvec[0:1, :] += dg
            dvec[1:2, :] += db

    loop(8, norm, 2)
    flush(gresid, gone)
    keep, back = ready(keep, back)
    gm[...] = (nt(gone[:, half_lanes(c)], keep[:DH, :]) + nt(gone[:, half_lanes(1 - c)], back[DH:, :])).astype(BF)
    packed, probs = ready(packed, probs)

    def att(s):
        rows = seq_rows(s)
        dq, dk, dv = attend_back(
            gm[rows, :], packed[rows, 0:DH], packed[rows, DH : 2 * DH], packed[rows, 2 * DH :], probs[s]
        )
        dpacked[rows, 0:DH] = dq
        dpacked[rows, DH : 2 * DH] = dk
        dpacked[rows, 2 * DH :] = dv

    loop(8, att, 2)
    flush(dpacked)
    wqkv, xhat = ready(wqkv, xhat)
    half = gfirst_own.shape[0]
    for b, dst in ((half, gfirst_other), (0, gfirst_own)):
        term = nt(dpacked[b : b + half, :], wqkv[...])
        dst[...] = term.astype(BF)
        flush(dst)
        dvec[2:3, :] += jnp.sum(term * xhat[b : b + half, :], 0, keepdims=True)
        dvec[3:4, :] += jnp.sum(term, 0, keepdims=True)


def dself_kernel(offs, core, mixed, mixed_other, gone, first, dpacked, dvec_two, dvec_one, *refs):
    outs, dw, vecs = refs[:4], refs[4], refs[5]
    mixed, mixed_other, gone = ready(mixed, mixed_other, gone)
    out_grad(dw, 0, core[0], mixed, mixed_other, gone)
    first, dpacked, dvec_two, dvec_one = ready(first, dpacked, dvec_two, dvec_one)
    for b in range(0, D, 256):
        dw[b : b + 256, DH : 4 * DH] = tn(first[:, b : b + 256], dpacked[...]).astype(BF)
    vecs[...] = jnp.zeros_like(vecs)
    for i, (v, row) in enumerate(((dvec_one, 2), (dvec_one, 0), (dvec_two, 0), (dvec_one, 3), (dvec_one, 1), (dvec_two, 1))):
        vecs[i : i + 1, :] = v[row : row + 1, :]
    dw[:, 4 * DH :] = jnp.transpose(vecs[...]).astype(BF)
    send_out(dw, offs, outs)


def self_back_and_grads_kernel(
    offs, core, vec, resid, part, recv, gresid_two, keep, back, packed, probs, wqkv, xhat, mixed, mixed_other, first, dvec_two,
    gresid, gfirst_own, gfirst_other, d_own, d_a, d_b, d_ab, gone, dpacked, dvec, gm, dw, vecs
):
    self_back_kernel(
        core, vec, resid, part, recv, gresid_two, keep, back, packed, probs, wqkv, xhat,
        gresid, gone, dpacked, gfirst_own, gfirst_other, dvec, gm
    )
    dself_kernel(offs, core, mixed, mixed_other, gone, first, dpacked, dvec_two, dvec, d_own, d_a, d_b, d_ab, dw, vecs)


def tokens_back_kernel(vec, tok, part, recv, gresid, gmem, gmem_recv, gtok, gmemory):
    vec, tok, part, recv, gresid = ready(vec, tok, part, recv, gresid)
    gain = vec[0:1]

    def norm(s):
        rows = seq_rows(s)
        dy = part[rows, :].astype(F32) + recv[rows, :].astype(F32)
        dx, _, _ = norm_back(tok[rows, :].astype(F32), gain, dy)
        gtok[rows, :] = (gresid[rows, :] + dx).astype(BF)

    loop(4, norm)
    flush(gtok)
    gmem, gmem_recv = ready(gmem, gmem_recv)
    gmemory[...] = (gmem[...].astype(F32) + gmem_recv[...].astype(F32)).astype(BF)


MERGES = {"pass": (2, 1), "sum": (3, 4), "end": (4, 1), "half": (3, 2), "near": (2, 2), "last": (2, 1)}


def merge_kernel(kinds, *refs):
    at, out = 0, sum(MERGES[kind][0] for kind in kinds)
    for kind in kinds:
        ins, outs = refs[at : at + MERGES[kind][0]], refs[out : out + MERGES[kind][1]]
        at, out = at + len(ins), out + len(outs)
        if kind == "sum" or kind == "half" or kind == "near":
            blk = outs[0].shape[0]
            for i, dst in enumerate(outs):
                rows = slice(i * blk, (i + 1) * blk)
                dst[...] = sum(x[rows, :].astype(F32) for x in ins).astype(dst.dtype)
        else:
            outs[0][...] = sum(x[...].astype(F32) for x in ins).astype(outs[0].dtype)


def merge(jobs, after=()):
    ins, outs = [], []
    for kind, *arrays in jobs:
        ins += arrays
        rows, width = arrays[0].shape
        parts = {"sum": 4, "half": 2, "near": 2}.get(kind, 1)
        outs.append(sds((rows // parts, width), BF if kind == "pass" else F32))
        outs += [sds((rows // parts, width), BF)] * (parts - 1)
    kinds = [job[0] for job in jobs]
    return kernel_call(
        lambda *refs: merge_kernel(kinds, *refs), ins, [VM] * len(ins), outs, cost=1, after=after
    )


def join_kernel(core, mine, got, *outs):
    c = core[0]
    mine, got = ready(mine, got)
    at = 0
    for out in outs[: 2 if mine.shape[1] > 4 * DH else 3]:
        for k in range(out.shape[1] // D):
            out[:, pl.ds(pl.multiple_of(k * D + c * DH, 128), DH)] = mine[:, at : at + DH]
            out[:, pl.ds(pl.multiple_of(k * D + (1 - c) * DH, 128), DH)] = got[:, at : at + DH]
            at += DH
    if mine.shape[1] > at:
        gains, biases, wide = outs[2:]
        rows = mine.shape[0]
        wide[...] = jnp.zeros_like(wide)
        wide[0:rows, :] = mine[:, at:] + got[:, at:]
        turned = jnp.transpose(wide[...])
        gains[...] = turned[0:3, 0:rows]
        biases[...] = turned[3:6, 0:rows]


CUTS = ((0, 512), (512, 256))


class Moves:
    def __init__(self, mesh):
        self.nz, self.nf = mesh.shape["dp"], mesh.shape["fsdp"]
        self.n = self.nz * self.nf
        self.doubling = self.nz == 4 and self.nf == 8

    def permute(self, x, target):
        pairs = [(d, target(d // self.nf, (d % self.nf) // 2, d % 2)) for d in range(self.n)]
        return lax.ppermute(x, AXES, [(a, (z * self.nf) + 2 * yx + c) for a, (z, yx, c) in pairs])

    def sibling(self, x):
        return self.permute(x, lambda z, yx, c: (z, yx, 1 - c))

    def near_z(self, x):
        return self.permute(x, lambda z, yx, c: (z ^ 1, yx, c))

    def far_z(self, x):
        return self.permute(x, lambda z, yx, c: (z ^ 2, yx, c))

    def side_a(self, x):
        return self.permute(x, lambda z, yx, c: (z, yx ^ (1 + c), c))

    def side_b(self, x):
        return self.permute(x, lambda z, yx, c: (z, yx ^ (2 - c), c))

    def opposite_z(self, x):
        return self.permute(x, lambda z, yx, c: (z ^ 3, yx, c))


def per_device(moves, tokens, memory, lengths, cotangent, self_qkv, self_out, cross_q, cross_kv, cross_out, mlp_in, mlp_out, norm_gains, norm_biases):
    seqs, mem_len = memory.shape[0], memory.shape[1]
    rows = seqs * LEN
    place = lax.axis_index(AXES)
    c = place % 2
    chip = place // 2
    core = jnp.reshape(c, (1,)).astype(jnp.int32)
    wr, hr = self_qkv.shape[0], mlp_out.shape[0]
    ff = mlp_in.shape[1]
    fh = ff // 2
    r2, s2 = 2 * rows, 2 * seqs
    wb = D // 16
    pad = -(-mem_len // 16) * 16
    fast = moves.doubling


    def prepare(lens, pairs, after=(), hold=()):
        return kernel_call(
            prepare_kernel,
            [lens, *pairs],
            [SM] + [STAGE] * 6,
            [sds((r2, D), BF)] * 2 + [sds((s2 * pad, D), BF), sds((r2, D), F32)],
            [STAGE] * 4,
            after=after,
            hold=hold,
        )

    def self_attention(pieces, lens, xhat, keep, back, after=()):
        return kernel_call(
            self_kernel,
            [lens, core, offs, *pieces, xhat, keep, back],
            [SM] * 3 + [VM] * 4 + [STAGE] * 3,
            [
                sds((r2, D), BF),
                sds((r2, 3 * DH), BF),
                sds((s2, LEN, DH), BF),
                sds((r2, 3 * DH), BF),
                sds((8, D), F32),
                sds((D, 3 * DH), BF),
            ],
            [STAGE] * 6,
            [pltpu.VMEM((D, 128), BF)],
            cost=6,
            after=after,
        )

    def cross_attention(pieces, mem, vec, tok, comb, recv, keep, back, after=()):
        kv_rows = s2 * pad
        return kernel_call(
            lambda *refs: keys_and_cross_kernel(mem_len, *refs),
            [offs, *pieces, mem, core, vec, tok, comb, recv, keep, back],
            [SM] + [VM] * 4 + [STAGE, SM] + [STAGE] * 6,
            [
                sds((kv_rows, D), BF),
                sds((D, 2 * DH), BF),
                sds((D, DH), BF),
                sds((r2, D), F32),
                sds((r2, D), BF),
                sds((r2, DH), BF),
                sds((s2, pad, DH), BF),
                sds((r2, 3 * DH), BF),
            ],
            [STAGE] * 8,
            cost=12,
            after=after,
        )

    def inner_part(resid_one, comb, recv, vec, w_in, hold=()):
        return kernel_call(
            inner_kernel,
            [resid_one, comb, recv, vec, w_in],
            [STAGE] * 5,
            [sds((r2, D), F32), sds((r2, D), BF), sds((r2, fh), BF), sds((r2, fh), BF)],
            [STAGE] * 4,
            cost=5,
            hold=hold,
        )

    def inner_weight(pieces, hold=()):
        return place_rows(pieces, offs, 0, [(0, fh, 0, wb, 0)], (D, fh), hold)

    def grads(body, ins, specs, ncols, extra=(), scratch=(), cost=5, after=(), hold=()):
        return kernel_call(
            body,
            [offs, *ins],
            [SM, *specs],
            [sds((4 * wb, ncols), BF)] * 4 + list(extra),
            scratch=[pltpu.VMEM((D, ncols), BF), *scratch],
            cost=cost,
            after=after,
            hold=hold,
        )

    def mlp_part(pieces, g, slope, w_in, hidden, third, after=(), hold=()):
        return kernel_call(
            mlp_and_grad_kernel,
            [offs, *pieces, g, slope, w_in, hidden, third],
            [SM] + [VM] * 12,
            [sds((rows, D), BF), sds((3 * rows, D), BF)] + [sds((4 * wb, fh), BF)] * 4,
            scratch=[pltpu.VMEM((r2, fh), BF), pltpu.VMEM((fh, D), BF), pltpu.VMEM((D, fh), BF)],
            cost=11,
            after=after,
            hold=hold,
        )

    def cross_back(resid_two, comb, recv, part, after=()):
        return kernel_call(
            cross_back_and_grads_kernel,
            [
                offs, core, vec, resid_two, comb, recv, part, g, *cout, kv, cq, cprobs, w_cq,
                *cross_mixed, second, w_ckv, mem,
            ],
            [SM] * 2 + [VM] * 17,
            [
                sds((rows, D), BF),
                sds((r2, D), F32),
                sds((r2, D), BF),
                sds((8, D), F32),
                sds((seqs * pad, D), BF),
                sds((seqs * pad, D), BF),
            ]
            + [sds((4 * wb, 4 * DH), BF)] * 4,
            scratch=[
                pltpu.VMEM((r2, D), BF),
                pltpu.VMEM((r2, DH), BF),
                pltpu.VMEM(kv.shape, BF),
                pltpu.VMEM((r2, DH), BF),
                pltpu.VMEM((D, 4 * DH), BF),
            ],
            cost=16,
            after=after,
            limit=24 << 20,
        )

    def self_back(gsecond, recv, gresid_two, after=()):
        return kernel_call(
            self_back_and_grads_kernel,
            [
                offs, core, vec, resid_one, gsecond, recv, gresid_two, *out, packed, probs, w_qkv, xhat,
                *self_mixed, first, dvec_two,
            ],
            [SM] * 2 + [STAGE] * 15,
            [sds((rows, D), F32), sds((rows, D), BF), sds((rows, D), BF)]
            + [sds((4 * wb, 4 * DH + 128), BF)] * 4,
            scratch=[
                pltpu.VMEM((r2, D), BF),
                pltpu.VMEM((r2, 3 * DH), BF),
                pltpu.VMEM((8, D), F32),
                pltpu.VMEM((r2, DH), BF),
                pltpu.VMEM((D, 4 * DH + 128), BF),
                pltpu.VMEM((128, D), F32),
            ],
            cost=11,
            after=after,
        )

    def tokens_back(recv, gmem_recv, after=()):
        return kernel_call(
            tokens_back_kernel,
            [vec, tokens.reshape(rows, D), gfirst, recv, gresid_one, gmem, gmem_recv],
            [STAGE] * 7,
            [sds((rows, D), BF), sds(gmem.shape, BF)],
            [STAGE] * 2,
            cost=4,
            after=after,
        )

    sib = moves.sibling
    pairs = []
    for x in (tokens.reshape(rows, D), cotangent.reshape(rows, D), memory):
        pairs += [x, sib(x)]
    lens = jnp.concatenate([lengths, sib(lengths)], 0)


    bits = jnp.arange(4, dtype=jnp.int32)
    if fast:
        plane = jnp.stack([jnp.int32(0), 1 + c, 2 - c, jnp.int32(3)]).astype(jnp.int32)
        z, yx = chip // 4, chip % 4
        chips = ((z ^ bits)[None, :] * 4 + (yx ^ plane)[:, None]).reshape(16).astype(jnp.int32)
    else:
        chips = jnp.arange(16, dtype=jnp.int32)
    turned = ((chips // 8) ^ c) * 8 + chips % 8
    offs = jnp.stack([chips, turned]).astype(jnp.int32)
    widths = (4 * DH + 128, 4 * DH, 4 * DH)

    if fast:
        keep, send = kernel_call(
            pack_kernel,
            [core, self_qkv, self_out, cross_q, cross_kv, cross_out, mlp_in, norm_gains, norm_biases],
            [SM] + ["stage"] * 8,
            [sds((wr, sum(widths)), BF)] * 2,
            [STAGE] * 2,
            scratch=[pltpu.VMEM((128, 128), F32)],
            cost=1,
            limit=60 << 20,
        )
        both, one, three, last = kernel_call(
            order_kernel,
            [core, keep, sib(send), mlp_out],
            [SM] + [STAGE] * 3,
            [sds((2 * wr, w), BF) for w in (widths[0] + widths[1], widths[0], 6 * DH, 2 * DH)],
            [STAGE] * 4,
            cost=1,
            after=[lens, pairs[1], pairs[3]],
        )
        near, far, side_a, side_b = moves.near_z, moves.far_z, moves.side_a, moves.side_b
        near_both, along = near(both), [far(one), moves.opposite_z(one)]
        tok, g, mem, xhat = prepare(lens, pairs, hold=(one, both, three, last))
        last = tie(last, tok)
        a_last, b_last = side_a(last), side_b(last)
        one, two = cats(
            [
                [(one, 0, widths[0]), (near_both, 0, widths[0]), *whole(*along)],
                [(both, widths[0], widths[1]), (near_both, widths[0], widths[1])],
            ],
            after=(tok, a_last, b_last),
        )
        three, ab_last = tie(three, one), tie(a_last, one)
        a1, b1, far_two, near_three, ab_last = side_a(one), side_b(one), far(two), near(three), side_b(ab_last)
        a1 = tie(a1, b1)
        two, last, three = cats(
            [whole(two, far_two), whole(last, a_last, b_last, ab_last), whole(three, near_three)], after=(a1,)
        )
        ab1, a2, b2, far_three, near_last = side_b(a1), side_a(two), side_b(two), far(three), near(last)
        a2 = tie(a2, b2, ab1)
        three, four, last, *parts = cats(
            [
                [(three, 0, 4 * DH), (far_three, 0, 4 * DH)],
                [(three, 4 * DH, D), (far_three, 4 * DH, D)],
                whole(last, near_last),
                *([(last, lo, width), (near_last, lo, width)] for lo, width in CUTS),
            ],
            after=(a2,),
        )
        out = out_rows([one, a1, b1, ab1], offs, 3 * DH)
        out = (out, sib(out))
        three, a2 = tie(three, out[1]), tie(a2, out[1])
        ab2, a3, b3, far_a = side_b(a2), side_a(three), side_b(three), far(tie(parts[0], out[1]))
        first, packed, probs, comb, vec, w_qkv = self_attention([one, a1, b1, ab1], lens, xhat, *out, after=(three,))
        a3 = tie(a3, b3, ab2, comb, far_a)
        four = tie(four, a3)
        comb = tie(comb, four)
        cout = out_rows([two, a2, b2, ab2], offs, 0)
        cout = (cout, sib(cout))
        self_mixed = (comb, sib(comb))
        ab3, a4, b4, far_b = side_b(a3), side_a(four), side_b(four), far(tie(parts[1], four))
        kv, w_ckv, w_cq, resid_one, second, cq, cprobs, comb = cross_attention(
            [two, a2, b2, ab2], mem, vec, tok, *self_mixed, *cout
        )
        comb = tie(comb, ab3, a4, b4, far_b)
        cross_mixed, ab4 = (comb, sib(comb)), side_b(tie(a4, comb))
        hold = [kv, cprobs, cq, w_cq, *cout, w_ckv, second]
        w_in = inner_weight([three, a3, b3, ab3], hold)
        resid_two, third, hidden, slope = inner_part(resid_one, *cross_mixed, vec, w_in, hold)
        last = [four, a4, b4, ab4, last, far_a, far_b]
    else:
        tok, g, mem, xhat = prepare(lens, pairs)
        everywhere = lambda w: lax.all_gather(w, AXES, axis=0, tiled=True)
        split = lambda w: [w[i * w.shape[0] // 4 : (i + 1) * w.shape[0] // 4] for i in range(4)]

        def col_half(w, groups):
            w = w.reshape(w.shape[0], groups, 2, w.shape[1] // (2 * groups))
            return lax.dynamic_index_in_dim(w, c, 2, keepdims=False).reshape(w.shape[0], -1)

        vectors = jnp.pad(jnp.concatenate([norm_gains, norm_biases], 0).T, ((0, 0), (0, 122)))
        one = jnp.concatenate([col_half(self_qkv, 3), col_half(self_out, 1), vectors], 1)
        two = jnp.concatenate([col_half(w, w.shape[1] // D) for w in (cross_out, cross_q, cross_kv)], 1)
        one, two = split(everywhere(one)), split(everywhere(two))
        three = split(everywhere(col_half(mlp_in, ff // (2 * hr))))
        out, cout = out_rows(one, offs, 3 * DH), out_rows(two, offs, 0)
        out, cout = (out, sib(out)), (cout, sib(cout))
        rowed = everywhere(mlp_out).reshape(moves.n // 2, 2, hr, D)
        rowed = lax.dynamic_index_in_dim(rowed, c, 1, keepdims=False).reshape(16, 2, fh // 32, D)
        rowed = rowed.transpose(1, 0, 2, 3)
        levels = rowed[1].reshape(4, 4, wb, D).transpose(1, 0, 2, 3).reshape(D, D)
        last = split(rowed[0].reshape(D, D)) + [levels[: D // 2]]
        last += [levels[D // 2 :, lo : lo + width] for lo, width in CUTS]
        hold = ()
        first, packed, probs, comb, vec, w_qkv = self_attention(one, lens, xhat, *out)
        self_mixed = (comb, sib(comb))
        kv, w_ckv, w_cq, resid_one, second, cq, cprobs, comb = cross_attention(
            two, mem, vec, tok, *self_mixed, *cout
        )
        cross_mixed = (comb, sib(comb))
        w_in = inner_weight(three)
        resid_two, third, hidden, slope = inner_part(resid_one, *cross_mixed, vec, w_in)


    near, far, side_a, side_b = moves.near_z, moves.far_z, moves.side_a, moves.side_b
    after = ()

    held = [resid_two, vec]
    d_mlpout = grads(dmlpout_kernel, [hidden, g], [STAGE] * 2, 2 * D, hold=[*hold, *held, third])
    if fast:
        got_ab1 = side_a(d_mlpout[3])
    part, comb, *d_mlpin = mlp_part(last, g, slope, w_in, hidden, third, after=d_mlpout[:1], hold=[*hold, *held])
    if fast:
        (on,) = merge([("pass", d_mlpout[2], got_ab1)], after=(part,))
        comb = tie(comb, on)
        got_b1, got_ab2, got_a1 = side_b(on), side_a(tie(d_mlpin[3], on)), side_a(tie(d_mlpout[1], on))
        after = (on,)
    recv = sib(comb)
    output, gresid_two, gsecond, dvec_two, gmem, gmem_other, *d_cross = cross_back(
        resid_two, comb, recv, part, after=after
    )
    if fast:
        on, kept1, on_far = merge(
            [("pass", d_mlpin[2], got_ab2), ("half", d_mlpout[0], got_a1, got_b1)], after=(dvec_two,)
        )
        gsecond = tie(gsecond, on)
        got_b2, got_far1 = side_b(on), far(on_far)
        got_a2, got_ab3 = side_a(tie(d_mlpin[1], on)), side_a(tie(d_cross[3], on))
        after = (on,)
    recv = sib(gsecond)
    gresid_one, gfirst, gfirst_other, *d_self = self_back(gsecond, recv, gresid_two, after=after)
    if fast:
        on, kept2, on_far, kept1, on_near = merge(
            [("pass", d_cross[2], got_ab3), ("half", d_mlpin[0], got_a2, got_b2), ("near", kept1, got_far1)],
            after=(gfirst,),
        )
        got_b3, got_a3, got_ab4 = side_b(on), side_a(tie(d_cross[1], on)), side_a(tie(d_self[3], on))
        got_far2, got_near1 = far(on_far), near(on_near)
        on, kept3, on_far, kept2, on_near, total1 = merge(
            [
                ("pass", d_self[2], got_ab4),
                ("half", d_cross[0], got_a3, got_b3),
                ("near", kept2, got_far2),
                ("last", kept1, got_near1),
            ]
        )
        gfirst_other, gmem_other = tie(gfirst_other, on), tie(gmem_other, on)
        got_b4, got_a4 = side_b(on), side_a(tie(d_self[1], on))
        got_far3, got_near2 = far(on_far), near(on_near)
    recv, gmem_recv = sib(gfirst_other), sib(gmem_other)
    grad_tokens, grad_memory = tokens_back(recv, gmem_recv)
    grad_memory = grad_memory.reshape(seqs, pad, D)[:, :mem_len]

    if fast:
        kept4, *blocks, kept3, on_near, total2 = merge(
            [("sum", d_self[0], got_a4, got_b4), ("near", kept3, got_far3), ("last", kept2, got_near2)], after=(grad_tokens,)
        )
        got_z4, got_near3 = [near(blocks[0]), far(blocks[1]), moves.opposite_z(blocks[2])], near(on_near)
        (total3,) = merge([("last", kept3, got_near3)])
        (total4,) = merge([("end", kept4, *got_z4)])
        total = [total1, total2, total3, total4]

        def own_rows(total):
            mine = lax.dynamic_slice_in_dim(total, c * wr, wr, 0)
            return mine, sib(lax.dynamic_slice_in_dim(total, (1 - c) * wr, wr, 0))

        def join(pair, *shapes, scratch=()):
            return kernel_call(
                join_kernel,
                [core, *pair],
                [SM, STAGE, STAGE],
                [sds(shape, F32) for shape in shapes],
                [STAGE] * len(shapes),
                scratch=scratch,
                cost=1,
            )

        sum_mlpout = jnp.concatenate([total[0][:, :D], total[0][:, D:]], 0)
        mine, got = own_rows(total[1])
        pair = (jnp.where(c == 0, mine, got), jnp.where(c == 0, got, mine))
        parts = [p.reshape(wr, ff // (2 * hr), 1, hr) for p in pair]
        grad_in = jnp.concatenate(parts, 2).reshape(wr, ff)
        grad_cout, grad_cq, grad_ckv = join(own_rows(total[2]), (wr, D), (wr, D), (wr, 2 * D))
        grad_out, grad_qkv, own_gains, own_biases = join(
            own_rows(total[3]), (wr, D), (wr, 3 * D), (3, wr), (3, wr), scratch=[pltpu.VMEM((128, 128), F32)]
        )
    else:

        def placed(parts):
            term = jnp.concatenate(parts, 0).astype(F32)
            both = jnp.stack([jnp.where(c == 0, term, 0.0), jnp.where(c == 1, term, 0.0)], 1)
            return lax.psum_scatter(both, AXES, scatter_dimension=0, tiled=True)

        def joined(total, lo, hi, groups):
            return total[:, :, lo:hi].reshape(wr, 2, groups, -1).transpose(0, 2, 1, 3).reshape(wr, -1)

        total = placed(d_cross)
        grad_cout, grad_cq, grad_ckv = (
            joined(total, 0, DH, 1),
            joined(total, DH, 2 * DH, 1),
            joined(total, 2 * DH, 4 * DH, 2),
        )
        total = placed(d_self)
        grad_out, grad_qkv = joined(total, 0, DH, 1), joined(total, DH, 4 * DH, 3)
        vectors = jnp.sum(total[:, :, 4 * DH : 4 * DH + 6], 1).T
        own_gains, own_biases = vectors[:3], vectors[3:]
        grad_in = joined(placed(d_mlpin), 0, fh, ff // (2 * hr))
        term = jnp.concatenate(d_mlpout, 0).astype(F32)
        term = term.reshape(16, wb, 2, D).transpose(0, 2, 1, 3).reshape(moves.n // 2, 1, hr, D)
        both = jnp.concatenate([jnp.where(c == 0, term, 0.0), jnp.where(c == 1, term, 0.0)], 1)
        sum_mlpout = lax.psum_scatter(both.reshape(ff, D), AXES, scatter_dimension=0, tiled=True)

    return (
        output.reshape(tokens.shape),
        grad_tokens.reshape(tokens.shape),
        grad_memory,
        grad_qkv,
        grad_out,
        grad_cq,
        grad_ckv,
        grad_cout,
        grad_in,
        sum_mlpout,
        own_gains,
        own_biases,
    )


def solution(mesh):
    batch = P(AXES, None, None)
    rows = P(AXES, None)
    cols = P(None, AXES)
    moves = Moves(mesh)
    in_specs = (batch, batch, P(AXES), batch) + (rows,) * 7 + (cols,) * 2
    out_specs = (batch,) * 3 + (rows,) * 7 + (cols,) * 2
    return jax.shard_map(
        lambda *args: per_device(moves, *args),
        mesh=mesh,
        in_specs=in_specs,
        out_specs=out_specs,
        check_vma=False,
    )
```

```python
import jax
import jax.numpy as jnp
import numpy as np
from jax import lax
from jax.experimental import pallas as pl
from jax.experimental.pallas import tpu as pltpu
from jax.sharding import PartitionSpec as P

AXES = ("dp", "fsdp")
HEADS = 12
HALF = HEADS // 2
HEAD = 64
D = 768
DH = D // 2
LEN = 64
EPS = 1e-06
NEG = -1e30
SCALE = HEAD ** (-0.5)
F32 = jnp.float32
BF = jnp.bfloat16
VMEM_LIMIT = 14 << 20

VM = pl.BlockSpec(memory_space=pltpu.VMEM)
SM = pl.BlockSpec(memory_space=pltpu.SMEM)
ANY = pl.BlockSpec(memory_space=pl.ANY)


def sds(shape, dtype):
    return jax.ShapeDtypeStruct(shape, dtype)


STAGE = VM


class Staged:
    def __init__(self, ref, copy):
        self.ref, self.copy, self.waited = ref, copy, False
        self.shape = ref.shape

    def ready(self):
        if not self.waited:
            self.copy.wait()
            self.waited = True
        return self.ref


PENDING = {}


def flush(*refs):
    for r in refs:
        if id(r) in PENDING:
            PENDING[id(r)].start()
            PENDING[id(r)] = None


def ready(*refs):
    out = [r.ready() if isinstance(r, Staged) else r for r in refs]
    return out[0] if len(out) == 1 else out


def kernel_call(body, ins, in_specs, outs, out_specs=None, scratch=(), cost=5, after=(), limit=None, hold=()):
    n, skip, m, k = len(ins), len(after) + len(hold), len(outs), len(scratch)
    out_specs = [VM] * m if out_specs is None else list(out_specs)
    staged_in = [i for i, spec in enumerate(in_specs) if spec == 'stage']
    staged_out = [i for i, spec in enumerate(out_specs) if spec == 'stage']
    buffers = [pltpu.VMEM(ins[i].shape, ins[i].dtype) for i in staged_in]
    buffers += [pltpu.VMEM(outs[i].shape, outs[i].dtype) for i in staged_out]
    extra = [*buffers, pltpu.SemaphoreType.DMA((len(buffers),))] if buffers else []

    def run(*refs):
        ins, outs = list(refs[:n]), list(refs[n + skip : n + skip + m])
        own = refs[n + skip + m : n + skip + m + k]
        PENDING.clear()
        if not buffers:
            body(*ins, *outs, *own)
            return
        held, sems = refs[n + skip + m + k : -1], refs[-1]
        for j, i in enumerate(staged_in):
            copy = pltpu.make_async_copy(ins[i], held[j], sems.at[j])
            copy.start()
            ins[i] = Staged(held[j], copy)
        copies = []
        for j, i in enumerate(staged_out, len(staged_in)):
            copies.append(pltpu.make_async_copy(held[j], outs[i], sems.at[j]))
            outs[i] = held[j]
            PENDING[id(held[j])] = copies[-1]
        body(*ins, *outs, *own)
        ready(*ins)
        for cp in PENDING.values():
            if cp is not None:
                cp.start()
        for cp in copies:
            cp.wait()

    space = lambda spec: ANY if spec == 'stage' else spec
    return pl.pallas_call(
        run,
        out_shape=list(outs),
        in_specs=[space(spec) for spec in in_specs] + [ANY] * len(after) + [VM] * len(hold),
        out_specs=[space(spec) for spec in out_specs],
        scratch_shapes=[*scratch, *extra],
        compiler_params=pltpu.CompilerParams(vmem_limit_bytes=limit or VMEM_LIMIT),
        cost_estimate=pl.CostEstimate(flops=cost * 7 * 10**9, bytes_accessed=0, transcendentals=0),
    )(*ins, *after, *hold)


def tie(x, *earlier):
    return pl.pallas_call(
        lambda *refs: None,
        out_shape=sds(x.shape, x.dtype),
        in_specs=[ANY] * (1 + len(earlier)),
        out_specs=ANY,
        input_output_aliases={0: 0},
        compiler_params=pltpu.CompilerParams(vmem_limit_bytes=1 << 20),
        cost_estimate=pl.CostEstimate(flops=0, bytes_accessed=0, transcendentals=0),
    )(x, *earlier)


def nn(a, b):
    return lax.dot_general(a, b, (((1,), (0,)), ((), ())), preferred_element_type=F32)


def nt(a, b):
    return lax.dot_general(a, b, (((1,), (1,)), ((), ())), preferred_element_type=F32)


def tn(a, b):
    return lax.dot_general(a, b, (((0,), (0,)), ((), ())), preferred_element_type=F32)


def normalise(v):
    mean = jnp.mean(v, -1, keepdims=True)
    cen = v - mean
    inv = lax.rsqrt(jnp.mean(cen * cen, -1, keepdims=True) + EPS)
    return cen * inv, inv


def norm_back(v, gain, dy):
    xhat, inv = normalise(v)
    dxh = dy * gain
    m1 = jnp.mean(dxh, -1, keepdims=True)
    m2 = jnp.mean(dxh * xhat, -1, keepdims=True)
    dx = inv * (dxh - m1 - xhat * m2)
    return dx, jnp.sum(dy * xhat, 0, keepdims=True), jnp.sum(dy, 0, keepdims=True)


GROUPS = ((0, 256), (256, DH))


def head_of_lane(rows, width):
    return lax.shift_right_logical(lax.broadcasted_iota(jnp.int32, (rows, width), 1), 6)


def spread(q):
    head = head_of_lane(1, q.shape[1])
    parts = [q * (head == h).astype(F32).astype(q.dtype) for h in range(q.shape[1] // HEAD)]
    return jnp.concatenate(parts, 0)


def fold(o):
    head = head_of_lane(LEN, o.shape[1])
    total = jnp.where(head == 0, o[:LEN], 0.0)
    for h in range(1, o.shape[1] // HEAD):
        total = jnp.where(head == h, o[h * LEN : (h + 1) * LEN], total)
    return total


def attend(q, k, v, allowed):
    probs, mixed = [], []
    for lo, hi in GROUPS:
        st = nt(k[:, lo:hi], spread(q[:, lo:hi])) * SCALE
        st = jnp.where(allowed[:, lo:hi], st, NEG)
        e = jnp.exp(st - jnp.max(st, 0, keepdims=True))
        p = (e * (1.0 / jnp.sum(e, 0, keepdims=True))).astype(BF)
        probs.append(p)
        mixed.append(fold(tn(p, v[:, lo:hi])).astype(BF))
    return jnp.concatenate(probs, 1), jnp.concatenate(mixed, 1)


def attend_back(g, q, k, v, p):
    dq, dk, dv = [], [], []
    for lo, hi in GROUPS:
        gs, qs, low = spread(g[:, lo:hi]), spread(q[:, lo:hi]), p[:, lo:hi]
        dp = nt(v[:, lo:hi], gs)
        pf = low.astype(F32)
        t = pf * dp
        ds = (t - pf * jnp.sum(t, 0, keepdims=True)).astype(BF)
        dq.append((fold(tn(ds, k[:, lo:hi])) * SCALE).astype(BF))
        dk.append((nn(ds, qs) * SCALE).astype(BF))
        dv.append(nn(low, gs).astype(BF))
    return [jnp.concatenate(x, 1) for x in (dq, dk, dv)]


def seq_rows(s):
    return pl.ds(pl.multiple_of(s * LEN, LEN), LEN)


def half_lanes(c):
    return pl.ds(pl.multiple_of(c * DH, DH), DH)


def loop(n, body, unroll=1):
    def step(i, carry):
        body(i)
        return carry

    lax.fori_loop(0, n, step, 0, unroll=unroll)


def columns_first(pieces, q, r):
    blk = pieces[0].shape[0] // 4
    return pieces[q], r * blk


def place(pieces, offs_ref, which, cols, targets):
    blk = pieces[0].shape[0] // 4
    for lo, hi, o, step, shift in cols:
        for q in range(4):
            for r in range(4):
                row = pl.multiple_of(offs_ref[which, q * 4 + r] * step + shift, 16)
                targets[o][pl.ds(row, blk), :] = pieces[q][r * blk : (r + 1) * blk, lo:hi]


def place_levels(near, far, offs_ref, step, shift, target):
    blk = near.shape[0] // 8
    lo = 0
    for level, src in ((0, near), *((2, part) for part in far)):
        at = 0 if level == 0 else lo
        for q in range(4):
            for r in range(2):
                row = pl.multiple_of(offs_ref[0, q * 4 + level + r] * step + shift, 16)
                rows = slice((r * 4 + q) * blk, (r * 4 + q + 1) * blk)
                target[pl.ds(row, blk), at : at + src.shape[1]] = src[rows, :]
        lo += src.shape[1] if level else 0


def place_rows(pieces, offs, which, cols, shape, hold=()):
    def body(offs_ref, *refs):
        place(refs[:4], offs_ref, which, cols, refs[4:5])

    return kernel_call(body, [offs, *pieces], [SM] + [VM] * 4, [sds(shape, BF)], cost=1, hold=hold)[0]


def out_rows(pieces, offs, lo):
    blk = pieces[0].shape[0] // 4
    return place_rows(pieces, offs, 1, [(lo, lo + DH, 0, blk, 0)], (16 * blk, DH))


def send_out(dw, offs_ref, outs):
    blk = dw.shape[0] // 16
    for q in range(4):
        for r in range(4):
            row = pl.multiple_of(offs_ref[0, q * 4 + r] * blk, 16)
            outs[q][r * blk : (r + 1) * blk, :] = dw[pl.ds(row, blk), :]


def pack_kernel(core, qkv, out, cq, ckv, cout, gains, biases, keep, send, vecs):
    c = core[0]
    qkv, out, cq, ckv, cout, gains, biases = ready(qkv, out, cq, ckv, cout, gains, biases)
    vecs[...] = jnp.zeros_like(vecs)
    vecs[0:3, 0:24] = gains[...].astype(F32)
    vecs[3:6, 0:24] = biases[...].astype(F32)
    rows = keep.shape[0]
    wide = jnp.transpose(vecs[...])[:rows].astype(BF)
    for dst, which in ((keep, c), (send, 1 - c)):
        at = 0
        for w, groups in ((qkv, 3), (out, 1), (None, 0), (cout, 1), (cq, 1), (ckv, 2)):
            if w is None:
                dst[:, at : at + 128] = wide
                at += 128
            for k in range(groups):
                lanes = pl.ds(pl.multiple_of(k * D + which * DH, 128), DH)
                dst[:, at : at + DH] = w[:, lanes]
                at += DH


def pack_inner_kernel(core, win, keep, send):
    c = core[0]
    win = ready(win)
    hr = 96
    for k in range(win.shape[1] // (2 * hr)):
        first = win[:, 2 * k * hr : (2 * k + 1) * hr]
        second = win[:, (2 * k + 1) * hr : (2 * k + 2) * hr]
        keep[:, k * hr : (k + 1) * hr] = jnp.where(c == 0, first, second)
        send[:, k * hr : (k + 1) * hr] = jnp.where(c == 0, second, first)


def order_kernel(core, keep, got, wout, last, *outs):
    c = core[0]
    rows = keep.shape[0]
    for b, (top, under) in enumerate(((keep, got), (got, keep))):
        for dst in outs:
            width = dst.shape[1]
            dst[b * rows : (b + 1) * rows, :] = jnp.where(c == 0, top[:, :width], under[:, :width])
    last[...] = wout[2 * rows :, :]


def order_mlp_kernel(core, keep, got, wout, three):
    c = core[0]
    rows, width = keep.shape
    for b, (top, under) in enumerate(((keep, got), (got, keep))):
        three[b * rows : (b + 1) * rows, :width] = jnp.where(c == 0, top[...], under[...])
    three[:, width:] = wout[0 : 2 * rows, :]


def cats(jobs, after=()):
    arrays, places, outs = [], [], []
    for job in jobs:
        at, outs = 0, [*outs, sds((sum(x.shape[0] for x, _, _ in job), job[0][2]), BF)]
        for x, lo, width in job:
            arrays.append(x)
            places.append((len(outs) - 1, at, lo, width))
            at += x.shape[0]
    n = len(arrays)

    def body(*refs):
        for src, (o, at, lo, width) in zip(refs[:n], places):
            refs[n + o][at : at + src.shape[0], :] = src[:, lo : lo + width]

    return kernel_call(body, arrays, [VM] * n, outs, cost=1, after=after)


def whole(*arrays):
    return [(x, 0, x.shape[1]) for x in arrays]


def prepare_kernel(lens, tok_own, tok_other, cot_own, cot_other, mem_own, mem_other, tok, g, mem, xhat):
    tok_own, tok_other = ready(tok_own, tok_other)
    rows = tok.shape[0] // 2
    seqs, length = mem_own.shape[0], mem_own.shape[1]
    pad = mem.shape[0] // (2 * seqs)
    for b, src in ((0, tok_own), (1, tok_other)):
        tok[b * rows : (b + 1) * rows, :] = src[...]
    flush(tok)

    def norm(s):
        xhat[seq_rows(s), :] = normalise(tok[seq_rows(s), :].astype(F32))[0]

    loop(2 * seqs, norm, 2)
    flush(xhat)
    mem_own, mem_other = ready(mem_own, mem_other)
    for b, src in ((0, mem_own), (1, mem_other)):
        for s in range(seqs):
            at = (b * seqs + s) * pad
            mem[at + length - length % 16 : at + pad, :] = jnp.zeros((pad - length + length % 16, D), BF)
            mem[at : at + length, :] = src[s]
    flush(mem)
    cot_own, cot_other = ready(cot_own, cot_other)
    place = lax.broadcasted_iota(jnp.int32, (LEN, D), 0)
    for b, src in ((0, cot_own), (1, cot_other)):
        for s in range(seqs):
            at = (b * seqs + s) * LEN
            live = (place < lens[b * seqs + s]).astype(F32)
            g[at : at + LEN, :] = (src[s * LEN : (s + 1) * LEN, :].astype(F32) * live).astype(BF)


def self_kernel(lens, core, offs, own, a, b, ab, xhat, keep, back, first, packed, probs, comb, vec, wqkv, gcol):
    c = core[0]
    blk = D // 16
    place((own, a, b, ab), offs, 0, [(4 * DH, 4 * DH + 128, 1, blk, 0), (0, 3 * DH, 0, blk, 0)], (wqkv, gcol))
    xhat = ready(xhat)
    vec[...] = jnp.transpose(gcol[...].astype(F32))[:8]
    gain, bias = vec[0:1], vec[3:4]

    def norm(s):
        first[seq_rows(s), :] = (xhat[seq_rows(s), :] * gain + bias).astype(BF)

    loop(8, norm, 2)
    flush(first)

    def proj(b):
        rows = pl.ds(pl.multiple_of(b * 256, 256), 256)
        packed[rows, :] = nn(first[rows, :], wqkv[...]).astype(BF)

    loop(2, proj)
    flush(packed)
    key = lax.broadcasted_iota(jnp.int32, (LEN, DH), 0)
    query = lax.broadcasted_iota(jnp.int32, (LEN, DH), 1) & (LEN - 1)

    def att(s):
        allowed = (key <= query) & (key < lens[s])
        rows = seq_rows(s)
        p, m = attend(packed[rows, 0:DH], packed[rows, DH : 2 * DH], packed[rows, 2 * DH :], allowed)
        probs[s] = p
        comb[rows, D:] = m

    loop(8, att, 2)
    flush(probs)
    keep, back = ready(keep, back)
    comb[:, half_lanes(c)] = nn(comb[:, D:], keep[:DH, :]).astype(BF)
    comb[:, half_lanes(1 - c)] = nn(comb[:, D:], back[DH:, :]).astype(BF)


def kv_kernel(offs, own, a, b, ab, mem, kv, wckv, wcq):
    blk = D // 16
    place((own, a, b, ab), offs, 0, [(2 * DH, 4 * DH, 0, blk, 0), (DH, 2 * DH, 1, blk, 0)], (wckv, wcq))
    mem = ready(mem)

    def step(b):
        rows = pl.ds(pl.multiple_of(b * 480, 480), 480)
        kv[rows, :] = nn(mem[rows, :], wckv[...]).astype(BF)

    loop(mem.shape[0] // 480, step)


def swapped(s):
    return pl.ds(pl.multiple_of(((s + 4) & 7) * LEN, LEN), LEN)


def cross_kernel(mem_len, core, vec, tok, part, recv, wcq, kv, keep, back, resid, second, cq, probs, comb):
    c = core[0]
    vec, tok, part, recv = ready(vec, tok, part, recv)
    gain, bias = vec[1:2], vec[4:5]

    def norm(s):
        rows = seq_rows(s)
        both = part[rows, 0:D].astype(F32) + recv[swapped(s), 0:D].astype(F32)
        v = tok[rows, :].astype(F32) + both
        resid[rows, :] = v
        xhat, _ = normalise(v)
        second[rows, :] = (xhat * gain + bias).astype(BF)

    loop(8, norm, 2)
    flush(resid, second)
    wcq = ready(wcq)
    cq[...] = nn(second[...], wcq[...]).astype(BF)
    flush(cq)
    kv = ready(kv)
    pad = probs.shape[1]
    allowed = lax.broadcasted_iota(jnp.int32, (pad, DH), 0) < mem_len

    def att(s):
        rows = seq_rows(s)
        keys = pl.ds(pl.multiple_of(s * pad, 16), pad)
        p, m = attend(cq[rows, :], kv[keys, 0:DH], kv[keys, DH:], allowed)
        probs[s] = p
        comb[rows, D:] = m

    loop(8, att, 2)
    flush(probs)
    keep, back = ready(keep, back)
    comb[:, half_lanes(c)] = nn(comb[:, D:], keep[:DH, :]).astype(BF)
    comb[:, half_lanes(1 - c)] = nn(comb[:, D:], back[DH:, :]).astype(BF)


def keys_and_cross_kernel(
    mem_len, offs, own, a, b, ab, mem, core, vec, tok, part, recv, keep, back, kv, wckv, wcq, resid, second, cq, probs, comb
):
    kv_kernel(offs, own, a, b, ab, mem, kv, wckv, wcq)
    cross_kernel(mem_len, core, vec, tok, part, recv, wcq, kv, keep, back, resid, second, cq, probs, comb)


def inner_kernel(resid, part, recv, vec, win, resid_two, third, hidden, slope):
    resid, part, recv, vec = ready(resid, part, recv, vec)
    gain, bias = vec[2:3], vec[5:6]

    def norm(s):
        rows = seq_rows(s)
        both = part[rows, 0:D].astype(F32) + recv[swapped(s), 0:D].astype(F32)
        v = resid[rows, :] + both
        resid_two[rows, :] = v
        xhat, _ = normalise(v)
        third[rows, :] = (xhat * gain + bias).astype(BF)

    loop(8, norm, 2)
    flush(resid_two, third)
    win = ready(win)

    def step(b):
        rows = pl.ds(pl.multiple_of(b * 128, 128), 128)
        x = nn(third[rows, :], win[...])
        cdf = 0.5 + 0.5 * lax.erf(x * (0.5**0.5))
        hidden[rows, :] = (x * cdf).astype(BF)
        density = jnp.exp(x * x * -0.5) * ((2.0 * np.pi) ** -0.5)
        slope[rows, :] = (cdf + x * density).astype(BF)

    loop(4, step)


def mlp_kernel(offs, pieces, near, far, g, slope, win, hidden, own, comb, ginner, wout):
    half = own.shape[0]
    blk = D // 16
    place(pieces, offs, 0, [(0, D, 0, 2 * blk, 0)], (wout,))
    place_levels(near, far, offs, 2 * blk, blk, wout)
    g, slope, win = ready(g, slope, win)

    def back(b):
        rows = pl.ds(pl.multiple_of(b * 256, 256), 256)
        gh = nt(g[rows, :], wout[...])
        ginner[rows, :] = (gh * slope[rows, :].astype(F32)).astype(BF)
        comb[rows, :] = nt(ginner[rows, :], win[...]).astype(BF)

    loop(2, back)
    flush(ginner)
    hidden = ready(hidden)
    own[...] = nn(hidden[0:half, :], wout[...]).astype(BF)
    comb[2 * half :, :] = nn(hidden[half:, :], wout[...]).astype(BF)


def dmlpout_kernel(offs, hidden, g, own, a, b, ab, near, *refs):
    far, dw, dz = refs[:-2], refs[-2], refs[-1]
    blk = dw.shape[0] // 16
    for i in range(4):
        part = tn(hidden[:, i * 8 * blk : (i + 1) * 8 * blk], g[...]).astype(BF)
        for k in range(8):
            dst = dz if k % 2 else dw
            row = (4 * i + k // 2) * blk
            dst[row : row + blk, :] = part[k * blk : (k + 1) * blk]
    send_out(dw, offs, (own, a, b, ab))
    for q in range(4):
        for r in range(4):
            rows = pl.ds(pl.multiple_of(offs[0, q * 4 + r] * blk, 16), blk)
            at = ((r % 2) * 4 + q) * blk
            if r < 2:
                near[at : at + blk, :] = dz[rows, :]
                continue
            for dst, (lo, width) in zip(far, FAR_CUTS):
                dst[at : at + blk, :] = dz[rows, lo : lo + width]


def mlp_and_grad_kernel(
    offs, pown, pa, pb, pab, near, far_a, far_b, g, slope, win, hidden, third, own, comb, d_own, d_a, d_b, d_ab, ginner, wout, dw
):
    mlp_kernel(offs, (pown, pa, pb, pab), near, (far_a, far_b), g, slope, win, hidden, own, comb, ginner, wout)
    dmlpin_kernel(offs, third, ginner, d_own, d_a, d_b, d_ab, dw)


def dmlpin_kernel(offs, third, ginner, *refs):
    third, ginner = ready(third, ginner)
    outs, dw = refs[:4], refs[4]
    for b in range(0, dw.shape[0], 256):
        dw[b : b + 256, :] = tn(third[:, b : b + 256], ginner[...]).astype(BF)
    send_out(dw, offs, outs)


def cross_back_kernel(
    core, vec, resid, part, recv, own, g, keep, back, kv, cq, probs, wcq, output, gresid, gtwo, dcq, dkv, gsecond, dvec, gm
):
    c = core[0]
    vec, resid, part, recv, own, g = ready(vec, resid, part, recv, own, g)
    gain = vec[2:3]
    dvec[...] = jnp.zeros_like(dvec)

    def norm(s):
        rows = seq_rows(s)
        dy = part[rows, :].astype(F32) + recv[swapped(s), :].astype(F32)
        dx, dg, db = norm_back(resid[rows, :], gain, dy)
        total = g[rows, :].astype(F32) + dx
        gresid[rows, :] = total
        gtwo[rows, :] = total.astype(BF)

        @pl.when(s < 4)
        def _():
            dvec[0:1, :] += dg
            dvec[1:2, :] += db
            extra = own[rows, :].astype(F32) + recv[pl.ds(pl.multiple_of(512 + s * LEN, LEN), LEN), :].astype(F32)
            output[rows, :] = (resid[rows, :] + extra).astype(BF)

    loop(8, norm, 2)
    flush(output, gresid, gtwo, dvec)
    keep, back = ready(keep, back)
    gm[...] = (nt(gtwo[:, half_lanes(c)], keep[:DH, :]) + nt(gtwo[:, half_lanes(1 - c)], back[DH:, :])).astype(BF)
    pad = probs.shape[1]
    kv, cq, probs = ready(kv, cq, probs)

    def att(s):
        rows = seq_rows(s)
        keys = pl.ds(pl.multiple_of(s * pad, 16), pad)
        dq, dk, dv = attend_back(gm[rows, :], cq[rows, :], kv[keys, 0:DH], kv[keys, DH:], probs[s])
        dcq[rows, :] = dq
        dkv[keys, 0:DH] = dk
        dkv[keys, DH:] = dv

    loop(8, att, 2)
    flush(dcq, dkv)
    wcq = ready(wcq)
    gsecond[...] = nt(dcq[...], wcq[...]).astype(BF)


def out_grad(dw, lo, c, mine, other, g):
    cols = half_lanes(c)
    dw[half_lanes(c), lo : lo + DH] = tn(mine[:, D:], g[:, cols]).astype(BF)
    rest = tn(other[256:, D:], g[:256, cols]) + tn(other[:256, D:], g[256:, cols])
    dw[half_lanes(1 - c), lo : lo + DH] = rest.astype(BF)


def dcross_kernel(offs, core, mixed, mixed_other, gtwo, second, dcq, dkv, mem, *refs):
    outs, dw = refs[:4], refs[4]
    mixed, mixed_other, gtwo = ready(mixed, mixed_other, gtwo)
    out_grad(dw, 0, core[0], mixed, mixed_other, gtwo)
    second, dcq = ready(second, dcq)
    dw[:, DH : 2 * DH] = tn(second[...], dcq[...]).astype(BF)
    mem = ready(mem)
    for b in range(0, D, 256):
        dw[b : b + 256, 2 * DH :] = tn(mem[:, b : b + 256], dkv[...]).astype(BF)
    send_out(dw, offs, outs)


def memory_kernel(dkv, wckv, own, other):
    half = own.shape[0]
    for i, dst in ((1, other), (0, own)):
        for b in range(0, half, 480):
            dst[b : b + 480, :] = nt(dkv[i * half + b : i * half + b + 480, :], wckv[...]).astype(BF)


def cross_back_and_grads_kernel(
    offs, core, vec, resid, part, recv, own, g, keep, back, kv, cq, probs, wcq, mixed, mixed_other, second, mem,
    output, gresid, gsecond, dvec, dkv, d_own, d_a, d_b, d_ab, gtwo, dcq, gm, dw
):
    cross_back_kernel(
        core, vec, resid, part, recv, own, g, keep, back, kv, cq, probs, wcq, output, gresid, gtwo, dcq, dkv, gsecond, dvec, gm
    )
    dcross_kernel(
        offs, core, mixed, mixed_other, gtwo, second, dcq, dkv, mem, d_own, d_a, d_b, d_ab, dw
    )


def self_back_kernel(
    core, vec, resid, part, recv, gresid_two, keep, back, packed, probs, wqkv, xhat, gresid, gone, dpacked, gfirst_own, gfirst_other, dvec, gm
):
    c = core[0]
    vec, resid, part, recv, gresid_two = ready(vec, resid, part, recv, gresid_two)
    gain = vec[1:2]
    dvec[...] = jnp.zeros_like(dvec)

    def norm(s):
        rows = seq_rows(s)
        dy = part[rows, :].astype(F32) + recv[swapped(s), :].astype(F32)
        dx, dg, db = norm_back(resid[rows, :], gain, dy)
        total = gresid_two[rows, :] + dx
        gone[rows, :] = total.astype(BF)

        @pl.when(s < 4)
        def _():
            gresid[rows, :] = total
            dvec[0:1, :] += dg
            dvec[1:2, :] += db

    loop(8, norm, 2)
    flush(gresid, gone)
    keep, back = ready(keep, back)
    gm[...] = (nt(gone[:, half_lanes(c)], keep[:DH, :]) + nt(gone[:, half_lanes(1 - c)], back[DH:, :])).astype(BF)
    packed, probs = ready(packed, probs)

    def att(s):
        rows = seq_rows(s)
        dq, dk, dv = attend_back(
            gm[rows, :], packed[rows, 0:DH], packed[rows, DH : 2 * DH], packed[rows, 2 * DH :], probs[s]
        )
        dpacked[rows, 0:DH] = dq
        dpacked[rows, DH : 2 * DH] = dk
        dpacked[rows, 2 * DH :] = dv

    loop(8, att, 2)
    flush(dpacked)
    wqkv, xhat = ready(wqkv, xhat)
    half = gfirst_own.shape[0]
    for b, dst in ((half, gfirst_other), (0, gfirst_own)):
        term = nt(dpacked[b : b + half, :], wqkv[...])
        dst[...] = term.astype(BF)
        flush(dst)
        dvec[2:3, :] += jnp.sum(term * xhat[b : b + half, :], 0, keepdims=True)
        dvec[3:4, :] += jnp.sum(term, 0, keepdims=True)


def dself_kernel(offs, core, mixed, mixed_other, gone, first, dpacked, dvec_two, dvec_one, *refs):
    outs, dw, vecs = refs[:4], refs[4], refs[5]
    mixed, mixed_other, gone = ready(mixed, mixed_other, gone)
    out_grad(dw, 0, core[0], mixed, mixed_other, gone)
    first, dpacked, dvec_two, dvec_one = ready(first, dpacked, dvec_two, dvec_one)
    for b in range(0, D, 256):
        dw[b : b + 256, DH : 4 * DH] = tn(first[:, b : b + 256], dpacked[...]).astype(BF)
    vecs[...] = jnp.zeros_like(vecs)
    for i, (v, row) in enumerate(((dvec_one, 2), (dvec_one, 0), (dvec_two, 0), (dvec_one, 3), (dvec_one, 1), (dvec_two, 1))):
        vecs[i : i + 1, :] = v[row : row + 1, :]
    dw[:, 4 * DH :] = jnp.transpose(vecs[...]).astype(BF)
    send_out(dw, offs, outs)


def self_back_and_grads_kernel(
    offs, core, vec, resid, part, recv, gresid_two, keep, back, packed, probs, wqkv, xhat, mixed, mixed_other, first, dvec_two,
    gresid, gfirst_own, gfirst_other, d_own, d_a, d_b, d_ab, gone, dpacked, dvec, gm, dw, vecs
):
    self_back_kernel(
        core, vec, resid, part, recv, gresid_two, keep, back, packed, probs, wqkv, xhat,
        gresid, gone, dpacked, gfirst_own, gfirst_other, dvec, gm
    )
    dself_kernel(offs, core, mixed, mixed_other, gone, first, dpacked, dvec_two, dvec, d_own, d_a, d_b, d_ab, dw, vecs)


def tokens_back_kernel(vec, tok, part, recv, gresid, gmem, gmem_recv, gtok, gmemory, token):
    token[...] = jnp.zeros_like(token)
    vec, tok, part, recv, gresid = ready(vec, tok, part, recv, gresid)
    gain = vec[0:1]

    def norm(s):
        rows = seq_rows(s)
        dy = part[rows, :].astype(F32) + recv[rows, :].astype(F32)
        dx, _, _ = norm_back(tok[rows, :].astype(F32), gain, dy)
        gtok[rows, :] = (gresid[rows, :] + dx).astype(BF)

    loop(4, norm)
    flush(gtok)
    gmem, gmem_recv = ready(gmem, gmem_recv)
    gmemory[...] = (gmem[...].astype(F32) + gmem_recv[...].astype(F32)).astype(BF)


MERGES = {"pass": (2, 1), "half": (3, 2), "near": (2, 2), "last": (2, 1)}
MERGES.update({"tail": (6, 1), "tail_near": (3, 1), "send": (3, 3), "send_near": (2, 1), "levels": (3, 2), "columns": (2, 3), "side": (3, 2)})


def merge_kernel(kinds, beside, *refs):
    if beside:
        n_in, (i, j) = sum(MERGES[kind][0] for kind in kinds), beside
        outs = list(refs[n_in:])
        wide, width = outs[i], outs[i].shape[1] - refs[n_in - 2].shape[1]
        outs[i] = wide.at[:, :width]
        outs.insert(j, wide.at[:, width:])
        refs = (*refs[:n_in], *outs)
    at, out = 0, sum(MERGES[kind][0] for kind in kinds)
    for kind in kinds:
        ins, outs = refs[at : at + MERGES[kind][0]], refs[out : out + MERGES[kind][1]]
        at, out = at + len(ins), out + len(outs)
        if kind == "levels":
            half = outs[0].shape[0]
            for i, dst in enumerate(outs):
                rows = slice(i * half, (i + 1) * half)
                for src, (lo, width) in zip(ins[1:], FAR_CUTS):
                    total = ins[0][rows, lo : lo + width].astype(F32) + src[rows, :].astype(F32)
                    dst[:, lo : lo + width] = total.astype(dst.dtype)
        elif kind == "columns":
            blk = outs[0].shape[0]
            for i, (dst, at) in enumerate(((outs[0], 0), (outs[2], 0), (outs[1], 0), (outs[2], blk))):
                rows = slice(i * blk, (i + 1) * blk)
                dst[at : at + blk, :] = (ins[0][rows, :] + ins[1][rows, :].astype(F32)).astype(dst.dtype)
        elif kind == "send" or kind == "send_near":
            blk = outs[0].shape[0]
            for i, dst in enumerate(outs):
                rows = slice((i + 1) * blk, (i + 2) * blk)
                dst[...] = sum(x[rows, :].astype(F32) for x in ins).astype(dst.dtype)
        elif kind == "tail" or kind == "tail_near":
            blk = outs[0].shape[0]
            outs[0][...] = sum(x[:blk, :].astype(F32) for x in ins)
        elif kind == "side":
            blk = outs[0].shape[0]
            outs[0][...] = ins[0][...] + ins[2][:blk, :].astype(F32)
            outs[1][...] = (ins[1][...] + ins[2][blk:, :].astype(F32)).astype(BF)
        elif kind == "half" or kind == "near":
            blk = outs[0].shape[0]
            for i, dst in enumerate(outs):
                rows = slice(i * blk, (i + 1) * blk)
                dst[...] = sum(x[rows, :].astype(F32) for x in ins).astype(dst.dtype)
        else:
            outs[0][...] = sum(x[...].astype(F32) for x in ins).astype(outs[0].dtype)


def merge(jobs, after=(), beside=None):
    ins, outs = [], []
    for kind, *arrays in jobs:
        ins += arrays
        rows, width = arrays[0].shape
        if kind == "levels":
            outs += [sds((rows // 2, width), F32), sds((rows // 2, width), BF)]
            continue
        if kind == "columns":
            outs += [sds((rows // 4, width), F32)] * 2 + [sds((rows // 2, width), BF)]
            continue
        if kind == "send":
            outs += [sds((rows // 4, width), BF)] * 3
            continue
        if kind == "send_near":
            outs.append(sds((rows // 2, width), BF))
            continue
        if kind == "tail" or kind == "tail_near":
            outs.append(sds((rows // (4 if kind == "tail" else 2), width), F32))
            continue
        if kind == "side":
            outs += [sds((rows, width), F32), sds((rows, width), BF)]
            continue
        parts = 1 if kind in ("pass", "last") else 2
        outs.append(sds((rows // parts, width), BF if kind == "pass" else F32))
        outs += [sds((rows // parts, width), BF)] * (parts - 1)
    kinds = [job[0] for job in jobs]
    if beside:
        i, j = beside
        outs[i] = sds((outs[i].shape[0], outs[i].shape[1] + outs[j].shape[1]), outs[i].dtype)
        del outs[j]
    return kernel_call(
        lambda *refs: merge_kernel(kinds, beside, *refs), ins, [VM] * len(ins), outs, cost=1, after=after
    )


def join_kernel(core, mine, got, *outs):
    c = core[0]
    mine, got = ready(mine, got)
    at = 0
    for out in outs[: 2 if mine.shape[1] > 4 * DH else 3]:
        for k in range(out.shape[1] // D):
            out[:, pl.ds(pl.multiple_of(k * D + c * DH, 128), DH)] = mine[:, at : at + DH]
            out[:, pl.ds(pl.multiple_of(k * D + (1 - c) * DH, 128), DH)] = got[:, at : at + DH]
            at += DH
    if mine.shape[1] > at:
        gains, biases, wide = outs[2:]
        rows = mine.shape[0]
        wide[...] = jnp.zeros_like(wide)
        wide[0:rows, :] = mine[:, at:] + got[:, at:]
        turned = jnp.transpose(wide[...])
        gains[...] = turned[0:3, 0:rows]
        biases[...] = turned[3:6, 0:rows]


CUTS = ((0, 512), (512, 256))
FAR_CUTS = ((0, 256), (256, 512))


class Moves:
    def __init__(self, mesh):
        self.nz, self.nf = mesh.shape["dp"], mesh.shape["fsdp"]
        self.n = self.nz * self.nf
        self.doubling = self.nz == 4 and self.nf == 8

    def permute(self, x, target):
        pairs = [(d, target(d // self.nf, (d % self.nf) // 2, d % 2)) for d in range(self.n)]
        return lax.ppermute(x, AXES, [(a, (z * self.nf) + 2 * yx + c) for a, (z, yx, c) in pairs])

    def sibling(self, x):
        return self.permute(x, lambda z, yx, c: (z, yx, 1 - c))

    def near_z(self, x):
        return self.permute(x, lambda z, yx, c: (z ^ 1, yx, c))

    def far_z(self, x):
        return self.permute(x, lambda z, yx, c: (z ^ 2, yx, c))

    def side_a(self, x):
        return self.permute(x, lambda z, yx, c: (z, yx ^ (1 + c), c))

    def side_b(self, x):
        return self.permute(x, lambda z, yx, c: (z, yx ^ (2 - c), c))

    def opposite_z(self, x):
        return self.permute(x, lambda z, yx, c: (z ^ 3, yx, c))


def per_device(moves, tokens, memory, lengths, cotangent, self_qkv, self_out, cross_q, cross_kv, cross_out, mlp_in, mlp_out, norm_gains, norm_biases):
    seqs, mem_len = memory.shape[0], memory.shape[1]
    rows = seqs * LEN
    place = lax.axis_index(AXES)
    c = place % 2
    chip = place // 2
    core = jnp.reshape(c, (1,)).astype(jnp.int32)
    wr, hr = self_qkv.shape[0], mlp_out.shape[0]
    ff = mlp_in.shape[1]
    fh = ff // 2
    r2, s2 = 2 * rows, 2 * seqs
    wb = D // 16
    pad = -(-mem_len // 16) * 16
    fast = moves.doubling


    def prepare(lens, pairs, after=(), hold=()):
        return kernel_call(
            prepare_kernel,
            [lens, *pairs],
            [SM] + [STAGE] * 6,
            [sds((r2, D), BF)] * 2 + [sds((s2 * pad, D), BF), sds((r2, D), F32)],
            [STAGE] * 4,
            after=after,
            hold=hold,
        )

    def self_attention(pieces, lens, xhat, keep, back, after=()):
        return kernel_call(
            self_kernel,
            [lens, core, offs, *pieces, xhat, keep, back],
            [SM] * 3 + [VM] * 4 + [STAGE] * 3,
            [
                sds((r2, D), BF),
                sds((r2, 3 * DH), BF),
                sds((s2, LEN, DH), BF),
                sds((r2, 3 * DH), BF),
                sds((8, D), F32),
                sds((D, 3 * DH), BF),
            ],
            [STAGE] * 6,
            [pltpu.VMEM((D, 128), BF)],
            cost=6,
            after=after,
        )

    def cross_attention(pieces, mem, vec, tok, comb, recv, keep, back, after=()):
        kv_rows = s2 * pad
        return kernel_call(
            lambda *refs: keys_and_cross_kernel(mem_len, *refs),
            [offs, *pieces, mem, core, vec, tok, comb, recv, keep, back],
            [SM] + [VM] * 4 + [STAGE, SM] + [STAGE] * 6,
            [
                sds((kv_rows, D), BF),
                sds((D, 2 * DH), BF),
                sds((D, DH), BF),
                sds((r2, D), F32),
                sds((r2, D), BF),
                sds((r2, DH), BF),
                sds((s2, pad, DH), BF),
                sds((r2, 3 * DH), BF),
            ],
            [STAGE] * 8,
            cost=12,
            after=after,
        )

    def inner_part(resid_one, comb, recv, vec, w_in, hold=()):
        return kernel_call(
            inner_kernel,
            [resid_one, comb, recv, vec, w_in],
            [STAGE] * 5,
            [sds((r2, D), F32), sds((r2, D), BF), sds((r2, fh), BF), sds((r2, fh), BF)],
            [STAGE] * 4,
            cost=5,
            hold=hold,
        )

    def inner_weight(pieces, hold=()):
        return place_rows(pieces, offs, 0, [(0, fh, 0, wb, 0)], (D, fh), hold)

    def grads(body, ins, specs, ncols, extra=(), scratch=(), cost=5, after=(), hold=()):
        return kernel_call(
            body,
            [offs, *ins],
            [SM, *specs],
            [sds((4 * wb, ncols), BF)] * 4 + list(extra),
            scratch=[pltpu.VMEM((D, ncols), BF), *scratch],
            cost=cost,
            after=after,
            hold=hold,
        )

    def mlp_part(pieces, g, slope, w_in, hidden, third, after=(), hold=()):
        return kernel_call(
            mlp_and_grad_kernel,
            [offs, *pieces, g, slope, w_in, hidden, third],
            [SM] + [VM] * 12,
            [sds((rows, D), BF), sds((3 * rows, D), BF)] + [sds((4 * wb, fh), BF)] * 4,
            scratch=[pltpu.VMEM((r2, fh), BF), pltpu.VMEM((fh, D), BF), pltpu.VMEM((D, fh), BF)],
            cost=11,
            after=after,
            hold=hold,
        )

    def cross_back(resid_two, comb, recv, part, after=()):
        return kernel_call(
            cross_back_and_grads_kernel,
            [
                offs, core, vec, resid_two, comb, recv, part, g, *cout, kv, cq, cprobs, w_cq,
                *cross_mixed, second, mem,
            ],
            [SM] * 2 + [VM] * 16,
            [
                sds((rows, D), BF),
                sds((r2, D), F32),
                sds((r2, D), BF),
                sds((8, D), F32),
                sds(kv.shape, BF),
            ]
            + [sds((4 * wb, 4 * DH), BF)] * 4,
            scratch=[
                pltpu.VMEM((r2, D), BF),
                pltpu.VMEM((r2, DH), BF),
                pltpu.VMEM((r2, DH), BF),
                pltpu.VMEM((D, 4 * DH), BF),
            ],
            cost=14,
            after=after,
            limit=24 << 20,
        )

    def self_back(gsecond, recv, gresid_two, after=()):
        return kernel_call(
            self_back_and_grads_kernel,
            [
                offs, core, vec, resid_one, gsecond, recv, gresid_two, *out, packed, probs, w_qkv, xhat,
                *self_mixed, first, dvec_two,
            ],
            [SM] * 2 + [STAGE] * 15,
            [sds((rows, D), F32), sds((rows, D), BF), sds((rows, D), BF)]
            + [sds((4 * wb, 4 * DH + 128), BF)] * 4,
            scratch=[
                pltpu.VMEM((r2, D), BF),
                pltpu.VMEM((r2, 3 * DH), BF),
                pltpu.VMEM((8, D), F32),
                pltpu.VMEM((r2, DH), BF),
                pltpu.VMEM((D, 4 * DH + 128), BF),
                pltpu.VMEM((128, D), F32),
            ],
            cost=11,
            after=after,
        )

    def tokens_back(recv, gmem_recv, after=()):
        return kernel_call(
            tokens_back_kernel,
            [vec, tokens.reshape(rows, D), gfirst, recv, gresid_one, gmem, gmem_recv],
            [STAGE] * 7,
            [sds((rows, D), BF), sds(gmem.shape, BF), sds((8, 128), F32)],
            [STAGE] * 3,
            cost=4,
            after=after,
        )

    sib = moves.sibling
    pairs = []
    for x in (tokens.reshape(rows, D), cotangent.reshape(rows, D), memory):
        pairs += [x, sib(x)]
    lens = jnp.concatenate([lengths, sib(lengths)], 0)


    bits = jnp.arange(4, dtype=jnp.int32)
    if fast:
        plane = jnp.stack([jnp.int32(0), 1 + c, 2 - c, jnp.int32(3)]).astype(jnp.int32)
        z, yx = chip // 4, chip % 4
        chips = ((z ^ bits)[None, :] * 4 + (yx ^ plane)[:, None]).reshape(16).astype(jnp.int32)
    else:
        chips = jnp.arange(16, dtype=jnp.int32)
    turned = ((chips // 8) ^ c) * 8 + chips % 8
    offs = jnp.stack([chips, turned]).astype(jnp.int32)
    widths = (4 * DH + 128, 4 * DH, 4 * DH)

    if fast:
        width = widths[0] + widths[1]
        keep, send = kernel_call(
            pack_kernel,
            [core, self_qkv, self_out, cross_q, cross_kv, cross_out, norm_gains, norm_biases],
            [SM] + ["stage"] * 7,
            [sds((wr, width), BF)] * 2,
            scratch=[pltpu.VMEM((128, 128), F32)],
            cost=1,
            limit=60 << 20,
        )
        last, both, one = kernel_call(
            order_kernel,
            [core, keep, sib(send), mlp_out],
            [SM] + [VM] * 3,
            [sds((2 * wr, D), BF), sds((2 * wr, width), BF), sds((2 * wr, widths[0]), BF)],
            cost=1,
            after=[pairs[1], pairs[3]],
        )
        near, far, side_a, side_b = moves.near_z, moves.far_z, moves.side_a, moves.side_b
        near_both, along = near(both), [far(one), moves.opposite_z(one)]
        tok, g, mem, xhat = prepare(lens, pairs, hold=(one, both))
        last = tie(last, tok)
        a_last, b_last = side_a(last), side_b(last)
        one, two = cats(
            [
                [(one, 0, widths[0]), (near_both, 0, widths[0]), *whole(*along)],
                [(both, widths[0], widths[1]), (near_both, widths[0], widths[1])],
            ],
            after=(tok, a_last, b_last),
        )
        keep, send = kernel_call(
            pack_inner_kernel, [core, mlp_in], [SM, VM], [sds((wr, fh), BF)] * 2, cost=1, after=(one,)
        )
        (three,) = kernel_call(
            order_mlp_kernel, [core, keep, sib(send), mlp_out], [SM] + [VM] * 3, [sds((2 * wr, 6 * DH), BF)], cost=1
        )
        ab_last = tie(a_last, one)
        a1, b1, far_two, near_three, ab_last = side_a(one), side_b(one), far(two), near(three), side_b(ab_last)
        a1 = tie(a1, b1)
        two, last, three = cats(
            [whole(two, far_two), whole(last, a_last, b_last, ab_last), whole(three, near_three)], after=(a1,)
        )
        ab1, a2, b2, far_three, near_last = side_b(a1), side_a(two), side_b(two), far(three), near(last)
        a2 = tie(a2, b2, ab1)
        three, four, last, *parts = cats(
            [
                [(three, 0, 4 * DH), (far_three, 0, 4 * DH)],
                [(three, 4 * DH, D), (far_three, 4 * DH, D)],
                whole(last, near_last),
                *([(last, lo, width), (near_last, lo, width)] for lo, width in CUTS),
            ],
            after=(a2,),
        )
        out = out_rows([one, a1, b1, ab1], offs, 3 * DH)
        out = (out, sib(out))
        three, a2 = tie(three, out[1]), tie(a2, out[1])
        ab2, a3, b3, far_a = side_b(a2), side_a(three), side_b(three), far(tie(parts[0], out[1]))
        first, packed, probs, comb, vec, w_qkv = self_attention([one, a1, b1, ab1], lens, xhat, *out, after=(three,))
        a3 = tie(a3, b3, ab2, comb, far_a)
        four = tie(four, a3)
        comb = tie(comb, four)
        cout = out_rows([two, a2, b2, ab2], offs, 0)
        cout = (cout, sib(cout))
        self_mixed = (comb, sib(comb))
        ab3, a4, b4, far_b = side_b(a3), side_a(four), side_b(four), far(tie(parts[1], four))
        kv, w_ckv, w_cq, resid_one, second, cq, cprobs, comb = cross_attention(
            [two, a2, b2, ab2], mem, vec, tok, *self_mixed, *cout
        )
        comb = tie(comb, ab3, a4, b4, far_b)
        cross_mixed, ab4 = (comb, sib(comb)), side_b(tie(a4, comb))
        hold = [kv, cprobs, cq, w_cq, *cout, w_ckv, second]
        w_in = inner_weight([three, a3, b3, ab3], hold)
        resid_two, third, hidden, slope = inner_part(resid_one, *cross_mixed, vec, w_in, hold)
        last = [four, a4, b4, ab4, last, far_a, far_b]
    else:
        tok, g, mem, xhat = prepare(lens, pairs)
        everywhere = lambda w: lax.all_gather(w, AXES, axis=0, tiled=True)
        split = lambda w: [w[i * w.shape[0] // 4 : (i + 1) * w.shape[0] // 4] for i in range(4)]

        def col_half(w, groups):
            w = w.reshape(w.shape[0], groups, 2, w.shape[1] // (2 * groups))
            return lax.dynamic_index_in_dim(w, c, 2, keepdims=False).reshape(w.shape[0], -1)

        vectors = jnp.pad(jnp.concatenate([norm_gains, norm_biases], 0).T, ((0, 0), (0, 122)))
        one = jnp.concatenate([col_half(self_qkv, 3), col_half(self_out, 1), vectors], 1)
        two = jnp.concatenate([col_half(w, w.shape[1] // D) for w in (cross_out, cross_q, cross_kv)], 1)
        one, two = split(everywhere(one)), split(everywhere(two))
        three = split(everywhere(col_half(mlp_in, ff // (2 * hr))))
        out, cout = out_rows(one, offs, 3 * DH), out_rows(two, offs, 0)
        out, cout = (out, sib(out)), (cout, sib(cout))
        rowed = everywhere(mlp_out).reshape(moves.n // 2, 2, hr, D)
        rowed = lax.dynamic_index_in_dim(rowed, c, 1, keepdims=False).reshape(16, 2, fh // 32, D)
        rowed = rowed.transpose(1, 0, 2, 3)
        levels = rowed[1].reshape(4, 4, wb, D).transpose(1, 0, 2, 3).reshape(D, D)
        last = split(rowed[0].reshape(D, D)) + [levels[: D // 2]]
        last += [levels[D // 2 :, lo : lo + width] for lo, width in CUTS]
        hold = ()
        first, packed, probs, comb, vec, w_qkv = self_attention(one, lens, xhat, *out)
        self_mixed = (comb, sib(comb))
        kv, w_ckv, w_cq, resid_one, second, cq, cprobs, comb = cross_attention(
            two, mem, vec, tok, *self_mixed, *cout
        )
        cross_mixed = (comb, sib(comb))
        w_in = inner_weight(three)
        resid_two, third, hidden, slope = inner_part(resid_one, *cross_mixed, vec, w_in)


    near, far, side_a, side_b = moves.near_z, moves.far_z, moves.side_a, moves.side_b
    after = ()

    held = [resid_two, vec]
    d_mlpout = kernel_call(
        dmlpout_kernel,
        [offs, hidden, g],
        [SM, VM, VM],
        [sds((4 * wb, D), BF)] * 4 + [sds((8 * wb, D), BF)] + [sds((8 * wb, width), BF) for _, width in FAR_CUTS],
        scratch=[pltpu.VMEM((D, D), BF)] * 2,
        cost=3,
        hold=[*hold, *held, third],
    )
    if fast:
        got_ab1, got_z1 = side_a(d_mlpout[3]), far(d_mlpout[5])
    part, comb, *d_mlpin = mlp_part(last, g, slope, w_in, hidden, third, after=d_mlpout[:1], hold=[*hold, *held])
    if fast:
        (on,) = merge([("pass", d_mlpout[2], got_ab1)], after=(part, got_z1))
        comb = tie(comb, on)
        got_b1, got_a1, got_z2 = side_b(on), side_a(tie(d_mlpout[1], on)), far(tie(d_mlpout[6], on))
        got_ab2, got_a2 = side_a(tie(d_mlpin[3], on)), side_a(tie(d_mlpin[1], on))
        after = (on,)
    recv = sib(comb)
    output, gresid_two, gsecond, dvec_two, dkv, *d_cross = cross_back(resid_two, comb, recv, part, after=after)
    if fast:
        on, kept1, on_far, kept_z, on_z = merge(
            [
                ("pass", d_mlpin[2], got_ab2),
                ("half", d_mlpout[0], got_a1, got_b1),
                ("levels", d_mlpout[4], got_z1, got_z2),
            ],
            after=(dvec_two, got_a2),
        )
        gsecond = tie(gsecond, on)
        got_b2, got_far1, got_near_z = side_b(on), far(on_far), near(on_z)
        got_ab3, got_a3 = side_a(tie(d_cross[3], on)), side_a(tie(d_cross[1], on))
        after = (on,)
    recv = sib(gsecond)
    gresid_one, gfirst, gfirst_other, *d_self = self_back(gsecond, recv, gresid_two, after=after)
    if fast:
        on, kept2, on_far, kept1, on_near, own_z, pass_z, on_z = merge(
            [
                ("pass", d_cross[2], got_ab3),
                ("half", d_mlpin[0], got_a2, got_b2),
                ("near", kept1, got_far1),
                ("columns", kept_z, got_near_z),
            ],
            after=(gfirst, got_a3),
        )
        got_b3, got_ab4 = side_b(on), side_a(tie(d_self[3], on))
        got_far2, got_near1, got_a_z = far(on_far), near(on_near), side_a(on_z)
        after = (on,)
    gmem, gmem_other = kernel_call(
        memory_kernel, [dkv, w_ckv], [VM, VM], [sds((seqs * pad, D), BF)] * 2, cost=3, after=after
    )
    if fast:
        on, kept3, on_far, kept2, on_near, total1, own_z, on_z = merge(
            [
                ("pass", d_self[2], got_ab4),
                ("half", d_cross[0], got_a3, got_b3),
                ("near", kept2, got_far2),
                ("last", kept1, got_near1),
                ("side", own_z, pass_z, got_a_z),
            ],
            after=(gmem,),
        )
        gfirst_other, gmem_other = tie(gfirst_other, on), tie(gmem_other, on)
        got_b4, got_a4 = side_b(on), side_a(tie(d_self[1], on))
        got_far3, got_near2, got_b_z = far(on_far), near(on_near), side_b(on_z)
    recv, gmem_recv = sib(gfirst_other), sib(gmem_other)
    grad_tokens, grad_memory, token = tokens_back(recv, gmem_recv)
    grad_memory = grad_memory.reshape(seqs, pad, D)[:, :mem_len]

    if fast:
        *blocks, total_z, total2 = merge(
            [
                ("send", d_self[0], got_a4, got_b4),
                ("send_near", kept3, got_far3),
                ("last", own_z, got_b_z),
                ("last", kept2, got_near2),
            ],
            after=(token,),
            beside=(0, 3),
        )
        got_far4, got_opp4, got_near = far(blocks[1]), moves.opposite_z(blocks[2]), near(blocks[0])
        width = 4 * DH + 128
        (total3,) = merge([("tail_near", kept3, got_far3, got_near[:, width:])])
        (total4,) = merge([("tail", d_self[0], got_a4, got_b4, got_near[:, :width], got_far4, got_opp4)])
        total = [total1, total2, total3, total4]

        def own_rows(total):
            mine = lax.dynamic_slice_in_dim(total, c * wr, wr, 0)
            return mine, sib(lax.dynamic_slice_in_dim(total, (1 - c) * wr, wr, 0))

        def join(pair, *shapes, scratch=()):
            return kernel_call(
                join_kernel,
                [core, *pair],
                [SM, STAGE, STAGE],
                [sds(shape, F32) for shape in shapes],
                [STAGE] * len(shapes),
                scratch=scratch,
                cost=1,
            )

        sum_mlpout = jnp.concatenate([total[0], total_z], 0)
        mine, got = own_rows(total[1])
        pair = (jnp.where(c == 0, mine, got), jnp.where(c == 0, got, mine))
        parts = [p.reshape(wr, ff // (2 * hr), 1, hr) for p in pair]
        grad_in = jnp.concatenate(parts, 2).reshape(wr, ff)
        grad_cout, grad_cq, grad_ckv = join(own_rows(total[2]), (wr, D), (wr, D), (wr, 2 * D))
        grad_out, grad_qkv, own_gains, own_biases = join(
            own_rows(total[3]), (wr, D), (wr, 3 * D), (3, wr), (3, wr), scratch=[pltpu.VMEM((128, 128), F32)]
        )
    else:

        def placed(parts):
            term = jnp.concatenate(parts, 0).astype(F32)
            both = jnp.stack([jnp.where(c == 0, term, 0.0), jnp.where(c == 1, term, 0.0)], 1)
            return lax.psum_scatter(both, AXES, scatter_dimension=0, tiled=True)

        def joined(total, lo, hi, groups):
            return total[:, :, lo:hi].reshape(wr, 2, groups, -1).transpose(0, 2, 1, 3).reshape(wr, -1)

        total = placed(d_cross)
        grad_cout, grad_cq, grad_ckv = (
            joined(total, 0, DH, 1),
            joined(total, DH, 2 * DH, 1),
            joined(total, 2 * DH, 4 * DH, 2),
        )
        total = placed(d_self)
        grad_out, grad_qkv = joined(total, 0, DH, 1), joined(total, DH, 4 * DH, 3)
        vectors = jnp.sum(total[:, :, 4 * DH : 4 * DH + 6], 1).T
        own_gains, own_biases = vectors[:3], vectors[3:]
        grad_in = joined(placed(d_mlpin), 0, fh, ff // (2 * hr))
        first_rows = jnp.concatenate(d_mlpout[:4], 0).reshape(16, 1, wb, D)
        levels = jnp.concatenate([d_mlpout[4], jnp.concatenate(d_mlpout[5:], 1)], 0).reshape(4, 4, wb, D)
        term = jnp.concatenate([first_rows, levels.transpose(1, 0, 2, 3).reshape(16, 1, wb, D)], 1).astype(F32)
        term = term.reshape(moves.n // 2, 1, hr, D)
        both = jnp.concatenate([jnp.where(c == 0, term, 0.0), jnp.where(c == 1, term, 0.0)], 1)
        sum_mlpout = lax.psum_scatter(both.reshape(ff, D), AXES, scatter_dimension=0, tiled=True)

    return (
        output.reshape(tokens.shape),
        grad_tokens.reshape(tokens.shape),
        grad_memory,
        grad_qkv,
        grad_out,
        grad_cq,
        grad_ckv,
        grad_cout,
        grad_in,
        sum_mlpout,
        own_gains,
        own_biases,
    )


def solution(mesh):
    batch = P(AXES, None, None)
    rows = P(AXES, None)
    cols = P(None, AXES)
    moves = Moves(mesh)
    in_specs = (batch, batch, P(AXES), batch) + (rows,) * 7 + (cols,) * 2
    out_specs = (batch,) * 3 + (rows,) * 7 + (cols,) * 2
    return jax.shard_map(
        lambda *args: per_device(moves, *args),
        mesh=mesh,
        in_specs=in_specs,
        out_specs=out_specs,
        check_vma=False,
    )
```

```python
import jax
import jax.numpy as jnp
import numpy as np
from jax import lax
from jax.experimental import pallas as pl
from jax.experimental.pallas import tpu as pltpu
from jax.sharding import PartitionSpec as P

AXES = ("dp", "fsdp")
HEADS = 12
HALF = HEADS // 2
HEAD = 64
D = 768
DH = D // 2
LEN = 64
EPS = 1e-06
NEG = -1e30
SCALE = HEAD ** (-0.5)
F32 = jnp.float32
BF = jnp.bfloat16
VMEM_LIMIT = 14 << 20

VM = pl.BlockSpec(memory_space=pltpu.VMEM)
SM = pl.BlockSpec(memory_space=pltpu.SMEM)
ANY = pl.BlockSpec(memory_space=pl.ANY)


def sds(shape, dtype):
    return jax.ShapeDtypeStruct(shape, dtype)


STAGE = VM


class Staged:
    def __init__(self, ref, copy):
        self.ref, self.copy, self.waited = ref, copy, False
        self.shape = ref.shape

    def ready(self):
        if not self.waited:
            self.copy.wait()
            self.waited = True
        return self.ref


PENDING = {}


def flush(*refs):
    for r in refs:
        if id(r) in PENDING:
            PENDING[id(r)].start()
            PENDING[id(r)] = None


def ready(*refs):
    out = [r.ready() if isinstance(r, Staged) else r for r in refs]
    return out[0] if len(out) == 1 else out


def kernel_call(body, ins, in_specs, outs, out_specs=None, scratch=(), cost=5, after=(), limit=None, hold=()):
    n, skip, m, k = len(ins), len(after) + len(hold), len(outs), len(scratch)
    out_specs = [VM] * m if out_specs is None else list(out_specs)
    staged_in = [i for i, spec in enumerate(in_specs) if spec == 'stage']
    staged_out = [i for i, spec in enumerate(out_specs) if spec == 'stage']
    buffers = [pltpu.VMEM(ins[i].shape, ins[i].dtype) for i in staged_in]
    buffers += [pltpu.VMEM(outs[i].shape, outs[i].dtype) for i in staged_out]
    extra = [*buffers, pltpu.SemaphoreType.DMA((len(buffers),))] if buffers else []

    def run(*refs):
        ins, outs = list(refs[:n]), list(refs[n + skip : n + skip + m])
        own = refs[n + skip + m : n + skip + m + k]
        PENDING.clear()
        if not buffers:
            body(*ins, *outs, *own)
            return
        held, sems = refs[n + skip + m + k : -1], refs[-1]
        for j, i in enumerate(staged_in):
            copy = pltpu.make_async_copy(ins[i], held[j], sems.at[j])
            copy.start()
            ins[i] = Staged(held[j], copy)
        copies = []
        for j, i in enumerate(staged_out, len(staged_in)):
            copies.append(pltpu.make_async_copy(held[j], outs[i], sems.at[j]))
            outs[i] = held[j]
            PENDING[id(held[j])] = copies[-1]
        body(*ins, *outs, *own)
        ready(*ins)
        for cp in PENDING.values():
            if cp is not None:
                cp.start()
        for cp in copies:
            cp.wait()

    space = lambda spec: ANY if spec == 'stage' else spec
    return pl.pallas_call(
        run,
        out_shape=list(outs),
        in_specs=[space(spec) for spec in in_specs] + [ANY] * len(after) + [VM] * len(hold),
        out_specs=[space(spec) for spec in out_specs],
        scratch_shapes=[*scratch, *extra],
        compiler_params=pltpu.CompilerParams(vmem_limit_bytes=limit or VMEM_LIMIT),
        cost_estimate=pl.CostEstimate(flops=cost * 7 * 10**9, bytes_accessed=0, transcendentals=0),
    )(*ins, *after, *hold)


def tie(x, *earlier):
    return pl.pallas_call(
        lambda *refs: None,
        out_shape=sds(x.shape, x.dtype),
        in_specs=[ANY] * (1 + len(earlier)),
        out_specs=ANY,
        input_output_aliases={0: 0},
        compiler_params=pltpu.CompilerParams(vmem_limit_bytes=1 << 20),
        cost_estimate=pl.CostEstimate(flops=0, bytes_accessed=0, transcendentals=0),
    )(x, *earlier)


def nn(a, b):
    return lax.dot_general(a, b, (((1,), (0,)), ((), ())), preferred_element_type=F32)


def nt(a, b):
    return lax.dot_general(a, b, (((1,), (1,)), ((), ())), preferred_element_type=F32)


def tn(a, b):
    return lax.dot_general(a, b, (((0,), (0,)), ((), ())), preferred_element_type=F32)


def normalise(v):
    mean = jnp.mean(v, -1, keepdims=True)
    cen = v - mean
    inv = lax.rsqrt(jnp.mean(cen * cen, -1, keepdims=True) + EPS)
    return cen * inv, inv


def norm_back(v, gain, dy):
    xhat, inv = normalise(v)
    dxh = dy * gain
    m1 = jnp.mean(dxh, -1, keepdims=True)
    m2 = jnp.mean(dxh * xhat, -1, keepdims=True)
    dx = inv * (dxh - m1 - xhat * m2)
    return dx, jnp.sum(dy * xhat, 0, keepdims=True), jnp.sum(dy, 0, keepdims=True)


GROUPS = ((0, 256), (256, DH))


def head_of_lane(rows, width):
    return lax.shift_right_logical(lax.broadcasted_iota(jnp.int32, (rows, width), 1), 6)


def spread(q):
    head = head_of_lane(1, q.shape[1])
    parts = [q * (head == h).astype(F32).astype(q.dtype) for h in range(q.shape[1] // HEAD)]
    return jnp.concatenate(parts, 0)


def fold(o):
    head = head_of_lane(LEN, o.shape[1])
    total = jnp.where(head == 0, o[:LEN], 0.0)
    for h in range(1, o.shape[1] // HEAD):
        total = jnp.where(head == h, o[h * LEN : (h + 1) * LEN], total)
    return total


def attend(q, k, v, allowed):
    probs, mixed = [], []
    for lo, hi in GROUPS:
        st = nt(k[:, lo:hi], spread(q[:, lo:hi])) * SCALE
        st = jnp.where(allowed[:, lo:hi], st, NEG)
        e = jnp.exp(st - jnp.max(st, 0, keepdims=True))
        p = (e * (1.0 / jnp.sum(e, 0, keepdims=True))).astype(BF)
        probs.append(p)
        mixed.append(fold(tn(p, v[:, lo:hi])).astype(BF))
    return jnp.concatenate(probs, 1), jnp.concatenate(mixed, 1)


def attend_back(g, q, k, v, p):
    dq, dk, dv = [], [], []
    for lo, hi in GROUPS:
        gs, qs, low = spread(g[:, lo:hi]), spread(q[:, lo:hi]), p[:, lo:hi]
        dp = nt(v[:, lo:hi], gs)
        pf = low.astype(F32)
        t = pf * dp
        ds = (t - pf * jnp.sum(t, 0, keepdims=True)).astype(BF)
        dq.append((fold(tn(ds, k[:, lo:hi])) * SCALE).astype(BF))
        dk.append((nn(ds, qs) * SCALE).astype(BF))
        dv.append(nn(low, gs).astype(BF))
    return [jnp.concatenate(x, 1) for x in (dq, dk, dv)]


def seq_rows(s):
    return pl.ds(pl.multiple_of(s * LEN, LEN), LEN)


def half_lanes(c):
    return pl.ds(pl.multiple_of(c * DH, DH), DH)


def loop(n, body, unroll=1):
    def step(i, carry):
        body(i)
        return carry

    lax.fori_loop(0, n, step, 0, unroll=unroll)


def columns_first(pieces, q, r):
    blk = pieces[0].shape[0] // 4
    return pieces[q], r * blk


def place(pieces, offs_ref, which, cols, targets):
    blk = pieces[0].shape[0] // 4
    for lo, hi, o, step, shift in cols:
        for q in range(4):
            for r in range(4):
                row = pl.multiple_of(offs_ref[which, q * 4 + r] * step + shift, 16)
                targets[o][pl.ds(row, blk), :] = pieces[q][r * blk : (r + 1) * blk, lo:hi]


def place_levels(near, far, offs_ref, step, shift, target):
    blk = near.shape[0] // 8
    lo = 0
    for level, src in ((0, near), *((2, part) for part in far)):
        at = 0 if level == 0 else lo
        for q in range(4):
            for r in range(2):
                row = pl.multiple_of(offs_ref[0, q * 4 + level + r] * step + shift, 16)
                rows = slice((r * 4 + q) * blk, (r * 4 + q + 1) * blk)
                target[pl.ds(row, blk), at : at + src.shape[1]] = src[rows, :]
        lo += src.shape[1] if level else 0


def place_rows(pieces, offs, which, cols, shape, hold=()):
    def body(offs_ref, *refs):
        place(refs[:4], offs_ref, which, cols, refs[4:5])

    return kernel_call(body, [offs, *pieces], [SM] + [VM] * 4, [sds(shape, BF)], cost=1, hold=hold)[0]


def out_rows(pieces, offs, lo):
    blk = pieces[0].shape[0] // 4
    return place_rows(pieces, offs, 1, [(lo, lo + DH, 0, blk, 0)], (16 * blk, DH))


def send_out(dw, offs_ref, outs):
    blk = dw.shape[0] // 16
    for q in range(4):
        for r in range(4):
            row = pl.multiple_of(offs_ref[0, q * 4 + r] * blk, 16)
            outs[q][r * blk : (r + 1) * blk, :] = dw[pl.ds(row, blk), :]


def pack_kernel(core, qkv, out, cq, ckv, cout, gains, biases, keep, send, vecs):
    c = core[0]
    qkv, out, cq, ckv, cout, gains, biases = ready(qkv, out, cq, ckv, cout, gains, biases)
    vecs[...] = jnp.zeros_like(vecs)
    vecs[0:3, 0:24] = gains[...].astype(F32)
    vecs[3:6, 0:24] = biases[...].astype(F32)
    rows = keep.shape[0]
    wide = jnp.transpose(vecs[...])[:rows].astype(BF)
    for dst, which in ((keep, c), (send, 1 - c)):
        at = 0
        for w, groups in ((qkv, 3), (out, 1), (None, 0), (cout, 1), (cq, 1), (ckv, 2)):
            if w is None:
                dst[:, at : at + 128] = wide
                at += 128
            for k in range(groups):
                lanes = pl.ds(pl.multiple_of(k * D + which * DH, 128), DH)
                dst[:, at : at + DH] = w[:, lanes]
                at += DH


def pack_inner_kernel(core, win, keep, send):
    c = core[0]
    win = ready(win)
    hr = 96
    for k in range(win.shape[1] // (2 * hr)):
        first = win[:, 2 * k * hr : (2 * k + 1) * hr]
        second = win[:, (2 * k + 1) * hr : (2 * k + 2) * hr]
        keep[:, k * hr : (k + 1) * hr] = jnp.where(c == 0, first, second)
        send[:, k * hr : (k + 1) * hr] = jnp.where(c == 0, second, first)


def order_kernel(core, keep, got, wout, last, *outs):
    c = core[0]
    rows = keep.shape[0]
    for b, (top, under) in enumerate(((keep, got), (got, keep))):
        for dst in outs:
            width = dst.shape[1]
            dst[b * rows : (b + 1) * rows, :] = jnp.where(c == 0, top[:, :width], under[:, :width])
    last[...] = wout[2 * rows :, :]


def order_mlp_kernel(core, keep, got, wout, three):
    c = core[0]
    rows, width = keep.shape
    for b, (top, under) in enumerate(((keep, got), (got, keep))):
        three[b * rows : (b + 1) * rows, :width] = jnp.where(c == 0, top[...], under[...])
    three[:, width:] = wout[0 : 2 * rows, :]


def cats(jobs, after=()):
    arrays, places, outs = [], [], []
    for job in jobs:
        at, outs = 0, [*outs, sds((sum(x.shape[0] for x, _, _ in job), job[0][2]), BF)]
        for x, lo, width in job:
            arrays.append(x)
            places.append((len(outs) - 1, at, lo, width))
            at += x.shape[0]
    n = len(arrays)

    def body(*refs):
        for src, (o, at, lo, width) in zip(refs[:n], places):
            refs[n + o][at : at + src.shape[0], :] = src[:, lo : lo + width]

    return kernel_call(body, arrays, [VM] * n, outs, cost=1, after=after)


def whole(*arrays):
    return [(x, 0, x.shape[1]) for x in arrays]


def prepare_kernel(lens, tok_own, tok_other, cot_own, cot_other, mem_own, mem_other, tok, g, mem, xhat):
    tok_own, tok_other = ready(tok_own, tok_other)
    rows = tok.shape[0] // 2
    seqs, length = mem_own.shape[0], mem_own.shape[1]
    pad = mem.shape[0] // (2 * seqs)
    for b, src in ((0, tok_own), (1, tok_other)):
        tok[b * rows : (b + 1) * rows, :] = src[...]
    flush(tok)

    def norm(s):
        xhat[seq_rows(s), :] = normalise(tok[seq_rows(s), :].astype(F32))[0]

    loop(2 * seqs, norm, 2)
    flush(xhat)
    mem_own, mem_other = ready(mem_own, mem_other)
    for b, src in ((0, mem_own), (1, mem_other)):
        for s in range(seqs):
            at = (b * seqs + s) * pad
            mem[at + length - length % 16 : at + pad, :] = jnp.zeros((pad - length + length % 16, D), BF)
            mem[at : at + length, :] = src[s]
    flush(mem)
    cot_own, cot_other = ready(cot_own, cot_other)
    place = lax.broadcasted_iota(jnp.int32, (LEN, D), 0)
    for b, src in ((0, cot_own), (1, cot_other)):
        for s in range(seqs):
            at = (b * seqs + s) * LEN
            live = (place < lens[b * seqs + s]).astype(F32)
            g[at : at + LEN, :] = (src[s * LEN : (s + 1) * LEN, :].astype(F32) * live).astype(BF)


def self_kernel(lens, core, offs, own, a, b, ab, xhat, keep, back, first, packed, probs, comb, vec, wqkv, gcol):
    c = core[0]
    blk = D // 16
    place((own, a, b, ab), offs, 0, [(4 * DH, 4 * DH + 128, 1, blk, 0), (0, 3 * DH, 0, blk, 0)], (wqkv, gcol))
    xhat = ready(xhat)
    vec[...] = jnp.transpose(gcol[...].astype(F32))[:8]
    gain, bias = vec[0:1], vec[3:4]

    def norm(s):
        first[seq_rows(s), :] = (xhat[seq_rows(s), :] * gain + bias).astype(BF)

    loop(8, norm, 2)
    flush(first)

    def proj(b):
        rows = pl.ds(pl.multiple_of(b * 256, 256), 256)
        packed[rows, :] = nn(first[rows, :], wqkv[...]).astype(BF)

    loop(2, proj)
    flush(packed)
    key = lax.broadcasted_iota(jnp.int32, (LEN, DH), 0)
    query = lax.broadcasted_iota(jnp.int32, (LEN, DH), 1) & (LEN - 1)

    def att(s):
        allowed = (key <= query) & (key < lens[s])
        rows = seq_rows(s)
        p, m = attend(packed[rows, 0:DH], packed[rows, DH : 2 * DH], packed[rows, 2 * DH :], allowed)
        probs[s] = p
        comb[rows, D:] = m

    loop(8, att, 2)
    flush(probs)
    keep, back = ready(keep, back)
    comb[:, half_lanes(c)] = nn(comb[:, D:], keep[:DH, :]).astype(BF)
    comb[:, half_lanes(1 - c)] = nn(comb[:, D:], back[DH:, :]).astype(BF)


def kv_kernel(offs, own, a, b, ab, mem, kv, wckv, wcq):
    blk = D // 16
    place((own, a, b, ab), offs, 0, [(2 * DH, 4 * DH, 0, blk, 0), (DH, 2 * DH, 1, blk, 0)], (wckv, wcq))
    mem = ready(mem)

    def step(b):
        rows = pl.ds(pl.multiple_of(b * 480, 480), 480)
        kv[rows, :] = nn(mem[rows, :], wckv[...]).astype(BF)

    loop(mem.shape[0] // 480, step)


def swapped(s):
    return pl.ds(pl.multiple_of(((s + 4) & 7) * LEN, LEN), LEN)


def cross_kernel(mem_len, core, vec, tok, part, recv, wcq, kv, keep, back, resid, second, cq, probs, comb):
    c = core[0]
    vec, tok, part, recv = ready(vec, tok, part, recv)
    gain, bias = vec[1:2], vec[4:5]

    def norm(s):
        rows = seq_rows(s)
        both = part[rows, 0:D].astype(F32) + recv[swapped(s), 0:D].astype(F32)
        v = tok[rows, :].astype(F32) + both
        resid[rows, :] = v
        xhat, _ = normalise(v)
        second[rows, :] = (xhat * gain + bias).astype(BF)

    loop(8, norm, 2)
    flush(resid, second)
    wcq = ready(wcq)
    cq[...] = nn(second[...], wcq[...]).astype(BF)
    flush(cq)
    kv = ready(kv)
    pad = probs.shape[1]
    allowed = lax.broadcasted_iota(jnp.int32, (pad, DH), 0) < mem_len

    def att(s):
        rows = seq_rows(s)
        keys = pl.ds(pl.multiple_of(s * pad, 16), pad)
        p, m = attend(cq[rows, :], kv[keys, 0:DH], kv[keys, DH:], allowed)
        probs[s] = p
        comb[rows, D:] = m

    loop(8, att, 2)
    flush(probs)
    keep, back = ready(keep, back)
    comb[:, half_lanes(c)] = nn(comb[:, D:], keep[:DH, :]).astype(BF)
    comb[:, half_lanes(1 - c)] = nn(comb[:, D:], back[DH:, :]).astype(BF)


def keys_and_cross_kernel(
    mem_len, offs, own, a, b, ab, mem, core, vec, tok, part, recv, keep, back, kv, wckv, wcq, resid, second, cq, probs, comb
):
    kv_kernel(offs, own, a, b, ab, mem, kv, wckv, wcq)
    cross_kernel(mem_len, core, vec, tok, part, recv, wcq, kv, keep, back, resid, second, cq, probs, comb)


def inner_kernel(resid, part, recv, vec, win, resid_two, third, hidden, slope):
    resid, part, recv, vec = ready(resid, part, recv, vec)
    gain, bias = vec[2:3], vec[5:6]

    def norm(s):
        rows = seq_rows(s)
        both = part[rows, 0:D].astype(F32) + recv[swapped(s), 0:D].astype(F32)
        v = resid[rows, :] + both
        resid_two[rows, :] = v
        xhat, _ = normalise(v)
        third[rows, :] = (xhat * gain + bias).astype(BF)

    loop(8, norm, 2)
    flush(resid_two, third)
    win = ready(win)

    def step(b):
        rows = pl.ds(pl.multiple_of(b * 128, 128), 128)
        x = nn(third[rows, :], win[...])
        cdf = 0.5 + 0.5 * lax.erf(x * (0.5**0.5))
        hidden[rows, :] = (x * cdf).astype(BF)
        density = jnp.exp(x * x * -0.5) * ((2.0 * np.pi) ** -0.5)
        slope[rows, :] = (cdf + x * density).astype(BF)

    loop(4, step)


def mlp_kernel(offs, pieces, near, far, g, slope, win, hidden, own, comb, ginner, wout):
    half = own.shape[0]
    blk = D // 16
    place(pieces, offs, 0, [(0, D, 0, 2 * blk, 0)], (wout,))
    place_levels(near, far, offs, 2 * blk, blk, wout)
    g, slope, win = ready(g, slope, win)

    def back(b):
        rows = pl.ds(pl.multiple_of(b * 256, 256), 256)
        gh = nt(g[rows, :], wout[...])
        ginner[rows, :] = (gh * slope[rows, :].astype(F32)).astype(BF)
        comb[rows, :] = nt(ginner[rows, :], win[...]).astype(BF)

    loop(2, back)
    flush(ginner)
    hidden = ready(hidden)
    own[...] = nn(hidden[0:half, :], wout[...]).astype(BF)
    comb[2 * half :, :] = nn(hidden[half:, :], wout[...]).astype(BF)


def dmlpout_kernel(offs, hidden, g, own, a, b, ab, near, *refs):
    far, dw, dz = refs[:-2], refs[-2], refs[-1]
    blk = dw.shape[0] // 16
    for i in range(4):
        part = tn(hidden[:, i * 8 * blk : (i + 1) * 8 * blk], g[...]).astype(BF)
        for k in range(8):
            row, rows = (4 * i + k // 2) * blk, slice(k * blk, (k + 1) * blk)
            if k % 2:
                dz[row : row + blk, :] = part[rows, :LEVELS]
                dw[row : row + blk, D:] = part[rows, LEVELS:]
            else:
                dw[row : row + blk, :D] = part[rows]
    send_out(dw, offs, (own, a, b, ab))
    for q in range(4):
        for r in range(4):
            rows = pl.ds(pl.multiple_of(offs[0, q * 4 + r] * blk, 16), blk)
            at = ((r % 2) * 4 + q) * blk
            if r < 2:
                near[at : at + blk, :] = dz[rows, :]
                continue
            for dst, (lo, width) in zip(far, FAR_CUTS):
                dst[at : at + blk, :] = dz[rows, lo : lo + width]


def mlp_and_grad_kernel(
    offs, pown, pa, pb, pab, near, far_a, far_b, g, slope, win, hidden, third, own, comb, d_own, d_a, d_b, d_ab, ginner, wout, dw
):
    mlp_kernel(offs, (pown, pa, pb, pab), near, (far_a, far_b), g, slope, win, hidden, own, comb, ginner, wout)
    dmlpin_kernel(offs, third, ginner, d_own, d_a, d_b, d_ab, dw)


def dmlpin_kernel(offs, third, ginner, *refs):
    third, ginner = ready(third, ginner)
    outs, dw = refs[:4], refs[4]
    for b in range(0, dw.shape[0], 256):
        dw[b : b + 256, :] = tn(third[:, b : b + 256], ginner[...]).astype(BF)
    send_out(dw, offs, outs)


def cross_back_kernel(
    core, vec, resid, part, recv, own, g, keep, back, kv, cq, probs, wcq, output, gresid, gtwo, dcq, dkv, gsecond, dvec, gm
):
    c = core[0]
    vec, resid, part, recv, own, g = ready(vec, resid, part, recv, own, g)
    gain = vec[2:3]
    dvec[...] = jnp.zeros_like(dvec)

    def norm(s):
        rows = seq_rows(s)
        dy = part[rows, :].astype(F32) + recv[swapped(s), :].astype(F32)
        dx, dg, db = norm_back(resid[rows, :], gain, dy)
        total = g[rows, :].astype(F32) + dx
        gresid[rows, :] = total
        gtwo[rows, :] = total.astype(BF)

        @pl.when(s < 4)
        def _():
            dvec[0:1, :] += dg
            dvec[1:2, :] += db
            extra = own[rows, :].astype(F32) + recv[pl.ds(pl.multiple_of(512 + s * LEN, LEN), LEN), :].astype(F32)
            output[rows, :] = (resid[rows, :] + extra).astype(BF)

    loop(8, norm, 2)
    flush(output, gresid, gtwo, dvec)
    keep, back = ready(keep, back)
    gm[...] = (nt(gtwo[:, half_lanes(c)], keep[:DH, :]) + nt(gtwo[:, half_lanes(1 - c)], back[DH:, :])).astype(BF)
    pad = probs.shape[1]
    kv, cq, probs = ready(kv, cq, probs)

    def att(s):
        rows = seq_rows(s)
        keys = pl.ds(pl.multiple_of(s * pad, 16), pad)
        dq, dk, dv = attend_back(gm[rows, :], cq[rows, :], kv[keys, 0:DH], kv[keys, DH:], probs[s])
        dcq[rows, :] = dq
        dkv[keys, 0:DH] = dk
        dkv[keys, DH:] = dv

    loop(8, att, 2)
    flush(dcq, dkv)
    wcq = ready(wcq)
    gsecond[...] = nt(dcq[...], wcq[...]).astype(BF)


def out_grad(dw, lo, c, mine, other, g):
    cols = half_lanes(c)
    dw[half_lanes(c), lo : lo + DH] = tn(mine[:, D:], g[:, cols]).astype(BF)
    rest = tn(other[256:, D:], g[:256, cols]) + tn(other[:256, D:], g[256:, cols])
    dw[half_lanes(1 - c), lo : lo + DH] = rest.astype(BF)


def dcross_kernel(offs, core, mixed, mixed_other, gtwo, second, dcq, dkv, mem, *refs):
    outs, dw = refs[:4], refs[4]
    mixed, mixed_other, gtwo = ready(mixed, mixed_other, gtwo)
    out_grad(dw, 0, core[0], mixed, mixed_other, gtwo)
    second, dcq = ready(second, dcq)
    dw[:, DH : 2 * DH] = tn(second[...], dcq[...]).astype(BF)
    mem = ready(mem)
    for b in range(0, D, 256):
        dw[b : b + 256, 2 * DH :] = tn(mem[:, b : b + 256], dkv[...]).astype(BF)
    send_out(dw, offs, outs)


def memory_kernel(dkv, wckv, own, other):
    half = own.shape[0]
    for i, dst in ((1, other), (0, own)):
        for b in range(0, half, 480):
            dst[b : b + 480, :] = nt(dkv[i * half + b : i * half + b + 480, :], wckv[...]).astype(BF)


def cross_back_and_grads_kernel(
    offs, core, vec, resid, part, recv, own, g, keep, back, kv, cq, probs, wcq, mixed, mixed_other, second, mem,
    output, gresid, gsecond, dvec, dkv, d_own, d_a, d_b, d_ab, gtwo, dcq, gm, dw
):
    cross_back_kernel(
        core, vec, resid, part, recv, own, g, keep, back, kv, cq, probs, wcq, output, gresid, gtwo, dcq, dkv, gsecond, dvec, gm
    )
    dcross_kernel(
        offs, core, mixed, mixed_other, gtwo, second, dcq, dkv, mem, d_own, d_a, d_b, d_ab, dw
    )


def self_back_kernel(
    core, vec, resid, part, recv, gresid_two, keep, back, packed, probs, wqkv, xhat, gresid, gone, dpacked, gfirst_own, gfirst_other, dvec, gm
):
    c = core[0]
    vec, resid, part, recv, gresid_two = ready(vec, resid, part, recv, gresid_two)
    gain = vec[1:2]
    dvec[...] = jnp.zeros_like(dvec)

    def norm(s):
        rows = seq_rows(s)
        dy = part[rows, :].astype(F32) + recv[swapped(s), :].astype(F32)
        dx, dg, db = norm_back(resid[rows, :], gain, dy)
        total = gresid_two[rows, :] + dx
        gone[rows, :] = total.astype(BF)

        @pl.when(s < 4)
        def _():
            gresid[rows, :] = total
            dvec[0:1, :] += dg
            dvec[1:2, :] += db

    loop(8, norm, 2)
    flush(gresid, gone)
    keep, back = ready(keep, back)
    gm[...] = (nt(gone[:, half_lanes(c)], keep[:DH, :]) + nt(gone[:, half_lanes(1 - c)], back[DH:, :])).astype(BF)
    packed, probs = ready(packed, probs)

    def att(s):
        rows = seq_rows(s)
        dq, dk, dv = attend_back(
            gm[rows, :], packed[rows, 0:DH], packed[rows, DH : 2 * DH], packed[rows, 2 * DH :], probs[s]
        )
        dpacked[rows, 0:DH] = dq
        dpacked[rows, DH : 2 * DH] = dk
        dpacked[rows, 2 * DH :] = dv

    loop(8, att, 2)
    flush(dpacked)
    wqkv, xhat = ready(wqkv, xhat)
    half = gfirst_own.shape[0]
    for b, dst in ((half, gfirst_other), (0, gfirst_own)):
        term = nt(dpacked[b : b + half, :], wqkv[...])
        dst[...] = term.astype(BF)
        flush(dst)
        dvec[2:3, :] += jnp.sum(term * xhat[b : b + half, :], 0, keepdims=True)
        dvec[3:4, :] += jnp.sum(term, 0, keepdims=True)


def dself_kernel(offs, core, mixed, mixed_other, gone, first, dpacked, dvec_two, dvec_one, *refs):
    outs, dw, vecs = refs[:4], refs[4], refs[5]
    mixed, mixed_other, gone = ready(mixed, mixed_other, gone)
    out_grad(dw, 0, core[0], mixed, mixed_other, gone)
    first, dpacked, dvec_two, dvec_one = ready(first, dpacked, dvec_two, dvec_one)
    for b in range(0, D, 256):
        dw[b : b + 256, DH : 4 * DH] = tn(first[:, b : b + 256], dpacked[...]).astype(BF)
    vecs[...] = jnp.zeros_like(vecs)
    for i, (v, row) in enumerate(((dvec_one, 2), (dvec_one, 0), (dvec_two, 0), (dvec_one, 3), (dvec_one, 1), (dvec_two, 1))):
        vecs[i : i + 1, :] = v[row : row + 1, :]
    dw[:, 4 * DH :] = jnp.transpose(vecs[...]).astype(BF)
    send_out(dw, offs, outs)


def self_back_and_grads_kernel(
    offs, core, vec, resid, part, recv, gresid_two, keep, back, packed, probs, wqkv, xhat, mixed, mixed_other, first, dvec_two,
    gresid, gfirst_own, gfirst_other, d_own, d_a, d_b, d_ab, gone, dpacked, dvec, gm, dw, vecs
):
    self_back_kernel(
        core, vec, resid, part, recv, gresid_two, keep, back, packed, probs, wqkv, xhat,
        gresid, gone, dpacked, gfirst_own, gfirst_other, dvec, gm
    )
    dself_kernel(offs, core, mixed, mixed_other, gone, first, dpacked, dvec_two, dvec, d_own, d_a, d_b, d_ab, dw, vecs)


def tokens_back_kernel(vec, tok, part, recv, gresid, gmem, gmem_recv, gtok, gmemory, token):
    token[...] = jnp.zeros_like(token)
    vec, tok, part, recv, gresid = ready(vec, tok, part, recv, gresid)
    gain = vec[0:1]

    def norm(s):
        rows = seq_rows(s)
        dy = part[rows, :].astype(F32) + recv[rows, :].astype(F32)
        dx, _, _ = norm_back(tok[rows, :].astype(F32), gain, dy)
        gtok[rows, :] = (gresid[rows, :] + dx).astype(BF)

    loop(4, norm)
    flush(gtok)
    gmem, gmem_recv = ready(gmem, gmem_recv)
    gmemory[...] = (gmem[...].astype(F32) + gmem_recv[...].astype(F32)).astype(BF)


MERGES = {"pass": (2, 1), "half": (3, 2), "near": (2, 2), "last": (2, 1)}
MERGES.update({"tail": (6, 1), "tail_near": (3, 1), "send": (3, 3), "send_near": (2, 1), "levels": (3, 2), "columns": (2, 3), "side": (3, 2)})


def merge_kernel(kinds, beside, *refs):
    if beside:
        n_in, (i, j) = sum(MERGES[kind][0] for kind in kinds), beside
        outs = list(refs[n_in:])
        wide, width = outs[i], outs[i].shape[1] - refs[n_in - 2].shape[1]
        outs[i] = wide.at[:, :width]
        outs.insert(j, wide.at[:, width:])
        refs = (*refs[:n_in], *outs)
    at, out = 0, sum(MERGES[kind][0] for kind in kinds)
    for kind in kinds:
        ins, outs = refs[at : at + MERGES[kind][0]], refs[out : out + MERGES[kind][1]]
        at, out = at + len(ins), out + len(outs)
        if kind == "levels":
            half = outs[0].shape[0]
            for i, dst in enumerate(outs):
                rows = slice(i * half, (i + 1) * half)
                for src, (lo, width) in zip(ins[1:], FAR_CUTS):
                    total = ins[0][rows, lo : lo + width].astype(F32) + src[rows, :].astype(F32)
                    dst[:, lo : lo + width] = total.astype(dst.dtype)
        elif kind == "columns":
            blk = outs[0].shape[0]
            for i, (dst, at) in enumerate(((outs[0], 0), (outs[2], 0), (outs[1], 0), (outs[2], blk))):
                rows = slice(i * blk, (i + 1) * blk)
                dst[at : at + blk, :] = (ins[0][rows, :] + ins[1][rows, :].astype(F32)).astype(dst.dtype)
        elif kind == "send" or kind == "send_near":
            blk = outs[0].shape[0]
            for i, dst in enumerate(outs):
                rows = slice((i + 1) * blk, (i + 2) * blk)
                dst[...] = sum(x[rows, :].astype(F32) for x in ins).astype(dst.dtype)
        elif kind == "tail" or kind == "tail_near":
            blk = outs[0].shape[0]
            outs[0][...] = sum(x[:blk, :].astype(F32) for x in ins)
        elif kind == "side":
            blk = outs[0].shape[0]
            outs[0][...] = ins[0][...] + ins[2][:blk, :].astype(F32)
            outs[1][...] = (ins[1][...] + ins[2][blk:, :].astype(F32)).astype(BF)
        elif kind == "half" or kind == "near":
            blk = outs[0].shape[0]
            for i, dst in enumerate(outs):
                rows = slice(i * blk, (i + 1) * blk)
                dst[...] = sum(x[rows, :].astype(F32) for x in ins).astype(dst.dtype)
        else:
            outs[0][...] = sum(x[...].astype(F32) for x in ins).astype(outs[0].dtype)


def merge(jobs, after=(), beside=None):
    ins, outs = [], []
    for kind, *arrays in jobs:
        ins += arrays
        rows, width = arrays[0].shape
        if kind == "levels":
            outs += [sds((rows // 2, width), F32), sds((rows // 2, width), BF)]
            continue
        if kind == "columns":
            outs += [sds((rows // 4, width), F32)] * 2 + [sds((rows // 2, width), BF)]
            continue
        if kind == "send":
            outs += [sds((rows // 4, width), BF)] * 3
            continue
        if kind == "send_near":
            outs.append(sds((rows // 2, width), BF))
            continue
        if kind == "tail" or kind == "tail_near":
            outs.append(sds((rows // (4 if kind == "tail" else 2), width), F32))
            continue
        if kind == "side":
            outs += [sds((rows, width), F32), sds((rows, width), BF)]
            continue
        parts = 1 if kind in ("pass", "last") else 2
        outs.append(sds((rows // parts, width), BF if kind == "pass" else F32))
        outs += [sds((rows // parts, width), BF)] * (parts - 1)
    kinds = [job[0] for job in jobs]
    if beside:
        i, j = beside
        outs[i] = sds((outs[i].shape[0], outs[i].shape[1] + outs[j].shape[1]), outs[i].dtype)
        del outs[j]
    return kernel_call(
        lambda *refs: merge_kernel(kinds, beside, *refs), ins, [VM] * len(ins), outs, cost=1, after=after
    )


def join_kernel(core, mine, got, *outs):
    c = core[0]
    mine, got = ready(mine, got)
    at = 0
    for out in outs[: 2 if mine.shape[1] > 4 * DH else 3]:
        for k in range(out.shape[1] // D):
            out[:, pl.ds(pl.multiple_of(k * D + c * DH, 128), DH)] = mine[:, at : at + DH]
            out[:, pl.ds(pl.multiple_of(k * D + (1 - c) * DH, 128), DH)] = got[:, at : at + DH]
            at += DH
    if mine.shape[1] > at:
        gains, biases, wide = outs[2:]
        rows = mine.shape[0]
        wide[...] = jnp.zeros_like(wide)
        wide[0:rows, :] = mine[:, at:] + got[:, at:]
        turned = jnp.transpose(wide[...])
        gains[...] = turned[0:3, 0:rows]
        biases[...] = turned[3:6, 0:rows]


def join_inner_kernel(core, mine, got, out):
    c = core[0]
    hr = 96
    for k in range(mine.shape[1] // hr):
        a, b = mine[:, k * hr : (k + 1) * hr], got[:, k * hr : (k + 1) * hr]
        out[:, 2 * k * hr : (2 * k + 1) * hr] = jnp.where(c == 0, a, b)
        out[:, (2 * k + 1) * hr : (2 * k + 2) * hr] = jnp.where(c == 0, b, a)


CUTS = ((0, 512), (512, 256))
FAR_CUTS = ((0, 128), (128, 512))
LEVELS = 640


class Moves:
    def __init__(self, mesh):
        self.nz, self.nf = mesh.shape["dp"], mesh.shape["fsdp"]
        self.n = self.nz * self.nf
        self.doubling = self.nz == 4 and self.nf == 8

    def permute(self, x, target):
        pairs = [(d, target(d // self.nf, (d % self.nf) // 2, d % 2)) for d in range(self.n)]
        return lax.ppermute(x, AXES, [(a, (z * self.nf) + 2 * yx + c) for a, (z, yx, c) in pairs])

    def sibling(self, x):
        return self.permute(x, lambda z, yx, c: (z, yx, 1 - c))

    def near_z(self, x):
        return self.permute(x, lambda z, yx, c: (z ^ 1, yx, c))

    def far_z(self, x):
        return self.permute(x, lambda z, yx, c: (z ^ 2, yx, c))

    def side_a(self, x):
        return self.permute(x, lambda z, yx, c: (z, yx ^ (1 + c), c))

    def side_b(self, x):
        return self.permute(x, lambda z, yx, c: (z, yx ^ (2 - c), c))

    def opposite_z(self, x):
        return self.permute(x, lambda z, yx, c: (z ^ 3, yx, c))


def per_device(moves, tokens, memory, lengths, cotangent, self_qkv, self_out, cross_q, cross_kv, cross_out, mlp_in, mlp_out, norm_gains, norm_biases):
    seqs, mem_len = memory.shape[0], memory.shape[1]
    rows = seqs * LEN
    place = lax.axis_index(AXES)
    c = place % 2
    chip = place // 2
    core = jnp.reshape(c, (1,)).astype(jnp.int32)
    wr, hr = self_qkv.shape[0], mlp_out.shape[0]
    ff = mlp_in.shape[1]
    fh = ff // 2
    r2, s2 = 2 * rows, 2 * seqs
    wb = D // 16
    pad = -(-mem_len // 16) * 16
    fast = moves.doubling


    def prepare(lens, pairs, after=(), hold=()):
        return kernel_call(
            prepare_kernel,
            [lens, *pairs],
            [SM] + [STAGE] * 6,
            [sds((r2, D), BF)] * 2 + [sds((s2 * pad, D), BF), sds((r2, D), F32)],
            [STAGE] * 4,
            after=after,
            hold=hold,
        )

    def self_attention(pieces, lens, xhat, keep, back, after=()):
        return kernel_call(
            self_kernel,
            [lens, core, offs, *pieces, xhat, keep, back],
            [SM] * 3 + [VM] * 4 + [STAGE] * 3,
            [
                sds((r2, D), BF),
                sds((r2, 3 * DH), BF),
                sds((s2, LEN, DH), BF),
                sds((r2, 3 * DH), BF),
                sds((8, D), F32),
                sds((D, 3 * DH), BF),
            ],
            [STAGE] * 6,
            [pltpu.VMEM((D, 128), BF)],
            cost=6,
            after=after,
        )

    def cross_attention(pieces, mem, vec, tok, comb, recv, keep, back, after=()):
        kv_rows = s2 * pad
        return kernel_call(
            lambda *refs: keys_and_cross_kernel(mem_len, *refs),
            [offs, *pieces, mem, core, vec, tok, comb, recv, keep, back],
            [SM] + [VM] * 4 + [STAGE, SM] + [STAGE] * 6,
            [
                sds((kv_rows, D), BF),
                sds((D, 2 * DH), BF),
                sds((D, DH), BF),
                sds((r2, D), F32),
                sds((r2, D), BF),
                sds((r2, DH), BF),
                sds((s2, pad, DH), BF),
                sds((r2, 3 * DH), BF),
            ],
            [STAGE] * 8,
            cost=12,
            after=after,
        )

    def inner_part(resid_one, comb, recv, vec, w_in, hold=()):
        return kernel_call(
            inner_kernel,
            [resid_one, comb, recv, vec, w_in],
            [STAGE] * 5,
            [sds((r2, D), F32), sds((r2, D), BF), sds((r2, fh), BF), sds((r2, fh), BF)],
            [STAGE] * 4,
            cost=5,
            hold=hold,
        )

    def inner_weight(pieces, hold=()):
        return place_rows(pieces, offs, 0, [(0, fh, 0, wb, 0)], (D, fh), hold)

    def grads(body, ins, specs, ncols, extra=(), scratch=(), cost=5, after=(), hold=()):
        return kernel_call(
            body,
            [offs, *ins],
            [SM, *specs],
            [sds((4 * wb, ncols), BF)] * 4 + list(extra),
            scratch=[pltpu.VMEM((D, ncols), BF), *scratch],
            cost=cost,
            after=after,
            hold=hold,
        )

    def mlp_part(pieces, g, slope, w_in, hidden, third, after=(), hold=()):
        return kernel_call(
            mlp_and_grad_kernel,
            [offs, *pieces, g, slope, w_in, hidden, third],
            [SM] + [VM] * 12,
            [sds((rows, D), BF), sds((3 * rows, D), BF)] + [sds((4 * wb, fh), BF)] * 4,
            scratch=[pltpu.VMEM((r2, fh), BF), pltpu.VMEM((fh, D), BF), pltpu.VMEM((D, fh), BF)],
            cost=11,
            after=after,
            hold=hold,
        )

    def cross_back(resid_two, comb, recv, part, after=()):
        return kernel_call(
            cross_back_and_grads_kernel,
            [
                offs, core, vec, resid_two, comb, recv, part, g, *cout, kv, cq, cprobs, w_cq,
                *cross_mixed, second, mem,
            ],
            [SM] * 2 + [VM] * 16,
            [
                sds((rows, D), BF),
                sds((r2, D), F32),
                sds((r2, D), BF),
                sds((8, D), F32),
                sds(kv.shape, BF),
            ]
            + [sds((4 * wb, 4 * DH), BF)] * 4,
            scratch=[
                pltpu.VMEM((r2, D), BF),
                pltpu.VMEM((r2, DH), BF),
                pltpu.VMEM((r2, DH), BF),
                pltpu.VMEM((D, 4 * DH), BF),
            ],
            cost=14,
            after=after,
            limit=24 << 20,
        )

    def self_back(gsecond, recv, gresid_two, after=()):
        return kernel_call(
            self_back_and_grads_kernel,
            [
                offs, core, vec, resid_one, gsecond, recv, gresid_two, *out, packed, probs, w_qkv, xhat,
                *self_mixed, first, dvec_two,
            ],
            [SM] * 2 + [STAGE] * 15,
            [sds((rows, D), F32), sds((rows, D), BF), sds((rows, D), BF)]
            + [sds((4 * wb, 4 * DH + 128), BF)] * 4,
            scratch=[
                pltpu.VMEM((r2, D), BF),
                pltpu.VMEM((r2, 3 * DH), BF),
                pltpu.VMEM((8, D), F32),
                pltpu.VMEM((r2, DH), BF),
                pltpu.VMEM((D, 4 * DH + 128), BF),
                pltpu.VMEM((128, D), F32),
            ],
            cost=11,
            after=after,
        )

    def tokens_back(recv, gmem_recv, after=()):
        return kernel_call(
            tokens_back_kernel,
            [vec, tokens.reshape(rows, D), gfirst, recv, gresid_one, gmem, gmem_recv],
            [STAGE] * 7,
            [sds((rows, D), BF), sds(gmem.shape, BF), sds((8, 128), F32)],
            [STAGE] * 3,
            cost=4,
            after=after,
        )

    sib = moves.sibling
    pairs = []
    for x in (tokens.reshape(rows, D), cotangent.reshape(rows, D), memory):
        pairs += [x, sib(x)]
    lens = jnp.concatenate([lengths, sib(lengths)], 0)


    bits = jnp.arange(4, dtype=jnp.int32)
    if fast:
        plane = jnp.stack([jnp.int32(0), 1 + c, 2 - c, jnp.int32(3)]).astype(jnp.int32)
        z, yx = chip // 4, chip % 4
        chips = ((z ^ bits)[None, :] * 4 + (yx ^ plane)[:, None]).reshape(16).astype(jnp.int32)
    else:
        chips = jnp.arange(16, dtype=jnp.int32)
    turned = ((chips // 8) ^ c) * 8 + chips % 8
    offs = jnp.stack([chips, turned]).astype(jnp.int32)
    widths = (4 * DH + 128, 4 * DH, 4 * DH)

    if fast:
        width = widths[0] + widths[1]
        keep, send = kernel_call(
            pack_kernel,
            [core, self_qkv, self_out, cross_q, cross_kv, cross_out, norm_gains, norm_biases],
            [SM] + ["stage"] * 7,
            [sds((wr, width), BF)] * 2,
            scratch=[pltpu.VMEM((128, 128), F32)],
            cost=1,
            limit=60 << 20,
        )
        last, both, one = kernel_call(
            order_kernel,
            [core, keep, sib(send), mlp_out],
            [SM] + [VM] * 3,
            [sds((2 * wr, D), BF), sds((2 * wr, width), BF), sds((2 * wr, widths[0]), BF)],
            cost=1,
            after=[pairs[1], pairs[3]],
        )
        near, far, side_a, side_b = moves.near_z, moves.far_z, moves.side_a, moves.side_b
        near_both, along = near(both), [far(one), moves.opposite_z(one)]
        tok, g, mem, xhat = prepare(lens, pairs, hold=(one, both))
        last = tie(last, tok)
        a_last, b_last = side_a(last), side_b(last)
        one, two = cats(
            [
                [(one, 0, widths[0]), (near_both, 0, widths[0]), *whole(*along)],
                [(both, widths[0], widths[1]), (near_both, widths[0], widths[1])],
            ],
            after=(tok, a_last, b_last),
        )
        keep, send = kernel_call(
            pack_inner_kernel, [core, mlp_in], [SM, VM], [sds((wr, fh), BF)] * 2, cost=1, after=(one,)
        )
        (three,) = kernel_call(
            order_mlp_kernel, [core, keep, sib(send), mlp_out], [SM] + [VM] * 3, [sds((2 * wr, 6 * DH), BF)], cost=1
        )
        ab_last = tie(a_last, one)
        a1, b1, far_two, near_three, ab_last = side_a(one), side_b(one), far(two), near(three), side_b(ab_last)
        a1 = tie(a1, b1)
        two, last, three = cats(
            [whole(two, far_two), whole(last, a_last, b_last, ab_last), whole(three, near_three)], after=(a1,)
        )
        ab1, a2, b2, far_three, near_last = side_b(a1), side_a(two), side_b(two), far(three), near(last)
        a2 = tie(a2, b2, ab1)
        three, four, last, *parts = cats(
            [
                [(three, 0, 4 * DH), (far_three, 0, 4 * DH)],
                [(three, 4 * DH, D), (far_three, 4 * DH, D)],
                whole(last, near_last),
                *([(last, lo, width), (near_last, lo, width)] for lo, width in CUTS),
            ],
            after=(a2,),
        )
        out = out_rows([one, a1, b1, ab1], offs, 3 * DH)
        out = (out, sib(out))
        three, a2 = tie(three, out[1]), tie(a2, out[1])
        ab2, a3, b3, far_a = side_b(a2), side_a(three), side_b(three), far(tie(parts[0], out[1]))
        first, packed, probs, comb, vec, w_qkv = self_attention([one, a1, b1, ab1], lens, xhat, *out, after=(three,))
        a3 = tie(a3, b3, ab2, comb, far_a)
        four = tie(four, a3)
        comb = tie(comb, four)
        cout = out_rows([two, a2, b2, ab2], offs, 0)
        cout = (cout, sib(cout))
        self_mixed = (comb, sib(comb))
        ab3, a4, b4, far_b = side_b(a3), side_a(four), side_b(four), far(tie(parts[1], four))
        kv, w_ckv, w_cq, resid_one, second, cq, cprobs, comb = cross_attention(
            [two, a2, b2, ab2], mem, vec, tok, *self_mixed, *cout
        )
        comb = tie(comb, ab3, a4, b4, far_b)
        cross_mixed, ab4 = (comb, sib(comb)), side_b(tie(a4, comb))
        hold = [kv, cprobs, cq, w_cq, *cout, w_ckv, second]
        w_in = inner_weight([three, a3, b3, ab3], hold)
        resid_two, third, hidden, slope = inner_part(resid_one, *cross_mixed, vec, w_in, hold)
        last = [four, a4, b4, ab4, last, far_a, far_b]
    else:
        tok, g, mem, xhat = prepare(lens, pairs)
        everywhere = lambda w: lax.all_gather(w, AXES, axis=0, tiled=True)
        split = lambda w: [w[i * w.shape[0] // 4 : (i + 1) * w.shape[0] // 4] for i in range(4)]

        def col_half(w, groups):
            w = w.reshape(w.shape[0], groups, 2, w.shape[1] // (2 * groups))
            return lax.dynamic_index_in_dim(w, c, 2, keepdims=False).reshape(w.shape[0], -1)

        vectors = jnp.pad(jnp.concatenate([norm_gains, norm_biases], 0).T, ((0, 0), (0, 122)))
        one = jnp.concatenate([col_half(self_qkv, 3), col_half(self_out, 1), vectors], 1)
        two = jnp.concatenate([col_half(w, w.shape[1] // D) for w in (cross_out, cross_q, cross_kv)], 1)
        one, two = split(everywhere(one)), split(everywhere(two))
        three = split(everywhere(col_half(mlp_in, ff // (2 * hr))))
        out, cout = out_rows(one, offs, 3 * DH), out_rows(two, offs, 0)
        out, cout = (out, sib(out)), (cout, sib(cout))
        rowed = everywhere(mlp_out).reshape(moves.n // 2, 2, hr, D)
        rowed = lax.dynamic_index_in_dim(rowed, c, 1, keepdims=False).reshape(16, 2, fh // 32, D)
        rowed = rowed.transpose(1, 0, 2, 3)
        levels = rowed[1].reshape(4, 4, wb, D).transpose(1, 0, 2, 3).reshape(D, D)
        last = split(rowed[0].reshape(D, D)) + [levels[: D // 2]]
        last += [levels[D // 2 :, lo : lo + width] for lo, width in CUTS]
        hold = ()
        first, packed, probs, comb, vec, w_qkv = self_attention(one, lens, xhat, *out)
        self_mixed = (comb, sib(comb))
        kv, w_ckv, w_cq, resid_one, second, cq, cprobs, comb = cross_attention(
            two, mem, vec, tok, *self_mixed, *cout
        )
        cross_mixed = (comb, sib(comb))
        w_in = inner_weight(three)
        resid_two, third, hidden, slope = inner_part(resid_one, *cross_mixed, vec, w_in)


    near, far, side_a, side_b = moves.near_z, moves.far_z, moves.side_a, moves.side_b
    after = ()

    held = [resid_two, vec]
    d_mlpout = kernel_call(
        dmlpout_kernel,
        [offs, hidden, g],
        [SM, VM, VM],
        [sds((4 * wb, 2 * D - LEVELS), BF)] * 4
        + [sds((8 * wb, LEVELS), BF)]
        + [sds((8 * wb, width), BF) for _, width in FAR_CUTS],
        scratch=[pltpu.VMEM((D, 2 * D - LEVELS), BF), pltpu.VMEM((D, LEVELS), BF)],
        cost=3,
        hold=[*hold, *held, third],
    )
    if fast:
        got_ab1, got_z1 = side_a(d_mlpout[3]), far(d_mlpout[5])
    part, comb, *d_mlpin = mlp_part(last, g, slope, w_in, hidden, third, after=d_mlpout[:1], hold=[*hold, *held])
    if fast:
        (on,) = merge([("pass", d_mlpout[2], got_ab1)], after=(part, got_z1))
        comb = tie(comb, on)
        got_b1, got_a1, got_z2 = side_b(on), side_a(tie(d_mlpout[1], on)), far(tie(d_mlpout[6], on))
        got_ab2, got_a2 = side_a(tie(d_mlpin[3], on)), side_a(tie(d_mlpin[1], on))
        after = (on,)
    recv = sib(comb)
    output, gresid_two, gsecond, dvec_two, dkv, *d_cross = cross_back(resid_two, comb, recv, part, after=after)
    if fast:
        on, kept1, on_far, kept_z, on_z = merge(
            [
                ("pass", d_mlpin[2], got_ab2),
                ("half", d_mlpout[0], got_a1, got_b1),
                ("levels", d_mlpout[4], got_z1, got_z2),
            ],
            after=(dvec_two, got_a2),
        )
        gsecond = tie(gsecond, on)
        got_b2, got_far1, got_near_z = side_b(on), far(on_far), near(on_z)
        got_ab3, got_a3 = side_a(tie(d_cross[3], on)), side_a(tie(d_cross[1], on))
        after = (on,)
    recv = sib(gsecond)
    gresid_one, gfirst, gfirst_other, *d_self = self_back(gsecond, recv, gresid_two, after=after)
    if fast:
        on, kept2, on_far, kept1, on_near, own_z, pass_z, on_z = merge(
            [
                ("pass", d_cross[2], got_ab3),
                ("half", d_mlpin[0], got_a2, got_b2),
                ("near", kept1, got_far1),
                ("columns", kept_z, got_near_z),
            ],
            after=(gfirst, got_a3),
        )
        got_b3, got_ab4 = side_b(on), side_a(tie(d_self[3], on))
        got_far2, got_near1, got_a_z = far(on_far), near(on_near), side_a(on_z)
        after = (on,)
    gmem, gmem_other = kernel_call(
        memory_kernel, [dkv, w_ckv], [VM, VM], [sds((seqs * pad, D), BF)] * 2, cost=3, after=after
    )
    if fast:
        on, kept3, on_far, kept2, on_near, total1, own_z, on_z = merge(
            [
                ("pass", d_self[2], got_ab4),
                ("half", d_cross[0], got_a3, got_b3),
                ("near", kept2, got_far2),
                ("last", kept1, got_near1),
                ("side", own_z, pass_z, got_a_z),
            ],
            after=(gmem,),
        )
        gfirst_other, gmem_other = tie(gfirst_other, on), tie(gmem_other, on)
        got_b4, got_a4 = side_b(on), side_a(tie(d_self[1], on))
        got_far3, got_near2, got_b_z = far(on_far), near(on_near), side_b(on_z)
    recv, gmem_recv = sib(gfirst_other), sib(gmem_other)
    grad_tokens, grad_memory, token = tokens_back(recv, gmem_recv)
    grad_memory = grad_memory.reshape(seqs, pad, D)[:, :mem_len]

    if fast:
        *blocks, total_z, total2 = merge(
            [
                ("send", d_self[0], got_a4, got_b4),
                ("send_near", kept3, got_far3),
                ("last", own_z, got_b_z),
                ("last", kept2, got_near2),
            ],
            after=(token,),
            beside=(0, 3),
        )
        got_far4, got_opp4, got_near = far(blocks[1]), moves.opposite_z(blocks[2]), near(blocks[0])
        width = 4 * DH + 128
        total2 = tie(total2, got_near)
        (total3,) = merge([("tail_near", kept3, got_far3, got_near[:, width:])])
        (total4,) = merge([("tail", d_self[0], got_a4, got_b4, got_near[:, :width], got_far4, got_opp4)])
        total = [total1, total2, total3, total4]

        def own_rows(total):
            mine = lax.dynamic_slice_in_dim(total, c * wr, wr, 0)
            return mine, sib(lax.dynamic_slice_in_dim(total, (1 - c) * wr, wr, 0))

        def join(pair, *shapes, scratch=()):
            return kernel_call(
                join_kernel,
                [core, *pair],
                [SM, STAGE, STAGE],
                [sds(shape, F32) for shape in shapes],
                [STAGE] * len(shapes),
                scratch=scratch,
                cost=1,
            )

        sum_mlpout = jnp.concatenate([total[0][:, :D], jnp.concatenate([total_z, total[0][:, D:]], 1)], 0)
        (grad_in,) = kernel_call(
            join_inner_kernel, [core, *own_rows(total[1])], [SM, VM, VM], [sds((wr, ff), F32)], cost=1
        )
        grad_cout, grad_cq, grad_ckv = join(own_rows(total[2]), (wr, D), (wr, D), (wr, 2 * D))
        grad_out, grad_qkv, own_gains, own_biases = join(
            own_rows(total[3]), (wr, D), (wr, 3 * D), (3, wr), (3, wr), scratch=[pltpu.VMEM((128, 128), F32)]
        )
    else:

        def placed(parts):
            term = jnp.concatenate(parts, 0).astype(F32)
            both = jnp.stack([jnp.where(c == 0, term, 0.0), jnp.where(c == 1, term, 0.0)], 1)
            return lax.psum_scatter(both, AXES, scatter_dimension=0, tiled=True)

        def joined(total, lo, hi, groups):
            return total[:, :, lo:hi].reshape(wr, 2, groups, -1).transpose(0, 2, 1, 3).reshape(wr, -1)

        total = placed(d_cross)
        grad_cout, grad_cq, grad_ckv = (
            joined(total, 0, DH, 1),
            joined(total, DH, 2 * DH, 1),
            joined(total, 2 * DH, 4 * DH, 2),
        )
        total = placed(d_self)
        grad_out, grad_qkv = joined(total, 0, DH, 1), joined(total, DH, 4 * DH, 3)
        vectors = jnp.sum(total[:, :, 4 * DH : 4 * DH + 6], 1).T
        own_gains, own_biases = vectors[:3], vectors[3:]
        grad_in = joined(placed(d_mlpin), 0, fh, ff // (2 * hr))
        first_rows = jnp.concatenate(d_mlpout[:4], 0)
        levels = jnp.concatenate([d_mlpout[4], jnp.concatenate(d_mlpout[5:], 1)], 0).reshape(4, 4, wb, LEVELS)
        levels = jnp.concatenate([levels.transpose(1, 0, 2, 3).reshape(D, LEVELS), first_rows[:, D:]], 1)
        term = jnp.stack([first_rows[:, :D].reshape(16, wb, D), levels.reshape(16, wb, D)], 1).astype(F32)
        term = term.reshape(moves.n // 2, 1, hr, D)
        both = jnp.concatenate([jnp.where(c == 0, term, 0.0), jnp.where(c == 1, term, 0.0)], 1)
        sum_mlpout = lax.psum_scatter(both.reshape(ff, D), AXES, scatter_dimension=0, tiled=True)

    return (
        output.reshape(tokens.shape),
        grad_tokens.reshape(tokens.shape),
        grad_memory,
        grad_qkv,
        grad_out,
        grad_cq,
        grad_ckv,
        grad_cout,
        grad_in,
        sum_mlpout,
        own_gains,
        own_biases,
    )


def solution(mesh):
    batch = P(AXES, None, None)
    rows = P(AXES, None)
    cols = P(None, AXES)
    moves = Moves(mesh)
    in_specs = (batch, batch, P(AXES), batch) + (rows,) * 7 + (cols,) * 2
    out_specs = (batch,) * 3 + (rows,) * 7 + (cols,) * 2
    return jax.shard_map(
        lambda *args: per_device(moves, *args),
        mesh=mesh,
        in_specs=in_specs,
        out_specs=out_specs,
        check_vma=False,
    )
```

```python
import jax
import jax.numpy as jnp
import numpy as np
from jax import lax
from jax.experimental import pallas as pl
from jax.experimental.pallas import tpu as pltpu
from jax.sharding import PartitionSpec as P

AXES = ("dp", "fsdp")
HEADS = 12
HALF = HEADS // 2
HEAD = 64
D = 768
DH = D // 2
LEN = 64
EPS = 1e-06
NEG = -1e30
SCALE = HEAD ** (-0.5)
F32 = jnp.float32
BF = jnp.bfloat16
VMEM_LIMIT = 14 << 20

VM = pl.BlockSpec(memory_space=pltpu.VMEM)
SM = pl.BlockSpec(memory_space=pltpu.SMEM)
ANY = pl.BlockSpec(memory_space=pl.ANY)


def sds(shape, dtype):
    return jax.ShapeDtypeStruct(shape, dtype)


STAGE = VM


class Staged:
    def __init__(self, ref, copy):
        self.ref, self.copy, self.waited = ref, copy, False
        self.shape = ref.shape

    def ready(self):
        if not self.waited:
            self.copy.wait()
            self.waited = True
        return self.ref


PENDING = {}


def flush(*refs):
    for r in refs:
        if id(r) in PENDING:
            PENDING[id(r)].start()
            PENDING[id(r)] = None


def ready(*refs):
    out = [r.ready() if isinstance(r, Staged) else r for r in refs]
    return out[0] if len(out) == 1 else out


def kernel_call(body, ins, in_specs, outs, out_specs=None, scratch=(), cost=5, after=(), limit=None, hold=()):
    n, skip, m, k = len(ins), len(after) + len(hold), len(outs), len(scratch)
    out_specs = [VM] * m if out_specs is None else list(out_specs)
    staged_in = [i for i, spec in enumerate(in_specs) if spec == 'stage']
    staged_out = [i for i, spec in enumerate(out_specs) if spec == 'stage']
    buffers = [pltpu.VMEM(ins[i].shape, ins[i].dtype) for i in staged_in]
    buffers += [pltpu.VMEM(outs[i].shape, outs[i].dtype) for i in staged_out]
    extra = [*buffers, pltpu.SemaphoreType.DMA((len(buffers),))] if buffers else []

    def run(*refs):
        ins, outs = list(refs[:n]), list(refs[n + skip : n + skip + m])
        own = refs[n + skip + m : n + skip + m + k]
        PENDING.clear()
        if not buffers:
            body(*ins, *outs, *own)
            return
        held, sems = refs[n + skip + m + k : -1], refs[-1]
        for j, i in enumerate(staged_in):
            copy = pltpu.make_async_copy(ins[i], held[j], sems.at[j])
            copy.start()
            ins[i] = Staged(held[j], copy)
        copies = []
        for j, i in enumerate(staged_out, len(staged_in)):
            copies.append(pltpu.make_async_copy(held[j], outs[i], sems.at[j]))
            outs[i] = held[j]
            PENDING[id(held[j])] = copies[-1]
        body(*ins, *outs, *own)
        ready(*ins)
        for cp in PENDING.values():
            if cp is not None:
                cp.start()
        for cp in copies:
            cp.wait()

    space = lambda spec: ANY if spec == 'stage' else spec
    return pl.pallas_call(
        run,
        out_shape=list(outs),
        in_specs=[space(spec) for spec in in_specs] + [ANY] * len(after) + [VM] * len(hold),
        out_specs=[space(spec) for spec in out_specs],
        scratch_shapes=[*scratch, *extra],
        compiler_params=pltpu.CompilerParams(vmem_limit_bytes=limit or VMEM_LIMIT),
        cost_estimate=pl.CostEstimate(flops=cost * 7 * 10**9, bytes_accessed=0, transcendentals=0),
    )(*ins, *after, *hold)


def tie(x, *earlier):
    return pl.pallas_call(
        lambda *refs: None,
        out_shape=sds(x.shape, x.dtype),
        in_specs=[ANY] * (1 + len(earlier)),
        out_specs=ANY,
        input_output_aliases={0: 0},
        compiler_params=pltpu.CompilerParams(vmem_limit_bytes=1 << 20),
        cost_estimate=pl.CostEstimate(flops=0, bytes_accessed=0, transcendentals=0),
    )(x, *earlier)


def nn(a, b):
    return lax.dot_general(a, b, (((1,), (0,)), ((), ())), preferred_element_type=F32)


def nt(a, b):
    return lax.dot_general(a, b, (((1,), (1,)), ((), ())), preferred_element_type=F32)


def tn(a, b):
    return lax.dot_general(a, b, (((0,), (0,)), ((), ())), preferred_element_type=F32)


def normalise(v):
    mean = jnp.mean(v, -1, keepdims=True)
    cen = v - mean
    inv = lax.rsqrt(jnp.mean(cen * cen, -1, keepdims=True) + EPS)
    return cen * inv, inv


def norm_back(v, gain, dy):
    xhat, inv = normalise(v)
    dxh = dy * gain
    m1 = jnp.mean(dxh, -1, keepdims=True)
    m2 = jnp.mean(dxh * xhat, -1, keepdims=True)
    dx = inv * (dxh - m1 - xhat * m2)
    return dx, jnp.sum(dy * xhat, 0, keepdims=True), jnp.sum(dy, 0, keepdims=True)


GROUPS = ((0, 256), (256, DH))


def head_of_lane(rows, width):
    return lax.shift_right_logical(lax.broadcasted_iota(jnp.int32, (rows, width), 1), 6)


def spread(q):
    head = head_of_lane(1, q.shape[1])
    parts = [q * (head == h).astype(F32).astype(q.dtype) for h in range(q.shape[1] // HEAD)]
    return jnp.concatenate(parts, 0)


def fold(o):
    head = head_of_lane(LEN, o.shape[1])
    total = jnp.where(head == 0, o[:LEN], 0.0)
    for h in range(1, o.shape[1] // HEAD):
        total = jnp.where(head == h, o[h * LEN : (h + 1) * LEN], total)
    return total


def attend(q, k, v, allowed):
    probs, mixed = [], []
    for lo, hi in GROUPS:
        st = nt(k[:, lo:hi], spread(q[:, lo:hi])) * SCALE
        st = jnp.where(allowed[:, lo:hi], st, NEG)
        e = jnp.exp(st - jnp.max(st, 0, keepdims=True))
        p = (e * (1.0 / jnp.sum(e, 0, keepdims=True))).astype(BF)
        probs.append(p)
        mixed.append(fold(tn(p, v[:, lo:hi])).astype(BF))
    return jnp.concatenate(probs, 1), jnp.concatenate(mixed, 1)


def attend_back(g, q, k, v, p):
    dq, dk, dv = [], [], []
    for lo, hi in GROUPS:
        gs, qs, low = spread(g[:, lo:hi]), spread(q[:, lo:hi]), p[:, lo:hi]
        dp = nt(v[:, lo:hi], gs)
        pf = low.astype(F32)
        t = pf * dp
        ds = (t - pf * jnp.sum(t, 0, keepdims=True)).astype(BF)
        dq.append((fold(tn(ds, k[:, lo:hi])) * SCALE).astype(BF))
        dk.append((nn(ds, qs) * SCALE).astype(BF))
        dv.append(nn(low, gs).astype(BF))
    return [jnp.concatenate(x, 1) for x in (dq, dk, dv)]


def seq_rows(s):
    return pl.ds(pl.multiple_of(s * LEN, LEN), LEN)


def half_lanes(c):
    return pl.ds(pl.multiple_of(c * DH, DH), DH)


def loop(n, body, unroll=1):
    def step(i, carry):
        body(i)
        return carry

    lax.fori_loop(0, n, step, 0, unroll=unroll)


def columns_first(pieces, q, r):
    blk = pieces[0].shape[0] // 4
    return pieces[q], r * blk


def place(pieces, offs_ref, which, cols, targets):
    blk = pieces[0].shape[0] // 4
    for lo, hi, o, step, shift in cols:
        for q in range(4):
            for r in range(4):
                row = pl.multiple_of(offs_ref[which, q * 4 + r] * step + shift, 16)
                targets[o][pl.ds(row, blk), :] = pieces[q][r * blk : (r + 1) * blk, lo:hi]


def place_last(own, far, near, offs_ref, target):
    blk = own.shape[0] // 4
    for q in range(4):
        for r in range(4):
            at = q * blk + (own.shape[0] if r == 3 else 0)
            for (lo, width), part in zip(CUTS, near):
                src, base = ((own, lo), (part, 0), (far, lo), (part, 0))[r]
                for first, end, shift, col in ((0, D, blk, 0), (D, LAST, 0, FIRST - D)):
                    a, b = max(lo, first), min(lo + width, end)
                    if a < b:
                        row = pl.multiple_of(offs_ref[0, q * 4 + r] * (2 * blk) + shift, 16)
                        values = src[at if r % 2 else q * blk : (at if r % 2 else q * blk) + blk, base + a - lo : base + b - lo]
                        target[pl.ds(row, blk), a + col : b + col] = values


def place_rows(pieces, offs, which, cols, shape, hold=()):
    def body(offs_ref, *refs):
        place(refs[:4], offs_ref, which, cols, refs[4:5])

    return kernel_call(body, [offs, *pieces], [SM] + [VM] * 4, [sds(shape, BF)], cost=1, hold=hold)[0]


def out_rows(pieces, offs, lo):
    blk = pieces[0].shape[0] // 4
    return place_rows(pieces, offs, 1, [(lo, lo + DH, 0, blk, 0)], (16 * blk, DH))


def send_out(dw, offs_ref, outs):
    blk = dw.shape[0] // 16
    for q in range(4):
        for r in range(4):
            row = pl.multiple_of(offs_ref[0, q * 4 + r] * blk, 16)
            outs[q][r * blk : (r + 1) * blk, :] = dw[pl.ds(row, blk), :]


def pack_kernel(core, qkv, out, cq, ckv, cout, gains, biases, keep, send, vecs):
    c = core[0]
    qkv, out, cq, ckv, cout, gains, biases = ready(qkv, out, cq, ckv, cout, gains, biases)
    vecs[...] = jnp.zeros_like(vecs)
    vecs[0:3, 0:24] = gains[...].astype(F32)
    vecs[3:6, 0:24] = biases[...].astype(F32)
    rows = keep.shape[0]
    wide = jnp.transpose(vecs[...])[:rows].astype(BF)
    for dst, which in ((keep, c), (send, 1 - c)):
        at = 0
        for w, groups in ((qkv, 3), (out, 1), (None, 0), (cout, 1), (cq, 1), (ckv, 2)):
            if w is None:
                dst[:, at : at + 128] = wide
                at += 128
            for k in range(groups):
                lanes = pl.ds(pl.multiple_of(k * D + which * DH, 128), DH)
                dst[:, at : at + DH] = w[:, lanes]
                at += DH


def pack_inner_kernel(core, win, keep, send):
    c = core[0]
    win = ready(win)
    hr = 96
    for k in range(win.shape[1] // (2 * hr)):
        first = win[:, 2 * k * hr : (2 * k + 1) * hr]
        second = win[:, (2 * k + 1) * hr : (2 * k + 2) * hr]
        keep[:, k * hr : (k + 1) * hr] = jnp.where(c == 0, first, second)
        send[:, k * hr : (k + 1) * hr] = jnp.where(c == 0, second, first)


def order_kernel(core, keep, got, wout, last, *outs):
    c = core[0]
    rows = keep.shape[0]
    for b, (top, under) in enumerate(((keep, got), (got, keep))):
        for dst in outs:
            width = dst.shape[1]
            dst[b * rows : (b + 1) * rows, :] = jnp.where(c == 0, top[:, :width], under[:, :width])
    last[:, :D] = wout[2 * rows :, :]
    last[:, D:] = wout[0 : 2 * rows, FIRST:]


def order_mlp_kernel(core, keep, got, wout, three):
    c = core[0]
    rows, width = keep.shape
    for b, (top, under) in enumerate(((keep, got), (got, keep))):
        three[b * rows : (b + 1) * rows, :width] = jnp.where(c == 0, top[...], under[...])
    three[:, width:] = wout[0 : 2 * rows, :FIRST]


def cats(jobs, after=()):
    arrays, places, outs = [], [], []
    for job in jobs:
        at, outs = 0, [*outs, sds((sum(x.shape[0] for x, _, _ in job), job[0][2]), BF)]
        for x, lo, width in job:
            arrays.append(x)
            places.append((len(outs) - 1, at, lo, width))
            at += x.shape[0]
    n = len(arrays)

    def body(*refs):
        for src, (o, at, lo, width) in zip(refs[:n], places):
            refs[n + o][at : at + src.shape[0], :] = src[:, lo : lo + width]

    return kernel_call(body, arrays, [VM] * n, outs, cost=1, after=after)


def whole(*arrays):
    return [(x, 0, x.shape[1]) for x in arrays]


def prepare_kernel(lens, tok_own, tok_other, cot_own, cot_other, mem_own, mem_other, tok, g, mem, xhat):
    tok_own, tok_other = ready(tok_own, tok_other)
    rows = tok.shape[0] // 2
    seqs, length = mem_own.shape[0], mem_own.shape[1]
    pad = mem.shape[0] // (2 * seqs)
    for b, src in ((0, tok_own), (1, tok_other)):
        tok[b * rows : (b + 1) * rows, :] = src[...]
    flush(tok)

    def norm(s):
        xhat[seq_rows(s), :] = normalise(tok[seq_rows(s), :].astype(F32))[0]

    loop(2 * seqs, norm, 2)
    flush(xhat)
    mem_own, mem_other = ready(mem_own, mem_other)
    for b, src in ((0, mem_own), (1, mem_other)):
        for s in range(seqs):
            at = (b * seqs + s) * pad
            mem[at + length - length % 16 : at + pad, :] = jnp.zeros((pad - length + length % 16, D), BF)
            mem[at : at + length, :] = src[s]
    flush(mem)
    cot_own, cot_other = ready(cot_own, cot_other)
    place = lax.broadcasted_iota(jnp.int32, (LEN, D), 0)
    for b, src in ((0, cot_own), (1, cot_other)):
        for s in range(seqs):
            at = (b * seqs + s) * LEN
            live = (place < lens[b * seqs + s]).astype(F32)
            g[at : at + LEN, :] = (src[s * LEN : (s + 1) * LEN, :].astype(F32) * live).astype(BF)


def self_kernel(lens, core, offs, own, a, b, ab, xhat, keep, back, first, packed, probs, comb, vec, wqkv, gcol):
    c = core[0]
    blk = D // 16
    place((own, a, b, ab), offs, 0, [(4 * DH, 4 * DH + 128, 1, blk, 0), (0, 3 * DH, 0, blk, 0)], (wqkv, gcol))
    xhat = ready(xhat)
    vec[...] = jnp.transpose(gcol[...].astype(F32))[:8]
    gain, bias = vec[0:1], vec[3:4]

    def norm(s):
        first[seq_rows(s), :] = (xhat[seq_rows(s), :] * gain + bias).astype(BF)

    loop(8, norm, 2)
    flush(first)

    def proj(b):
        rows = pl.ds(pl.multiple_of(b * 256, 256), 256)
        packed[rows, :] = nn(first[rows, :], wqkv[...]).astype(BF)

    loop(2, proj)
    flush(packed)
    key = lax.broadcasted_iota(jnp.int32, (LEN, DH), 0)
    query = lax.broadcasted_iota(jnp.int32, (LEN, DH), 1) & (LEN - 1)

    def att(s):
        allowed = (key <= query) & (key < lens[s])
        rows = seq_rows(s)
        p, m = attend(packed[rows, 0:DH], packed[rows, DH : 2 * DH], packed[rows, 2 * DH :], allowed)
        probs[s] = p
        comb[rows, D:] = m

    loop(8, att, 2)
    flush(probs)
    keep, back = ready(keep, back)
    comb[:, half_lanes(c)] = nn(comb[:, D:], keep[:DH, :]).astype(BF)
    comb[:, half_lanes(1 - c)] = nn(comb[:, D:], back[DH:, :]).astype(BF)


def kv_kernel(offs, own, a, b, ab, mem, kv, wckv, wcq):
    blk = D // 16
    place((own, a, b, ab), offs, 0, [(2 * DH, 4 * DH, 0, blk, 0), (DH, 2 * DH, 1, blk, 0)], (wckv, wcq))
    mem = ready(mem)

    def step(b):
        rows = pl.ds(pl.multiple_of(b * 480, 480), 480)
        kv[rows, :] = nn(mem[rows, :], wckv[...]).astype(BF)

    loop(mem.shape[0] // 480, step)


def swapped(s):
    return pl.ds(pl.multiple_of(((s + 4) & 7) * LEN, LEN), LEN)


def cross_kernel(mem_len, core, vec, tok, part, recv, wcq, kv, keep, back, resid, second, cq, probs, comb):
    c = core[0]
    vec, tok, part, recv = ready(vec, tok, part, recv)
    gain, bias = vec[1:2], vec[4:5]

    def norm(s):
        rows = seq_rows(s)
        both = part[rows, 0:D].astype(F32) + recv[swapped(s), 0:D].astype(F32)
        v = tok[rows, :].astype(F32) + both
        resid[rows, :] = v
        xhat, _ = normalise(v)
        second[rows, :] = (xhat * gain + bias).astype(BF)

    loop(8, norm, 2)
    flush(resid, second)
    wcq = ready(wcq)
    cq[...] = nn(second[...], wcq[...]).astype(BF)
    flush(cq)
    kv = ready(kv)
    pad = probs.shape[1]
    allowed = lax.broadcasted_iota(jnp.int32, (pad, DH), 0) < mem_len

    def att(s):
        rows = seq_rows(s)
        keys = pl.ds(pl.multiple_of(s * pad, 16), pad)
        p, m = attend(cq[rows, :], kv[keys, 0:DH], kv[keys, DH:], allowed)
        probs[s] = p
        comb[rows, D:] = m

    loop(8, att, 2)
    flush(probs)
    keep, back = ready(keep, back)
    comb[:, half_lanes(c)] = nn(comb[:, D:], keep[:DH, :]).astype(BF)
    comb[:, half_lanes(1 - c)] = nn(comb[:, D:], back[DH:, :]).astype(BF)


def keys_and_cross_kernel(
    mem_len, offs, own, a, b, ab, mem, core, vec, tok, part, recv, keep, back, kv, wckv, wcq, resid, second, cq, probs, comb
):
    kv_kernel(offs, own, a, b, ab, mem, kv, wckv, wcq)
    cross_kernel(mem_len, core, vec, tok, part, recv, wcq, kv, keep, back, resid, second, cq, probs, comb)


def inner_kernel(resid, part, recv, vec, win, resid_two, third, hidden, slope):
    resid, part, recv, vec = ready(resid, part, recv, vec)
    gain, bias = vec[2:3], vec[5:6]

    def norm(s):
        rows = seq_rows(s)
        both = part[rows, 0:D].astype(F32) + recv[swapped(s), 0:D].astype(F32)
        v = resid[rows, :] + both
        resid_two[rows, :] = v
        xhat, _ = normalise(v)
        third[rows, :] = (xhat * gain + bias).astype(BF)

    loop(8, norm, 2)
    flush(resid_two, third)
    win = ready(win)

    def step(b):
        rows = pl.ds(pl.multiple_of(b * 128, 128), 128)
        x = nn(third[rows, :], win[...])
        cdf = 0.5 + 0.5 * lax.erf(x * (0.5**0.5))
        hidden[rows, :] = (x * cdf).astype(BF)
        density = jnp.exp(x * x * -0.5) * ((2.0 * np.pi) ** -0.5)
        slope[rows, :] = (cdf + x * density).astype(BF)

    loop(4, step)


def mlp_kernel(offs, pieces, plane, far, near, g, slope, win, hidden, own, comb, ginner, wout):
    half = own.shape[0]
    blk = D // 16
    place(pieces, offs, 0, [(0, FIRST, 0, 2 * blk, 0)], (wout.at[:, :FIRST],))
    place_last(plane, far, near, offs, wout)
    g, slope, win = ready(g, slope, win)

    def back(b):
        rows = pl.ds(pl.multiple_of(b * 256, 256), 256)
        gh = nt(g[rows, :], wout[...])
        ginner[rows, :] = (gh * slope[rows, :].astype(F32)).astype(BF)
        comb[rows, :] = nt(ginner[rows, :], win[...]).astype(BF)

    loop(2, back)
    flush(ginner)
    hidden = ready(hidden)
    own[...] = nn(hidden[0:half, :], wout[...]).astype(BF)
    comb[2 * half :, :] = nn(hidden[half:, :], wout[...]).astype(BF)


def dmlpout_kernel(offs, hidden, g, own, a, b, ab, near, *refs):
    far, dw, dz = refs[:-2], refs[-2], refs[-1]
    blk = dw.shape[0] // 16
    for i in range(4):
        part = tn(hidden[:, i * 8 * blk : (i + 1) * 8 * blk], g[...]).astype(BF)
        for k in range(8):
            row, rows = (4 * i + k // 2) * blk, slice(k * blk, (k + 1) * blk)
            if k % 2:
                dz[row : row + blk, :] = part[rows, :LEVELS]
                if LEVELS < D:
                    dw[row : row + blk, D:] = part[rows, LEVELS:]
            else:
                dw[row : row + blk, :D] = part[rows]
    send_out(dw, offs, (own, a, b, ab))
    for q in range(4):
        for r in range(4):
            rows = pl.ds(pl.multiple_of(offs[0, q * 4 + r] * blk, 16), blk)
            at = ((r // 2) * 4 + q) * blk
            if r % 2 == 0:
                near[at : at + blk, :] = dz[rows, :]
                continue
            for dst, (lo, width) in zip(far, FAR_CUTS):
                dst[at : at + blk, :] = dz[rows, lo : lo + width]


def mlp_and_grad_kernel(
    offs, pown, pa, pb, pab, plane, far, near_a, near_b, g, slope, win, hidden, third, own, comb, d_own, d_a, d_b, d_ab, ginner, wout, dw
):
    mlp_kernel(offs, (pown, pa, pb, pab), plane, far, (near_a, near_b), g, slope, win, hidden, own, comb, ginner, wout)
    dmlpin_kernel(offs, third, ginner, d_own, d_a, d_b, d_ab, dw)


def dmlpin_kernel(offs, third, ginner, *refs):
    third, ginner = ready(third, ginner)
    outs, dw = refs[:4], refs[4]
    for b in range(0, dw.shape[0], 256):
        dw[b : b + 256, :] = tn(third[:, b : b + 256], ginner[...]).astype(BF)
    send_out(dw, offs, outs)


def cross_back_kernel(
    core, vec, resid, part, recv, own, g, keep, back, kv, cq, probs, wcq, output, gresid, gtwo, dcq, dkv, gsecond, dvec, gm
):
    c = core[0]
    vec, resid, part, recv, own, g = ready(vec, resid, part, recv, own, g)
    gain = vec[2:3]
    dvec[...] = jnp.zeros_like(dvec)

    def norm(s):
        rows = seq_rows(s)
        dy = part[rows, :].astype(F32) + recv[swapped(s), :].astype(F32)
        dx, dg, db = norm_back(resid[rows, :], gain, dy)
        total = g[rows, :].astype(F32) + dx
        gresid[rows, :] = total
        gtwo[rows, :] = total.astype(BF)

        @pl.when(s < 4)
        def _():
            dvec[0:1, :] += dg
            dvec[1:2, :] += db
            extra = own[rows, :].astype(F32) + recv[pl.ds(pl.multiple_of(512 + s * LEN, LEN), LEN), :].astype(F32)
            output[rows, :] = (resid[rows, :] + extra).astype(BF)

    loop(8, norm, 2)
    flush(output, gresid, gtwo, dvec)
    keep, back = ready(keep, back)
    gm[...] = (nt(gtwo[:, half_lanes(c)], keep[:DH, :]) + nt(gtwo[:, half_lanes(1 - c)], back[DH:, :])).astype(BF)
    pad = probs.shape[1]
    kv, cq, probs = ready(kv, cq, probs)

    def att(s):
        rows = seq_rows(s)
        keys = pl.ds(pl.multiple_of(s * pad, 16), pad)
        dq, dk, dv = attend_back(gm[rows, :], cq[rows, :], kv[keys, 0:DH], kv[keys, DH:], probs[s])
        dcq[rows, :] = dq
        dkv[keys, 0:DH] = dk
        dkv[keys, DH:] = dv

    loop(8, att, 2)
    flush(dcq, dkv)
    wcq = ready(wcq)
    gsecond[...] = nt(dcq[...], wcq[...]).astype(BF)


def out_grad(dw, lo, c, mine, other, g):
    cols = half_lanes(c)
    dw[half_lanes(c), lo : lo + DH] = tn(mine[:, D:], g[:, cols]).astype(BF)
    rest = tn(other[256:, D:], g[:256, cols]) + tn(other[:256, D:], g[256:, cols])
    dw[half_lanes(1 - c), lo : lo + DH] = rest.astype(BF)


def dcross_kernel(offs, core, mixed, mixed_other, gtwo, second, dcq, dkv, mem, *refs):
    outs, dw = refs[:4], refs[4]
    mixed, mixed_other, gtwo = ready(mixed, mixed_other, gtwo)
    out_grad(dw, 0, core[0], mixed, mixed_other, gtwo)
    second, dcq = ready(second, dcq)
    dw[:, DH : 2 * DH] = tn(second[...], dcq[...]).astype(BF)
    mem = ready(mem)
    for b in range(0, D, 256):
        dw[b : b + 256, 2 * DH :] = tn(mem[:, b : b + 256], dkv[...]).astype(BF)
    send_out(dw, offs, outs)


def memory_kernel(dkv, wckv, own, other):
    half = own.shape[0]
    for i, dst in ((1, other), (0, own)):
        for b in range(0, half, 480):
            dst[b : b + 480, :] = nt(dkv[i * half + b : i * half + b + 480, :], wckv[...]).astype(BF)


def cross_back_and_grads_kernel(
    offs, core, vec, resid, part, recv, own, g, keep, back, kv, cq, probs, wcq, mixed, mixed_other, second, mem,
    output, gresid, gsecond, dvec, dkv, d_own, d_a, d_b, d_ab, gtwo, dcq, gm, dw
):
    cross_back_kernel(
        core, vec, resid, part, recv, own, g, keep, back, kv, cq, probs, wcq, output, gresid, gtwo, dcq, dkv, gsecond, dvec, gm
    )
    dcross_kernel(
        offs, core, mixed, mixed_other, gtwo, second, dcq, dkv, mem, d_own, d_a, d_b, d_ab, dw
    )


def self_back_kernel(
    core, vec, resid, part, recv, gresid_two, keep, back, packed, probs, wqkv, xhat, gresid, gone, dpacked, gfirst_own, gfirst_other, dvec, gm
):
    c = core[0]
    vec, resid, part, recv, gresid_two = ready(vec, resid, part, recv, gresid_two)
    gain = vec[1:2]
    dvec[...] = jnp.zeros_like(dvec)

    def norm(s):
        rows = seq_rows(s)
        dy = part[rows, :].astype(F32) + recv[swapped(s), :].astype(F32)
        dx, dg, db = norm_back(resid[rows, :], gain, dy)
        total = gresid_two[rows, :] + dx
        gone[rows, :] = total.astype(BF)

        @pl.when(s < 4)
        def _():
            gresid[rows, :] = total
            dvec[0:1, :] += dg
            dvec[1:2, :] += db

    loop(8, norm, 2)
    flush(gresid, gone)
    keep, back = ready(keep, back)
    gm[...] = (nt(gone[:, half_lanes(c)], keep[:DH, :]) + nt(gone[:, half_lanes(1 - c)], back[DH:, :])).astype(BF)
    packed, probs = ready(packed, probs)

    def att(s):
        rows = seq_rows(s)
        dq, dk, dv = attend_back(
            gm[rows, :], packed[rows, 0:DH], packed[rows, DH : 2 * DH], packed[rows, 2 * DH :], probs[s]
        )
        dpacked[rows, 0:DH] = dq
        dpacked[rows, DH : 2 * DH] = dk
        dpacked[rows, 2 * DH :] = dv

    loop(8, att, 2)
    flush(dpacked)
    wqkv, xhat = ready(wqkv, xhat)
    half = gfirst_own.shape[0]
    for b, dst in ((half, gfirst_other), (0, gfirst_own)):
        term = nt(dpacked[b : b + half, :], wqkv[...])
        dst[...] = term.astype(BF)
        flush(dst)
        dvec[2:3, :] += jnp.sum(term * xhat[b : b + half, :], 0, keepdims=True)
        dvec[3:4, :] += jnp.sum(term, 0, keepdims=True)


def dself_kernel(offs, core, mixed, mixed_other, gone, first, dpacked, dvec_two, dvec_one, *refs):
    outs, dw, vecs = refs[:4], refs[4], refs[5]
    mixed, mixed_other, gone = ready(mixed, mixed_other, gone)
    out_grad(dw, 0, core[0], mixed, mixed_other, gone)
    first, dpacked, dvec_two, dvec_one = ready(first, dpacked, dvec_two, dvec_one)
    for b in range(0, D, 256):
        dw[b : b + 256, DH : 4 * DH] = tn(first[:, b : b + 256], dpacked[...]).astype(BF)
    vecs[...] = jnp.zeros_like(vecs)
    for i, (v, row) in enumerate(((dvec_one, 2), (dvec_one, 0), (dvec_two, 0), (dvec_one, 3), (dvec_one, 1), (dvec_two, 1))):
        vecs[i : i + 1, :] = v[row : row + 1, :]
    dw[:, 4 * DH :] = jnp.transpose(vecs[...]).astype(BF)
    send_out(dw, offs, outs)


def self_back_and_grads_kernel(
    offs, core, vec, resid, part, recv, gresid_two, keep, back, packed, probs, wqkv, xhat, mixed, mixed_other, first, dvec_two,
    gresid, gfirst_own, gfirst_other, d_own, d_a, d_b, d_ab, gone, dpacked, dvec, gm, dw, vecs
):
    self_back_kernel(
        core, vec, resid, part, recv, gresid_two, keep, back, packed, probs, wqkv, xhat,
        gresid, gone, dpacked, gfirst_own, gfirst_other, dvec, gm
    )
    dself_kernel(offs, core, mixed, mixed_other, gone, first, dpacked, dvec_two, dvec, d_own, d_a, d_b, d_ab, dw, vecs)


def tokens_back_kernel(vec, tok, part, recv, gresid, gmem, gmem_recv, gtok, gmemory, token):
    token[...] = jnp.zeros_like(token)
    vec, tok, part, recv, gresid = ready(vec, tok, part, recv, gresid)
    gain = vec[0:1]

    def norm(s):
        rows = seq_rows(s)
        dy = part[rows, :].astype(F32) + recv[rows, :].astype(F32)
        dx, _, _ = norm_back(tok[rows, :].astype(F32), gain, dy)
        gtok[rows, :] = (gresid[rows, :] + dx).astype(BF)

    loop(4, norm)
    flush(gtok)
    gmem, gmem_recv = ready(gmem, gmem_recv)
    gmemory[...] = (gmem[...].astype(F32) + gmem_recv[...].astype(F32)).astype(BF)


MERGES = {"pass": (2, 1), "half": (3, 2), "near": (2, 2), "last": (2, 1)}
MERGES.update({"tail": (6, 1), "tail_near": (3, 1), "send": (3, 3), "send_near": (2, 1), "levels": (3, 2), "columns": (2, 3), "side": (3, 2)})


def merge_kernel(kinds, beside, *refs):
    if beside:
        n_in, (i, j) = sum(MERGES[kind][0] for kind in kinds), beside
        outs = list(refs[n_in:])
        wide, width = outs[i], outs[i].shape[1] - refs[n_in - 2].shape[1]
        outs[i] = wide.at[:, :width]
        outs.insert(j, wide.at[:, width:])
        refs = (*refs[:n_in], *outs)
    at, out = 0, sum(MERGES[kind][0] for kind in kinds)
    for kind in kinds:
        ins, outs = refs[at : at + MERGES[kind][0]], refs[out : out + MERGES[kind][1]]
        at, out = at + len(ins), out + len(outs)
        if kind == "levels":
            half = outs[0].shape[0]
            for i, dst in enumerate(outs):
                rows = slice(i * half, (i + 1) * half)
                for src, (lo, width) in zip(ins[1:], FAR_CUTS):
                    total = ins[0][rows, lo : lo + width].astype(F32) + src[rows, :].astype(F32)
                    dst[:, lo : lo + width] = total.astype(dst.dtype)
        elif kind == "columns":
            blk = outs[0].shape[0]
            for i, (dst, at) in enumerate(((outs[0], 0), (outs[2], 0), (outs[1], 0), (outs[2], blk))):
                rows = slice(i * blk, (i + 1) * blk)
                dst[at : at + blk, :] = (ins[0][rows, :] + ins[1][rows, :].astype(F32)).astype(dst.dtype)
        elif kind == "send" or kind == "send_near":
            blk = outs[0].shape[0]
            for i, dst in enumerate(outs):
                rows = slice((i + 1) * blk, (i + 2) * blk)
                dst[...] = sum(x[rows, :].astype(F32) for x in ins).astype(dst.dtype)
        elif kind == "tail" or kind == "tail_near":
            blk = outs[0].shape[0]
            outs[0][...] = sum(x[:blk, :].astype(F32) for x in ins)
        elif kind == "side":
            blk = outs[0].shape[0]
            outs[0][...] = ins[0][...] + ins[2][:blk, :].astype(F32)
            outs[1][...] = (ins[1][...] + ins[2][blk:, :].astype(F32)).astype(BF)
        elif kind == "half" or kind == "near":
            blk = outs[0].shape[0]
            for i, dst in enumerate(outs):
                rows = slice(i * blk, (i + 1) * blk)
                dst[...] = sum(x[rows, :].astype(F32) for x in ins).astype(dst.dtype)
        else:
            outs[0][...] = sum(x[...].astype(F32) for x in ins).astype(outs[0].dtype)


def merge(jobs, after=(), beside=None):
    ins, outs = [], []
    for kind, *arrays in jobs:
        ins += arrays
        rows, width = arrays[0].shape
        if kind == "levels":
            outs += [sds((rows // 2, width), F32), sds((rows // 2, width), BF)]
            continue
        if kind == "columns":
            outs += [sds((rows // 4, width), F32)] * 2 + [sds((rows // 2, width), BF)]
            continue
        if kind == "send":
            outs += [sds((rows // 4, width), BF)] * 3
            continue
        if kind == "send_near":
            outs.append(sds((rows // 2, width), BF))
            continue
        if kind == "tail" or kind == "tail_near":
            outs.append(sds((rows // (4 if kind == "tail" else 2), width), F32))
            continue
        if kind == "side":
            outs += [sds((rows, width), F32), sds((rows, width), BF)]
            continue
        parts = 1 if kind in ("pass", "last") else 2
        outs.append(sds((rows // parts, width), BF if kind == "pass" else F32))
        outs += [sds((rows // parts, width), BF)] * (parts - 1)
    kinds = [job[0] for job in jobs]
    if beside:
        i, j = beside
        outs[i] = sds((outs[i].shape[0], outs[i].shape[1] + outs[j].shape[1]), outs[i].dtype)
        del outs[j]
    return kernel_call(
        lambda *refs: merge_kernel(kinds, beside, *refs), ins, [VM] * len(ins), outs, cost=1, after=after
    )


def join_kernel(core, mine, got, *outs):
    c = core[0]
    mine, got = ready(mine, got)
    at = 0
    for out in outs[: 2 if mine.shape[1] > 4 * DH else 3]:
        for k in range(out.shape[1] // D):
            out[:, pl.ds(pl.multiple_of(k * D + c * DH, 128), DH)] = mine[:, at : at + DH]
            out[:, pl.ds(pl.multiple_of(k * D + (1 - c) * DH, 128), DH)] = got[:, at : at + DH]
            at += DH
    if mine.shape[1] > at:
        gains, biases, wide = outs[2:]
        rows = mine.shape[0]
        wide[...] = jnp.zeros_like(wide)
        wide[0:rows, :] = mine[:, at:] + got[:, at:]
        turned = jnp.transpose(wide[...])
        gains[...] = turned[0:3, 0:rows]
        biases[...] = turned[3:6, 0:rows]


def join_inner_kernel(core, mine, got, out):
    c = core[0]
    hr = 96
    for k in range(mine.shape[1] // hr):
        a, b = mine[:, k * hr : (k + 1) * hr], got[:, k * hr : (k + 1) * hr]
        out[:, 2 * k * hr : (2 * k + 1) * hr] = jnp.where(c == 0, a, b)
        out[:, (2 * k + 1) * hr : (2 * k + 2) * hr] = jnp.where(c == 0, b, a)


FIRST = 512
LAST = 2 * D - FIRST
CUTS = ((0, 512), (512, 512))
FAR_CUTS = ((0, 256), (256, 384))
LEVELS = 640


class Moves:
    def __init__(self, mesh):
        self.nz, self.nf = mesh.shape["dp"], mesh.shape["fsdp"]
        self.n = self.nz * self.nf
        self.doubling = self.nz == 4 and self.nf == 8

    def permute(self, x, target):
        pairs = [(d, target(d // self.nf, (d % self.nf) // 2, d % 2)) for d in range(self.n)]
        return lax.ppermute(x, AXES, [(a, (z * self.nf) + 2 * yx + c) for a, (z, yx, c) in pairs])

    def sibling(self, x):
        return self.permute(x, lambda z, yx, c: (z, yx, 1 - c))

    def near_z(self, x):
        return self.permute(x, lambda z, yx, c: (z ^ 1, yx, c))

    def far_z(self, x):
        return self.permute(x, lambda z, yx, c: (z ^ 2, yx, c))

    def side_a(self, x):
        return self.permute(x, lambda z, yx, c: (z, yx ^ (1 + c), c))

    def side_b(self, x):
        return self.permute(x, lambda z, yx, c: (z, yx ^ (2 - c), c))

    def opposite_z(self, x):
        return self.permute(x, lambda z, yx, c: (z ^ 3, yx, c))


def per_device(moves, tokens, memory, lengths, cotangent, self_qkv, self_out, cross_q, cross_kv, cross_out, mlp_in, mlp_out, norm_gains, norm_biases):
    seqs, mem_len = memory.shape[0], memory.shape[1]
    rows = seqs * LEN
    place = lax.axis_index(AXES)
    c = place % 2
    chip = place // 2
    core = jnp.reshape(c, (1,)).astype(jnp.int32)
    wr, hr = self_qkv.shape[0], mlp_out.shape[0]
    ff = mlp_in.shape[1]
    fh = ff // 2
    r2, s2 = 2 * rows, 2 * seqs
    wb = D // 16
    pad = -(-mem_len // 16) * 16
    fast = moves.doubling


    def prepare(lens, pairs, after=(), hold=()):
        return kernel_call(
            prepare_kernel,
            [lens, *pairs],
            [SM] + [STAGE] * 6,
            [sds((r2, D), BF)] * 2 + [sds((s2 * pad, D), BF), sds((r2, D), F32)],
            [STAGE] * 4,
            after=after,
            hold=hold,
        )

    def self_attention(pieces, lens, xhat, keep, back, after=()):
        return kernel_call(
            self_kernel,
            [lens, core, offs, *pieces, xhat, keep, back],
            [SM] * 3 + [VM] * 4 + [STAGE] * 3,
            [
                sds((r2, D), BF),
                sds((r2, 3 * DH), BF),
                sds((s2, LEN, DH), BF),
                sds((r2, 3 * DH), BF),
                sds((8, D), F32),
                sds((D, 3 * DH), BF),
            ],
            [STAGE] * 6,
            [pltpu.VMEM((D, 128), BF)],
            cost=6,
            after=after,
        )

    def cross_attention(pieces, mem, vec, tok, comb, recv, keep, back, after=()):
        kv_rows = s2 * pad
        return kernel_call(
            lambda *refs: keys_and_cross_kernel(mem_len, *refs),
            [offs, *pieces, mem, core, vec, tok, comb, recv, keep, back],
            [SM] + [VM] * 4 + [STAGE, SM] + [STAGE] * 6,
            [
                sds((kv_rows, D), BF),
                sds((D, 2 * DH), BF),
                sds((D, DH), BF),
                sds((r2, D), F32),
                sds((r2, D), BF),
                sds((r2, DH), BF),
                sds((s2, pad, DH), BF),
                sds((r2, 3 * DH), BF),
            ],
            [STAGE] * 8,
            cost=12,
            after=after,
        )

    def inner_part(resid_one, comb, recv, vec, w_in, hold=()):
        return kernel_call(
            inner_kernel,
            [resid_one, comb, recv, vec, w_in],
            [STAGE] * 5,
            [sds((r2, D), F32), sds((r2, D), BF), sds((r2, fh), BF), sds((r2, fh), BF)],
            [STAGE] * 4,
            cost=5,
            hold=hold,
        )

    def inner_weight(pieces, hold=()):
        return place_rows(pieces, offs, 0, [(0, fh, 0, wb, 0)], (D, fh), hold)

    def grads(body, ins, specs, ncols, extra=(), scratch=(), cost=5, after=(), hold=()):
        return kernel_call(
            body,
            [offs, *ins],
            [SM, *specs],
            [sds((4 * wb, ncols), BF)] * 4 + list(extra),
            scratch=[pltpu.VMEM((D, ncols), BF), *scratch],
            cost=cost,
            after=after,
            hold=hold,
        )

    def mlp_part(pieces, g, slope, w_in, hidden, third, after=(), hold=()):
        return kernel_call(
            mlp_and_grad_kernel,
            [offs, *pieces, g, slope, w_in, hidden, third],
            [SM] + [VM] * 13,
            [sds((rows, D), BF), sds((3 * rows, D), BF)] + [sds((4 * wb, fh), BF)] * 4,
            scratch=[pltpu.VMEM((r2, fh), BF), pltpu.VMEM((fh, D), BF), pltpu.VMEM((D, fh), BF)],
            cost=11,
            after=after,
            hold=hold,
        )

    def cross_back(resid_two, comb, recv, part, after=()):
        return kernel_call(
            cross_back_and_grads_kernel,
            [
                offs, core, vec, resid_two, comb, recv, part, g, *cout, kv, cq, cprobs, w_cq,
                *cross_mixed, second, mem,
            ],
            [SM] * 2 + [VM] * 16,
            [
                sds((rows, D), BF),
                sds((r2, D), F32),
                sds((r2, D), BF),
                sds((8, D), F32),
                sds(kv.shape, BF),
            ]
            + [sds((4 * wb, 4 * DH), BF)] * 4,
            scratch=[
                pltpu.VMEM((r2, D), BF),
                pltpu.VMEM((r2, DH), BF),
                pltpu.VMEM((r2, DH), BF),
                pltpu.VMEM((D, 4 * DH), BF),
            ],
            cost=14,
            after=after,
            limit=24 << 20,
        )

    def self_back(gsecond, recv, gresid_two, after=()):
        return kernel_call(
            self_back_and_grads_kernel,
            [
                offs, core, vec, resid_one, gsecond, recv, gresid_two, *out, packed, probs, w_qkv, xhat,
                *self_mixed, first, dvec_two,
            ],
            [SM] * 2 + [STAGE] * 15,
            [sds((rows, D), F32), sds((rows, D), BF), sds((rows, D), BF)]
            + [sds((4 * wb, 4 * DH + 128), BF)] * 4,
            scratch=[
                pltpu.VMEM((r2, D), BF),
                pltpu.VMEM((r2, 3 * DH), BF),
                pltpu.VMEM((8, D), F32),
                pltpu.VMEM((r2, DH), BF),
                pltpu.VMEM((D, 4 * DH + 128), BF),
                pltpu.VMEM((128, D), F32),
            ],
            cost=11,
            after=after,
        )

    def tokens_back(recv, gmem_recv, after=()):
        return kernel_call(
            tokens_back_kernel,
            [vec, tokens.reshape(rows, D), gfirst, recv, gresid_one, gmem, gmem_recv],
            [STAGE] * 7,
            [sds((rows, D), BF), sds(gmem.shape, BF), sds((8, 128), F32)],
            [STAGE] * 3,
            cost=4,
            after=after,
        )

    sib = moves.sibling
    pairs = []
    for x in (tokens.reshape(rows, D), cotangent.reshape(rows, D), memory):
        pairs += [x, sib(x)]
    lens = jnp.concatenate([lengths, sib(lengths)], 0)


    bits = jnp.arange(4, dtype=jnp.int32)
    if fast:
        plane = jnp.stack([jnp.int32(0), 1 + c, 2 - c, jnp.int32(3)]).astype(jnp.int32)
        z, yx = chip // 4, chip % 4
        chips = ((z ^ bits)[None, :] * 4 + (yx ^ plane)[:, None]).reshape(16).astype(jnp.int32)
    else:
        chips = jnp.arange(16, dtype=jnp.int32)
    turned = ((chips // 8) ^ c) * 8 + chips % 8
    offs = jnp.stack([chips, turned]).astype(jnp.int32)
    widths = (4 * DH + 128, 4 * DH, 4 * DH)

    if fast:
        width = widths[0] + widths[1]
        keep, send = kernel_call(
            pack_kernel,
            [core, self_qkv, self_out, cross_q, cross_kv, cross_out, norm_gains, norm_biases],
            [SM] + ["stage"] * 7,
            [sds((wr, width), BF)] * 2,
            scratch=[pltpu.VMEM((128, 128), F32)],
            cost=1,
            limit=60 << 20,
        )
        last, both, one = kernel_call(
            order_kernel,
            [core, keep, sib(send), mlp_out],
            [SM] + [VM] * 3,
            [sds((2 * wr, LAST), BF), sds((2 * wr, width), BF), sds((2 * wr, widths[0]), BF)],
            cost=1,
            after=[pairs[1], pairs[3]],
        )
        near, far, side_a, side_b = moves.near_z, moves.far_z, moves.side_a, moves.side_b
        near_both, along = near(both), [far(one), moves.opposite_z(one)]
        tok, g, mem, xhat = prepare(lens, pairs, hold=(one, both))
        last = tie(last, tok)
        a_last, b_last = side_a(last), side_b(last)
        one, two = cats(
            [
                [(one, 0, widths[0]), (near_both, 0, widths[0]), *whole(*along)],
                [(both, widths[0], widths[1]), (near_both, widths[0], widths[1])],
            ],
            after=(tok, a_last, b_last),
        )
        keep, send = kernel_call(
            pack_inner_kernel, [core, mlp_in], [SM, VM], [sds((wr, fh), BF)] * 2, cost=1, after=(one,)
        )
        (three,) = kernel_call(
            order_mlp_kernel, [core, keep, sib(send), mlp_out], [SM] + [VM] * 3, [sds((2 * wr, 4 * DH + FIRST), BF)], cost=1
        )
        ab_last = tie(a_last, one)
        a1, b1, far_two, near_three, ab_last = side_a(one), side_b(one), far(two), near(three), side_b(ab_last)
        a1 = tie(a1, b1)
        two, last, three = cats(
            [whole(two, far_two), whole(last, a_last, b_last, ab_last), whole(three, near_three)], after=(a1,)
        )
        ab1, a2, b2, far_three = side_b(a1), side_a(two), side_b(two), far(three)
        a2 = tie(a2, b2, ab1)
        three, four = cats(
            [
                [(three, 0, 4 * DH), (far_three, 0, 4 * DH)],
                [(three, 4 * DH, FIRST), (far_three, 4 * DH, FIRST)],
            ],
            after=(a2,),
        )
        out = out_rows([one, a1, b1, ab1], offs, 3 * DH)
        out = (out, sib(out))
        three, a2 = tie(three, out[1]), tie(a2, out[1])
        last = tie(last, out[1])
        ab2, a3, b3, far_last = side_b(a2), side_a(three), side_b(three), far(last)
        first, packed, probs, comb, vec, w_qkv = self_attention([one, a1, b1, ab1], lens, xhat, *out, after=(three,))
        cout = out_rows([two, a2, b2, ab2], offs, 0)
        a3 = tie(a3, b3, comb, far_last, cout)
        four = tie(four, a3)
        parts = cats([[(last, lo, width), (far_last, lo, width)] for lo, width in CUTS], after=(four,))
        comb = tie(comb, four)
        cout = (cout, sib(cout))
        self_mixed = (comb, sib(comb))
        ab3, a4, b4, near_a = side_b(a3), side_a(four), side_b(four), near(parts[0])
        kv, w_ckv, w_cq, resid_one, second, cq, cprobs, comb = cross_attention(
            [two, a2, b2, ab2], mem, vec, tok, *self_mixed, *cout
        )
        comb = tie(comb, ab3, a4, b4, near_a)
        cross_mixed, ab4, near_b = (comb, sib(comb)), side_b(tie(a4, comb)), near(tie(parts[1], comb))
        hold = [kv, cprobs, cq, w_cq, *cout, w_ckv, second]
        w_in = inner_weight([three, a3, b3, ab3], hold)
        resid_two, third, hidden, slope = inner_part(resid_one, *cross_mixed, vec, w_in, hold)
        last = [four, a4, b4, ab4, last, far_last, near_a, near_b]
    else:
        tok, g, mem, xhat = prepare(lens, pairs)
        everywhere = lambda w: lax.all_gather(w, AXES, axis=0, tiled=True)
        split = lambda w: [w[i * w.shape[0] // 4 : (i + 1) * w.shape[0] // 4] for i in range(4)]

        def col_half(w, groups):
            w = w.reshape(w.shape[0], groups, 2, w.shape[1] // (2 * groups))
            return lax.dynamic_index_in_dim(w, c, 2, keepdims=False).reshape(w.shape[0], -1)

        vectors = jnp.pad(jnp.concatenate([norm_gains, norm_biases], 0).T, ((0, 0), (0, 122)))
        one = jnp.concatenate([col_half(self_qkv, 3), col_half(self_out, 1), vectors], 1)
        two = jnp.concatenate([col_half(w, w.shape[1] // D) for w in (cross_out, cross_q, cross_kv)], 1)
        one, two = split(everywhere(one)), split(everywhere(two))
        three = split(everywhere(col_half(mlp_in, ff // (2 * hr))))
        out, cout = out_rows(one, offs, 3 * DH), out_rows(two, offs, 0)
        out, cout = (out, sib(out)), (cout, sib(cout))
        rowed = everywhere(mlp_out).reshape(moves.n // 2, 2, hr, D)
        rowed = lax.dynamic_index_in_dim(rowed, c, 1, keepdims=False).reshape(16, 2, fh // 32, D)
        rowed = rowed.transpose(1, 0, 2, 3)
        levels = jnp.concatenate([rowed[1].reshape(D, D), rowed[0].reshape(D, D)[:, FIRST:]], 1)
        levels = levels.reshape(4, 4, wb, LAST).transpose(1, 0, 2, 3).reshape(4, 4 * wb, LAST)
        odd = levels[1::2].reshape(8 * wb, LAST)
        last = split(rowed[0].reshape(D, D)[:, :FIRST]) + [levels[0], levels[2]]
        last += [odd[:, lo : lo + width] for lo, width in CUTS]
        hold = ()
        first, packed, probs, comb, vec, w_qkv = self_attention(one, lens, xhat, *out)
        self_mixed = (comb, sib(comb))
        kv, w_ckv, w_cq, resid_one, second, cq, cprobs, comb = cross_attention(
            two, mem, vec, tok, *self_mixed, *cout
        )
        cross_mixed = (comb, sib(comb))
        w_in = inner_weight(three)
        resid_two, third, hidden, slope = inner_part(resid_one, *cross_mixed, vec, w_in)


    near, far, side_a, side_b = moves.near_z, moves.far_z, moves.side_a, moves.side_b
    after = ()

    held = [resid_two, vec]
    d_mlpout = kernel_call(
        dmlpout_kernel,
        [offs, hidden, g],
        [SM, VM, VM],
        [sds((4 * wb, 2 * D - LEVELS), BF)] * 4
        + [sds((8 * wb, LEVELS), BF)]
        + [sds((8 * wb, width), BF) for _, width in FAR_CUTS],
        scratch=[pltpu.VMEM((D, 2 * D - LEVELS), BF), pltpu.VMEM((D, LEVELS), BF)],
        cost=3,
        hold=[*hold, *held, third],
    )
    if fast:
        got_ab1, got_z1 = side_a(d_mlpout[3]), near(d_mlpout[5])
    part, comb, *d_mlpin = mlp_part(last, g, slope, w_in, hidden, third, after=d_mlpout[:1], hold=[*hold, *held])
    if fast:
        (on,) = merge([("pass", d_mlpout[2], got_ab1)], after=(part, got_z1))
        comb = tie(comb, on)
        got_b1, got_a1, got_z2 = side_b(on), side_a(tie(d_mlpout[1], on)), near(tie(d_mlpout[6], on))
        got_ab2, got_a2 = side_a(tie(d_mlpin[3], on)), side_a(tie(d_mlpin[1], on))
        after = (on,)
    recv = sib(comb)
    output, gresid_two, gsecond, dvec_two, dkv, *d_cross = cross_back(resid_two, comb, recv, part, after=after)
    if fast:
        on, kept1, on_far, kept_z, on_z = merge(
            [
                ("pass", d_mlpin[2], got_ab2),
                ("half", d_mlpout[0], got_a1, got_b1),
                ("levels", d_mlpout[4], got_z1, got_z2),
            ],
            after=(dvec_two, got_a2),
        )
        gsecond = tie(gsecond, on)
        got_b2, got_far1, got_far_z = side_b(on), far(on_far), far(on_z)
        got_ab3, got_a3 = side_a(tie(d_cross[3], on)), side_a(tie(d_cross[1], on))
        after = (on,)
    recv = sib(gsecond)
    gresid_one, gfirst, gfirst_other, *d_self = self_back(gsecond, recv, gresid_two, after=after)
    if fast:
        on, kept2, on_far, kept1, on_near, own_z, pass_z, on_z = merge(
            [
                ("pass", d_cross[2], got_ab3),
                ("half", d_mlpin[0], got_a2, got_b2),
                ("near", kept1, got_far1),
                ("columns", kept_z, got_far_z),
            ],
            after=(gfirst, got_a3),
        )
        got_b3, got_ab4 = side_b(on), side_a(tie(d_self[3], on))
        got_far2, got_near1, got_a_z = far(on_far), near(on_near), side_a(on_z)
        after = (on,)
    gmem, gmem_other = kernel_call(
        memory_kernel, [dkv, w_ckv], [VM, VM], [sds((seqs * pad, D), BF)] * 2, cost=3, after=after
    )
    if fast:
        on, kept3, on_far, kept2, on_near, total1, own_z, on_z = merge(
            [
                ("pass", d_self[2], got_ab4),
                ("half", d_cross[0], got_a3, got_b3),
                ("near", kept2, got_far2),
                ("last", kept1, got_near1),
                ("side", own_z, pass_z, got_a_z),
            ],
            after=(gmem,),
        )
        gfirst_other, gmem_other = tie(gfirst_other, on), tie(gmem_other, on)
        got_b4, got_a4 = side_b(on), side_a(tie(d_self[1], on))
        got_far3, got_near2, got_b_z = far(on_far), near(on_near), side_b(on_z)
    recv, gmem_recv = sib(gfirst_other), sib(gmem_other)
    grad_tokens, grad_memory, token = tokens_back(recv, gmem_recv)
    grad_memory = grad_memory.reshape(seqs, pad, D)[:, :mem_len]

    if fast:
        *blocks, total_z, total2 = merge(
            [
                ("send", d_self[0], got_a4, got_b4),
                ("send_near", kept3, got_far3),
                ("last", own_z, got_b_z),
                ("last", kept2, got_near2),
            ],
            after=(token,),
            beside=(0, 3),
        )
        got_far4, got_opp4, got_near = far(blocks[1]), moves.opposite_z(blocks[2]), near(blocks[0])
        width = 4 * DH + 128
        total2 = tie(total2, got_near)
        (total3,) = merge([("tail_near", kept3, got_far3, got_near[:, width:])])
        (total4,) = merge([("tail", d_self[0], got_a4, got_b4, got_near[:, :width], got_far4, got_opp4)])
        total = [total1, total2, total3, total4]

        def own_rows(total):
            mine = lax.dynamic_slice_in_dim(total, c * wr, wr, 0)
            return mine, sib(lax.dynamic_slice_in_dim(total, (1 - c) * wr, wr, 0))

        def join(pair, *shapes, scratch=()):
            return kernel_call(
                join_kernel,
                [core, *pair],
                [SM, STAGE, STAGE],
                [sds(shape, F32) for shape in shapes],
                [STAGE] * len(shapes),
                scratch=scratch,
                cost=1,
            )

        sum_mlpout = jnp.concatenate([total[0][:, :D], jnp.concatenate([total_z, total[0][:, D:]], 1)], 0)
        (grad_in,) = kernel_call(
            join_inner_kernel, [core, *own_rows(total[1])], [SM, VM, VM], [sds((wr, ff), F32)], cost=1
        )
        grad_cout, grad_cq, grad_ckv = join(own_rows(total[2]), (wr, D), (wr, D), (wr, 2 * D))
        grad_out, grad_qkv, own_gains, own_biases = join(
            own_rows(total[3]), (wr, D), (wr, 3 * D), (3, wr), (3, wr), scratch=[pltpu.VMEM((128, 128), F32)]
        )
    else:

        def placed(parts):
            term = jnp.concatenate(parts, 0).astype(F32)
            both = jnp.stack([jnp.where(c == 0, term, 0.0), jnp.where(c == 1, term, 0.0)], 1)
            return lax.psum_scatter(both, AXES, scatter_dimension=0, tiled=True)

        def joined(total, lo, hi, groups):
            return total[:, :, lo:hi].reshape(wr, 2, groups, -1).transpose(0, 2, 1, 3).reshape(wr, -1)

        total = placed(d_cross)
        grad_cout, grad_cq, grad_ckv = (
            joined(total, 0, DH, 1),
            joined(total, DH, 2 * DH, 1),
            joined(total, 2 * DH, 4 * DH, 2),
        )
        total = placed(d_self)
        grad_out, grad_qkv = joined(total, 0, DH, 1), joined(total, DH, 4 * DH, 3)
        vectors = jnp.sum(total[:, :, 4 * DH : 4 * DH + 6], 1).T
        own_gains, own_biases = vectors[:3], vectors[3:]
        grad_in = joined(placed(d_mlpin), 0, fh, ff // (2 * hr))
        first_rows = jnp.concatenate(d_mlpout[:4], 0)
        levels = jnp.stack([d_mlpout[4], jnp.concatenate(d_mlpout[5:], 1)], 0).reshape(2, 2, 4, wb, LEVELS)
        levels = levels.transpose(1, 0, 2, 3, 4).reshape(4, 4, wb, LEVELS)
        levels = jnp.concatenate([levels.transpose(1, 0, 2, 3).reshape(D, LEVELS), first_rows[:, D:]], 1)
        term = jnp.stack([first_rows[:, :D].reshape(16, wb, D), levels.reshape(16, wb, D)], 1).astype(F32)
        term = term.reshape(moves.n // 2, 1, hr, D)
        both = jnp.concatenate([jnp.where(c == 0, term, 0.0), jnp.where(c == 1, term, 0.0)], 1)
        sum_mlpout = lax.psum_scatter(both.reshape(ff, D), AXES, scatter_dimension=0, tiled=True)

    return (
        output.reshape(tokens.shape),
        grad_tokens.reshape(tokens.shape),
        grad_memory,
        grad_qkv,
        grad_out,
        grad_cq,
        grad_ckv,
        grad_cout,
        grad_in,
        sum_mlpout,
        own_gains,
        own_biases,
    )


def solution(mesh):
    batch = P(AXES, None, None)
    rows = P(AXES, None)
    cols = P(None, AXES)
    moves = Moves(mesh)
    in_specs = (batch, batch, P(AXES), batch) + (rows,) * 7 + (cols,) * 2
    out_specs = (batch,) * 3 + (rows,) * 7 + (cols,) * 2
    return jax.shard_map(
        lambda *args: per_device(moves, *args),
        mesh=mesh,
        in_specs=in_specs,
        out_specs=out_specs,
        check_vma=False,
    )
```

```python
import jax
import jax.numpy as jnp
import numpy as np
from jax import lax
from jax.experimental import pallas as pl
from jax.experimental.pallas import tpu as pltpu
from jax.sharding import PartitionSpec as P

AXES = ("dp", "fsdp")
HEADS = 12
HALF = HEADS // 2
HEAD = 64
D = 768
DH = D // 2
LEN = 64
EPS = 1e-06
NEG = -1e30
SCALE = HEAD ** (-0.5)
F32 = jnp.float32
BF = jnp.bfloat16
VMEM_LIMIT = 14 << 20

VM = pl.BlockSpec(memory_space=pltpu.VMEM)
SM = pl.BlockSpec(memory_space=pltpu.SMEM)
ANY = pl.BlockSpec(memory_space=pl.ANY)


def sds(shape, dtype):
    return jax.ShapeDtypeStruct(shape, dtype)


STAGE = VM


class Staged:
    def __init__(self, ref, copy):
        self.ref, self.copy, self.waited = ref, copy, False
        self.shape = ref.shape

    def ready(self):
        if not self.waited:
            self.copy.wait()
            self.waited = True
        return self.ref


PENDING = {}


def flush(*refs):
    for r in refs:
        if id(r) in PENDING:
            PENDING[id(r)].start()
            PENDING[id(r)] = None


def ready(*refs):
    out = [r.ready() if isinstance(r, Staged) else r for r in refs]
    return out[0] if len(out) == 1 else out


def kernel_call(body, ins, in_specs, outs, out_specs=None, scratch=(), cost=5, after=(), limit=None, hold=()):
    n, skip, m, k = len(ins), len(after) + len(hold), len(outs), len(scratch)
    out_specs = [VM] * m if out_specs is None else list(out_specs)
    staged_in = [i for i, spec in enumerate(in_specs) if spec == 'stage']
    staged_out = [i for i, spec in enumerate(out_specs) if spec == 'stage']
    buffers = [pltpu.VMEM(ins[i].shape, ins[i].dtype) for i in staged_in]
    buffers += [pltpu.VMEM(outs[i].shape, outs[i].dtype) for i in staged_out]
    extra = [*buffers, pltpu.SemaphoreType.DMA((len(buffers),))] if buffers else []

    def run(*refs):
        ins, outs = list(refs[:n]), list(refs[n + skip : n + skip + m])
        own = refs[n + skip + m : n + skip + m + k]
        PENDING.clear()
        if not buffers:
            body(*ins, *outs, *own)
            return
        held, sems = refs[n + skip + m + k : -1], refs[-1]
        for j, i in enumerate(staged_in):
            copy = pltpu.make_async_copy(ins[i], held[j], sems.at[j])
            copy.start()
            ins[i] = Staged(held[j], copy)
        copies = []
        for j, i in enumerate(staged_out, len(staged_in)):
            copies.append(pltpu.make_async_copy(held[j], outs[i], sems.at[j]))
            outs[i] = held[j]
            PENDING[id(held[j])] = copies[-1]
        body(*ins, *outs, *own)
        ready(*ins)
        for cp in PENDING.values():
            if cp is not None:
                cp.start()
        for cp in copies:
            cp.wait()

    space = lambda spec: ANY if spec == 'stage' else spec
    return pl.pallas_call(
        run,
        out_shape=list(outs),
        in_specs=[space(spec) for spec in in_specs] + [ANY] * len(after) + [VM] * len(hold),
        out_specs=[space(spec) for spec in out_specs],
        scratch_shapes=[*scratch, *extra],
        compiler_params=pltpu.CompilerParams(vmem_limit_bytes=limit or VMEM_LIMIT),
        cost_estimate=pl.CostEstimate(flops=cost * 7 * 10**9, bytes_accessed=0, transcendentals=0),
    )(*ins, *after, *hold)


def tie(x, *earlier):
    return pl.pallas_call(
        lambda *refs: None,
        out_shape=sds(x.shape, x.dtype),
        in_specs=[ANY] * (1 + len(earlier)),
        out_specs=ANY,
        input_output_aliases={0: 0},
        compiler_params=pltpu.CompilerParams(vmem_limit_bytes=1 << 20),
        cost_estimate=pl.CostEstimate(flops=0, bytes_accessed=0, transcendentals=0),
    )(x, *earlier)


def nn(a, b):
    return lax.dot_general(a, b, (((1,), (0,)), ((), ())), preferred_element_type=F32)


def nt(a, b):
    return lax.dot_general(a, b, (((1,), (1,)), ((), ())), preferred_element_type=F32)


def tn(a, b):
    return lax.dot_general(a, b, (((0,), (0,)), ((), ())), preferred_element_type=F32)


def normalise(v):
    mean = jnp.mean(v, -1, keepdims=True)
    cen = v - mean
    inv = lax.rsqrt(jnp.mean(cen * cen, -1, keepdims=True) + EPS)
    return cen * inv, inv


def norm_back(v, gain, dy):
    xhat, inv = normalise(v)
    dxh = dy * gain
    m1 = jnp.mean(dxh, -1, keepdims=True)
    m2 = jnp.mean(dxh * xhat, -1, keepdims=True)
    dx = inv * (dxh - m1 - xhat * m2)
    return dx, jnp.sum(dy * xhat, 0, keepdims=True), jnp.sum(dy, 0, keepdims=True)


GROUPS = ((0, 256), (256, DH))


def head_of_lane(rows, width):
    return lax.shift_right_logical(lax.broadcasted_iota(jnp.int32, (rows, width), 1), 6)


def spread(q):
    head = head_of_lane(1, q.shape[1])
    parts = [q * (head == h).astype(F32).astype(q.dtype) for h in range(q.shape[1] // HEAD)]
    return jnp.concatenate(parts, 0)


def fold(o):
    head = head_of_lane(LEN, o.shape[1])
    total = jnp.where(head == 0, o[:LEN], 0.0)
    for h in range(1, o.shape[1] // HEAD):
        total = jnp.where(head == h, o[h * LEN : (h + 1) * LEN], total)
    return total


def attend(q, k, v, allowed):
    probs, mixed = [], []
    for lo, hi in GROUPS:
        st = nt(k[:, lo:hi], spread(q[:, lo:hi])) * SCALE
        st = jnp.where(allowed[:, lo:hi], st, NEG)
        e = jnp.exp(st - jnp.max(st, 0, keepdims=True))
        p = (e * (1.0 / jnp.sum(e, 0, keepdims=True))).astype(BF)
        probs.append(p)
        mixed.append(fold(tn(p, v[:, lo:hi])).astype(BF))
    return jnp.concatenate(probs, 1), jnp.concatenate(mixed, 1)


def attend_back(g, q, k, v, p):
    dq, dk, dv = [], [], []
    for lo, hi in GROUPS:
        gs, qs, low = spread(g[:, lo:hi]), spread(q[:, lo:hi]), p[:, lo:hi]
        dp = nt(v[:, lo:hi], gs)
        pf = low.astype(F32)
        t = pf * dp
        ds = (t - pf * jnp.sum(t, 0, keepdims=True)).astype(BF)
        dq.append((fold(tn(ds, k[:, lo:hi])) * SCALE).astype(BF))
        dk.append((nn(ds, qs) * SCALE).astype(BF))
        dv.append(nn(low, gs).astype(BF))
    return [jnp.concatenate(x, 1) for x in (dq, dk, dv)]


def seq_rows(s):
    return pl.ds(pl.multiple_of(s * LEN, LEN), LEN)


def half_lanes(c):
    return pl.ds(pl.multiple_of(c * DH, DH), DH)


def loop(n, body, unroll=1):
    def step(i, carry):
        body(i)
        return carry

    lax.fori_loop(0, n, step, 0, unroll=unroll)


def columns_first(pieces, q, r):
    blk = pieces[0].shape[0] // 4
    return pieces[q], r * blk


def place(pieces, offs_ref, which, cols, targets):
    blk = pieces[0].shape[0] // 4
    for lo, hi, o, step, shift in cols:
        for q in range(4):
            for r in range(4):
                row = pl.multiple_of(offs_ref[which, q * 4 + r] * step + shift, 16)
                targets[o][pl.ds(row, blk), :] = pieces[q][r * blk : (r + 1) * blk, lo:hi]


def place_last(own, far, near, offs_ref, target):
    blk = own.shape[0] // 4
    for q in range(4):
        for r in range(4):
            at = q * blk + (own.shape[0] if r == 3 else 0)
            for (lo, width), part in zip(CUTS, near):
                src, base = ((own, lo), (part, 0), (far, lo), (part, 0))[r]
                for first, end, shift, col in ((0, D, blk, 0), (D, LAST, 0, FIRST - D)):
                    a, b = max(lo, first), min(lo + width, end)
                    if a < b:
                        row = pl.multiple_of(offs_ref[0, q * 4 + r] * (2 * blk) + shift, 16)
                        values = src[at if r % 2 else q * blk : (at if r % 2 else q * blk) + blk, base + a - lo : base + b - lo]
                        target[pl.ds(row, blk), a + col : b + col] = values


def place_rows(pieces, offs, which, cols, shape, hold=()):
    def body(offs_ref, *refs):
        place(refs[:4], offs_ref, which, cols, refs[4:5])

    return kernel_call(body, [offs, *pieces], [SM] + [VM] * 4, [sds(shape, BF)], cost=1, hold=hold)[0]


def out_rows(pieces, offs, lo):
    blk = pieces[0].shape[0] // 4
    return place_rows(pieces, offs, 1, [(lo, lo + DH, 0, blk, 0)], (16 * blk, DH))


def send_out(dw, offs_ref, outs):
    blk = dw.shape[0] // 16
    for q in range(4):
        for r in range(4):
            row = pl.multiple_of(offs_ref[0, q * 4 + r] * blk, 16)
            outs[q][r * blk : (r + 1) * blk, :] = dw[pl.ds(row, blk), :]


def pack_kernel(core, qkv, out, cq, ckv, cout, gains, biases, keep, send, vecs):
    c = core[0]
    qkv, out, cq, ckv, cout, gains, biases = ready(qkv, out, cq, ckv, cout, gains, biases)
    vecs[...] = jnp.zeros_like(vecs)
    vecs[0:3, 0:24] = gains[...].astype(F32)
    vecs[3:6, 0:24] = biases[...].astype(F32)
    rows = keep.shape[0]
    wide = jnp.transpose(vecs[...])[:rows].astype(BF)
    for dst, which in ((keep, c), (send, 1 - c)):
        at = 0
        for w, groups in ((qkv, 3), (out, 1), (None, 0), (cout, 1), (cq, 1), (ckv, 2)):
            if w is None:
                dst[:, at : at + 128] = wide
                at += 128
            for k in range(groups):
                lanes = pl.ds(pl.multiple_of(k * D + which * DH, 128), DH)
                dst[:, at : at + DH] = w[:, lanes]
                at += DH


def pack_inner_kernel(core, win, keep, send):
    c = core[0]
    win = ready(win)
    hr = 96
    for k in range(win.shape[1] // (2 * hr)):
        first = win[:, 2 * k * hr : (2 * k + 1) * hr]
        second = win[:, (2 * k + 1) * hr : (2 * k + 2) * hr]
        keep[:, k * hr : (k + 1) * hr] = jnp.where(c == 0, first, second)
        send[:, k * hr : (k + 1) * hr] = jnp.where(c == 0, second, first)


def order_kernel(core, keep, got, wout, last, *outs):
    c = core[0]
    rows = keep.shape[0]
    for b, (top, under) in enumerate(((keep, got), (got, keep))):
        for dst in outs:
            width = dst.shape[1]
            dst[b * rows : (b + 1) * rows, :] = jnp.where(c == 0, top[:, :width], under[:, :width])
    last[:, :D] = wout[2 * rows :, :]
    last[:, D:] = wout[0 : 2 * rows, FIRST:]


def order_mlp_kernel(core, keep, got, wout, three):
    c = core[0]
    rows, width = keep.shape
    for b, (top, under) in enumerate(((keep, got), (got, keep))):
        three[b * rows : (b + 1) * rows, :width] = jnp.where(c == 0, top[...], under[...])
    three[:, width:] = wout[0 : 2 * rows, :FIRST]


def cats(jobs, after=()):
    arrays, places, outs = [], [], []
    for job in jobs:
        at, outs = 0, [*outs, sds((sum(x.shape[0] for x, _, _ in job), job[0][2]), BF)]
        for x, lo, width in job:
            arrays.append(x)
            places.append((len(outs) - 1, at, lo, width))
            at += x.shape[0]
    n = len(arrays)

    def body(*refs):
        for src, (o, at, lo, width) in zip(refs[:n], places):
            refs[n + o][at : at + src.shape[0], :] = src[:, lo : lo + width]

    return kernel_call(body, arrays, [VM] * n, outs, cost=1, after=after)


def whole(*arrays):
    return [(x, 0, x.shape[1]) for x in arrays]


def prepare_kernel(lens, tok_own, tok_other, cot_own, cot_other, mem_own, mem_other, tok, g, mem, xhat):
    tok_own, tok_other = ready(tok_own, tok_other)
    rows = tok.shape[0] // 2
    seqs, length = mem_own.shape[0], mem_own.shape[1]
    pad = mem.shape[0] // (2 * seqs)
    for b, src in ((0, tok_own), (1, tok_other)):
        tok[b * rows : (b + 1) * rows, :] = src[...]
    flush(tok)

    def norm(s):
        xhat[seq_rows(s), :] = normalise(tok[seq_rows(s), :].astype(F32))[0]

    loop(2 * seqs, norm, 2)
    flush(xhat)
    mem_own, mem_other = ready(mem_own, mem_other)
    for b, src in ((0, mem_own), (1, mem_other)):
        for s in range(seqs):
            at = (b * seqs + s) * pad
            mem[at + length - length % 16 : at + pad, :] = jnp.zeros((pad - length + length % 16, D), BF)
            mem[at : at + length, :] = src[s]
    flush(mem)
    cot_own, cot_other = ready(cot_own, cot_other)
    place = lax.broadcasted_iota(jnp.int32, (LEN, D), 0)
    for b, src in ((0, cot_own), (1, cot_other)):
        for s in range(seqs):
            at = (b * seqs + s) * LEN
            live = (place < lens[b * seqs + s]).astype(F32)
            g[at : at + LEN, :] = (src[s * LEN : (s + 1) * LEN, :].astype(F32) * live).astype(BF)


def self_kernel(lens, core, offs, own, a, b, ab, xhat, keep, back, first, packed, probs, comb, vec, wqkv, gcol):
    c = core[0]
    blk = D // 16
    place((own, a, b, ab), offs, 0, [(4 * DH, 4 * DH + 128, 1, blk, 0), (0, 3 * DH, 0, blk, 0)], (wqkv, gcol))
    xhat = ready(xhat)
    vec[...] = jnp.transpose(gcol[...].astype(F32))[:8]
    gain, bias = vec[0:1], vec[3:4]

    def norm(s):
        first[seq_rows(s), :] = (xhat[seq_rows(s), :] * gain + bias).astype(BF)

    loop(8, norm, 2)
    flush(first)

    def proj(b):
        rows = pl.ds(pl.multiple_of(b * 256, 256), 256)
        packed[rows, :] = nn(first[rows, :], wqkv[...]).astype(BF)

    loop(2, proj)
    flush(packed)
    key = lax.broadcasted_iota(jnp.int32, (LEN, DH), 0)
    query = lax.broadcasted_iota(jnp.int32, (LEN, DH), 1) & (LEN - 1)

    def att(s):
        allowed = (key <= query) & (key < lens[s])
        rows = seq_rows(s)
        p, m = attend(packed[rows, 0:DH], packed[rows, DH : 2 * DH], packed[rows, 2 * DH :], allowed)
        probs[s] = p
        comb[rows, D:] = m

    loop(8, att, 2)
    flush(probs)
    keep, back = ready(keep, back)
    comb[:, half_lanes(c)] = nn(comb[:, D:], keep[:DH, :]).astype(BF)
    comb[:, half_lanes(1 - c)] = nn(comb[:, D:], back[DH:, :]).astype(BF)


def kv_kernel(offs, own, a, b, ab, mem, kv, wckv, wcq):
    blk = D // 16
    place((own, a, b, ab), offs, 0, [(2 * DH, 4 * DH, 0, blk, 0), (DH, 2 * DH, 1, blk, 0)], (wckv, wcq))
    mem = ready(mem)

    def step(b):
        rows = pl.ds(pl.multiple_of(b * 480, 480), 480)
        kv[rows, :] = nn(mem[rows, :], wckv[...]).astype(BF)

    loop(mem.shape[0] // 480, step)


def swapped(s):
    return pl.ds(pl.multiple_of(((s + 4) & 7) * LEN, LEN), LEN)


def cross_kernel(mem_len, core, vec, tok, part, recv, wcq, kv, keep, back, resid, second, cq, probs, comb):
    c = core[0]
    vec, tok, part, recv = ready(vec, tok, part, recv)
    gain, bias = vec[1:2], vec[4:5]

    def norm(s):
        rows = seq_rows(s)
        both = part[rows, 0:D].astype(F32) + recv[swapped(s), 0:D].astype(F32)
        v = tok[rows, :].astype(F32) + both
        resid[rows, :] = v
        xhat, _ = normalise(v)
        second[rows, :] = (xhat * gain + bias).astype(BF)

    loop(8, norm, 2)
    flush(resid, second)
    wcq = ready(wcq)
    cq[...] = nn(second[...], wcq[...]).astype(BF)
    flush(cq)
    kv = ready(kv)
    pad = probs.shape[1]
    allowed = lax.broadcasted_iota(jnp.int32, (pad, DH), 0) < mem_len

    def att(s):
        rows = seq_rows(s)
        keys = pl.ds(pl.multiple_of(s * pad, 16), pad)
        p, m = attend(cq[rows, :], kv[keys, 0:DH], kv[keys, DH:], allowed)
        probs[s] = p
        comb[rows, D:] = m

    loop(8, att, 2)
    flush(probs)
    keep, back = ready(keep, back)
    comb[:, half_lanes(c)] = nn(comb[:, D:], keep[:DH, :]).astype(BF)
    comb[:, half_lanes(1 - c)] = nn(comb[:, D:], back[DH:, :]).astype(BF)


def keys_and_cross_kernel(
    mem_len, offs, own, a, b, ab, mem, core, vec, tok, part, recv, keep, back, kv, wckv, wcq, resid, second, cq, probs, comb
):
    kv_kernel(offs, own, a, b, ab, mem, kv, wckv, wcq)
    cross_kernel(mem_len, core, vec, tok, part, recv, wcq, kv, keep, back, resid, second, cq, probs, comb)


def inner_kernel(resid, part, recv, vec, win, resid_two, third, hidden, slope):
    resid, part, recv, vec = ready(resid, part, recv, vec)
    gain, bias = vec[2:3], vec[5:6]

    def norm(s):
        rows = seq_rows(s)
        both = part[rows, 0:D].astype(F32) + recv[swapped(s), 0:D].astype(F32)
        v = resid[rows, :] + both
        resid_two[rows, :] = v
        xhat, _ = normalise(v)
        third[rows, :] = (xhat * gain + bias).astype(BF)

    loop(8, norm, 2)
    flush(resid_two, third)
    win = ready(win)

    def step(b):
        rows = pl.ds(pl.multiple_of(b * 128, 128), 128)
        x = nn(third[rows, :], win[...])
        cdf = 0.5 + 0.5 * lax.erf(x * (0.5**0.5))
        hidden[rows, :] = (x * cdf).astype(BF)
        density = jnp.exp(x * x * -0.5) * ((2.0 * np.pi) ** -0.5)
        slope[rows, :] = (cdf + x * density).astype(BF)

    loop(4, step)


def mlp_kernel(offs, pieces, plane, far, near, g, slope, win, hidden, own, comb, ginner, wout):
    half = own.shape[0]
    blk = D // 16
    place(pieces, offs, 0, [(0, FIRST, 0, 2 * blk, 0)], (wout.at[:, :FIRST],))
    place_last(plane, far, near, offs, wout)
    g, slope, win = ready(g, slope, win)

    def back(b):
        rows = pl.ds(pl.multiple_of(b * 256, 256), 256)
        gh = nt(g[rows, :], wout[...])
        ginner[rows, :] = (gh * slope[rows, :].astype(F32)).astype(BF)
        comb[rows, :] = nt(ginner[rows, :], win[...]).astype(BF)

    loop(2, back)
    flush(ginner)
    hidden = ready(hidden)
    own[...] = nn(hidden[0:half, :], wout[...]).astype(BF)
    comb[2 * half :, :] = nn(hidden[half:, :], wout[...]).astype(BF)


def dmlpout_kernel(offs, hidden, g, own, a, b, ab, near, *refs):
    far, dw, dz = refs[:-2], refs[-2], refs[-1]
    blk = dw.shape[0] // 16
    for i in range(4):
        part = tn(hidden[:, i * 8 * blk : (i + 1) * 8 * blk], g[...]).astype(BF)
        for k in range(8):
            row, rows = (4 * i + k // 2) * blk, slice(k * blk, (k + 1) * blk)
            if k % 2:
                dz[row : row + blk, :] = part[rows, :LEVELS]
                if LEVELS < D:
                    dw[row : row + blk, D:] = part[rows, LEVELS:]
            else:
                dw[row : row + blk, :D] = part[rows]
    send_out(dw, offs, (own, a, b, ab))
    for q in range(4):
        for r in range(4):
            rows = pl.ds(pl.multiple_of(offs[0, q * 4 + r] * blk, 16), blk)
            at = ((r % 2) * 4 + q) * blk
            if r < 2:
                near[at : at + blk, :] = dz[rows, :]
                continue
            for dst, (lo, width) in zip(far, FAR_CUTS):
                dst[at : at + blk, :] = dz[rows, lo : lo + width]


def mlp_and_grad_kernel(
    offs, pown, pa, pb, pab, plane, far, near_a, near_b, g, slope, win, hidden, third, own, comb, d_own, d_a, d_b, d_ab, ginner, wout, dw
):
    mlp_kernel(offs, (pown, pa, pb, pab), plane, far, (near_a, near_b), g, slope, win, hidden, own, comb, ginner, wout)
    dmlpin_kernel(offs, third, ginner, d_own, d_a, d_b, d_ab, dw)


def dmlpin_kernel(offs, third, ginner, *refs):
    third, ginner = ready(third, ginner)
    outs, dw = refs[:4], refs[4]
    for b in range(0, dw.shape[0], 256):
        dw[b : b + 256, :] = tn(third[:, b : b + 256], ginner[...]).astype(BF)
    send_out(dw, offs, outs)


def cross_back_kernel(
    core, vec, resid, part, recv, own, g, keep, back, kv, cq, probs, wcq, output, gresid, gtwo, dcq, dkv, gsecond, dvec, gm
):
    c = core[0]
    vec, resid, part, recv, own, g = ready(vec, resid, part, recv, own, g)
    gain = vec[2:3]
    dvec[...] = jnp.zeros_like(dvec)

    def norm(s):
        rows = seq_rows(s)
        dy = part[rows, :].astype(F32) + recv[swapped(s), :].astype(F32)
        dx, dg, db = norm_back(resid[rows, :], gain, dy)
        total = g[rows, :].astype(F32) + dx
        gresid[rows, :] = total
        gtwo[rows, :] = total.astype(BF)

        @pl.when(s < 4)
        def _():
            dvec[0:1, :] += dg
            dvec[1:2, :] += db
            extra = own[rows, :].astype(F32) + recv[pl.ds(pl.multiple_of(512 + s * LEN, LEN), LEN), :].astype(F32)
            output[rows, :] = (resid[rows, :] + extra).astype(BF)

    loop(8, norm, 2)
    flush(output, gresid, gtwo, dvec)
    keep, back = ready(keep, back)
    gm[...] = (nt(gtwo[:, half_lanes(c)], keep[:DH, :]) + nt(gtwo[:, half_lanes(1 - c)], back[DH:, :])).astype(BF)
    pad = probs.shape[1]
    kv, cq, probs = ready(kv, cq, probs)

    def att(s):
        rows = seq_rows(s)
        keys = pl.ds(pl.multiple_of(s * pad, 16), pad)
        dq, dk, dv = attend_back(gm[rows, :], cq[rows, :], kv[keys, 0:DH], kv[keys, DH:], probs[s])
        dcq[rows, :] = dq
        dkv[keys, 0:DH] = dk
        dkv[keys, DH:] = dv

    loop(8, att, 2)
    flush(dcq, dkv)
    wcq = ready(wcq)
    gsecond[...] = nt(dcq[...], wcq[...]).astype(BF)


def out_grad(dw, lo, c, mine, other, g):
    cols = half_lanes(c)
    dw[half_lanes(c), lo : lo + DH] = tn(mine[:, D:], g[:, cols]).astype(BF)
    rest = tn(other[256:, D:], g[:256, cols]) + tn(other[:256, D:], g[256:, cols])
    dw[half_lanes(1 - c), lo : lo + DH] = rest.astype(BF)


def dcross_kernel(offs, core, mixed, mixed_other, gtwo, second, dcq, dkv, mem, *refs):
    outs, dw = refs[:4], refs[4]
    mixed, mixed_other, gtwo = ready(mixed, mixed_other, gtwo)
    out_grad(dw, 0, core[0], mixed, mixed_other, gtwo)
    second, dcq = ready(second, dcq)
    dw[:, DH : 2 * DH] = tn(second[...], dcq[...]).astype(BF)
    mem = ready(mem)
    for b in range(0, D, 256):
        dw[b : b + 256, 2 * DH :] = tn(mem[:, b : b + 256], dkv[...]).astype(BF)
    send_out(dw, offs, outs)


def memory_kernel(dkv, wckv, own, other):
    half = own.shape[0]
    for i, dst in ((1, other), (0, own)):
        for b in range(0, half, 480):
            dst[b : b + 480, :] = nt(dkv[i * half + b : i * half + b + 480, :], wckv[...]).astype(BF)


def cross_back_and_grads_kernel(
    offs, core, vec, resid, part, recv, own, g, keep, back, kv, cq, probs, wcq, mixed, mixed_other, second, mem,
    output, gresid, gsecond, dvec, dkv, d_own, d_a, d_b, d_ab, gtwo, dcq, gm, dw
):
    cross_back_kernel(
        core, vec, resid, part, recv, own, g, keep, back, kv, cq, probs, wcq, output, gresid, gtwo, dcq, dkv, gsecond, dvec, gm
    )
    dcross_kernel(
        offs, core, mixed, mixed_other, gtwo, second, dcq, dkv, mem, d_own, d_a, d_b, d_ab, dw
    )


def self_back_kernel(
    core, vec, resid, part, recv, gresid_two, keep, back, packed, probs, wqkv, xhat, gresid, gone, dpacked, gfirst_own, gfirst_other, dvec, gm
):
    c = core[0]
    vec, resid, part, recv, gresid_two = ready(vec, resid, part, recv, gresid_two)
    gain = vec[1:2]
    dvec[...] = jnp.zeros_like(dvec)

    def norm(s):
        rows = seq_rows(s)
        dy = part[rows, :].astype(F32) + recv[swapped(s), :].astype(F32)
        dx, dg, db = norm_back(resid[rows, :], gain, dy)
        total = gresid_two[rows, :] + dx
        gone[rows, :] = total.astype(BF)

        @pl.when(s < 4)
        def _():
            gresid[rows, :] = total
            dvec[0:1, :] += dg
            dvec[1:2, :] += db

    loop(8, norm, 2)
    flush(gresid, gone)
    keep, back = ready(keep, back)
    gm[...] = (nt(gone[:, half_lanes(c)], keep[:DH, :]) + nt(gone[:, half_lanes(1 - c)], back[DH:, :])).astype(BF)
    packed, probs = ready(packed, probs)

    def att(s):
        rows = seq_rows(s)
        dq, dk, dv = attend_back(
            gm[rows, :], packed[rows, 0:DH], packed[rows, DH : 2 * DH], packed[rows, 2 * DH :], probs[s]
        )
        dpacked[rows, 0:DH] = dq
        dpacked[rows, DH : 2 * DH] = dk
        dpacked[rows, 2 * DH :] = dv

    loop(8, att, 2)
    flush(dpacked)
    wqkv, xhat = ready(wqkv, xhat)
    half = gfirst_own.shape[0]
    for b, dst in ((half, gfirst_other), (0, gfirst_own)):
        term = nt(dpacked[b : b + half, :], wqkv[...])
        dst[...] = term.astype(BF)
        flush(dst)
        dvec[2:3, :] += jnp.sum(term * xhat[b : b + half, :], 0, keepdims=True)
        dvec[3:4, :] += jnp.sum(term, 0, keepdims=True)


def dself_kernel(offs, core, mixed, mixed_other, gone, first, dpacked, dvec_two, dvec_one, *refs):
    outs, dw, vecs = refs[:4], refs[4], refs[5]
    mixed, mixed_other, gone = ready(mixed, mixed_other, gone)
    out_grad(dw, 0, core[0], mixed, mixed_other, gone)
    first, dpacked, dvec_two, dvec_one = ready(first, dpacked, dvec_two, dvec_one)
    for b in range(0, D, 256):
        dw[b : b + 256, DH : 4 * DH] = tn(first[:, b : b + 256], dpacked[...]).astype(BF)
    vecs[...] = jnp.zeros_like(vecs)
    for i, (v, row) in enumerate(((dvec_one, 2), (dvec_one, 0), (dvec_two, 0), (dvec_one, 3), (dvec_one, 1), (dvec_two, 1))):
        vecs[i : i + 1, :] = v[row : row + 1, :]
    dw[:, 4 * DH :] = jnp.transpose(vecs[...]).astype(BF)
    send_out(dw, offs, outs)


def self_back_and_grads_kernel(
    offs, core, vec, resid, part, recv, gresid_two, keep, back, packed, probs, wqkv, xhat, mixed, mixed_other, first, dvec_two,
    gresid, gfirst_own, gfirst_other, d_own, d_a, d_b, d_ab, gone, dpacked, dvec, gm, dw, vecs
):
    self_back_kernel(
        core, vec, resid, part, recv, gresid_two, keep, back, packed, probs, wqkv, xhat,
        gresid, gone, dpacked, gfirst_own, gfirst_other, dvec, gm
    )
    dself_kernel(offs, core, mixed, mixed_other, gone, first, dpacked, dvec_two, dvec, d_own, d_a, d_b, d_ab, dw, vecs)


def tokens_back_kernel(vec, tok, part, recv, gresid, gmem, gmem_recv, gtok, gmemory, token):
    token[...] = jnp.zeros_like(token)
    vec, tok, part, recv, gresid = ready(vec, tok, part, recv, gresid)
    gain = vec[0:1]

    def norm(s):
        rows = seq_rows(s)
        dy = part[rows, :].astype(F32) + recv[rows, :].astype(F32)
        dx, _, _ = norm_back(tok[rows, :].astype(F32), gain, dy)
        gtok[rows, :] = (gresid[rows, :] + dx).astype(BF)

    loop(4, norm)
    flush(gtok)
    gmem, gmem_recv = ready(gmem, gmem_recv)
    gmemory[...] = (gmem[...].astype(F32) + gmem_recv[...].astype(F32)).astype(BF)


MERGES = {"pass": (2, 1), "half": (3, 2), "near": (2, 2), "last": (2, 1)}
MERGES.update({"tail": (6, 1), "tail_near": (3, 1), "send": (3, 3), "send_near": (2, 1), "levels": (3, 2), "columns": (2, 3), "side": (3, 2)})


def merge_kernel(kinds, beside, *refs):
    if beside:
        n_in, (i, j) = sum(MERGES[kind][0] for kind in kinds), beside
        outs = list(refs[n_in:])
        wide, width = outs[i], outs[i].shape[1] - refs[n_in - 2].shape[1]
        outs[i] = wide.at[:, :width]
        outs.insert(j, wide.at[:, width:])
        refs = (*refs[:n_in], *outs)
    at, out = 0, sum(MERGES[kind][0] for kind in kinds)
    for kind in kinds:
        ins, outs = refs[at : at + MERGES[kind][0]], refs[out : out + MERGES[kind][1]]
        at, out = at + len(ins), out + len(outs)
        if kind == "levels":
            half = outs[0].shape[0]
            for i, dst in enumerate(outs):
                rows = slice(i * half, (i + 1) * half)
                for src, (lo, width) in zip(ins[1:], FAR_CUTS):
                    total = ins[0][rows, lo : lo + width].astype(F32) + src[rows, :].astype(F32)
                    dst[:, lo : lo + width] = total.astype(dst.dtype)
        elif kind == "columns":
            blk = outs[0].shape[0]
            for i, (dst, at) in enumerate(((outs[0], 0), (outs[2], 0), (outs[1], 0), (outs[2], blk))):
                rows = slice(i * blk, (i + 1) * blk)
                dst[at : at + blk, :] = (ins[0][rows, :] + ins[1][rows, :].astype(F32)).astype(dst.dtype)
        elif kind == "send" or kind == "send_near":
            blk = outs[0].shape[0]
            for i, dst in enumerate(outs):
                rows = slice((i + 1) * blk, (i + 2) * blk)
                dst[...] = sum(x[rows, :].astype(F32) for x in ins).astype(dst.dtype)
        elif kind == "tail" or kind == "tail_near":
            blk = outs[0].shape[0]
            outs[0][...] = sum(x[:blk, :].astype(F32) for x in ins)
        elif kind == "side":
            blk = outs[0].shape[0]
            outs[0][...] = ins[0][...] + ins[2][:blk, :].astype(F32)
            outs[1][...] = (ins[1][...] + ins[2][blk:, :].astype(F32)).astype(BF)
        elif kind == "half" or kind == "near":
            blk = outs[0].shape[0]
            for i, dst in enumerate(outs):
                rows = slice(i * blk, (i + 1) * blk)
                dst[...] = sum(x[rows, :].astype(F32) for x in ins).astype(dst.dtype)
        else:
            outs[0][...] = sum(x[...].astype(F32) for x in ins).astype(outs[0].dtype)


def merge(jobs, after=(), beside=None):
    ins, outs = [], []
    for kind, *arrays in jobs:
        ins += arrays
        rows, width = arrays[0].shape
        if kind == "levels":
            outs += [sds((rows // 2, width), F32), sds((rows // 2, width), BF)]
            continue
        if kind == "columns":
            outs += [sds((rows // 4, width), F32)] * 2 + [sds((rows // 2, width), BF)]
            continue
        if kind == "send":
            outs += [sds((rows // 4, width), BF)] * 3
            continue
        if kind == "send_near":
            outs.append(sds((rows // 2, width), BF))
            continue
        if kind == "tail" or kind == "tail_near":
            outs.append(sds((rows // (4 if kind == "tail" else 2), width), F32))
            continue
        if kind == "side":
            outs += [sds((rows, width), F32), sds((rows, width), BF)]
            continue
        parts = 1 if kind in ("pass", "last") else 2
        outs.append(sds((rows // parts, width), BF if kind == "pass" else F32))
        outs += [sds((rows // parts, width), BF)] * (parts - 1)
    kinds = [job[0] for job in jobs]
    if beside:
        i, j = beside
        outs[i] = sds((outs[i].shape[0], outs[i].shape[1] + outs[j].shape[1]), outs[i].dtype)
        del outs[j]
    return kernel_call(
        lambda *refs: merge_kernel(kinds, beside, *refs), ins, [VM] * len(ins), outs, cost=1, after=after
    )


def join_kernel(core, mine, got, *outs):
    c = core[0]
    mine, got = ready(mine, got)
    at = 0
    for out in outs[: 2 if mine.shape[1] > 4 * DH else 3]:
        for k in range(out.shape[1] // D):
            out[:, pl.ds(pl.multiple_of(k * D + c * DH, 128), DH)] = mine[:, at : at + DH]
            out[:, pl.ds(pl.multiple_of(k * D + (1 - c) * DH, 128), DH)] = got[:, at : at + DH]
            at += DH
    if mine.shape[1] > at:
        gains, biases, wide = outs[2:]
        rows = mine.shape[0]
        wide[...] = jnp.zeros_like(wide)
        wide[0:rows, :] = mine[:, at:] + got[:, at:]
        turned = jnp.transpose(wide[...])
        gains[...] = turned[0:3, 0:rows]
        biases[...] = turned[3:6, 0:rows]


def join_inner_kernel(core, mine, got, out):
    c = core[0]
    hr = 96
    for k in range(mine.shape[1] // hr):
        a, b = mine[:, k * hr : (k + 1) * hr], got[:, k * hr : (k + 1) * hr]
        out[:, 2 * k * hr : (2 * k + 1) * hr] = jnp.where(c == 0, a, b)
        out[:, (2 * k + 1) * hr : (2 * k + 2) * hr] = jnp.where(c == 0, b, a)


FIRST = 512
LAST = 2 * D - FIRST
CUTS = ((0, 512), (512, 512))
FAR_CUTS = ((0, 128), (128, 512))
LEVELS = 640


class Moves:
    def __init__(self, mesh):
        self.nz, self.nf = mesh.shape["dp"], mesh.shape["fsdp"]
        self.n = self.nz * self.nf
        self.doubling = self.nz == 4 and self.nf == 8

    def permute(self, x, target):
        pairs = [(d, target(d // self.nf, (d % self.nf) // 2, d % 2)) for d in range(self.n)]
        return lax.ppermute(x, AXES, [(a, (z * self.nf) + 2 * yx + c) for a, (z, yx, c) in pairs])

    def sibling(self, x):
        return self.permute(x, lambda z, yx, c: (z, yx, 1 - c))

    def near_z(self, x):
        return self.permute(x, lambda z, yx, c: (z ^ 1, yx, c))

    def far_z(self, x):
        return self.permute(x, lambda z, yx, c: (z ^ 2, yx, c))

    def side_a(self, x):
        return self.permute(x, lambda z, yx, c: (z, yx ^ (1 + c), c))

    def side_b(self, x):
        return self.permute(x, lambda z, yx, c: (z, yx ^ (2 - c), c))

    def opposite_z(self, x):
        return self.permute(x, lambda z, yx, c: (z ^ 3, yx, c))


def per_device(moves, tokens, memory, lengths, cotangent, self_qkv, self_out, cross_q, cross_kv, cross_out, mlp_in, mlp_out, norm_gains, norm_biases):
    seqs, mem_len = memory.shape[0], memory.shape[1]
    rows = seqs * LEN
    place = lax.axis_index(AXES)
    c = place % 2
    chip = place // 2
    core = jnp.reshape(c, (1,)).astype(jnp.int32)
    wr, hr = self_qkv.shape[0], mlp_out.shape[0]
    ff = mlp_in.shape[1]
    fh = ff // 2
    r2, s2 = 2 * rows, 2 * seqs
    wb = D // 16
    pad = -(-mem_len // 16) * 16
    fast = moves.doubling


    def prepare(lens, pairs, after=(), hold=()):
        return kernel_call(
            prepare_kernel,
            [lens, *pairs],
            [SM] + [STAGE] * 6,
            [sds((r2, D), BF)] * 2 + [sds((s2 * pad, D), BF), sds((r2, D), F32)],
            [STAGE] * 4,
            after=after,
            hold=hold,
        )

    def self_attention(pieces, lens, xhat, keep, back, after=()):
        return kernel_call(
            self_kernel,
            [lens, core, offs, *pieces, xhat, keep, back],
            [SM] * 3 + [VM] * 4 + [STAGE] * 3,
            [
                sds((r2, D), BF),
                sds((r2, 3 * DH), BF),
                sds((s2, LEN, DH), BF),
                sds((r2, 3 * DH), BF),
                sds((8, D), F32),
                sds((D, 3 * DH), BF),
            ],
            [STAGE] * 6,
            [pltpu.VMEM((D, 128), BF)],
            cost=6,
            after=after,
        )

    def cross_attention(pieces, mem, vec, tok, comb, recv, keep, back, after=()):
        kv_rows = s2 * pad
        return kernel_call(
            lambda *refs: keys_and_cross_kernel(mem_len, *refs),
            [offs, *pieces, mem, core, vec, tok, comb, recv, keep, back],
            [SM] + [VM] * 4 + [STAGE, SM] + [STAGE] * 6,
            [
                sds((kv_rows, D), BF),
                sds((D, 2 * DH), BF),
                sds((D, DH), BF),
                sds((r2, D), F32),
                sds((r2, D), BF),
                sds((r2, DH), BF),
                sds((s2, pad, DH), BF),
                sds((r2, 3 * DH), BF),
            ],
            [STAGE] * 8,
            cost=12,
            after=after,
        )

    def inner_part(resid_one, comb, recv, vec, w_in, hold=()):
        return kernel_call(
            inner_kernel,
            [resid_one, comb, recv, vec, w_in],
            [STAGE] * 5,
            [sds((r2, D), F32), sds((r2, D), BF), sds((r2, fh), BF), sds((r2, fh), BF)],
            [STAGE] * 4,
            cost=5,
            hold=hold,
        )

    def inner_weight(pieces, hold=()):
        return place_rows(pieces, offs, 0, [(0, fh, 0, wb, 0)], (D, fh), hold)

    def grads(body, ins, specs, ncols, extra=(), scratch=(), cost=5, after=(), hold=()):
        return kernel_call(
            body,
            [offs, *ins],
            [SM, *specs],
            [sds((4 * wb, ncols), BF)] * 4 + list(extra),
            scratch=[pltpu.VMEM((D, ncols), BF), *scratch],
            cost=cost,
            after=after,
            hold=hold,
        )

    def mlp_part(pieces, g, slope, w_in, hidden, third, after=(), hold=()):
        return kernel_call(
            mlp_and_grad_kernel,
            [offs, *pieces, g, slope, w_in, hidden, third],
            [SM] + [VM] * 13,
            [sds((rows, D), BF), sds((3 * rows, D), BF)] + [sds((4 * wb, fh), BF)] * 4,
            scratch=[pltpu.VMEM((r2, fh), BF), pltpu.VMEM((fh, D), BF), pltpu.VMEM((D, fh), BF)],
            cost=11,
            after=after,
            hold=hold,
        )

    def cross_back(resid_two, comb, recv, part, after=()):
        return kernel_call(
            cross_back_and_grads_kernel,
            [
                offs, core, vec, resid_two, comb, recv, part, g, *cout, kv, cq, cprobs, w_cq,
                *cross_mixed, second, mem,
            ],
            [SM] * 2 + [VM] * 16,
            [
                sds((rows, D), BF),
                sds((r2, D), F32),
                sds((r2, D), BF),
                sds((8, D), F32),
                sds(kv.shape, BF),
            ]
            + [sds((4 * wb, 4 * DH), BF)] * 4,
            scratch=[
                pltpu.VMEM((r2, D), BF),
                pltpu.VMEM((r2, DH), BF),
                pltpu.VMEM((r2, DH), BF),
                pltpu.VMEM((D, 4 * DH), BF),
            ],
            cost=14,
            after=after,
            limit=24 << 20,
        )

    def self_back(gsecond, recv, gresid_two, after=()):
        return kernel_call(
            self_back_and_grads_kernel,
            [
                offs, core, vec, resid_one, gsecond, recv, gresid_two, *out, packed, probs, w_qkv, xhat,
                *self_mixed, first, dvec_two,
            ],
            [SM] * 2 + [STAGE] * 15,
            [sds((rows, D), F32), sds((rows, D), BF), sds((rows, D), BF)]
            + [sds((4 * wb, 4 * DH + 128), BF)] * 4,
            scratch=[
                pltpu.VMEM((r2, D), BF),
                pltpu.VMEM((r2, 3 * DH), BF),
                pltpu.VMEM((8, D), F32),
                pltpu.VMEM((r2, DH), BF),
                pltpu.VMEM((D, 4 * DH + 128), BF),
                pltpu.VMEM((128, D), F32),
            ],
            cost=11,
            after=after,
        )

    def tokens_back(recv, gmem_recv, after=()):
        return kernel_call(
            tokens_back_kernel,
            [vec, tokens.reshape(rows, D), gfirst, recv, gresid_one, gmem, gmem_recv],
            [STAGE] * 7,
            [sds((rows, D), BF), sds(gmem.shape, BF), sds((8, 128), F32)],
            [STAGE] * 3,
            cost=4,
            after=after,
        )

    sib = moves.sibling
    pairs = []
    for x in (tokens.reshape(rows, D), cotangent.reshape(rows, D), memory):
        pairs += [x, sib(x)]
    lens = jnp.concatenate([lengths, sib(lengths)], 0)


    bits = jnp.arange(4, dtype=jnp.int32)
    if fast:
        plane = jnp.stack([jnp.int32(0), 1 + c, 2 - c, jnp.int32(3)]).astype(jnp.int32)
        z, yx = chip // 4, chip % 4
        chips = ((z ^ bits)[None, :] * 4 + (yx ^ plane)[:, None]).reshape(16).astype(jnp.int32)
    else:
        chips = jnp.arange(16, dtype=jnp.int32)
    turned = ((chips // 8) ^ c) * 8 + chips % 8
    offs = jnp.stack([chips, turned]).astype(jnp.int32)
    widths = (4 * DH + 128, 4 * DH, 4 * DH)

    if fast:
        width = widths[0] + widths[1]
        keep, send = kernel_call(
            pack_kernel,
            [core, self_qkv, self_out, cross_q, cross_kv, cross_out, norm_gains, norm_biases],
            [SM] + ["stage"] * 7,
            [sds((wr, width), BF)] * 2,
            scratch=[pltpu.VMEM((128, 128), F32)],
            cost=1,
            limit=60 << 20,
        )
        last, both, one = kernel_call(
            order_kernel,
            [core, keep, sib(send), mlp_out],
            [SM] + [VM] * 3,
            [sds((2 * wr, LAST), BF), sds((2 * wr, width), BF), sds((2 * wr, widths[0]), BF)],
            cost=1,
            after=[pairs[1], pairs[3]],
        )
        near, far, side_a, side_b = moves.near_z, moves.far_z, moves.side_a, moves.side_b
        near_both, along = near(both), [far(one), moves.opposite_z(one)]
        tok, g, mem, xhat = prepare(lens, pairs, hold=(one, both))
        last = tie(last, tok)
        a_last, b_last = side_a(last), side_b(last)
        one, two = cats(
            [
                [(one, 0, widths[0]), (near_both, 0, widths[0]), *whole(*along)],
                [(both, widths[0], widths[1]), (near_both, widths[0], widths[1])],
            ],
            after=(tok, a_last, b_last),
        )
        keep, send = kernel_call(
            pack_inner_kernel, [core, mlp_in], [SM, VM], [sds((wr, fh), BF)] * 2, cost=1, after=(one,)
        )
        (three,) = kernel_call(
            order_mlp_kernel, [core, keep, sib(send), mlp_out], [SM] + [VM] * 3, [sds((2 * wr, 4 * DH + FIRST), BF)], cost=1
        )
        ab_last = tie(a_last, one)
        a1, b1, far_two, near_three, ab_last = side_a(one), side_b(one), far(two), near(three), side_b(ab_last)
        a1 = tie(a1, b1)
        two, last, three = cats(
            [whole(two, far_two), whole(last, a_last, b_last, ab_last), whole(three, near_three)], after=(a1,)
        )
        ab1, a2, b2, far_three = side_b(a1), side_a(two), side_b(two), far(three)
        a2 = tie(a2, b2, ab1)
        three, four = cats(
            [
                [(three, 0, 4 * DH), (far_three, 0, 4 * DH)],
                [(three, 4 * DH, FIRST), (far_three, 4 * DH, FIRST)],
            ],
            after=(a2,),
        )
        out = out_rows([one, a1, b1, ab1], offs, 3 * DH)
        out = (out, sib(out))
        three, a2 = tie(three, out[1]), tie(a2, out[1])
        last = tie(last, out[1])
        ab2, a3, b3, far_last = side_b(a2), side_a(three), side_b(three), far(last)
        first, packed, probs, comb, vec, w_qkv = self_attention([one, a1, b1, ab1], lens, xhat, *out, after=(three,))
        cout = out_rows([two, a2, b2, ab2], offs, 0)
        a3 = tie(a3, b3, comb, far_last, cout)
        four = tie(four, a3)
        parts = cats([[(last, lo, width), (far_last, lo, width)] for lo, width in CUTS], after=(four,))
        comb = tie(comb, four)
        cout = (cout, sib(cout))
        self_mixed = (comb, sib(comb))
        ab3, a4, b4, near_a = side_b(a3), side_a(four), side_b(four), near(parts[0])
        kv, w_ckv, w_cq, resid_one, second, cq, cprobs, comb = cross_attention(
            [two, a2, b2, ab2], mem, vec, tok, *self_mixed, *cout
        )
        comb = tie(comb, ab3, a4, b4, near_a)
        cross_mixed, ab4, near_b = (comb, sib(comb)), side_b(tie(a4, comb)), near(tie(parts[1], comb))
        hold = [kv, cprobs, cq, w_cq, *cout, w_ckv, second]
        w_in = inner_weight([three, a3, b3, ab3], hold)
        resid_two, third, hidden, slope = inner_part(resid_one, *cross_mixed, vec, w_in, hold)
        last = [four, a4, b4, ab4, last, far_last, near_a, near_b]
    else:
        tok, g, mem, xhat = prepare(lens, pairs)
        everywhere = lambda w: lax.all_gather(w, AXES, axis=0, tiled=True)
        split = lambda w: [w[i * w.shape[0] // 4 : (i + 1) * w.shape[0] // 4] for i in range(4)]

        def col_half(w, groups):
            w = w.reshape(w.shape[0], groups, 2, w.shape[1] // (2 * groups))
            return lax.dynamic_index_in_dim(w, c, 2, keepdims=False).reshape(w.shape[0], -1)

        vectors = jnp.pad(jnp.concatenate([norm_gains, norm_biases], 0).T, ((0, 0), (0, 122)))
        one = jnp.concatenate([col_half(self_qkv, 3), col_half(self_out, 1), vectors], 1)
        two = jnp.concatenate([col_half(w, w.shape[1] // D) for w in (cross_out, cross_q, cross_kv)], 1)
        one, two = split(everywhere(one)), split(everywhere(two))
        three = split(everywhere(col_half(mlp_in, ff // (2 * hr))))
        out, cout = out_rows(one, offs, 3 * DH), out_rows(two, offs, 0)
        out, cout = (out, sib(out)), (cout, sib(cout))
        rowed = everywhere(mlp_out).reshape(moves.n // 2, 2, hr, D)
        rowed = lax.dynamic_index_in_dim(rowed, c, 1, keepdims=False).reshape(16, 2, fh // 32, D)
        rowed = rowed.transpose(1, 0, 2, 3)
        levels = jnp.concatenate([rowed[1].reshape(D, D), rowed[0].reshape(D, D)[:, FIRST:]], 1)
        levels = levels.reshape(4, 4, wb, LAST).transpose(1, 0, 2, 3).reshape(4, 4 * wb, LAST)
        odd = levels[1::2].reshape(8 * wb, LAST)
        last = split(rowed[0].reshape(D, D)[:, :FIRST]) + [levels[0], levels[2]]
        last += [odd[:, lo : lo + width] for lo, width in CUTS]
        hold = ()
        first, packed, probs, comb, vec, w_qkv = self_attention(one, lens, xhat, *out)
        self_mixed = (comb, sib(comb))
        kv, w_ckv, w_cq, resid_one, second, cq, cprobs, comb = cross_attention(
            two, mem, vec, tok, *self_mixed, *cout
        )
        cross_mixed = (comb, sib(comb))
        w_in = inner_weight(three)
        resid_two, third, hidden, slope = inner_part(resid_one, *cross_mixed, vec, w_in)


    near, far, side_a, side_b = moves.near_z, moves.far_z, moves.side_a, moves.side_b
    after = ()

    held = [resid_two, vec]
    d_mlpout = kernel_call(
        dmlpout_kernel,
        [offs, hidden, g],
        [SM, VM, VM],
        [sds((4 * wb, 2 * D - LEVELS), BF)] * 4
        + [sds((8 * wb, LEVELS), BF)]
        + [sds((8 * wb, width), BF) for _, width in FAR_CUTS],
        scratch=[pltpu.VMEM((D, 2 * D - LEVELS), BF), pltpu.VMEM((D, LEVELS), BF)],
        cost=3,
        hold=[*hold, *held, third],
    )
    if fast:
        got_ab1, got_z1 = side_a(d_mlpout[3]), far(d_mlpout[5])
    part, comb, *d_mlpin = mlp_part(last, g, slope, w_in, hidden, third, after=d_mlpout[:1], hold=[*hold, *held])
    if fast:
        (on,) = merge([("pass", d_mlpout[2], got_ab1)], after=(part, got_z1))
        comb = tie(comb, on)
        got_b1, got_a1, got_z2 = side_b(on), side_a(tie(d_mlpout[1], on)), far(tie(d_mlpout[6], on))
        got_ab2, got_a2 = side_a(tie(d_mlpin[3], on)), side_a(tie(d_mlpin[1], on))
        after = (on,)
    recv = sib(comb)
    output, gresid_two, gsecond, dvec_two, dkv, *d_cross = cross_back(resid_two, comb, recv, part, after=after)
    if fast:
        on, kept1, on_far, kept_z, on_z = merge(
            [
                ("pass", d_mlpin[2], got_ab2),
                ("half", d_mlpout[0], got_a1, got_b1),
                ("levels", d_mlpout[4], got_z1, got_z2),
            ],
            after=(dvec_two, got_a2),
        )
        gsecond = tie(gsecond, on)
        got_b2, got_far1, got_far_z = side_b(on), far(on_far), near(on_z)
        got_ab3, got_a3 = side_a(tie(d_cross[3], on)), side_a(tie(d_cross[1], on))
        after = (on,)
    recv = sib(gsecond)
    gresid_one, gfirst, gfirst_other, *d_self = self_back(gsecond, recv, gresid_two, after=after)
    if fast:
        on, kept2, on_far, kept1, on_near, own_z, pass_z, on_z = merge(
            [
                ("pass", d_cross[2], got_ab3),
                ("half", d_mlpin[0], got_a2, got_b2),
                ("near", kept1, got_far1),
                ("columns", kept_z, got_far_z),
            ],
            after=(gfirst, got_a3),
        )
        got_b3, got_ab4 = side_b(on), side_a(tie(d_self[3], on))
        got_far2, got_near1, got_a_z = far(on_far), near(on_near), side_a(on_z)
        after = (on,)
    gmem, gmem_other = kernel_call(
        memory_kernel, [dkv, w_ckv], [VM, VM], [sds((seqs * pad, D), BF)] * 2, cost=3, after=after
    )
    if fast:
        on, kept3, on_far, kept2, on_near, total1, own_z, on_z = merge(
            [
                ("pass", d_self[2], got_ab4),
                ("half", d_cross[0], got_a3, got_b3),
                ("near", kept2, got_far2),
                ("last", kept1, got_near1),
                ("side", own_z, pass_z, got_a_z),
            ],
            after=(gmem,),
        )
        gfirst_other, gmem_other = tie(gfirst_other, on), tie(gmem_other, on)
        got_b4, got_a4 = side_b(on), side_a(tie(d_self[1], on))
        got_far3, got_near2, got_b_z = far(on_far), near(on_near), side_b(on_z)
    recv, gmem_recv = sib(gfirst_other), sib(gmem_other)
    grad_tokens, grad_memory, token = tokens_back(recv, gmem_recv)
    grad_memory = grad_memory.reshape(seqs, pad, D)[:, :mem_len]

    if fast:
        *blocks, total_z, total2 = merge(
            [
                ("send", d_self[0], got_a4, got_b4),
                ("send_near", kept3, got_far3),
                ("last", own_z, got_b_z),
                ("last", kept2, got_near2),
            ],
            after=(token,),
            beside=(0, 3),
        )
        got_far4, got_opp4, got_near = far(blocks[1]), moves.opposite_z(blocks[2]), near(blocks[0])
        width = 4 * DH + 128
        total2 = tie(total2, got_near)
        (total3,) = merge([("tail_near", kept3, got_far3, got_near[:, width:])])
        (total4,) = merge([("tail", d_self[0], got_a4, got_b4, got_near[:, :width], got_far4, got_opp4)])
        total = [total1, total2, total3, total4]

        def own_rows(total):
            mine = lax.dynamic_slice_in_dim(total, c * wr, wr, 0)
            return mine, sib(lax.dynamic_slice_in_dim(total, (1 - c) * wr, wr, 0))

        def join(pair, *shapes, scratch=()):
            return kernel_call(
                join_kernel,
                [core, *pair],
                [SM, STAGE, STAGE],
                [sds(shape, F32) for shape in shapes],
                [STAGE] * len(shapes),
                scratch=scratch,
                cost=1,
            )

        sum_mlpout = jnp.concatenate([total[0][:, :D], jnp.concatenate([total_z, total[0][:, D:]], 1)], 0)
        (grad_in,) = kernel_call(
            join_inner_kernel, [core, *own_rows(total[1])], [SM, VM, VM], [sds((wr, ff), F32)], cost=1
        )
        grad_cout, grad_cq, grad_ckv = join(own_rows(total[2]), (wr, D), (wr, D), (wr, 2 * D))
        grad_out, grad_qkv, own_gains, own_biases = join(
            own_rows(total[3]), (wr, D), (wr, 3 * D), (3, wr), (3, wr), scratch=[pltpu.VMEM((128, 128), F32)]
        )
    else:

        def placed(parts):
            term = jnp.concatenate(parts, 0).astype(F32)
            both = jnp.stack([jnp.where(c == 0, term, 0.0), jnp.where(c == 1, term, 0.0)], 1)
            return lax.psum_scatter(both, AXES, scatter_dimension=0, tiled=True)

        def joined(total, lo, hi, groups):
            return total[:, :, lo:hi].reshape(wr, 2, groups, -1).transpose(0, 2, 1, 3).reshape(wr, -1)

        total = placed(d_cross)
        grad_cout, grad_cq, grad_ckv = (
            joined(total, 0, DH, 1),
            joined(total, DH, 2 * DH, 1),
            joined(total, 2 * DH, 4 * DH, 2),
        )
        total = placed(d_self)
        grad_out, grad_qkv = joined(total, 0, DH, 1), joined(total, DH, 4 * DH, 3)
        vectors = jnp.sum(total[:, :, 4 * DH : 4 * DH + 6], 1).T
        own_gains, own_biases = vectors[:3], vectors[3:]
        grad_in = joined(placed(d_mlpin), 0, fh, ff // (2 * hr))
        first_rows = jnp.concatenate(d_mlpout[:4], 0)
        levels = jnp.concatenate([d_mlpout[4], jnp.concatenate(d_mlpout[5:], 1)], 0).reshape(4, 4, wb, LEVELS)
        levels = jnp.concatenate([levels.transpose(1, 0, 2, 3).reshape(D, LEVELS), first_rows[:, D:]], 1)
        term = jnp.stack([first_rows[:, :D].reshape(16, wb, D), levels.reshape(16, wb, D)], 1).astype(F32)
        term = term.reshape(moves.n // 2, 1, hr, D)
        both = jnp.concatenate([jnp.where(c == 0, term, 0.0), jnp.where(c == 1, term, 0.0)], 1)
        sum_mlpout = lax.psum_scatter(both.reshape(ff, D), AXES, scatter_dimension=0, tiled=True)

    return (
        output.reshape(tokens.shape),
        grad_tokens.reshape(tokens.shape),
        grad_memory,
        grad_qkv,
        grad_out,
        grad_cq,
        grad_ckv,
        grad_cout,
        grad_in,
        sum_mlpout,
        own_gains,
        own_biases,
    )


def solution(mesh):
    batch = P(AXES, None, None)
    rows = P(AXES, None)
    cols = P(None, AXES)
    moves = Moves(mesh)
    in_specs = (batch, batch, P(AXES), batch) + (rows,) * 7 + (cols,) * 2
    out_specs = (batch,) * 3 + (rows,) * 7 + (cols,) * 2
    return jax.shard_map(
        lambda *args: per_device(moves, *args),
        mesh=mesh,
        in_specs=in_specs,
        out_specs=out_specs,
        check_vma=False,
    )
```
